32 devices in a mesh: section: 4 (over z), expert: 2 (over y), dp: 4 (over x, core).
Axes of the slice: x: 2, y: 2, z: 4, core: 2. Of those that a mesh axis runs over, the one named last changes fastest.
Arguments:
- tokens: bfloat16 [1024, 2048], P(('expert', 'dp')), may hold values from -6 to 6
- expert_ids: int32 [1024, 2], P(('expert', 'dp')), may hold values from 0 to 7, all different within a row; in each aligned block of 128 rows (0 to 127, 128 to 255, ...) at most 48 rows name the same one
- gate_weights: float32 [1024, 2], P(('expert', 'dp')), may hold values from 0.1 to 0.9
- out_grad: bfloat16 [1024, 2048], P(('expert', 'dp')), may hold values from -6 to 6
- inner_weight: bfloat16 [8, 2048, 4096], P(('expert', 'dp'), None, 'section'), may hold values from -0.125 to 0.125
- outer_weight: bfloat16 [8, 4096, 2048], P(('expert', 'dp'), 'section'), may hold values from -0.09375 to 0.09375
- final_gain: float32 [2048], replicated, may hold values from 0.25 to 1.75
- dec_states: bfloat16 [4, 512, 2048], P('section', 'expert'), may hold values from -6 to 6
- src_lengths: int32 [4], P('expert'), may hold values from 64 to 256
- tgt_lengths: int32 [4], P('expert'), may hold values from 32 to 128
- norm_gain: float32 [4, 2048], P('section'), may hold values from 0.25 to 1.75
- query_weight: bfloat16 [4, 2048, 2048], P('section', 'expert', 'dp'), may hold values from -16 to 16
- key_weight: bfloat16 [4, 2048, 2048], P('section', 'expert', 'dp'), may hold values from -16 to 16
- value_weight: bfloat16 [4, 2048, 2048], P('section', 'expert', 'dp'), may hold values from -0.125 to 0.125
- out_weight: bfloat16 [4, 2048, 2048], P('section', 'dp', 'expert'), may hold values from -0.125 to 0.125
Outputs:
- dec_out: bfloat16 [4, 512, 2048], P('section', 'expert', 'dp')
- token_grad: bfloat16 [1024, 2048], P(('expert', 'dp'), 'section')
The draws below stay inside these ranges and needn't reach their ends.
Inputs may be any that keep to these rules, and one draw needn't show every extreme that they name: `expert_ids`: each token names two different experts; among the 128 tokens of one device no expert is named more than 48 times.
All inputs are finite; a program needn't handle non-finite values.
Results may differ from the reference program's by a relative error of at most 0.014.
The reference program's roundings to bfloat16 on the way count: a program that leaves them out, or rounds other values in their place, can miss the bound.
Values may be sent and summed in bfloat16 or wider, within the bound.
No kernel may reach another device: no remote copies, remote signals or barrier semaphores. Data moves between devices by JAX's collectives and lax.ppermute only.
A program may use at most 128 MiB of HBM per device.

```python
import math
import jax
import jax.numpy as jnp
import numpy as np
from jax import lax

D = 2048
HEAD_DIM = 128
FF = 4096
EXPERTS = 8
TOK_DEV = 128
CAP = 48
TOK = 1024
SRC_LEN = 256
TGT_LEN = 128
SEQ_ALL = 4
DEC_ROWS = 512
LAYERS = 4


def shared_weight(key):
    return jax.random.normal(key, (LAYERS, D, D), jnp.float32) * D ** (-0.5)


def draw_key_weight(key, part):
    base = shared_weight(key)
    return base.astype(jnp.bfloat16)


def draw_query_weight(key, part):
    key = jax.random.fold_in(key, 11)
    return (jax.random.normal(key, (LAYERS, D, D), jnp.float32) * D ** (-0.5)).astype(jnp.bfloat16)


def draw_src_lengths(key, part):
    key = jax.random.fold_in(key, 5)
    first_key, second_key = jax.random.split(key)
    lengths = jax.random.randint(first_key, (SEQ_ALL,), SRC_LEN // 4, SRC_LEN + 1)
    longest = jax.random.randint(second_key, (), 0, SEQ_ALL)
    return jnp.where(jnp.arange(SEQ_ALL) == longest, SRC_LEN, lengths).astype(jnp.int32)


def draw_tgt_lengths(key, part):
    key = jax.random.fold_in(key, 7)
    first_key, second_key = jax.random.split(key)
    lengths = jax.random.randint(first_key, (SEQ_ALL,), TGT_LEN // 4, TGT_LEN + 1)
    longest = jax.random.randint(second_key, (), 0, SEQ_ALL)
    return jnp.where(jnp.arange(SEQ_ALL) == longest, TGT_LEN, lengths).astype(jnp.int32)


def block_scale(key, shape, pieces, low, largest):
    def one(axis_at, shards_of):
        draws = jax.random.uniform(jax.random.fold_in(jax.random.fold_in(key, 6), axis_at), (shards_of,), jnp.float32, low / len(pieces), largest / len(pieces))
        return jnp.repeat(jnp.exp(draws), shape[axis_at] // shards_of).reshape((-1,) + (1,) * (len(shape) - axis_at - 1))

    loudness = one(*pieces[0])
    for cut in pieces[1:]:
        loudness = loudness * one(*cut)
    return loudness


def shared_out(rng, own, number, rows, count, top, limit, skew):
    order = jax.random.permutation(rng, count)
    crowded, usual = portions_of(count, rows * top, limit, skew, True), portions_of(count, rows * top, limit, skew, False)
    places = jnp.arange(count)

    def named(tallies, offset_by):
        used = int((tallies > 0).sum())
        fixed = max(1, used // 4)
        shifted = fixed + (places - fixed + offset_by * (used - fixed)) % max(1, count - fixed)
        return jnp.zeros((count,), jnp.int32).at[order[jnp.where(places < fixed, places, shifted)]].set(jnp.asarray(tallies, jnp.int32))

    tallies = jnp.where(number % 4 == 0, named(crowded, number // 4), named(usual, number - number // 4 - 1))
    mixed = jax.random.permutation(jax.random.fold_in(own, 3), count)
    donor, taker = mixed[0:count // 2 * 2:2], mixed[1:count // 2 * 2:2]
    margin = jnp.minimum(tallies[donor] - 1, limit - tallies[taker]) // 2
    margin = jnp.where((donor == order[0]) | (taker == order[0]) | (tallies[taker] == 0), 0, jnp.maximum(margin, 0))
    shifted = jax.random.randint(jax.random.fold_in(own, 4), (count // 2,), 0, 1 << 20) % (margin + 1)
    tallies = tallies.at[donor].add(-shifted).at[taker].add(shifted)
    members = jnp.searchsorted(jnp.cumsum(tallies), jnp.arange(rows * top), side="right").astype(jnp.int32)
    grid = members.reshape(top, rows).T
    grid = grid[jax.random.permutation(jax.random.fold_in(own, 1), rows)]
    offset_by = jax.random.randint(jax.random.fold_in(own, 2), (rows, 1), 0, top)
    return jnp.take_along_axis(grid, (jnp.arange(top)[None, :] + offset_by) % top, axis=1)


def portions_of(amount, total, reach, lean, full):
    portions = [(1 << 20) // math.isqrt(standing ** lean) + 1 for standing in range(1, amount + 1)]
    largest = reach if full else min(reach, max(-(-total // amount), total * portions[0] // sum(portions)))
    least = 1 if total - largest >= amount - 1 else 0
    given, surplus = [largest] + [least] * (amount - 1), total - largest - least * (amount - 1)
    while surplus > 0:
        candidates = [i for i in range(1, amount) if given[i] < largest] or [i for i in range(1, amount) if given[i] < reach]
        whole, remaining = sum([portions[i] for i in candidates]), surplus
        for i in candidates:
            addition = min(reach - given[i], max(1, remaining * portions[i] // whole), surplus)
            given[i] = given[i] + addition
            surplus = surplus - addition
    return np.array(given)


def normal_values(rng, dims, width, reach, pieces=(), held_as=jnp.bfloat16):
    factor_of = block_scale(rng, dims, pieces, -0.22, 0.18) if pieces else 1.0
    values = jax.random.normal(rng, dims, jnp.float32) * width * factor_of
    return jnp.minimum(jnp.maximum(values, -reach), reach).astype(held_as)


def setup_inputs(seed: int = 0) -> dict:
    key_of = jax.random.split(jax.random.key(seed), 16)
    tokens = normal_values(key_of[0], (TOK, D), 1.0, 6.0, ((0, 8),))
    expert_ids_keys = jax.random.split(jax.random.fold_in(key_of[1], 1), TOK // TOK_DEV)
    expert_ids_turns = jax.random.permutation(jax.random.fold_in(key_of[1], 3), TOK // TOK_DEV)
    expert_ids = jax.vmap(lambda own, number: shared_out(jax.random.fold_in(key_of[1], 2), own, number, TOK_DEV, EXPERTS, 2, CAP, 2))(expert_ids_keys, expert_ids_turns).reshape((TOK, 2))
    gate_weights = jnp.clip(0.1 + 0.79999997 * jax.random.uniform(key_of[2], (TOK, 2), jnp.float32) ** block_scale(key_of[2], (TOK, 2), ((0, 8),), -0.2, 0.2), 0.1, 0.9)
    out_grad = normal_values(key_of[3], (TOK, D), 1.0, 6.0, ((0, 8),))
    inner_weight = normal_values(key_of[4], (EXPERTS, D, FF), D ** -0.5, 0.125, ((0, 8), (2, 4)))
    outer_weight = normal_values(key_of[5], (EXPERTS, FF, D), FF ** -0.5, 0.09375, ((0, 8), (1, 4)))
    final_gain = jnp.clip(1.0 + 0.15 * jax.random.normal(key_of[6], (D,), jnp.float32), 0.25, 1.75)
    dec_states = normal_values(key_of[7], (LAYERS, DEC_ROWS, D), 1.0, 6.0, ((0, 4), (1, 2)))
    src_lengths = draw_src_lengths(jax.random.fold_in(key_of[15], 71), 0)
    tgt_lengths = draw_tgt_lengths(jax.random.fold_in(key_of[15], 71), 0)
    norm_gain = jnp.clip(1.0 + 0.15 * jax.random.normal(key_of[10], (LAYERS, D), jnp.float32), 0.25, 1.75)
    query_weight = draw_query_weight(jax.random.fold_in(key_of[15], 71), 0)
    key_weight = draw_key_weight(jax.random.fold_in(key_of[15], 71), 0)
    value_weight = normal_values(key_of[13], (LAYERS, D, D), D ** -0.5, 0.125, ((0, 4), (1, 2), (2, 4)))
    out_weight = normal_values(key_of[14], (LAYERS, D, D), D ** -0.5, 0.125, ((0, 4), (1, 4), (2, 2)))
    return {"tokens": tokens, "expert_ids": expert_ids, "gate_weights": gate_weights, "out_grad": out_grad, "inner_weight": inner_weight, "outer_weight": outer_weight, "final_gain": final_gain, "dec_states": dec_states, "src_lengths": src_lengths, "tgt_lengths": tgt_lengths, "norm_gain": norm_gain, "query_weight": query_weight, "key_weight": key_weight, "value_weight": value_weight, "out_weight": out_weight}


EPSILON = 1e-05

def normalize(values, gain):
    centre = lax.optimization_barrier(jnp.mean(values, axis=-1, keepdims=True))
    centred = values - centre
    spread = lax.optimization_barrier(jnp.mean(centred * centred, axis=-1, keepdims=True))
    return centred * lax.rsqrt(spread + EPSILON) * gain

def contract_last(left, right):
    return lax.dot_general(left, right, (((1,), (1,)), ((), ())), preferred_element_type=jnp.float32)

def attend(query, keys, values, key_mask):
    sequences = key_mask.shape[0]
    head_count = query.shape[1] // HEAD_DIM
    query_split = query.reshape(sequences, -1, head_count, HEAD_DIM).astype(jnp.float32)
    keys_split = keys.reshape(sequences, -1, head_count, HEAD_DIM).astype(jnp.float32)
    values_split = values.reshape(sequences, -1, head_count, HEAD_DIM).astype(jnp.float32)
    scores = jnp.einsum('bqhd,bkhd->bhqk', query_split, keys_split) * HEAD_DIM ** (-0.5)
    scores = jnp.where(key_mask[:, None, None, :], scores, -1e+30)
    highest = lax.optimization_barrier(jnp.max(scores, axis=-1, keepdims=True))
    weights = jnp.exp(scores - highest)
    probs = (weights / lax.optimization_barrier(jnp.sum(weights, axis=-1, keepdims=True))).astype(jnp.bfloat16)
    context = jnp.einsum('bhqk,bkhd->bqhd', probs.astype(jnp.float32), values_split)
    return context.astype(jnp.bfloat16).reshape(-1, head_count * HEAD_DIM)

def reference(tokens, expert_ids, gate_weights, out_grad, inner_weight, outer_weight, final_gain, dec_states, src_lengths, tgt_lengths, norm_gain, query_weight, key_weight, value_weight, out_weight):
    block_count = TOK // TOK_DEV
    flat_ids = expert_ids.reshape(block_count, TOK_DEV * 2)
    one_hot = (flat_ids[:, :, None] == jnp.arange(EXPERTS, dtype=jnp.int32)[None, None, :]).astype(jnp.int32)
    earlier = jnp.cumsum(one_hot, axis=1) - one_hot
    slot_index = lax.optimization_barrier(jnp.sum(earlier * one_hot, axis=2))
    position = (jnp.arange(block_count, dtype=jnp.int32)[:, None] * CAP + slot_index).reshape(-1).astype(jnp.int32)
    target = flat_ids.reshape(-1).astype(jnp.int32)
    source = jnp.repeat(jnp.arange(TOK, dtype=jnp.int32), 2)
    table = jnp.zeros((EXPERTS, block_count * CAP), jnp.int32).at[target, position].set(source)

    def expert_pass(operands):
        row_index, weight_in, weight_out = operands
        inputs = tokens[row_index]
        grads = out_grad[row_index]
        pre_act = jnp.dot(inputs, weight_in, preferred_element_type=jnp.float32)
        hidden = jax.nn.gelu(pre_act).astype(jnp.bfloat16)
        result = jnp.dot(hidden, weight_out, preferred_element_type=jnp.float32).astype(jnp.bfloat16)
        back = contract_last(grads, weight_out)
        slope = jax.vjp(jax.nn.gelu, pre_act)[1](back)[0].astype(jnp.bfloat16)
        input_grad = contract_last(slope, weight_in).astype(jnp.bfloat16)
        return (result, input_grad)
    results, input_grads = lax.map(expert_pass, (table, inner_weight, outer_weight))
    gates = gate_weights[:, :, None]
    picked = results[target, position].reshape(TOK, 2, D).astype(jnp.float32)
    mixed = lax.optimization_barrier(jnp.sum(gates * picked, axis=1))
    picked_grads = input_grads[target, position].reshape(TOK, 2, D).astype(jnp.float32)
    token_grad = lax.optimization_barrier(jnp.sum(gates * picked_grads, axis=1)).astype(jnp.bfloat16)
    memory = normalize(tokens.astype(jnp.float32) + mixed, final_gain).astype(jnp.bfloat16)
    key_mask = jnp.arange(SRC_LEN, dtype=jnp.int32)[None, :] < src_lengths[:, None]
    row_mask = (jnp.arange(TGT_LEN, dtype=jnp.int32)[None, :] < tgt_lengths[:, None]).reshape(-1, 1)
    layer_outputs = []
    for layer_index in range(LAYERS):
        states = dec_states[layer_index]
        normed = normalize(states.astype(jnp.float32), norm_gain[layer_index]).astype(jnp.bfloat16)
        query = jnp.dot(normed, query_weight[layer_index], preferred_element_type=jnp.float32).astype(jnp.bfloat16)
        keys = jnp.dot(memory, key_weight[layer_index], preferred_element_type=jnp.float32).astype(jnp.bfloat16)
        values = jnp.dot(memory, value_weight[layer_index], preferred_element_type=jnp.float32).astype(jnp.bfloat16)
        context = attend(query, keys, values, key_mask)
        attended = jnp.dot(context, out_weight[layer_index], preferred_element_type=jnp.float32)
        layer_outputs.append((states.astype(jnp.float32) + jnp.where(row_mask, attended, 0.0)).astype(jnp.bfloat16))
    return (jnp.stack(layer_outputs), token_grad)
```

```python
import jax
import jax.numpy as jnp
from jax import lax
from jax.sharding import PartitionSpec as P

HEAD_DIM = 128
SRC_LEN = 256
TGT_LEN = 128


EPSILON = 1e-05


def normalize(values, gain):
    centre = jnp.mean(values, axis=-1, keepdims=True)
    centred = values - centre
    spread = jnp.mean(centred * centred, axis=-1, keepdims=True)
    return centred * lax.rsqrt(spread + EPSILON) * gain


def contract_last(left, right):
    return lax.dot_general(
        left, right, (((1,), (1,)), ((), ())), preferred_element_type=jnp.float32
    )


def shift(value, axis, step):
    size = lax.axis_size(axis)
    return lax.ppermute(value, axis, [(i, (i + step) % size) for i in range(size)])


def swap(value, axis, mask):
    size = lax.axis_size(axis)
    return lax.ppermute(value, axis, [(i, i ^ mask) for i in range(size)])


def sum_sections(partial):
    count = lax.axis_size("section")
    me = lax.axis_index("section")
    width = partial.shape[1] // count

    def piece(owner):
        return lax.dynamic_slice_in_dim(partial, owner * width, width, 1)

    total = piece(me).astype(jnp.float32)
    for step in range(1, count):
        sent = piece(lax.rem(me + step, count)).astype(jnp.bfloat16)
        total = total + shift(sent, "section", step).astype(jnp.float32)
    return total


def gather_sections(mine):
    count = lax.axis_size("section")
    me = lax.axis_index("section")
    width = mine.shape[1]
    whole = jnp.zeros((mine.shape[0], width * count), mine.dtype)
    whole = lax.dynamic_update_slice_in_dim(whole, mine, me * width, 1)
    for step in range(1, count):
        owner = lax.rem(me - step + count, count)
        whole = lax.dynamic_update_slice_in_dim(
            whole, shift(mine, "section", step), owner * width, 1
        )
    return whole


def gather_rows(mine, axis):
    held = mine
    me = lax.axis_index(axis)
    mask = lax.axis_size(axis) // 2
    blocks = [mine]
    while mask >= 1:
        blocks = blocks + [swap(block, axis, mask) for block in blocks]
        mask //= 2
    codes = [0]
    mask = lax.axis_size(axis) // 2
    while mask >= 1:
        codes = codes + [code ^ mask for code in codes]
        mask //= 2
    ordered = []
    for place in range(len(blocks)):
        chosen = blocks[0]
        for code, block in zip(codes[1:], blocks[1:]):
            chosen = jnp.where((me ^ code) == place, block, chosen)
        ordered.append(chosen)
    return jnp.concatenate(ordered, axis=0)


def gather_weight(weight, dimension):
    if lax.axis_size("expert") != 2:
        return lax.all_gather(weight, "expert", axis=dimension, tiled=True)
    other = swap(weight, "expert", 1)
    first = lax.axis_index("expert") == 0
    return jnp.concatenate(
        [jnp.where(first, weight, other), jnp.where(first, other, weight)], axis=dimension
    )


def sum_heads(partial):
    me = lax.axis_index("dp")
    count = lax.axis_size("dp")
    rows, columns = partial.shape
    total = partial.reshape(rows, count, columns // count)
    mask = 1
    while mask < count:
        paired = total.reshape(rows, -1, 2, columns // count)
        bit = (me // mask) % 2
        sent = lax.dynamic_index_in_dim(paired, 1 - bit, 2, False).astype(jnp.bfloat16)
        kept = lax.dynamic_index_in_dim(paired, bit, 2, False)
        total = kept + swap(sent, "dp", mask).astype(jnp.float32)
        mask *= 2
    return total.reshape(rows, columns // count)


def slot_matrix(positions, slots):
    places = lax.broadcasted_iota(jnp.int32, (positions.shape[0], slots), 1)
    return (positions[:, None] == places).astype(jnp.bfloat16)


def attend(query, keys, values, key_mask):
    sequences = key_mask.shape[0]
    head_count = query.shape[1] // HEAD_DIM
    query_split = query.reshape(sequences, -1, head_count, HEAD_DIM)
    keys_split = keys.reshape(sequences, -1, head_count, HEAD_DIM)
    values_split = values.reshape(sequences, -1, head_count, HEAD_DIM)
    scores = jnp.einsum(
        "bqhd,bkhd->bhqk", query_split, keys_split, preferred_element_type=jnp.float32
    ) * HEAD_DIM ** (-0.5)
    scores = jnp.where(key_mask[:, None, None, :], scores, -1e30)
    highest = jnp.max(scores, axis=-1, keepdims=True)
    weights = jnp.exp(scores - highest)
    probs = (weights / jnp.sum(weights, axis=-1, keepdims=True)).astype(jnp.bfloat16)
    context = jnp.einsum("bhqk,bkhd->bqhd", probs, values_split, preferred_element_type=jnp.float32)
    return context.astype(jnp.bfloat16).reshape(-1, head_count * HEAD_DIM)


def exchange(values, group_size, capacity):
    sent = values.reshape(group_size, capacity, values.shape[1])
    arrived = lax.all_to_all(sent, ("expert", "dp"), split_axis=0, concat_axis=0, tiled=True)
    return arrived.reshape(values.shape)


def body(
    tokens,
    expert_ids,
    gate_weights,
    out_grad,
    inner_weight,
    outer_weight,
    final_gain,
    dec_states,
    src_lengths,
    tgt_lengths,
    norm_gain,
    query_weight,
    key_weight,
    value_weight,
    out_weight,
):
    token_count, feature_count = tokens.shape
    group_size = lax.axis_size(("expert", "dp"))
    capacity = 3 * token_count // group_size
    slots = group_size * capacity

    named = expert_ids[:, :, None] == jnp.arange(group_size, dtype=jnp.int32)[None, None, :]
    either = (named[:, 0] | named[:, 1]).astype(jnp.bfloat16)
    row = lax.broadcasted_iota(jnp.int32, (token_count, token_count), 0)
    column = lax.broadcasted_iota(jnp.int32, (token_count, token_count), 1)
    earlier = jnp.dot(
        (column < row).astype(jnp.bfloat16), either, preferred_element_type=jnp.float32
    ).astype(jnp.int32)
    rank = jnp.sum(jnp.where(named, earlier[:, None, :], 0), axis=2)
    position = expert_ids * capacity + rank
    pick_first = slot_matrix(position[:, 0], slots)
    pick_second = slot_matrix(position[:, 1], slots)
    fill = (pick_first + pick_second).T

    def place(values):
        return jnp.dot(fill, values, preferred_element_type=jnp.float32).astype(jnp.bfloat16)

    def combine(arrived):
        first = jnp.dot(pick_first, arrived, preferred_element_type=jnp.float32)
        second = jnp.dot(pick_second, arrived, preferred_element_type=jnp.float32)
        return gate_weights[:, :1] * first + gate_weights[:, 1:] * second

    weight_in = inner_weight[0]
    weight_out = outer_weight[0]
    arrived_rows = exchange(place(tokens), group_size, capacity)
    pre_act = jnp.dot(arrived_rows, weight_in, preferred_element_type=jnp.float32)
    hidden = jax.nn.gelu(pre_act).astype(jnp.bfloat16)
    forward_part = jnp.dot(hidden, weight_out, preferred_element_type=jnp.float32)
    arrived_grads = exchange(place(out_grad), group_size, capacity)
    outputs_home = exchange(forward_part.astype(jnp.bfloat16), group_size, capacity)
    mixed_slice = sum_sections(combine(outputs_home)).astype(jnp.bfloat16)
    mixed = gather_sections(mixed_slice).astype(jnp.float32)
    memory = normalize(tokens.astype(jnp.float32) + mixed, final_gain).astype(jnp.bfloat16)

    back = contract_last(arrived_grads, weight_out)
    slope = jax.vjp(jax.nn.gelu, pre_act)[1](back)[0].astype(jnp.bfloat16)
    backward_part = contract_last(slope, weight_in)
    backward_slice = sum_sections(backward_part).astype(jnp.bfloat16)
    grads_home = exchange(backward_slice, group_size, capacity)
    token_grad = combine(grads_home).astype(jnp.bfloat16)

    states = dec_states[0]
    normed = normalize(states.astype(jnp.float32), norm_gain[0]).astype(jnp.bfloat16)
    full_query = gather_weight(query_weight[0], 0)
    full_key = gather_weight(key_weight[0], 0)
    full_value = gather_weight(value_weight[0], 0)
    full_out = gather_weight(out_weight[0], 1)
    query_sum = jnp.dot(normed, full_query, preferred_element_type=jnp.float32)
    source = gather_rows(memory, "dp")
    key_sum = jnp.dot(source, full_key, preferred_element_type=jnp.float32)
    value_sum = jnp.dot(source, full_value, preferred_element_type=jnp.float32)
    key_mask = jnp.arange(SRC_LEN, dtype=jnp.int32)[None, :] < src_lengths[:, None]
    context = attend(
        query_sum.astype(jnp.bfloat16),
        key_sum.astype(jnp.bfloat16),
        value_sum.astype(jnp.bfloat16),
        key_mask,
    )
    attended = sum_heads(jnp.dot(context, full_out, preferred_element_type=jnp.float32))
    my_columns = attended.shape[1]
    residual = lax.dynamic_slice_in_dim(
        states, lax.axis_index("dp") * my_columns, my_columns, 1
    ).astype(jnp.float32)
    row_mask = (jnp.arange(TGT_LEN, dtype=jnp.int32)[None, :] < tgt_lengths[:, None]).reshape(-1, 1)
    dec_out = (residual + jnp.where(row_mask, attended, 0.0)).astype(jnp.bfloat16)
    return (dec_out[None], token_grad)


def solution(mesh):
    in_specs = (
        P(("expert", "dp"), None),
        P(("expert", "dp"), None),
        P(("expert", "dp"), None),
        P(("expert", "dp"), None),
        P(("expert", "dp"), None, "section"),
        P(("expert", "dp"), "section", None),
        P(),
        P("section", "expert", None),
        P("expert"),
        P("expert"),
        P("section", None),
        P("section", "expert", "dp"),
        P("section", "expert", "dp"),
        P("section", "expert", "dp"),
        P("section", "dp", "expert"),
    )
    out_specs = (P("section", "expert", "dp"), P(("expert", "dp"), "section"))
    return jax.shard_map(body, mesh=mesh, in_specs=in_specs, out_specs=out_specs, check_vma=False)
```

```python
import functools

import jax
import jax.numpy as jnp
from jax import lax
from jax.experimental import pallas as pl
from jax.experimental.pallas import tpu as pltpu
from jax.sharding import PartitionSpec as P

HEAD_DIM = 128
SRC_LEN = 256
TGT_LEN = 128


EPSILON = 1e-05


def normalize(values, gain):
    centre = jnp.mean(values, axis=-1, keepdims=True)
    centred = values - centre
    spread = jnp.mean(centred * centred, axis=-1, keepdims=True)
    return centred * lax.rsqrt(spread + EPSILON) * gain


def contract_last(left, right):
    return lax.dot_general(
        left, right, (((1,), (1,)), ((), ())), preferred_element_type=jnp.float32
    )


def shift(value, axis, step):
    size = lax.axis_size(axis)
    return lax.ppermute(value, axis, [(i, (i + step) % size) for i in range(size)])


def swap(value, axis, mask):
    size = lax.axis_size(axis)
    return lax.ppermute(value, axis, [(i, i ^ mask) for i in range(size)])


def sum_sections(partial):
    count = lax.axis_size("section")
    me = lax.axis_index("section")
    width = partial.shape[1] // count

    def piece(owner):
        return lax.dynamic_slice_in_dim(partial, owner * width, width, 1)

    total = piece(me).astype(jnp.float32)
    for step in range(1, count):
        sent = piece(lax.rem(me + step, count)).astype(jnp.bfloat16)
        total = total + shift(sent, "section", step).astype(jnp.float32)
    return total


def gather_sections(mine):
    count = lax.axis_size("section")
    me = lax.axis_index("section")
    width = mine.shape[1]
    whole = jnp.zeros((mine.shape[0], width * count), mine.dtype)
    whole = lax.dynamic_update_slice_in_dim(whole, mine, me * width, 1)
    for step in range(1, count):
        owner = lax.rem(me - step + count, count)
        whole = lax.dynamic_update_slice_in_dim(
            whole, shift(mine, "section", step), owner * width, 1
        )
    return whole


def gather_rows(mine, axis):
    held = mine
    me = lax.axis_index(axis)
    mask = lax.axis_size(axis) // 2
    blocks = [mine]
    while mask >= 1:
        blocks = blocks + [swap(block, axis, mask) for block in blocks]
        mask //= 2
    codes = [0]
    mask = lax.axis_size(axis) // 2
    while mask >= 1:
        codes = codes + [code ^ mask for code in codes]
        mask //= 2
    ordered = []
    for place in range(len(blocks)):
        chosen = blocks[0]
        for code, block in zip(codes[1:], blocks[1:]):
            chosen = jnp.where((me ^ code) == place, block, chosen)
        ordered.append(chosen)
    return jnp.concatenate(ordered, axis=0)


def gather_weight(weight, dimension):
    if lax.axis_size("expert") != 2:
        return lax.all_gather(weight, "expert", axis=dimension, tiled=True)
    other = swap(weight, "expert", 1)
    first = lax.axis_index("expert") == 0
    return jnp.concatenate(
        [jnp.where(first, weight, other), jnp.where(first, other, weight)], axis=dimension
    )


def sum_heads(partial):
    me = lax.axis_index("dp")
    count = lax.axis_size("dp")
    rows, columns = partial.shape
    total = partial.reshape(rows, count, columns // count)
    mask = 1
    while mask < count:
        paired = total.reshape(rows, -1, 2, columns // count)
        bit = (me // mask) % 2
        sent = lax.dynamic_index_in_dim(paired, 1 - bit, 2, False).astype(jnp.bfloat16)
        kept = lax.dynamic_index_in_dim(paired, bit, 2, False)
        total = kept + swap(sent, "dp", mask).astype(jnp.float32)
        mask *= 2
    return total.reshape(rows, columns // count)


def slot_matrix(positions, slots):
    places = lax.broadcasted_iota(jnp.int32, (positions.shape[0], slots), 1)
    return (positions[:, None] == places).astype(jnp.bfloat16)


def attend(query, keys, values, key_mask):
    sequences = key_mask.shape[0]
    head_count = query.shape[1] // HEAD_DIM
    query_split = query.reshape(sequences, -1, head_count, HEAD_DIM)
    keys_split = keys.reshape(sequences, -1, head_count, HEAD_DIM)
    values_split = values.reshape(sequences, -1, head_count, HEAD_DIM)
    scores = jnp.einsum(
        "bqhd,bkhd->bhqk", query_split, keys_split, preferred_element_type=jnp.float32
    ) * HEAD_DIM ** (-0.5)
    scores = jnp.where(key_mask[:, None, None, :], scores, -1e30)
    highest = jnp.max(scores, axis=-1, keepdims=True)
    weights = jnp.exp(scores - highest)
    probs = (weights / jnp.sum(weights, axis=-1, keepdims=True)).astype(jnp.bfloat16)
    context = jnp.einsum("bhqk,bkhd->bqhd", probs, values_split, preferred_element_type=jnp.float32)
    return context.astype(jnp.bfloat16).reshape(-1, head_count * HEAD_DIM)


def exchange(values, group_size, capacity):
    sent = values.reshape(group_size, capacity, values.shape[1])
    arrived = lax.all_to_all(sent, ("expert", "dp"), split_axis=0, concat_axis=0, tiled=True)
    return arrived.reshape(values.shape)


def gate(value, *after):
    held = lax.optimization_barrier((value,) + after)
    return held


def plane_gather(own):
    over_y = swap(own, "expert", 1)
    over_x = swap(own, "dp", 2)
    far = swap(over_y, "dp", 2)
    near = [own, over_x, over_y, far]
    blocks = []
    for block in near:
        blocks += [block, swap(block, "dp", 1)]
    return blocks


def plane_gather_shared(own, *after):
    count = lax.axis_size("section")
    me = lax.axis_index("section")
    share = own.shape[0] // count
    mine = lax.dynamic_slice_in_dim(own, me * share, share, 0)
    fetched = swap(mine, "expert", 1)
    over_y = lax.dynamic_update_slice_in_dim(jnp.zeros_like(own), fetched, me * share, 0)
    for step in range(1, count):
        owner = lax.rem(me - step + count, count)
        over_y = lax.dynamic_update_slice_in_dim(
            over_y, shift(fetched, "section", step), owner * share, 0
        )
    over_x = swap(own, "dp", 2)
    return own, over_x, over_y


def plane_gather_rest(own, over_x, over_y):
    far = swap(over_y, "dp", 2)
    blocks = []
    for block in (own, over_x, over_y, far):
        blocks += [block, swap(block, "dp", 1)]
    return blocks


def plane_ids(ids):
    held = ids[None]
    for axis, mask in (("dp", 1), ("dp", 2), ("expert", 1)):
        held = jnp.concatenate([held, swap(held, axis, mask)], axis=0)
    return held


def dispatch_kernel(capacity, code_ref, *refs):
    blocks, out_ref = refs[:-1], refs[-1]
    for place, block in enumerate(blocks):
        code = code_ref[place : place + 1, :]
        slot = lax.broadcasted_iota(jnp.int32, (capacity, code.shape[1]), 0)
        pick = jnp.where(slot == code, 1.0, 0.0).astype(jnp.bfloat16)
        rows = jnp.dot(pick, block[...], preferred_element_type=jnp.float32)
        out_ref[place * capacity : (place + 1) * capacity, :] = rows.astype(jnp.bfloat16)


def dispatch(code, blocks, capacity):
    features = blocks[0].shape[1]
    return pl.pallas_call(
        functools.partial(dispatch_kernel, capacity),
        out_shape=jax.ShapeDtypeStruct((len(blocks) * capacity, features), jnp.bfloat16),
        in_specs=[pl.BlockSpec(memory_space=pltpu.VMEM)] * (1 + len(blocks)),
        out_specs=pl.BlockSpec(memory_space=pltpu.VMEM),
        compiler_params=pltpu.CompilerParams(vmem_limit_bytes=40 * 1024 * 1024),
        name="dispatch",
    )(code, *blocks)


def plane_return(values, capacity):
    arrived = [values[:capacity]]
    for place in range(1, values.shape[0] // capacity):
        sent = values[place * capacity : (place + 1) * capacity]
        size = lax.axis_size(("expert", "dp"))
        arrived.append(
            lax.ppermute(sent, ("expert", "dp"), [(i, i ^ place) for i in range(size)])
        )
    return jnp.concatenate(arrived, axis=0)


def small_body(
    tokens,
    expert_ids,
    gate_weights,
    out_grad,
    inner_weight,
    outer_weight,
    final_gain,
    dec_states,
    src_lengths,
    tgt_lengths,
    norm_gain,
    query_weight,
    key_weight,
    value_weight,
    out_weight,
):
    token_count, feature_count = tokens.shape
    group_size = lax.axis_size(("expert", "dp"))
    capacity = 3 * token_count // group_size
    slots = group_size * capacity
    here = lax.axis_index(("expert", "dp"))
    y = lax.axis_index("expert")

    token_blocks = plane_gather(tokens)
    ids = plane_ids(expert_ids.T)
    row = lax.broadcasted_iota(jnp.int32, (token_count, token_count), 0)
    column = lax.broadcasted_iota(jnp.int32, (token_count, token_count), 1)
    named_here = (ids == here).any(axis=1)
    before = jnp.dot(
        named_here.astype(jnp.bfloat16),
        (row < column).astype(jnp.bfloat16),
        preferred_element_type=jnp.float32,
    ).astype(jnp.int32)
    code = jnp.where(named_here, before, -1)

    named = expert_ids[:, :, None] == jnp.arange(group_size, dtype=jnp.int32)[None, None, :]
    either = (named[:, 0] | named[:, 1]).astype(jnp.bfloat16)
    earlier = jnp.dot(
        (column < row).astype(jnp.bfloat16), either, preferred_element_type=jnp.float32
    ).astype(jnp.int32)
    rank = jnp.sum(jnp.where(named, earlier[:, None, :], 0), axis=2)
    position = (expert_ids ^ here) * capacity + rank
    pick_first = slot_matrix(position[:, 0], slots)
    pick_second = slot_matrix(position[:, 1], slots)

    def combine(arrived):
        first = jnp.dot(pick_first, arrived, preferred_element_type=jnp.float32)
        second = jnp.dot(pick_second, arrived, preferred_element_type=jnp.float32)
        return gate_weights[:, :1] * first + gate_weights[:, 1:] * second

    weight_in = inner_weight[0]
    weight_out = outer_weight[0]
    rows = dispatch(code, token_blocks, capacity)

    states = dec_states[0]
    normed = normalize(states.astype(jnp.float32), norm_gain[0]).astype(jnp.bfloat16)
    half = feature_count // 2
    key_top, key_low = key_weight[0, : half // 2], key_weight[0, half // 2 :]
    quarter = normed.shape[0] // lax.axis_size("dp")
    d = lax.axis_index("dp")
    asked = lax.dynamic_slice(normed, (d * quarter, (1 - y) * half), (quarter, half))
    key_top, held_grad, asked, rows = gate(key_top, out_grad, asked, rows)
    grad_parts = plane_gather_shared(held_grad)
    key_top_other = swap(key_top, "expert", 1)
    asked_here = swap(asked, "expert", 1)

    pre_act = jnp.dot(rows, weight_in, preferred_element_type=jnp.float32)
    hidden = jax.nn.gelu(pre_act).astype(jnp.bfloat16)
    forward_part = jnp.dot(hidden, weight_out, preferred_element_type=jnp.float32)
    outputs_home = plane_return(forward_part.astype(jnp.bfloat16), capacity)

    value_own, out_own = value_weight[0], out_weight[0]
    key_low, value_own, out_own, asked_here, over_y, outputs_home = gate(
        key_low, value_own, out_own, asked_here, grad_parts[2], outputs_home
    )
    grad_blocks = plane_gather_rest(grad_parts[0], grad_parts[1], over_y)
    asked_rows = gather_rows(asked_here, "dp")
    query_own = query_weight[0]
    query_there = jnp.dot(asked_rows, query_own, preferred_element_type=jnp.float32)
    key_low_other = swap(key_low, "expert", 1)
    value_other = swap(value_own, "expert", 1)
    query_other = swap(query_there.astype(jnp.bfloat16), "expert", 1)
    out_other = swap(out_own, "expert", 1)

    mixed_slice = sum_sections(combine(outputs_home)).astype(jnp.bfloat16)
    mixed = gather_sections(mixed_slice).astype(jnp.float32)
    memory = normalize(tokens.astype(jnp.float32) + mixed, final_gain).astype(jnp.bfloat16)

    arrived_grads = dispatch(code, grad_blocks, capacity)
    back = contract_last(arrived_grads, weight_out)
    slope = jax.vjp(jax.nn.gelu, pre_act)[1](back)[0].astype(jnp.bfloat16)
    backward_part = contract_last(slope, weight_in).astype(jnp.bfloat16)
    backward_part, memory = gate(backward_part, memory)
    backward_slice = sum_sections(backward_part).astype(jnp.bfloat16)
    grads_home = plane_return(backward_slice, capacity)
    token_grad = combine(grads_home).astype(jnp.bfloat16)

    normed_own = lax.dynamic_slice_in_dim(normed, y * half, half, 1)
    query = (
        jnp.dot(normed_own, query_own, preferred_element_type=jnp.float32)
        + query_other.astype(jnp.float32)
    ).astype(jnp.bfloat16)
    source = gather_rows(memory, "dp")
    first = y == 0

    def ordered(own, other, dimension):
        return jnp.concatenate(
            [jnp.where(first, own, other), jnp.where(first, other, own)], axis=dimension
        )

    full_key = ordered(
        key_weight[0], jnp.concatenate([key_top_other, key_low_other], axis=0), 0
    )
    full_value = ordered(value_own, value_other, 0)
    full_out = ordered(out_own, out_other, 1)
    key_sum = jnp.dot(source, full_key, preferred_element_type=jnp.float32)
    value_sum = jnp.dot(source, full_value, preferred_element_type=jnp.float32)
    key_mask = jnp.arange(SRC_LEN, dtype=jnp.int32)[None, :] < src_lengths[:, None]
    context = attend(
        query, key_sum.astype(jnp.bfloat16), value_sum.astype(jnp.bfloat16), key_mask
    )
    dec_out = finish(context, full_out, states, tgt_lengths)
    return (dec_out[None], token_grad)


def finish(context, full_out, states, tgt_lengths):
    attended = sum_heads(jnp.dot(context, full_out, preferred_element_type=jnp.float32))
    my_columns = attended.shape[1]
    residual = lax.dynamic_slice_in_dim(
        states, lax.axis_index("dp") * my_columns, my_columns, 1
    ).astype(jnp.float32)
    row_mask = (jnp.arange(TGT_LEN, dtype=jnp.int32)[None, :] < tgt_lengths[:, None]).reshape(-1, 1)
    return (residual + jnp.where(row_mask, attended, 0.0)).astype(jnp.bfloat16)


def body(
    tokens,
    expert_ids,
    gate_weights,
    out_grad,
    inner_weight,
    outer_weight,
    final_gain,
    dec_states,
    src_lengths,
    tgt_lengths,
    norm_gain,
    query_weight,
    key_weight,
    value_weight,
    out_weight,
):
    token_count, feature_count = tokens.shape
    group_size = lax.axis_size(("expert", "dp"))
    capacity = 3 * token_count // group_size
    slots = group_size * capacity

    named = expert_ids[:, :, None] == jnp.arange(group_size, dtype=jnp.int32)[None, None, :]
    either = (named[:, 0] | named[:, 1]).astype(jnp.bfloat16)
    row = lax.broadcasted_iota(jnp.int32, (token_count, token_count), 0)
    column = lax.broadcasted_iota(jnp.int32, (token_count, token_count), 1)
    earlier = jnp.dot(
        (column < row).astype(jnp.bfloat16), either, preferred_element_type=jnp.float32
    ).astype(jnp.int32)
    rank = jnp.sum(jnp.where(named, earlier[:, None, :], 0), axis=2)
    position = expert_ids * capacity + rank
    pick_first = slot_matrix(position[:, 0], slots)
    pick_second = slot_matrix(position[:, 1], slots)
    fill = (pick_first + pick_second).T

    def place(values):
        return jnp.dot(fill, values, preferred_element_type=jnp.float32).astype(jnp.bfloat16)

    def combine(arrived):
        first = jnp.dot(pick_first, arrived, preferred_element_type=jnp.float32)
        second = jnp.dot(pick_second, arrived, preferred_element_type=jnp.float32)
        return gate_weights[:, :1] * first + gate_weights[:, 1:] * second

    weight_in = inner_weight[0]
    weight_out = outer_weight[0]
    arrived_rows = exchange(place(tokens), group_size, capacity)
    pre_act = jnp.dot(arrived_rows, weight_in, preferred_element_type=jnp.float32)
    hidden = jax.nn.gelu(pre_act).astype(jnp.bfloat16)
    forward_part = jnp.dot(hidden, weight_out, preferred_element_type=jnp.float32)
    arrived_grads = exchange(place(out_grad), group_size, capacity)
    outputs_home = exchange(forward_part.astype(jnp.bfloat16), group_size, capacity)
    mixed_slice = sum_sections(combine(outputs_home)).astype(jnp.bfloat16)
    mixed = gather_sections(mixed_slice).astype(jnp.float32)
    memory = normalize(tokens.astype(jnp.float32) + mixed, final_gain).astype(jnp.bfloat16)

    back = contract_last(arrived_grads, weight_out)
    slope = jax.vjp(jax.nn.gelu, pre_act)[1](back)[0].astype(jnp.bfloat16)
    backward_part = contract_last(slope, weight_in)
    backward_slice = sum_sections(backward_part).astype(jnp.bfloat16)
    grads_home = exchange(backward_slice, group_size, capacity)
    token_grad = combine(grads_home).astype(jnp.bfloat16)

    states = dec_states[0]
    normed = normalize(states.astype(jnp.float32), norm_gain[0]).astype(jnp.bfloat16)
    full_query = gather_weight(query_weight[0], 0)
    full_key = gather_weight(key_weight[0], 0)
    full_value = gather_weight(value_weight[0], 0)
    full_out = gather_weight(out_weight[0], 1)
    query_sum = jnp.dot(normed, full_query, preferred_element_type=jnp.float32)
    source = gather_rows(memory, "dp")
    key_sum = jnp.dot(source, full_key, preferred_element_type=jnp.float32)
    value_sum = jnp.dot(source, full_value, preferred_element_type=jnp.float32)
    key_mask = jnp.arange(SRC_LEN, dtype=jnp.int32)[None, :] < src_lengths[:, None]
    context = attend(
        query_sum.astype(jnp.bfloat16),
        key_sum.astype(jnp.bfloat16),
        value_sum.astype(jnp.bfloat16),
        key_mask,
    )
    dec_out = finish(context, full_out, states, tgt_lengths)
    return (dec_out[None], token_grad)


def solution(mesh):
    in_specs = (
        P(("expert", "dp"), None),
        P(("expert", "dp"), None),
        P(("expert", "dp"), None),
        P(("expert", "dp"), None),
        P(("expert", "dp"), None, "section"),
        P(("expert", "dp"), "section", None),
        P(),
        P("section", "expert", None),
        P("expert"),
        P("expert"),
        P("section", None),
        P("section", "expert", "dp"),
        P("section", "expert", "dp"),
        P("section", "expert", "dp"),
        P("section", "dp", "expert"),
    )
    out_specs = (P("section", "expert", "dp"), P(("expert", "dp"), "section"))
    small = mesh.shape["expert"] == 2 and mesh.shape["dp"] == 4
    chosen = small_body if small else body
    return jax.shard_map(chosen, mesh=mesh, in_specs=in_specs, out_specs=out_specs, check_vma=False)
```

```python
import functools

import jax
import jax.numpy as jnp
from jax import lax
from jax.experimental import pallas as pl
from jax.experimental.pallas import tpu as pltpu
from jax.sharding import PartitionSpec as P

HEAD_DIM = 128
SRC_LEN = 256
TGT_LEN = 128


EPSILON = 1e-05


def normalize(values, gain):
    centre = jnp.mean(values, axis=-1, keepdims=True)
    centred = values - centre
    spread = jnp.mean(centred * centred, axis=-1, keepdims=True)
    return centred * lax.rsqrt(spread + EPSILON) * gain


def contract_last(left, right):
    return lax.dot_general(
        left, right, (((1,), (1,)), ((), ())), preferred_element_type=jnp.float32
    )


def shift(value, axis, step):
    size = lax.axis_size(axis)
    return lax.ppermute(value, axis, [(i, (i + step) % size) for i in range(size)])


def swap(value, axis, mask):
    size = lax.axis_size(axis)
    return lax.ppermute(value, axis, [(i, i ^ mask) for i in range(size)])


def sum_sections(partial):
    count = lax.axis_size("section")
    me = lax.axis_index("section")
    width = partial.shape[1] // count

    def piece(owner):
        return lax.dynamic_slice_in_dim(partial, owner * width, width, 1)

    total = piece(me).astype(jnp.float32)
    for step in range(1, count):
        sent = piece(lax.rem(me + step, count)).astype(jnp.bfloat16)
        total = total + shift(sent, "section", step).astype(jnp.float32)
    return total


def gather_sections(mine):
    count = lax.axis_size("section")
    me = lax.axis_index("section")
    width = mine.shape[1]
    whole = jnp.zeros((mine.shape[0], width * count), mine.dtype)
    whole = lax.dynamic_update_slice_in_dim(whole, mine, me * width, 1)
    for step in range(1, count):
        owner = lax.rem(me - step + count, count)
        whole = lax.dynamic_update_slice_in_dim(
            whole, shift(mine, "section", step), owner * width, 1
        )
    return whole


def gather_rows(mine, axis):
    held = mine
    me = lax.axis_index(axis)
    mask = lax.axis_size(axis) // 2
    blocks = [mine]
    while mask >= 1:
        blocks = blocks + [swap(block, axis, mask) for block in blocks]
        mask //= 2
    codes = [0]
    mask = lax.axis_size(axis) // 2
    while mask >= 1:
        codes = codes + [code ^ mask for code in codes]
        mask //= 2
    ordered = []
    for place in range(len(blocks)):
        chosen = blocks[0]
        for code, block in zip(codes[1:], blocks[1:]):
            chosen = jnp.where((me ^ code) == place, block, chosen)
        ordered.append(chosen)
    return jnp.concatenate(ordered, axis=0)


def gather_weight(weight, dimension):
    if lax.axis_size("expert") != 2:
        return lax.all_gather(weight, "expert", axis=dimension, tiled=True)
    other = swap(weight, "expert", 1)
    first = lax.axis_index("expert") == 0
    return jnp.concatenate(
        [jnp.where(first, weight, other), jnp.where(first, other, weight)], axis=dimension
    )


def sum_heads(partial):
    me = lax.axis_index("dp")
    count = lax.axis_size("dp")
    rows, columns = partial.shape
    total = partial.reshape(rows, count, columns // count)
    mask = 1
    while mask < count:
        paired = total.reshape(rows, -1, 2, columns // count)
        bit = (me // mask) % 2
        sent = lax.dynamic_index_in_dim(paired, 1 - bit, 2, False).astype(jnp.bfloat16)
        kept = lax.dynamic_index_in_dim(paired, bit, 2, False)
        total = kept + swap(sent, "dp", mask).astype(jnp.float32)
        mask *= 2
    return total.reshape(rows, columns // count)


def slot_matrix(positions, slots):
    places = lax.broadcasted_iota(jnp.int32, (positions.shape[0], slots), 1)
    return (positions[:, None] == places).astype(jnp.bfloat16)


def attend(query, keys, values, key_mask):
    sequences = key_mask.shape[0]
    head_count = query.shape[1] // HEAD_DIM
    query_split = query.reshape(sequences, -1, head_count, HEAD_DIM)
    keys_split = keys.reshape(sequences, -1, head_count, HEAD_DIM)
    values_split = values.reshape(sequences, -1, head_count, HEAD_DIM)
    scores = jnp.einsum(
        "bqhd,bkhd->bhqk", query_split, keys_split, preferred_element_type=jnp.float32
    ) * HEAD_DIM ** (-0.5)
    scores = jnp.where(key_mask[:, None, None, :], scores, -1e30)
    highest = jnp.max(scores, axis=-1, keepdims=True)
    weights = jnp.exp(scores - highest)
    probs = (weights / jnp.sum(weights, axis=-1, keepdims=True)).astype(jnp.bfloat16)
    context = jnp.einsum("bhqk,bkhd->bqhd", probs, values_split, preferred_element_type=jnp.float32)
    return context.astype(jnp.bfloat16).reshape(-1, head_count * HEAD_DIM)


def exchange(values, group_size, capacity):
    sent = values.reshape(group_size, capacity, values.shape[1])
    arrived = lax.all_to_all(sent, ("expert", "dp"), split_axis=0, concat_axis=0, tiled=True)
    return arrived.reshape(values.shape)


def gate(value, *after):
    return lax.optimization_barrier((value,) + after)[0]


def vmem(shape, dtype):
    return pltpu.VMEM(shape, dtype)


def dispatch_kernel(capacity, count, code_ref, *refs):
    blocks, held, sems = refs[:count], refs[count + 2], refs[count + 3]
    copies = [
        pltpu.make_async_copy(block, held.at[place], sems.at[place])
        for place, block in enumerate(blocks)
    ]
    for copy in copies:
        copy.start()
    for place, copy in enumerate(copies):
        copy.wait()
        for which, out_ref in enumerate(refs[count : count + 2]):
            line = which * count + place
            code = code_ref[line : line + 1, :]
            slot = lax.broadcasted_iota(jnp.int32, (capacity, code.shape[1]), 0)
            pick = jnp.where(slot == code, 1.0, 0.0).astype(jnp.bfloat16)
            rows = jnp.dot(pick, held[place], preferred_element_type=jnp.float32)
            out_ref[place * capacity : (place + 1) * capacity, :] = rows.astype(jnp.bfloat16)


def dispatch(code, blocks, capacity):
    rows, features = blocks[0].shape
    count = len(blocks)
    picked = jax.ShapeDtypeStruct((count * capacity, features), jnp.bfloat16)
    return pl.pallas_call(
        functools.partial(dispatch_kernel, capacity, count),
        out_shape=(picked, picked),
        in_specs=[pl.BlockSpec(memory_space=pltpu.VMEM)]
        + [pl.BlockSpec(memory_space=pl.ANY)] * count,
        out_specs=[pl.BlockSpec(memory_space=pltpu.VMEM)] * 2,
        scratch_shapes=[
            vmem((count, rows, features), jnp.bfloat16),
            pltpu.SemaphoreType.DMA((count,)),
        ],
        compiler_params=pltpu.CompilerParams(vmem_limit_bytes=32 * 1024 * 1024),
        cost_estimate=pl.CostEstimate(
            flops=4 * count * capacity * rows * features,
            bytes_accessed=2 * count * (rows + 2 * capacity) * features,
            transcendentals=0,
        ),
        name="dispatch",
    )(code, *blocks)


def send_home(part, codes, capacity):
    size = lax.axis_size(("expert", "dp"))
    arrived = []
    for place, code in enumerate(codes):
        block = part[place * capacity : (place + 1) * capacity]
        if code:
            block = lax.ppermute(block, ("expert", "dp"), [(i, i ^ code) for i in range(size)])
        arrived.append(block)
    return arrived


def combine_kernel(count, split, section_ref, position_ref, gates_ref, *refs):
    blocks = refs[:count]
    outs = refs[count : count + split]
    held, total, sems = refs[count + split :]
    capacity, features = blocks[0].shape
    copies = [
        pltpu.make_async_copy(block, held.at[pl.ds(i * capacity, capacity)], sems.at[i])
        for i, block in enumerate(blocks)
    ]
    for copy in copies:
        copy.start()
    position = position_ref[...]
    slot = lax.broadcasted_iota(jnp.int32, (position.shape[0], count * capacity), 1)
    picks = [
        jnp.where(position[:, k : k + 1] == slot, 1.0, 0.0).astype(jnp.bfloat16) for k in range(2)
    ]
    for copy in copies:
        copy.wait()
    first = jnp.dot(picks[0], held[...], preferred_element_type=jnp.float32)
    second = jnp.dot(picks[1], held[...], preferred_element_type=jnp.float32)
    total[...] = gates_ref[:, 0:1] * first + gates_ref[:, 1:2] * second
    width = features // split
    for step, out_ref in enumerate(outs):
        owner = lax.rem(section_ref[0] + step, split)
        start = pl.multiple_of(owner * width, width)
        out_ref[...] = total[:, pl.ds(start, width)].astype(out_ref.dtype)


def combine(section, position, gates, blocks, split, kept):
    capacity, features = blocks[0].shape
    rows = position.shape[0]
    count = len(blocks)
    width = features // split
    types = [kept] + [jnp.bfloat16] * (split - 1)
    full = pl.BlockSpec(memory_space=pltpu.VMEM)
    return pl.pallas_call(
        functools.partial(combine_kernel, count, split),
        out_shape=tuple(jax.ShapeDtypeStruct((rows, width), kind) for kind in types),
        in_specs=[pl.BlockSpec(memory_space=pltpu.SMEM), full, full]
        + [pl.BlockSpec(memory_space=pl.ANY)] * count,
        out_specs=[full] * split,
        scratch_shapes=[
            vmem((count * capacity, features), jnp.bfloat16),
            vmem((rows, features), jnp.float32),
            pltpu.SemaphoreType.DMA((count,)),
        ],
        compiler_params=pltpu.CompilerParams(vmem_limit_bytes=32 * 1024 * 1024),
        cost_estimate=pl.CostEstimate(
            flops=4 * rows * count * capacity * features,
            bytes_accessed=2 * count * capacity * features,
            transcendentals=0,
        ),
        name="combine",
    )(section, position, gates, *blocks)


def memory_kernel(count, section_ref, tokens_ref, gain_ref, *refs):
    slices, out_ref, mixed = refs[:count], refs[count], refs[count + 1]
    me = section_ref[0]
    width = slices[0].shape[1]
    for step, piece in enumerate(slices):
        owner = lax.rem(me - step + count, count)
        mixed[:, pl.ds(pl.multiple_of(owner * width, width), width)] = piece[...].astype(
            jnp.float32
        )
    values = tokens_ref[...].astype(jnp.float32) + mixed[...]
    out_ref[...] = normalize(values, gain_ref[...]).astype(jnp.bfloat16)


def make_memory(tokens, slices, gain):
    me = lax.axis_index("section").astype(jnp.int32).reshape(1)
    return pl.pallas_call(
        functools.partial(memory_kernel, len(slices)),
        out_shape=jax.ShapeDtypeStruct(tokens.shape, jnp.bfloat16),
        in_specs=[pl.BlockSpec(memory_space=pltpu.SMEM)]
        + [pl.BlockSpec(memory_space=pltpu.VMEM)] * (2 + len(slices)),
        out_specs=pl.BlockSpec(memory_space=pltpu.VMEM),
        scratch_shapes=[vmem(tokens.shape, jnp.float32)],
        compiler_params=pltpu.CompilerParams(vmem_limit_bytes=20 * 1024 * 1024),
        name="memory",
    )(me, tokens, gain[None], *slices)


def attend_kernel(
    place_ref,
    lengths_ref,
    query_ref,
    near_ref,
    far_ref,
    key_own,
    key_other,
    value_own,
    value_other,
    out_ref,
    source,
    key_weight,
    value_weight,
    keys,
    values,
    sems,
):
    y, core, sentence = place_ref[0], place_ref[1], place_ref[2]
    rows = near_ref.shape[0]
    depth = key_own.shape[0]
    moves = (
        (near_ref, source.at[pl.ds(0, rows)]),
        (far_ref, source.at[pl.ds(rows, rows)]),
        (key_own, key_weight.at[y]),
        (key_other, key_weight.at[1 - y]),
        (value_own, value_weight.at[y]),
        (value_other, value_weight.at[1 - y]),
    )
    copies = [
        pltpu.make_async_copy(here, there, sems.at[i]) for i, (here, there) in enumerate(moves)
    ]
    for copy in copies:
        copy.start()

    def project(weight, result):
        total = jnp.dot(source[:, :depth], weight[0], preferred_element_type=jnp.float32)
        total += jnp.dot(source[:, depth:], weight[1], preferred_element_type=jnp.float32)
        result[...] = total.astype(jnp.bfloat16)

    for copy in copies[:4]:
        copy.wait()
    project(key_weight, keys)
    for copy in copies[4:]:
        copy.wait()
    project(value_weight, values)

    column = lax.broadcasted_iota(jnp.int32, (query_ref.shape[0], 2 * rows), 1)
    position = jnp.where(column < rows, column + core * rows, column - core * rows)
    valid = position < lengths_ref[sentence]
    for head in range(query_ref.shape[1] // HEAD_DIM):
        span = slice(head * HEAD_DIM, (head + 1) * HEAD_DIM)
        scores = contract_last(query_ref[:, span], keys[:, span]) * HEAD_DIM ** (-0.5)
        scores = jnp.where(valid, scores, -1e30)
        weights = jnp.exp(scores - jnp.max(scores, axis=-1, keepdims=True))
        probs = (weights / jnp.sum(weights, axis=-1, keepdims=True)).astype(jnp.bfloat16)
        context = jnp.dot(probs, values[:, span], preferred_element_type=jnp.float32)
        out_ref[:, span] = context.astype(jnp.bfloat16)


def attend_sentence(place, lengths, query, near, far, key_pair, value_pair):
    rows, features = near.shape
    depth, width = key_pair[0].shape
    hold = pl.BlockSpec(memory_space=pl.ANY)
    smem = pl.BlockSpec(memory_space=pltpu.SMEM)
    full = pl.BlockSpec(memory_space=pltpu.VMEM)
    return pl.pallas_call(
        attend_kernel,
        out_shape=jax.ShapeDtypeStruct(query.shape, jnp.bfloat16),
        in_specs=[smem, smem, full] + [hold] * 6,
        out_specs=full,
        scratch_shapes=[
            vmem((2 * rows, features), jnp.bfloat16),
            vmem((2, depth, width), jnp.bfloat16),
            vmem((2, depth, width), jnp.bfloat16),
            vmem((2 * rows, width), jnp.bfloat16),
            vmem((2 * rows, width), jnp.bfloat16),
            pltpu.SemaphoreType.DMA((6,)),
        ],
        compiler_params=pltpu.CompilerParams(vmem_limit_bytes=32 * 1024 * 1024),
        cost_estimate=pl.CostEstimate(
            flops=8 * rows * features * width,
            bytes_accessed=4 * rows * features + 8 * depth * width,
            transcendentals=query.shape[0] * 8 * rows,
        ),
        name="attend_sentence",
    )(place, lengths, query, near, far, *key_pair, *value_pair)


def small_body(
    tokens,
    expert_ids,
    gate_weights,
    out_grad,
    inner_weight,
    outer_weight,
    final_gain,
    dec_states,
    src_lengths,
    tgt_lengths,
    norm_gain,
    query_weight,
    key_weight,
    value_weight,
    out_weight,
):
    token_count, feature_count = tokens.shape
    group_size = lax.axis_size(("expert", "dp"))
    capacity = 3 * token_count // group_size
    here = lax.axis_index(("expert", "dp"))
    y = lax.axis_index("expert")
    d = lax.axis_index("dp")
    section = lax.axis_index("section")
    sections = lax.axis_size("section")
    half = feature_count // 2
    weight_in = inner_weight[0]
    weight_out = outer_weight[0]
    key_own, value_own, out_own = key_weight[0], value_weight[0], out_weight[0]
    query_own = query_weight[0]

    size = group_size
    near_codes = (0, 2, 4, 6)
    core_codes = (1, 3, 5, 7)

    token_y = swap(tokens, "expert", 1)
    token_x = swap(tokens, "dp", 2)
    all_ids = lax.all_gather(expert_ids.T, ("expert", "dp"), axis=0)
    token_far = swap(token_y, "dp", 2)

    share = token_count // sections
    grad_share = lax.dynamic_slice_in_dim(out_grad, section * share, share, 0)
    grad_fetched = swap(gate(grad_share, token_y), "expert", 1)
    key_other = swap(gate(key_own, token_y), "expert", 1)
    grad_y = lax.all_gather(grad_fetched, "section", axis=0, tiled=True)
    grad_x = swap(gate(out_grad, token_far), "dp", 2)

    row = lax.broadcasted_iota(jnp.int32, (token_count, token_count), 0)
    column = lax.broadcasted_iota(jnp.int32, (token_count, token_count), 1)
    ids = jnp.stack(
        [lax.dynamic_index_in_dim(all_ids, here ^ code, 0, False) for code in near_codes]
    )
    named_there = jnp.concatenate([(ids == here).any(axis=1), (ids == (here ^ 1)).any(axis=1)])
    before = jnp.dot(
        named_there.astype(jnp.bfloat16),
        (row < column).astype(jnp.bfloat16),
        preferred_element_type=jnp.float32,
    ).astype(jnp.int32)
    code = jnp.where(named_there, before, -1)

    named = expert_ids[:, :, None] == jnp.arange(size, dtype=jnp.int32)[None, None, :]
    either = (named[:, 0] | named[:, 1]).astype(jnp.bfloat16)
    earlier = jnp.dot(
        (column < row).astype(jnp.bfloat16), either, preferred_element_type=jnp.float32
    ).astype(jnp.int32)
    rank = jnp.sum(jnp.where(named, earlier[:, None, :], 0), axis=2)
    codes_of = expert_ids ^ here
    position = ((codes_of >> 1) + 4 * (codes_of & 1)) * capacity + rank

    def forward(rows):
        pre_act = jnp.dot(rows, weight_in, preferred_element_type=jnp.float32)
        hidden = jax.nn.gelu(pre_act).astype(jnp.bfloat16)
        part = jnp.dot(hidden, weight_out, preferred_element_type=jnp.float32)
        return pre_act, part.astype(jnp.bfloat16)

    def backward(grads, pre_act):
        back = contract_last(grads, weight_out)
        slope = jax.vjp(jax.nn.gelu, pre_act)[1](back)[0].astype(jnp.bfloat16)
        return contract_last(slope, weight_in).astype(jnp.bfloat16)

    rows_own, rows_sent = dispatch(code, [tokens, token_x, token_y, token_far], capacity)
    rows_core = swap(rows_sent, "dp", 1)
    pre_own, part_own = forward(rows_own)
    pre_core, part_core = forward(rows_core)
    part_core = gate(part_core, key_other, grad_x)
    home = send_home(part_own, near_codes, capacity) + send_home(part_core, core_codes, capacity)

    which_section = section.astype(jnp.int32).reshape(1)
    cuts = combine(which_section, position, gate_weights, home, sections, jnp.float32)
    mixed_sum = cuts[0]
    for step in range(1, sections):
        mixed_sum = mixed_sum + shift(cuts[step], "section", step).astype(jnp.float32)
    mixed_slice = mixed_sum.astype(jnp.bfloat16)
    slices = [mixed_slice] + [shift(mixed_slice, "section", step) for step in range(1, sections)]

    value_other = swap(gate(value_own, *home), "expert", 1)
    grad_far = swap(gate(grad_y, *home), "dp", 2)
    states = dec_states[0]
    normed = normalize(states.astype(jnp.float32), norm_gain[0]).astype(jnp.bfloat16)
    quarter = normed.shape[0] // lax.axis_size("dp")
    asked = lax.dynamic_slice(normed, (d * quarter, (1 - y) * half), (quarter, half))
    asked_here = swap(gate(asked, *home), "expert", 1)
    asked_rows = lax.all_gather(asked_here, "dp", axis=0, tiled=True)
    query_there = jnp.dot(asked_rows, query_own, preferred_element_type=jnp.float32)
    query_other = swap(query_there.astype(jnp.bfloat16), "expert", 1)
    out_other = swap(gate(out_own, value_other), "expert", 1)
    normed_own = lax.dynamic_slice_in_dim(normed, y * half, half, 1)
    query = (
        jnp.dot(normed_own, query_own, preferred_element_type=jnp.float32)
        + query_other.astype(jnp.float32)
    ).astype(jnp.bfloat16)

    grads_own, grads_sent = dispatch(
        gate(code, mixed_slice), [out_grad, grad_x, grad_y, grad_far], capacity
    )
    grads_core = swap(grads_sent, "dp", 1)
    backward_own = backward(grads_own, pre_own)
    backward_core = backward(grads_core, pre_core)
    held_tokens = gate(tokens, value_other, backward_own, backward_core)
    memory = make_memory(held_tokens, slices, final_gain)

    core, x = d % 2, d // 2
    memory_x = swap(memory, "dp", 2)
    memory_core = swap(memory, "dp", 1)
    memory_far = swap(memory_x, "dp", 1)

    def sentence(which, near, far):
        place = jnp.stack([y, core, which]).astype(jnp.int32)
        rows_of = lax.dynamic_slice_in_dim(query, which * TGT_LEN, TGT_LEN, 0)
        return attend_sentence(
            place, src_lengths, rows_of, near, far, (key_own, key_other), (value_own, value_other)
        )

    context_own = sentence(x, memory, memory_core)
    context_other = sentence(1 - x, gate(memory_x, out_other), memory_far)

    backward_part = jnp.concatenate([backward_own, backward_core], axis=0)
    backward_part = gate(backward_part, context_own)
    width = half * 2 // sections

    def piece(owner):
        return lax.dynamic_slice_in_dim(backward_part, owner * width, width, 1)

    arrived = [
        shift(piece(lax.rem(section + step, sections)), "section", step)
        for step in range(1, sections)
    ]
    backward_sum = gate(piece(section), context_other).astype(jnp.float32)
    for part in arrived:
        backward_sum = backward_sum + part.astype(jnp.float32)
    backward_slice = backward_sum.astype(jnp.bfloat16)
    grads_home = send_home(backward_slice, near_codes + core_codes, capacity)
    (token_grad,) = combine(which_section, position, gate_weights, grads_home, 1, jnp.bfloat16)

    context = jnp.concatenate(
        [jnp.where(x == 0, context_own, context_other), jnp.where(x == 0, context_other, context_own)],
        axis=0,
    )
    columns = feature_count // lax.axis_size("dp")

    def project(weight, which):
        part = lax.dynamic_slice_in_dim(weight, which * columns, columns, 1)
        return jnp.dot(context, part, preferred_element_type=jnp.float32)

    def by_x(which):
        own, other = project(out_own, which), project(out_other, which)
        first = y == 0
        return jnp.stack([jnp.where(first, own, other), jnp.where(first, other, own)])

    sent = by_x(1 - core).astype(jnp.bfloat16)
    total = by_x(core) + swap(sent, "dp", 1).astype(jnp.float32)
    last = lax.dynamic_index_in_dim(total, 1 - x, 0, False).astype(jnp.bfloat16)
    attended = lax.dynamic_index_in_dim(total, x, 0, False) + swap(last, "dp", 2).astype(
        jnp.float32
    )
    dec_out = add_residual(attended, states, tgt_lengths)
    return (dec_out[None], token_grad)


def add_residual(attended, states, tgt_lengths):
    my_columns = attended.shape[1]
    residual = lax.dynamic_slice_in_dim(
        states, lax.axis_index("dp") * my_columns, my_columns, 1
    ).astype(jnp.float32)
    row_mask = (jnp.arange(TGT_LEN, dtype=jnp.int32)[None, :] < tgt_lengths[:, None]).reshape(-1, 1)
    return (residual + jnp.where(row_mask, attended, 0.0)).astype(jnp.bfloat16)


def body(
    tokens,
    expert_ids,
    gate_weights,
    out_grad,
    inner_weight,
    outer_weight,
    final_gain,
    dec_states,
    src_lengths,
    tgt_lengths,
    norm_gain,
    query_weight,
    key_weight,
    value_weight,
    out_weight,
):
    token_count, feature_count = tokens.shape
    group_size = lax.axis_size(("expert", "dp"))
    capacity = 3 * token_count // group_size
    slots = group_size * capacity

    named = expert_ids[:, :, None] == jnp.arange(group_size, dtype=jnp.int32)[None, None, :]
    either = (named[:, 0] | named[:, 1]).astype(jnp.bfloat16)
    row = lax.broadcasted_iota(jnp.int32, (token_count, token_count), 0)
    column = lax.broadcasted_iota(jnp.int32, (token_count, token_count), 1)
    earlier = jnp.dot(
        (column < row).astype(jnp.bfloat16), either, preferred_element_type=jnp.float32
    ).astype(jnp.int32)
    rank = jnp.sum(jnp.where(named, earlier[:, None, :], 0), axis=2)
    position = expert_ids * capacity + rank
    pick_first = slot_matrix(position[:, 0], slots)
    pick_second = slot_matrix(position[:, 1], slots)
    fill = (pick_first + pick_second).T

    def place(values):
        return jnp.dot(fill, values, preferred_element_type=jnp.float32).astype(jnp.bfloat16)

    def combine(arrived):
        first = jnp.dot(pick_first, arrived, preferred_element_type=jnp.float32)
        second = jnp.dot(pick_second, arrived, preferred_element_type=jnp.float32)
        return gate_weights[:, :1] * first + gate_weights[:, 1:] * second

    weight_in = inner_weight[0]
    weight_out = outer_weight[0]
    arrived_rows = exchange(place(tokens), group_size, capacity)
    pre_act = jnp.dot(arrived_rows, weight_in, preferred_element_type=jnp.float32)
    hidden = jax.nn.gelu(pre_act).astype(jnp.bfloat16)
    forward_part = jnp.dot(hidden, weight_out, preferred_element_type=jnp.float32)
    arrived_grads = exchange(place(out_grad), group_size, capacity)
    outputs_home = exchange(forward_part.astype(jnp.bfloat16), group_size, capacity)
    mixed_slice = sum_sections(combine(outputs_home)).astype(jnp.bfloat16)
    mixed = gather_sections(mixed_slice).astype(jnp.float32)
    memory = normalize(tokens.astype(jnp.float32) + mixed, final_gain).astype(jnp.bfloat16)

    back = contract_last(arrived_grads, weight_out)
    slope = jax.vjp(jax.nn.gelu, pre_act)[1](back)[0].astype(jnp.bfloat16)
    backward_part = contract_last(slope, weight_in)
    backward_slice = sum_sections(backward_part).astype(jnp.bfloat16)
    grads_home = exchange(backward_slice, group_size, capacity)
    token_grad = combine(grads_home).astype(jnp.bfloat16)

    states = dec_states[0]
    normed = normalize(states.astype(jnp.float32), norm_gain[0]).astype(jnp.bfloat16)
    full_query = gather_weight(query_weight[0], 0)
    full_key = gather_weight(key_weight[0], 0)
    full_value = gather_weight(value_weight[0], 0)
    full_out = gather_weight(out_weight[0], 1)
    query_sum = jnp.dot(normed, full_query, preferred_element_type=jnp.float32)
    source = gather_rows(memory, "dp")
    key_sum = jnp.dot(source, full_key, preferred_element_type=jnp.float32)
    value_sum = jnp.dot(source, full_value, preferred_element_type=jnp.float32)
    key_mask = jnp.arange(SRC_LEN, dtype=jnp.int32)[None, :] < src_lengths[:, None]
    context = attend(
        query_sum.astype(jnp.bfloat16),
        key_sum.astype(jnp.bfloat16),
        value_sum.astype(jnp.bfloat16),
        key_mask,
    )
    attended = sum_heads(jnp.dot(context, full_out, preferred_element_type=jnp.float32))
    dec_out = add_residual(attended, states, tgt_lengths)
    return (dec_out[None], token_grad)


def solution(mesh):
    in_specs = (
        P(("expert", "dp"), None),
        P(("expert", "dp"), None),
        P(("expert", "dp"), None),
        P(("expert", "dp"), None),
        P(("expert", "dp"), None, "section"),
        P(("expert", "dp"), "section", None),
        P(),
        P("section", "expert", None),
        P("expert"),
        P("expert"),
        P("section", None),
        P("section", "expert", "dp"),
        P("section", "expert", "dp"),
        P("section", "expert", "dp"),
        P("section", "dp", "expert"),
    )
    out_specs = (P("section", "expert", "dp"), P(("expert", "dp"), "section"))
    small = mesh.shape["expert"] == 2 and mesh.shape["dp"] == 4
    chosen = small_body if small else body
    return jax.shard_map(chosen, mesh=mesh, in_specs=in_specs, out_specs=out_specs, check_vma=False)
```

```python
import functools
import math

import jax
import jax.numpy as jnp
from jax import lax
from jax.experimental import pallas as pl
from jax.experimental.pallas import tpu as pltpu
from jax.sharding import PartitionSpec as P

HEAD_DIM = 128
SRC_LEN = 256
TGT_LEN = 128


EPSILON = 1e-05


def normalize(values, gain):
    centre = jnp.mean(values, axis=-1, keepdims=True)
    centred = values - centre
    spread = jnp.mean(centred * centred, axis=-1, keepdims=True)
    return centred * lax.rsqrt(spread + EPSILON) * gain


def contract_last(left, right):
    return lax.dot_general(
        left, right, (((1,), (1,)), ((), ())), preferred_element_type=jnp.float32
    )


def shift(value, axis, step):
    size = lax.axis_size(axis)
    return lax.ppermute(value, axis, [(i, (i + step) % size) for i in range(size)])


def swap(value, axis, mask):
    size = lax.axis_size(axis)
    return lax.ppermute(value, axis, [(i, i ^ mask) for i in range(size)])


def sum_sections(partial):
    count = lax.axis_size("section")
    me = lax.axis_index("section")
    width = partial.shape[1] // count

    def piece(owner):
        return lax.dynamic_slice_in_dim(partial, owner * width, width, 1)

    total = piece(me).astype(jnp.float32)
    for step in range(1, count):
        sent = piece(lax.rem(me + step, count)).astype(jnp.bfloat16)
        total = total + shift(sent, "section", step).astype(jnp.float32)
    return total


def gather_sections(mine):
    count = lax.axis_size("section")
    me = lax.axis_index("section")
    width = mine.shape[1]
    whole = jnp.zeros((mine.shape[0], width * count), mine.dtype)
    whole = lax.dynamic_update_slice_in_dim(whole, mine, me * width, 1)
    for step in range(1, count):
        owner = lax.rem(me - step + count, count)
        whole = lax.dynamic_update_slice_in_dim(
            whole, shift(mine, "section", step), owner * width, 1
        )
    return whole


def gather_rows(mine, axis):
    held = mine
    me = lax.axis_index(axis)
    mask = lax.axis_size(axis) // 2
    blocks = [mine]
    while mask >= 1:
        blocks = blocks + [swap(block, axis, mask) for block in blocks]
        mask //= 2
    codes = [0]
    mask = lax.axis_size(axis) // 2
    while mask >= 1:
        codes = codes + [code ^ mask for code in codes]
        mask //= 2
    ordered = []
    for place in range(len(blocks)):
        chosen = blocks[0]
        for code, block in zip(codes[1:], blocks[1:]):
            chosen = jnp.where((me ^ code) == place, block, chosen)
        ordered.append(chosen)
    return jnp.concatenate(ordered, axis=0)


def gather_weight(weight, dimension):
    if lax.axis_size("expert") != 2:
        return lax.all_gather(weight, "expert", axis=dimension, tiled=True)
    other = swap(weight, "expert", 1)
    first = lax.axis_index("expert") == 0
    return jnp.concatenate(
        [jnp.where(first, weight, other), jnp.where(first, other, weight)], axis=dimension
    )


def sum_heads(partial):
    me = lax.axis_index("dp")
    count = lax.axis_size("dp")
    rows, columns = partial.shape
    total = partial.reshape(rows, count, columns // count)
    mask = 1
    while mask < count:
        paired = total.reshape(rows, -1, 2, columns // count)
        bit = (me // mask) % 2
        sent = lax.dynamic_index_in_dim(paired, 1 - bit, 2, False).astype(jnp.bfloat16)
        kept = lax.dynamic_index_in_dim(paired, bit, 2, False)
        total = kept + swap(sent, "dp", mask).astype(jnp.float32)
        mask *= 2
    return total.reshape(rows, columns // count)


def slot_matrix(positions, slots):
    places = lax.broadcasted_iota(jnp.int32, (positions.shape[0], slots), 1)
    return (positions[:, None] == places).astype(jnp.bfloat16)


def attend(query, keys, values, key_mask):
    sequences = key_mask.shape[0]
    head_count = query.shape[1] // HEAD_DIM
    query_split = query.reshape(sequences, -1, head_count, HEAD_DIM)
    keys_split = keys.reshape(sequences, -1, head_count, HEAD_DIM)
    values_split = values.reshape(sequences, -1, head_count, HEAD_DIM)
    scores = jnp.einsum(
        "bqhd,bkhd->bhqk", query_split, keys_split, preferred_element_type=jnp.float32
    ) * HEAD_DIM ** (-0.5)
    scores = jnp.where(key_mask[:, None, None, :], scores, -1e30)
    highest = jnp.max(scores, axis=-1, keepdims=True)
    weights = jnp.exp(scores - highest)
    probs = (weights / jnp.sum(weights, axis=-1, keepdims=True)).astype(jnp.bfloat16)
    context = jnp.einsum("bhqk,bkhd->bqhd", probs, values_split, preferred_element_type=jnp.float32)
    return context.astype(jnp.bfloat16).reshape(-1, head_count * HEAD_DIM)


def exchange(values, group_size, capacity):
    sent = values.reshape(group_size, capacity, values.shape[1])
    arrived = lax.all_to_all(sent, ("expert", "dp"), split_axis=0, concat_axis=0, tiled=True)
    return arrived.reshape(values.shape)


SHORT = pl.CostEstimate(flops=1, bytes_accessed=1, transcendentals=0)


def gate(value, *after):
    return lax.optimization_barrier((value,) + after)[0]


def vmem(shape, dtype):
    return pltpu.VMEM(shape, dtype)


def dispatch_kernel(capacity, count, share, section_ref, code_ref, *refs):
    blocks, held, sems = refs[:count], refs[count + 2], refs[count + 3]
    copies = []
    for place, block in enumerate(blocks):
        rows = block.shape[0]
        if share and place >= count // 2:
            pieces = rows // share
            copies.append([])
            for step in range(pieces):
                owner = lax.rem(section_ref[0] - step + pieces, pieces)
                there = held.at[place, pl.ds(pl.multiple_of(owner * share, share), share)]
                here = block.at[pl.ds(step * share, share)]
                copies[-1].append(pltpu.make_async_copy(here, there, sems.at[place, step]))
        else:
            copies.append([pltpu.make_async_copy(block, held.at[place], sems.at[place, 0])])
    for group in copies:
        for copy in group:
            copy.start()
    for place, group in enumerate(copies):
        for copy in group:
            copy.wait()
        picks = []
        for which in range(2):
            line = which * count + place
            code = code_ref[line : line + 1, :]
            slot = lax.broadcasted_iota(jnp.int32, (capacity, code.shape[1]), 0)
            picks.append(jnp.where(slot == code, 1.0, 0.0))
        pick = jnp.concatenate(picks, axis=0).astype(jnp.bfloat16)
        rows = jnp.dot(pick, held[place], preferred_element_type=jnp.float32).astype(jnp.bfloat16)
        for which, out_ref in enumerate(refs[count : count + 2]):
            out_ref[place * capacity : (place + 1) * capacity, :] = rows[
                which * capacity : (which + 1) * capacity
            ]


def dispatch(section, code, blocks, capacity, share=0):
    rows, features = blocks[0].shape
    count = len(blocks)
    picked = jax.ShapeDtypeStruct((count * capacity, features), jnp.bfloat16)
    return pl.pallas_call(
        functools.partial(dispatch_kernel, capacity, count, share),
        out_shape=(picked, picked),
        in_specs=[
            pl.BlockSpec(memory_space=pltpu.SMEM),
            pl.BlockSpec(memory_space=pltpu.VMEM),
        ]
        + [pl.BlockSpec(memory_space=pl.ANY)] * count,
        out_specs=[pl.BlockSpec(memory_space=pltpu.VMEM)] * 2,
        scratch_shapes=[
            vmem((count, rows, features), jnp.bfloat16),
            pltpu.SemaphoreType.DMA((count, 4)),
        ],
        compiler_params=pltpu.CompilerParams(vmem_limit_bytes=32 * 1024 * 1024),
        cost_estimate=SHORT,
        name="dispatch",
    )(section, code, *blocks)


def send_home(part, codes, capacity):
    size = lax.axis_size(("expert", "dp"))
    arrived = []
    for place, code in enumerate(codes):
        block = part[place * capacity : (place + 1) * capacity]
        if code:
            block = lax.ppermute(block, ("expert", "dp"), [(i, i ^ code) for i in range(size)])
        arrived.append(block)
    return arrived


def combine_kernel(count, split, section_ref, position_ref, gates_ref, *refs):
    blocks = refs[:count]
    outs = refs[count : count + split]
    held, total, sems = refs[count + split :]
    capacity, features = blocks[0].shape
    copies = [
        pltpu.make_async_copy(block, held.at[pl.ds(i * capacity, capacity)], sems.at[i])
        for i, block in enumerate(blocks)
    ]
    for copy in copies:
        copy.start()
    position = position_ref[...]
    slot = lax.broadcasted_iota(jnp.int32, (position.shape[0], count * capacity), 1)
    picks = [
        jnp.where(position[:, k : k + 1] == slot, 1.0, 0.0).astype(jnp.bfloat16) for k in range(2)
    ]
    for copy in copies:
        copy.wait()
    pick = jnp.concatenate(picks, axis=0)
    rows = position.shape[0]
    both = jnp.dot(pick, held[...], preferred_element_type=jnp.float32)
    total[...] = gates_ref[:, 0:1] * both[:rows] + gates_ref[:, 1:2] * both[rows:]
    width = features // split
    for step, out_ref in enumerate(outs):
        owner = lax.rem(section_ref[0] + step, split)
        start = pl.multiple_of(owner * width, width)
        out_ref[...] = total[:, pl.ds(start, width)].astype(out_ref.dtype)


def combine(section, position, gates, blocks, split, kept):
    capacity, features = blocks[0].shape
    rows = position.shape[0]
    count = len(blocks)
    width = features // split
    types = [kept] + [jnp.bfloat16] * (split - 1)
    full = pl.BlockSpec(memory_space=pltpu.VMEM)
    return pl.pallas_call(
        functools.partial(combine_kernel, count, split),
        out_shape=tuple(jax.ShapeDtypeStruct((rows, width), kind) for kind in types),
        in_specs=[pl.BlockSpec(memory_space=pltpu.SMEM), full, full]
        + [pl.BlockSpec(memory_space=pl.ANY)] * count,
        out_specs=[full] * split,
        scratch_shapes=[
            vmem((count * capacity, features), jnp.bfloat16),
            vmem((rows, features), jnp.float32),
            pltpu.SemaphoreType.DMA((count,)),
        ],
        compiler_params=pltpu.CompilerParams(vmem_limit_bytes=32 * 1024 * 1024),
        cost_estimate=SHORT,
        name="combine",
    )(section, position, gates, *blocks)


def memory_kernel(count, section_ref, tokens_ref, gain_ref, *refs):
    slices, out_ref, mixed, held, sem = refs[:count], refs[count], *refs[count + 1 :]
    fetch = pltpu.make_async_copy(tokens_ref, held, sem)
    fetch.start()
    me = section_ref[0]
    width = slices[0].shape[1]
    for step, piece in enumerate(slices):
        owner = lax.rem(me - step + count, count)
        mixed[:, pl.ds(pl.multiple_of(owner * width, width), width)] = piece[...].astype(
            jnp.float32
        )
    fetch.wait()
    values = held[...].astype(jnp.float32) + mixed[...]
    out_ref[...] = normalize(values, gain_ref[...]).astype(jnp.bfloat16)


def make_memory(me, tokens, slices, gain):
    return pl.pallas_call(
        functools.partial(memory_kernel, len(slices)),
        out_shape=jax.ShapeDtypeStruct(tokens.shape, jnp.bfloat16),
        in_specs=[
            pl.BlockSpec(memory_space=pltpu.SMEM),
            pl.BlockSpec(memory_space=pl.ANY),
        ]
        + [pl.BlockSpec(memory_space=pltpu.VMEM)] * (1 + len(slices)),
        out_specs=pl.BlockSpec(memory_space=pltpu.VMEM),
        scratch_shapes=[
            vmem(tokens.shape, jnp.float32),
            vmem(tokens.shape, tokens.dtype),
            pltpu.SemaphoreType.DMA,
        ],
        compiler_params=pltpu.CompilerParams(vmem_limit_bytes=20 * 1024 * 1024),
        cost_estimate=SHORT,
        name="memory",
    )(me, tokens, gain[None], *slices)


def attend_kernel(project, place_ref, lengths_ref, query_ref, *refs):
    near_ref, far_ref, key_own, key_other, value_own, value_other = refs[:6]
    y, core, sentence = place_ref[0], place_ref[1], place_ref[2]
    if project:
        done_ref, out_own, out_other, sent_ref, kept_ref = refs[6:11]
        source, key_weight, value_weight, keys, values, sems, out_weight, context = refs[11:]
    else:
        out_ref = refs[6]
        source, key_weight, value_weight, keys, values, sems = refs[7:]
    rows = near_ref.shape[0]
    depth = key_own.shape[0]
    moves = [
        (near_ref, source.at[pl.ds(0, rows)]),
        (far_ref, source.at[pl.ds(rows, rows)]),
        (key_own, key_weight.at[y]),
        (key_other, key_weight.at[1 - y]),
        (value_own, value_weight.at[y]),
        (value_other, value_weight.at[1 - y]),
    ]
    if project:
        moves += [(out_own, out_weight.at[y]), (out_other, out_weight.at[1 - y])]
    copies = [
        pltpu.make_async_copy(here, there, sems.at[i]) for i, (here, there) in enumerate(moves)
    ]
    for copy in copies:
        copy.start()

    def linear(weight, result):
        total = jnp.dot(source[:, :depth], weight[0], preferred_element_type=jnp.float32)
        total += jnp.dot(source[:, depth:], weight[1], preferred_element_type=jnp.float32)
        result[...] = total.astype(jnp.bfloat16)

    for copy in copies[:4]:
        copy.wait()
    linear(key_weight, keys)
    for copy in copies[4:6]:
        copy.wait()
    linear(value_weight, values)

    targets = query_ref.shape[0]
    mine = pl.ds(pl.multiple_of(sentence * targets, targets), targets)
    column = lax.broadcasted_iota(jnp.int32, (targets, 2 * rows), 1)
    position = jnp.where(column < rows, column + core * rows, column - core * rows)
    valid = position < lengths_ref[sentence]
    for head in range(query_ref.shape[1] // HEAD_DIM):
        span = slice(head * HEAD_DIM, (head + 1) * HEAD_DIM)
        scores = contract_last(query_ref[:, span], keys[:, span]) * HEAD_DIM ** (-0.5)
        scores = jnp.where(valid, scores, -1e30)
        weights = jnp.exp(scores - jnp.max(scores, axis=-1, keepdims=True))
        probs = (weights / jnp.sum(weights, axis=-1, keepdims=True)).astype(jnp.bfloat16)
        result = jnp.dot(probs, values[:, span], preferred_element_type=jnp.float32)
        if project:
            context[mine, span] = result.astype(jnp.bfloat16)
        else:
            out_ref[:, span] = result.astype(jnp.bfloat16)

    if project:
        others = pl.ds(pl.multiple_of((1 - sentence) * targets, targets), targets)
        context[others, :] = done_ref[...]
        for copy in copies[6:]:
            copy.wait()
        columns = sent_ref.shape[2]
        x = 1 - sentence
        for which in range(2):
            half = jnp.where(which == 0, x, 1 - x)
            for out, side in ((sent_ref, 1 - core), (kept_ref, core)):
                span = pl.ds(pl.multiple_of(side * columns, columns), columns)
                part = jnp.dot(
                    context[...], out_weight[half, :, span], preferred_element_type=jnp.float32
                )
                out[which] = part.astype(out.dtype)


def attend_sentence(place, lengths, query, near, far, key_pair, value_pair, done=None, out_pair=()):
    rows, features = near.shape
    depth, width = key_pair[0].shape
    project = done is not None
    hold = pl.BlockSpec(memory_space=pl.ANY)
    smem = pl.BlockSpec(memory_space=pltpu.SMEM)
    full = pl.BlockSpec(memory_space=pltpu.VMEM)
    operands = [place, lengths, query, near, far, *key_pair, *value_pair]
    in_specs = [smem, smem, full] + [hold] * 6
    scratch = [
        vmem((2 * rows, features), jnp.bfloat16),
        vmem((2, depth, width), jnp.bfloat16),
        vmem((2, depth, width), jnp.bfloat16),
        vmem((2 * rows, width), jnp.bfloat16),
        vmem((2 * rows, width), jnp.bfloat16),
        pltpu.SemaphoreType.DMA((8,)),
    ]
    if project:
        targets = 2 * query.shape[0]
        columns = out_pair[0].shape[1] // 2
        operands += [done, *out_pair]
        in_specs += [full, hold, hold]
        scratch += [
            vmem((2,) + out_pair[0].shape, jnp.bfloat16),
            vmem((targets, width), jnp.bfloat16),
        ]
        out_shape = (
            jax.ShapeDtypeStruct((2, targets, columns), jnp.bfloat16),
            jax.ShapeDtypeStruct((2, targets, columns), jnp.float32),
        )
        out_specs = [full, full]
    else:
        out_shape, out_specs = jax.ShapeDtypeStruct(query.shape, jnp.bfloat16), full
    return pl.pallas_call(
        functools.partial(attend_kernel, project),
        out_shape=out_shape,
        in_specs=in_specs,
        out_specs=out_specs,
        scratch_shapes=scratch,
        compiler_params=pltpu.CompilerParams(vmem_limit_bytes=32 * 1024 * 1024),
        cost_estimate=SHORT,
        name="attend_sentence",
    )(*operands)


def backward_kernel(split, section_ref, own_ref, core_ref, pre_own, pre_core, out_ref, in_ref, *refs):
    outs = refs[:split]
    grads, pre_act, weight_out, weight_in, slope, sems = refs[split:]
    rows = own_ref.shape[0]
    hidden, features = weight_out.shape
    width = features // split
    chunk = hidden // 4
    moves = [
        (own_ref, grads.at[pl.ds(0, rows)]),
        (core_ref, grads.at[pl.ds(rows, rows)]),
        (pre_own, pre_act.at[pl.ds(0, rows)]),
        (pre_core, pre_act.at[pl.ds(rows, rows)]),
    ]
    for part in range(4):
        span = pl.ds(part * chunk, chunk)
        moves.append((out_ref.at[span], weight_out.at[span]))
    moves.append((in_ref, weight_in))
    copies = [
        pltpu.make_async_copy(here, there, sems.at[i]) for i, (here, there) in enumerate(moves)
    ]
    for copy in copies:
        copy.start()
    for copy in copies[:4]:
        copy.wait()
    scale = (2.0 / math.pi) ** 0.5
    for part in range(4):
        copies[4 + part].wait()
        span = slice(part * chunk, (part + 1) * chunk)
        back = contract_last(grads[...], weight_out[span, :])
        value = pre_act[:, span]
        square = value * value
        bent = jnp.tanh(scale * (value + 0.044715 * (square * value)))
        inner = scale * (1.0 + 3.0 * 0.044715 * square)
        rise = 0.5 * (1.0 + bent) + 0.5 * value * ((1.0 - bent * bent) * inner)
        slope[:, span] = (back * rise).astype(jnp.bfloat16)
    copies[8].wait()
    for step in range(split):
        owner = lax.rem(section_ref[0] + step, split)
        start = pl.multiple_of(owner * width, width)
        part = contract_last(slope[...], weight_in[pl.ds(start, width), :])
        outs[step][...] = part.astype(outs[step].dtype)


def expert_backward(section, grads_own, grads_core, pre_own, pre_core, weight_out, weight_in, split):
    rows = 2 * grads_own.shape[0]
    hidden, features = weight_out.shape
    hold = pl.BlockSpec(memory_space=pl.ANY)
    width = features // split
    kinds = [jnp.float32] + [jnp.bfloat16] * (split - 1)
    return pl.pallas_call(
        functools.partial(backward_kernel, split),
        out_shape=tuple(jax.ShapeDtypeStruct((rows, width), kind) for kind in kinds),
        in_specs=[pl.BlockSpec(memory_space=pltpu.SMEM)] + [hold] * 6,
        out_specs=[pl.BlockSpec(memory_space=pltpu.VMEM)] * split,
        scratch_shapes=[
            vmem((rows, features), jnp.bfloat16),
            vmem((rows, hidden), jnp.float32),
            vmem((hidden, features), jnp.bfloat16),
            vmem((features, hidden), jnp.bfloat16),
            vmem((rows, hidden), jnp.bfloat16),
            pltpu.SemaphoreType.DMA((9,)),
        ],
        compiler_params=pltpu.CompilerParams(vmem_limit_bytes=40 * 1024 * 1024),
        cost_estimate=SHORT,
        name="expert_backward",
    )(section, grads_own, grads_core, pre_own, pre_core, weight_out, weight_in)


def small_body(
    tokens,
    expert_ids,
    gate_weights,
    out_grad,
    inner_weight,
    outer_weight,
    final_gain,
    dec_states,
    src_lengths,
    tgt_lengths,
    norm_gain,
    query_weight,
    key_weight,
    value_weight,
    out_weight,
):
    token_count, feature_count = tokens.shape
    group_size = lax.axis_size(("expert", "dp"))
    capacity = 3 * token_count // group_size
    here = lax.axis_index(("expert", "dp"))
    y = lax.axis_index("expert")
    d = lax.axis_index("dp")
    section = lax.axis_index("section")
    sections = lax.axis_size("section")
    half = feature_count // 2
    weight_in = inner_weight[0]
    weight_out = outer_weight[0]
    key_own, value_own, out_own = key_weight[0], value_weight[0], out_weight[0]
    query_own = query_weight[0]

    size = group_size
    near_codes = (0, 2, 4, 6)
    core_codes = (1, 3, 5, 7)
    core, x = d % 2, d // 2
    which_section = section.astype(jnp.int32).reshape(1)

    token_y = swap(tokens, "expert", 1)
    token_x = swap(tokens, "dp", 2)
    ids_y = jnp.stack([expert_ids.T, swap(expert_ids.T, "expert", 1)])
    ids_x = swap(ids_y, "dp", 2)
    token_far = swap(token_y, "dp", 2)

    share = token_count // sections
    grad_share = lax.dynamic_slice_in_dim(out_grad, section * share, share, 0)
    grad_fetched = swap(gate(grad_share, token_y), "expert", 1)
    key_other = swap(gate(key_own, token_y), "expert", 1)
    states = dec_states[0]
    normed = normalize(states.astype(jnp.float32), norm_gain[0]).astype(jnp.bfloat16)
    quarter = normed.shape[0] // lax.axis_size("dp")
    asked = lax.dynamic_slice(normed, (d * quarter, (1 - y) * half), (quarter, half))
    asked_here = swap(gate(asked, grad_fetched), "expert", 1)
    grad_y = jnp.concatenate(
        [grad_fetched] + [shift(grad_fetched, "section", step) for step in range(1, sections)],
        axis=0,
    )
    grad_x = swap(gate(out_grad, token_far), "dp", 2)

    row = lax.broadcasted_iota(jnp.int32, (token_count, token_count), 0)
    column = lax.broadcasted_iota(jnp.int32, (token_count, token_count), 1)
    ids = jnp.stack([ids_y[0], ids_x[0], ids_y[1], ids_x[1]])
    named_there = jnp.concatenate([(ids == here).any(axis=1), (ids == (here ^ 1)).any(axis=1)])
    before = jnp.dot(
        named_there.astype(jnp.bfloat16),
        (row < column).astype(jnp.bfloat16),
        preferred_element_type=jnp.float32,
    ).astype(jnp.int32)
    code = jnp.where(named_there, before, -1)

    named = expert_ids[:, :, None] == jnp.arange(size, dtype=jnp.int32)[None, None, :]
    either = (named[:, 0] | named[:, 1]).astype(jnp.bfloat16)
    earlier = jnp.dot(
        (column < row).astype(jnp.bfloat16), either, preferred_element_type=jnp.float32
    ).astype(jnp.int32)
    rank = jnp.sum(jnp.where(named, earlier[:, None, :], 0), axis=2)
    codes_of = expert_ids ^ here
    position = ((codes_of >> 1) + 4 * (codes_of & 1)) * capacity + rank

    def forward(rows):
        pre_act = jnp.dot(rows, weight_in, preferred_element_type=jnp.float32)
        hidden = jax.nn.gelu(pre_act).astype(jnp.bfloat16)
        part = jnp.dot(hidden, weight_out, preferred_element_type=jnp.float32)
        return pre_act, part.astype(jnp.bfloat16)

    rows_own, rows_sent = dispatch(
        which_section, code, [tokens, token_x, token_y, token_far], capacity
    )
    rows_core = swap(rows_sent, "dp", 1)
    pre_own, part_own = forward(rows_own)
    pre_core, part_core = forward(rows_core)
    part_core = gate(part_core, key_other, grad_x)
    home = send_home(part_own, near_codes, capacity) + send_home(part_core, core_codes, capacity)

    asked_pair = jnp.concatenate([asked_here, swap(gate(asked_here, token_far), "dp", 2)], axis=0)
    asked_rows = jnp.concatenate([asked_pair, swap(asked_pair, "dp", 1)], axis=0)
    query_there = jnp.dot(asked_rows, query_own, preferred_element_type=jnp.float32)

    held_gates = gate(gate_weights, query_there)
    cuts = combine(which_section, position, held_gates, home, sections, jnp.float32)
    mixed_sum = cuts[0]
    for step in range(1, sections):
        mixed_sum = mixed_sum + shift(cuts[step], "section", step).astype(jnp.float32)
    mixed_slice = mixed_sum.astype(jnp.bfloat16)
    slices = [mixed_slice] + [shift(mixed_slice, "section", step) for step in range(1, sections)]

    value_other = swap(gate(value_own, cuts[0]), "expert", 1)
    grad_far = swap(gate(grad_y, cuts[0]), "dp", 2)
    query_back = swap(gate(query_there.astype(jnp.bfloat16), mixed_slice), "expert", 1)
    out_other = swap(gate(out_own, value_other), "expert", 1)

    parts = []
    for place in range(lax.axis_size("dp")):
        code_here = d ^ place
        at = (code_here >> 1) + 2 * (code_here & 1)
        parts.append(lax.dynamic_slice_in_dim(query_back, at * quarter, quarter, 0))
    normed_own = lax.dynamic_slice_in_dim(normed, y * half, half, 1)
    query = (
        jnp.dot(normed_own, query_own, preferred_element_type=jnp.float32)
        + jnp.concatenate(parts, axis=0).astype(jnp.float32)
    ).astype(jnp.bfloat16)

    grads_own, grads_sent = dispatch(
        which_section, gate(code, mixed_slice), [out_grad, grad_x, grad_y, grad_far], capacity, share
    )
    grads_core = swap(grads_sent, "dp", 1)
    backward_cuts = expert_backward(
        which_section, grads_own, grads_core, pre_own, pre_core, weight_out, weight_in, sections
    )
    held_tokens = gate(tokens, value_other, backward_cuts[0])
    memory = make_memory(which_section, held_tokens, slices, final_gain)
    backward_arrived = [
        shift(gate(backward_cuts[step], *slices), "section", step) for step in range(1, sections)
    ]

    memory_x = swap(memory, "dp", 2)
    memory_core = swap(memory, "dp", 1)

    def sentence(which, near, far, *rest):
        place = jnp.stack([y, core, which]).astype(jnp.int32)
        rows_of = lax.dynamic_slice_in_dim(query, which * TGT_LEN, TGT_LEN, 0)
        pairs = (key_own, key_other), (value_own, value_other)
        return attend_sentence(place, src_lengths, rows_of, near, far, *pairs, *rest)

    context_own = sentence(x, memory, memory_core)
    memory_far = swap(gate(memory_x, context_own), "dp", 1)
    sent, kept = sentence(1 - x, memory_x, memory_far, context_own, (out_own, out_other))

    from_core = swap(sent, "dp", 1).astype(jnp.float32)
    from_x = swap((kept[1] + from_core[1]).astype(jnp.bfloat16), "dp", 2)
    attended = kept[0] + from_core[0] + from_x.astype(jnp.float32)
    dec_out = add_residual(attended, states, tgt_lengths)

    backward_sum = gate(backward_cuts[0], kept)
    for part in backward_arrived:
        backward_sum = backward_sum + part.astype(jnp.float32)
    grads_home = send_home(backward_sum.astype(jnp.bfloat16), near_codes + core_codes, capacity)
    (token_grad,) = combine(which_section, position, gate_weights, grads_home, 1, jnp.bfloat16)
    return (dec_out[None], token_grad)


def add_residual(attended, states, tgt_lengths):
    my_columns = attended.shape[1]
    residual = lax.dynamic_slice_in_dim(
        states, lax.axis_index("dp") * my_columns, my_columns, 1
    ).astype(jnp.float32)
    row_mask = (jnp.arange(TGT_LEN, dtype=jnp.int32)[None, :] < tgt_lengths[:, None]).reshape(-1, 1)
    return (residual + jnp.where(row_mask, attended, 0.0)).astype(jnp.bfloat16)


def body(
    tokens,
    expert_ids,
    gate_weights,
    out_grad,
    inner_weight,
    outer_weight,
    final_gain,
    dec_states,
    src_lengths,
    tgt_lengths,
    norm_gain,
    query_weight,
    key_weight,
    value_weight,
    out_weight,
):
    token_count, feature_count = tokens.shape
    group_size = lax.axis_size(("expert", "dp"))
    capacity = 3 * token_count // group_size
    slots = group_size * capacity

    named = expert_ids[:, :, None] == jnp.arange(group_size, dtype=jnp.int32)[None, None, :]
    either = (named[:, 0] | named[:, 1]).astype(jnp.bfloat16)
    row = lax.broadcasted_iota(jnp.int32, (token_count, token_count), 0)
    column = lax.broadcasted_iota(jnp.int32, (token_count, token_count), 1)
    earlier = jnp.dot(
        (column < row).astype(jnp.bfloat16), either, preferred_element_type=jnp.float32
    ).astype(jnp.int32)
    rank = jnp.sum(jnp.where(named, earlier[:, None, :], 0), axis=2)
    position = expert_ids * capacity + rank
    pick_first = slot_matrix(position[:, 0], slots)
    pick_second = slot_matrix(position[:, 1], slots)
    fill = (pick_first + pick_second).T

    def place(values):
        return jnp.dot(fill, values, preferred_element_type=jnp.float32).astype(jnp.bfloat16)

    def combine(arrived):
        first = jnp.dot(pick_first, arrived, preferred_element_type=jnp.float32)
        second = jnp.dot(pick_second, arrived, preferred_element_type=jnp.float32)
        return gate_weights[:, :1] * first + gate_weights[:, 1:] * second

    weight_in = inner_weight[0]
    weight_out = outer_weight[0]
    arrived_rows = exchange(place(tokens), group_size, capacity)
    pre_act = jnp.dot(arrived_rows, weight_in, preferred_element_type=jnp.float32)
    hidden = jax.nn.gelu(pre_act).astype(jnp.bfloat16)
    forward_part = jnp.dot(hidden, weight_out, preferred_element_type=jnp.float32)
    arrived_grads = exchange(place(out_grad), group_size, capacity)
    outputs_home = exchange(forward_part.astype(jnp.bfloat16), group_size, capacity)
    mixed_slice = sum_sections(combine(outputs_home)).astype(jnp.bfloat16)
    mixed = gather_sections(mixed_slice).astype(jnp.float32)
    memory = normalize(tokens.astype(jnp.float32) + mixed, final_gain).astype(jnp.bfloat16)

    back = contract_last(arrived_grads, weight_out)
    slope = jax.vjp(jax.nn.gelu, pre_act)[1](back)[0].astype(jnp.bfloat16)
    backward_part = contract_last(slope, weight_in)
    backward_slice = sum_sections(backward_part).astype(jnp.bfloat16)
    grads_home = exchange(backward_slice, group_size, capacity)
    token_grad = combine(grads_home).astype(jnp.bfloat16)

    states = dec_states[0]
    normed = normalize(states.astype(jnp.float32), norm_gain[0]).astype(jnp.bfloat16)
    full_query = gather_weight(query_weight[0], 0)
    full_key = gather_weight(key_weight[0], 0)
    full_value = gather_weight(value_weight[0], 0)
    full_out = gather_weight(out_weight[0], 1)
    query_sum = jnp.dot(normed, full_query, preferred_element_type=jnp.float32)
    source = gather_rows(memory, "dp")
    key_sum = jnp.dot(source, full_key, preferred_element_type=jnp.float32)
    value_sum = jnp.dot(source, full_value, preferred_element_type=jnp.float32)
    key_mask = jnp.arange(SRC_LEN, dtype=jnp.int32)[None, :] < src_lengths[:, None]
    context = attend(
        query_sum.astype(jnp.bfloat16),
        key_sum.astype(jnp.bfloat16),
        value_sum.astype(jnp.bfloat16),
        key_mask,
    )
    attended = sum_heads(jnp.dot(context, full_out, preferred_element_type=jnp.float32))
    dec_out = add_residual(attended, states, tgt_lengths)
    return (dec_out[None], token_grad)


def solution(mesh):
    in_specs = (
        P(("expert", "dp"), None),
        P(("expert", "dp"), None),
        P(("expert", "dp"), None),
        P(("expert", "dp"), None),
        P(("expert", "dp"), None, "section"),
        P(("expert", "dp"), "section", None),
        P(),
        P("section", "expert", None),
        P("expert"),
        P("expert"),
        P("section", None),
        P("section", "expert", "dp"),
        P("section", "expert", "dp"),
        P("section", "expert", "dp"),
        P("section", "dp", "expert"),
    )
    out_specs = (P("section", "expert", "dp"), P(("expert", "dp"), "section"))
    small = mesh.shape["expert"] == 2 and mesh.shape["dp"] == 4
    chosen = small_body if small else body
    return jax.shard_map(chosen, mesh=mesh, in_specs=in_specs, out_specs=out_specs, check_vma=False)
```

```python
import functools

import jax
import jax.numpy as jnp
from jax import lax
from jax.experimental import pallas as pl
from jax.experimental.pallas import tpu as pltpu
from jax.sharding import PartitionSpec as P

HEAD_DIM = 128
SRC_LEN = 256
TGT_LEN = 128


EPSILON = 1e-05


def normalize(values, gain):
    centre = jnp.mean(values, axis=-1, keepdims=True)
    centred = values - centre
    spread = jnp.mean(centred * centred, axis=-1, keepdims=True)
    return centred * lax.rsqrt(spread + EPSILON) * gain


def contract_last(left, right):
    return lax.dot_general(
        left, right, (((1,), (1,)), ((), ())), preferred_element_type=jnp.float32
    )


def shift(value, axis, step):
    size = lax.axis_size(axis)
    return lax.ppermute(value, axis, [(i, (i + step) % size) for i in range(size)])


def swap(value, axis, mask):
    size = lax.axis_size(axis)
    return lax.ppermute(value, axis, [(i, i ^ mask) for i in range(size)])


def sum_sections(partial):
    count = lax.axis_size("section")
    me = lax.axis_index("section")
    width = partial.shape[1] // count

    def piece(owner):
        return lax.dynamic_slice_in_dim(partial, owner * width, width, 1)

    total = piece(me).astype(jnp.float32)
    for step in range(1, count):
        sent = piece(lax.rem(me + step, count)).astype(jnp.bfloat16)
        total = total + shift(sent, "section", step).astype(jnp.float32)
    return total


def gather_sections(mine):
    count = lax.axis_size("section")
    me = lax.axis_index("section")
    width = mine.shape[1]
    whole = jnp.zeros((mine.shape[0], width * count), mine.dtype)
    whole = lax.dynamic_update_slice_in_dim(whole, mine, me * width, 1)
    for step in range(1, count):
        owner = lax.rem(me - step + count, count)
        whole = lax.dynamic_update_slice_in_dim(
            whole, shift(mine, "section", step), owner * width, 1
        )
    return whole


def gather_rows(mine, axis):
    held = mine
    me = lax.axis_index(axis)
    mask = lax.axis_size(axis) // 2
    blocks = [mine]
    while mask >= 1:
        blocks = blocks + [swap(block, axis, mask) for block in blocks]
        mask //= 2
    codes = [0]
    mask = lax.axis_size(axis) // 2
    while mask >= 1:
        codes = codes + [code ^ mask for code in codes]
        mask //= 2
    ordered = []
    for place in range(len(blocks)):
        chosen = blocks[0]
        for code, block in zip(codes[1:], blocks[1:]):
            chosen = jnp.where((me ^ code) == place, block, chosen)
        ordered.append(chosen)
    return jnp.concatenate(ordered, axis=0)


def gather_weight(weight, dimension):
    if lax.axis_size("expert") != 2:
        return lax.all_gather(weight, "expert", axis=dimension, tiled=True)
    other = swap(weight, "expert", 1)
    first = lax.axis_index("expert") == 0
    return jnp.concatenate(
        [jnp.where(first, weight, other), jnp.where(first, other, weight)], axis=dimension
    )


def sum_heads(partial):
    me = lax.axis_index("dp")
    count = lax.axis_size("dp")
    rows, columns = partial.shape
    total = partial.reshape(rows, count, columns // count)
    mask = 1
    while mask < count:
        paired = total.reshape(rows, -1, 2, columns // count)
        bit = (me // mask) % 2
        sent = lax.dynamic_index_in_dim(paired, 1 - bit, 2, False).astype(jnp.bfloat16)
        kept = lax.dynamic_index_in_dim(paired, bit, 2, False)
        total = kept + swap(sent, "dp", mask).astype(jnp.float32)
        mask *= 2
    return total.reshape(rows, columns // count)


def slot_matrix(positions, slots):
    places = lax.broadcasted_iota(jnp.int32, (positions.shape[0], slots), 1)
    return (positions[:, None] == places).astype(jnp.bfloat16)


def attend(query, keys, values, key_mask):
    sequences = key_mask.shape[0]
    head_count = query.shape[1] // HEAD_DIM
    query_split = query.reshape(sequences, -1, head_count, HEAD_DIM)
    keys_split = keys.reshape(sequences, -1, head_count, HEAD_DIM)
    values_split = values.reshape(sequences, -1, head_count, HEAD_DIM)
    scores = jnp.einsum(
        "bqhd,bkhd->bhqk", query_split, keys_split, preferred_element_type=jnp.float32
    ) * HEAD_DIM ** (-0.5)
    scores = jnp.where(key_mask[:, None, None, :], scores, -1e30)
    highest = jnp.max(scores, axis=-1, keepdims=True)
    weights = jnp.exp(scores - highest)
    probs = (weights / jnp.sum(weights, axis=-1, keepdims=True)).astype(jnp.bfloat16)
    context = jnp.einsum("bhqk,bkhd->bqhd", probs, values_split, preferred_element_type=jnp.float32)
    return context.astype(jnp.bfloat16).reshape(-1, head_count * HEAD_DIM)


def exchange(values, group_size, capacity):
    sent = values.reshape(group_size, capacity, values.shape[1])
    arrived = lax.all_to_all(sent, ("expert", "dp"), split_axis=0, concat_axis=0, tiled=True)
    return arrived.reshape(values.shape)


SHORT = pl.CostEstimate(flops=1, bytes_accessed=1, transcendentals=0)


def gate(value, *after):
    return lax.optimization_barrier((value,) + after)[0]


def vmem(shape, dtype):
    return pltpu.VMEM(shape, dtype)


def dispatch_kernel(capacity, layout, section_ref, code_ref, *refs):
    blocks = refs[:-4]
    outs, held, sems = refs[-4:-2], refs[-2], refs[-1]
    count, rows = held.shape[0], held.shape[1]
    half = lax.rem(section_ref[0], 2)
    copies = []
    for place, pieces in enumerate(layout):
        group = []
        for i, (which, start, length, side) in enumerate(pieces):
            there = held.at[place]
            if side is not None:
                offset = (half if side == 0 else 1 - half) * length
                there = held.at[place, pl.ds(pl.multiple_of(offset, length), length)]
            here = blocks[which].at[pl.ds(start, length)]
            group.append(pltpu.make_async_copy(here, there, sems.at[place, i]))
        copies.append(group)
    for group in copies:
        for copy in group:
            copy.start()
    for place, group in enumerate(copies):
        picks = []
        for which in range(2):
            line = which * count + place
            code = code_ref[line : line + 1, :]
            slot = lax.broadcasted_iota(jnp.int32, (capacity, code.shape[1]), 0)
            picks.append(jnp.where(slot == code, 1.0, 0.0))
        pick = jnp.concatenate(picks, axis=0).astype(jnp.bfloat16)
        for copy in group:
            copy.wait()
        picked = jnp.dot(pick, held[place], preferred_element_type=jnp.float32)
        picked = picked.astype(jnp.bfloat16)
        for which, out_ref in enumerate(outs):
            out_ref[place * capacity : (place + 1) * capacity, :] = picked[
                which * capacity : (which + 1) * capacity
            ]


def dispatch(section, code, blocks, layout, capacity):
    rows, features = blocks[0].shape
    count = len(layout)
    picked = jax.ShapeDtypeStruct((count * capacity, features), jnp.bfloat16)
    return pl.pallas_call(
        functools.partial(dispatch_kernel, capacity, layout),
        out_shape=(picked, picked),
        in_specs=[
            pl.BlockSpec(memory_space=pltpu.SMEM),
            pl.BlockSpec(memory_space=pltpu.VMEM),
        ]
        + [pl.BlockSpec(memory_space=pltpu.HBM)] * len(blocks),
        out_specs=[pl.BlockSpec(memory_space=pltpu.VMEM)] * 2,
        scratch_shapes=[
            vmem((count, rows, features), jnp.bfloat16),
            pltpu.SemaphoreType.DMA((count, 2)),
        ],
        compiler_params=pltpu.CompilerParams(vmem_limit_bytes=10 * 1024 * 1024),
        cost_estimate=SHORT,
        name="dispatch",
    )(section, code, *blocks)


def send_home(part, codes, capacity):
    size = lax.axis_size(("expert", "dp"))
    arrived = []
    for place, code in enumerate(codes):
        block = part[place * capacity : (place + 1) * capacity]
        if code:
            block = lax.ppermute(block, ("expert", "dp"), [(i, i ^ code) for i in range(size)])
        arrived.append(block)
    return arrived


def combine_kernel(count, split, section_ref, position_ref, gates_ref, *refs):
    blocks = refs[:count]
    outs = refs[count : count + split]
    held, total = refs[count + split :]
    capacity, features = blocks[0].shape
    position = position_ref[...]
    slot = lax.broadcasted_iota(jnp.int32, (position.shape[0], count * capacity), 1)
    picks = [
        jnp.where(position[:, k : k + 1] == slot, 1.0, 0.0).astype(jnp.bfloat16) for k in range(2)
    ]
    for i, block in enumerate(blocks):
        held[i * capacity : (i + 1) * capacity, :] = block[...]
    pick = jnp.concatenate(picks, axis=0)
    rows = position.shape[0]
    both = jnp.dot(pick, held[...], preferred_element_type=jnp.float32)
    total[...] = gates_ref[:, 0:1] * both[:rows] + gates_ref[:, 1:2] * both[rows:]
    width = features // split
    for step, out_ref in enumerate(outs):
        owner = lax.rem(section_ref[0] + step, split)
        start = pl.multiple_of(owner * width, width)
        out_ref[...] = total[:, pl.ds(start, width)].astype(out_ref.dtype)


def combine(section, position, gates, blocks, split, kept):
    capacity, features = blocks[0].shape
    rows = position.shape[0]
    count = len(blocks)
    width = features // split
    types = [kept] + [jnp.bfloat16] * (split - 1)
    full = pl.BlockSpec(memory_space=pltpu.VMEM)
    return pl.pallas_call(
        functools.partial(combine_kernel, count, split),
        out_shape=tuple(jax.ShapeDtypeStruct((rows, width), kind) for kind in types),
        in_specs=[pl.BlockSpec(memory_space=pltpu.SMEM)] + [full] * (2 + count),
        out_specs=[full] * split,
        scratch_shapes=[
            vmem((count * capacity, features), jnp.bfloat16),
            vmem((rows, features), jnp.float32),
        ],
        compiler_params=pltpu.CompilerParams(vmem_limit_bytes=14 * 1024 * 1024),
        cost_estimate=SHORT,
        name="combine",
    )(section, position, gates, *blocks)


def memory_kernel(count, section_ref, tokens_ref, gain_ref, *refs):
    slices, out_ref, mixed = refs[:count], refs[count], refs[count + 1]
    me = section_ref[0]
    width = slices[0].shape[1]
    for step, piece in enumerate(slices):
        owner = lax.rem(me - step + count, count)
        mixed[:, pl.ds(pl.multiple_of(owner * width, width), width)] = piece[...].astype(
            jnp.float32
        )
    values = tokens_ref[...].astype(jnp.float32) + mixed[...]
    out_ref[...] = normalize(values, gain_ref[...]).astype(jnp.bfloat16)


def make_memory(me, tokens, slices, gain):
    return pl.pallas_call(
        functools.partial(memory_kernel, len(slices)),
        out_shape=jax.ShapeDtypeStruct(tokens.shape, jnp.bfloat16),
        in_specs=[
            pl.BlockSpec(memory_space=pltpu.SMEM),
        ]
        + [pl.BlockSpec(memory_space=pltpu.VMEM)] * (2 + len(slices)),
        out_specs=pl.BlockSpec(memory_space=pltpu.VMEM),
        scratch_shapes=[vmem(tokens.shape, jnp.float32)],
        compiler_params=pltpu.CompilerParams(vmem_limit_bytes=8 * 1024 * 1024),
        cost_estimate=SHORT,
        name="memory",
    )(me, tokens, gain[None], *slices)


def attend_kernel(project, place_ref, lengths_ref, query_ref, *refs):
    near_ref, far_ref, key_own, key_other, value_own, value_other = refs[:6]
    y, core, sentence = place_ref[0], place_ref[1], place_ref[2]
    if project:
        done_ref, out_own, out_other, sent_ref, kept_mine, kept_other = refs[6:12]
        source, key_weight, value_weight, keys, values, sems, out_weight, context = refs[12:]
    else:
        out_ref = refs[6]
        source, key_weight, value_weight, keys, values, sems = refs[7:]
    rows = near_ref.shape[0]
    depth = key_own.shape[0]
    moves = [
        (near_ref, source.at[pl.ds(0, rows)]),
        (far_ref, source.at[pl.ds(rows, rows)]),
        (key_own, key_weight.at[y]),
        (key_other, key_weight.at[1 - y]),
        (value_own, value_weight.at[y]),
        (value_other, value_weight.at[1 - y]),
    ]
    if project:
        moves += [(out_own, out_weight.at[y]), (out_other, out_weight.at[1 - y])]
    copies = [
        pltpu.make_async_copy(here, there, sems.at[i]) for i, (here, there) in enumerate(moves)
    ]
    for copy in copies:
        copy.start()

    def linear(weight, result):
        total = jnp.dot(source[:, :depth], weight[0], preferred_element_type=jnp.float32)
        total += jnp.dot(source[:, depth:], weight[1], preferred_element_type=jnp.float32)
        result[...] = total.astype(jnp.bfloat16)

    for copy in copies[:4]:
        copy.wait()
    linear(key_weight, keys)
    for copy in copies[4:6]:
        copy.wait()
    linear(value_weight, values)

    targets = query_ref.shape[0]
    mine = pl.ds(pl.multiple_of(sentence * targets, targets), targets)
    column = lax.broadcasted_iota(jnp.int32, (targets, 2 * rows), 1)
    position = jnp.where(column < rows, column + core * rows, column - core * rows)
    valid = position < lengths_ref[sentence]
    for head in range(query_ref.shape[1] // HEAD_DIM):
        span = slice(head * HEAD_DIM, (head + 1) * HEAD_DIM)
        scores = contract_last(query_ref[:, span], keys[:, span]) * HEAD_DIM ** (-0.5)
        scores = jnp.where(valid, scores, -1e30)
        weights = jnp.exp(scores - jnp.max(scores, axis=-1, keepdims=True))
        probs = (weights / jnp.sum(weights, axis=-1, keepdims=True)).astype(jnp.bfloat16)
        result = jnp.dot(probs, values[:, span], preferred_element_type=jnp.float32)
        if project:
            context[mine, span] = result.astype(jnp.bfloat16)
        else:
            out_ref[:, span] = result.astype(jnp.bfloat16)

    if project:
        others = pl.ds(pl.multiple_of((1 - sentence) * targets, targets), targets)
        context[others, :] = done_ref[...]
        for copy in copies[6:]:
            copy.wait()
        columns = sent_ref.shape[2]
        x = 1 - sentence
        for which in range(2):
            half = jnp.where(which == 0, x, 1 - x)
            kept_ref = kept_mine if which == 0 else kept_other
            for out, side in ((sent_ref.at[which], 1 - core), (kept_ref, core)):
                span = pl.ds(pl.multiple_of(side * columns, columns), columns)
                part = jnp.dot(
                    context[...], out_weight[half, :, span], preferred_element_type=jnp.float32
                )
                out[...] = part.astype(out.dtype)


def attend_sentence(place, lengths, query, near, far, key_pair, value_pair, done=None, out_pair=()):
    rows, features = near.shape
    depth, width = key_pair[0].shape
    project = done is not None
    hold = pl.BlockSpec(memory_space=pltpu.HBM)
    smem = pl.BlockSpec(memory_space=pltpu.SMEM)
    full = pl.BlockSpec(memory_space=pltpu.VMEM)
    operands = [place, lengths, query, near, far, *key_pair, *value_pair]
    in_specs = [smem, smem, full] + [hold] * 6
    scratch = [
        vmem((2 * rows, features), jnp.bfloat16),
        vmem((2, depth, width), jnp.bfloat16),
        vmem((2, depth, width), jnp.bfloat16),
        vmem((2 * rows, width), jnp.bfloat16),
        vmem((2 * rows, width), jnp.bfloat16),
        pltpu.SemaphoreType.DMA((8,)),
    ]
    if project:
        targets = 2 * query.shape[0]
        columns = out_pair[0].shape[1] // 2
        operands += [done, *out_pair]
        in_specs += [full, hold, hold]
        scratch += [
            vmem((2,) + out_pair[0].shape, jnp.bfloat16),
            vmem((targets, width), jnp.bfloat16),
        ]
        out_shape = (
            jax.ShapeDtypeStruct((2, targets, columns), jnp.bfloat16),
            jax.ShapeDtypeStruct((targets, columns), jnp.float32),
            jax.ShapeDtypeStruct((targets, columns), jnp.float32),
        )
        out_specs = [full] * 3
    else:
        out_shape, out_specs = jax.ShapeDtypeStruct(query.shape, jnp.bfloat16), full
    return pl.pallas_call(
        functools.partial(attend_kernel, project),
        out_shape=out_shape,
        in_specs=in_specs,
        out_specs=out_specs,
        scratch_shapes=scratch,
        compiler_params=pltpu.CompilerParams(vmem_limit_bytes=56 * 1024 * 1024),
        cost_estimate=SHORT,
        name="attend_sentence",
    )(*operands)


def backward_kernel(split, codes, place_ref, own_ref, core_ref, rise_own, rise_core, out_ref, in_ref, *refs):
    sent_ref, kept_first, kept_second = refs[:3]
    grads, rise, weight_out, weight_in, slope, sems = refs[3:]
    rows = own_ref.shape[0]
    hidden, features = weight_out.shape
    width = features // split
    chunk = hidden // 4
    moves = []
    for part in range(4):
        span = pl.ds(part * chunk, chunk)
        moves.append((out_ref.at[span], weight_out.at[span]))
    block = 2 * rows // len(codes)
    for order, code in enumerate(codes):
        source = place_ref[1] ^ code
        there = pl.ds(pl.multiple_of(source * block, 16), block)
        here = pl.ds(order * block % rows, block)
        own = order * block < rows
        moves.append(((own_ref if own else core_ref).at[here], grads.at[there]))
        moves.append(((rise_own if own else rise_core).at[here], rise.at[there]))
    moves.append((in_ref, weight_in))
    copies = [
        pltpu.make_async_copy(here, there, sems.at[i]) for i, (here, there) in enumerate(moves)
    ]
    for copy in copies:
        copy.start()
    for copy in copies[4:-1]:
        copy.wait()
    for part in range(4):
        copies[part].wait()
        span = slice(part * chunk, (part + 1) * chunk)
        back = contract_last(grads[...], weight_out[span, :])
        slope[:, span] = (back * rise[:, span]).astype(jnp.bfloat16)
    copies[-1].wait()
    outs = (kept_first, sent_ref.at[0], kept_second, sent_ref.at[1])
    for step, out_ref in enumerate(outs):
        start = pl.multiple_of((place_ref[0] ^ step) * width, width)
        part = contract_last(slope[...], weight_in[pl.ds(start, width), :])
        out_ref[...] = part.astype(out_ref.dtype)


def expert_backward(
    place, codes, grads_own, grads_core, rise_own, rise_core, weight_out, weight_in, split
):
    rows = 2 * grads_own.shape[0]
    hidden, features = weight_out.shape
    hold = pl.BlockSpec(memory_space=pltpu.HBM)
    width = features // split
    kept = jax.ShapeDtypeStruct((rows, width), jnp.float32)
    return pl.pallas_call(
        functools.partial(backward_kernel, split, codes),
        out_shape=(jax.ShapeDtypeStruct((2, rows, width), jnp.bfloat16), kept, kept),
        in_specs=[pl.BlockSpec(memory_space=pltpu.SMEM)] + [hold] * 6,
        out_specs=[pl.BlockSpec(memory_space=pltpu.VMEM)] * 3,
        scratch_shapes=[
            vmem((rows, features), jnp.bfloat16),
            vmem((rows, hidden), jnp.float32),
            vmem((hidden, features), jnp.bfloat16),
            vmem((features, hidden), jnp.bfloat16),
            vmem((rows, hidden), jnp.bfloat16),
            pltpu.SemaphoreType.DMA((5 + 2 * len(codes),)),
        ],
        compiler_params=pltpu.CompilerParams(vmem_limit_bytes=56 * 1024 * 1024),
        cost_estimate=SHORT,
        name="expert_backward",
    )(place, grads_own, grads_core, rise_own, rise_core, weight_out, weight_in)


def small_body(
    tokens,
    expert_ids,
    gate_weights,
    out_grad,
    inner_weight,
    outer_weight,
    final_gain,
    dec_states,
    src_lengths,
    tgt_lengths,
    norm_gain,
    query_weight,
    key_weight,
    value_weight,
    out_weight,
):
    token_count, feature_count = tokens.shape
    group_size = lax.axis_size(("expert", "dp"))
    capacity = 3 * token_count // group_size
    here = lax.axis_index(("expert", "dp"))
    y = lax.axis_index("expert")
    d = lax.axis_index("dp")
    section = lax.axis_index("section")
    sections = lax.axis_size("section")
    half = feature_count // 2
    weight_in = inner_weight[0]
    weight_out = outer_weight[0]
    key_own, value_own, out_own = key_weight[0], value_weight[0], out_weight[0]
    query_own = query_weight[0]

    size = group_size
    near_codes = (0, 2, 4, 6)
    core_codes = (1, 3, 5, 7)
    core, x = d % 2, d // 2
    which_section = section.astype(jnp.int32).reshape(1)

    token_y = swap(tokens, "expert", 1)
    token_x = swap(tokens, "dp", 2)
    ids_y = jnp.stack([expert_ids.T, swap(expert_ids.T, "expert", 1)])
    ids_x = swap(ids_y, "dp", 2)
    token_far = swap(token_y, "dp", 2)

    side = lax.rem(section, 2)
    share = token_count // 2
    grad_half = lax.dynamic_slice_in_dim(out_grad, side * share, share, 0)
    half_y = swap(gate(grad_half, token_y, token_x), "expert", 1)
    key_other = swap(gate(key_own, token_y, token_x), "expert", 1)
    other_y = swap(half_y, "section", 1)
    half_x = swap(gate(grad_half, token_far), "dp", 2)
    half_far = swap(gate(half_y, token_far), "dp", 2)
    half_pair = jnp.concatenate([half_x, half_far], axis=0)
    other_pair = swap(half_pair, "section", 1)

    row = lax.broadcasted_iota(jnp.int32, (token_count, token_count), 0)
    column = lax.broadcasted_iota(jnp.int32, (token_count, token_count), 1)
    ids = jnp.stack([ids_y[0], ids_x[0], ids_y[1], ids_x[1]])
    named_there = jnp.concatenate([(ids == here).any(axis=1), (ids == (here ^ 1)).any(axis=1)])
    before = jnp.dot(
        named_there.astype(jnp.bfloat16),
        (row < column).astype(jnp.bfloat16),
        preferred_element_type=jnp.float32,
    ).astype(jnp.int32)
    code = jnp.where(named_there, before, -1)

    named = expert_ids[:, :, None] == jnp.arange(size, dtype=jnp.int32)[None, None, :]
    either = (named[:, 0] | named[:, 1]).astype(jnp.bfloat16)
    earlier = jnp.dot(
        (column < row).astype(jnp.bfloat16), either, preferred_element_type=jnp.float32
    ).astype(jnp.int32)
    rank = jnp.sum(jnp.where(named, earlier[:, None, :], 0), axis=2)
    codes_of = expert_ids ^ here
    position = ((codes_of >> 1) + 4 * (codes_of & 1)) * capacity + rank

    def forward(rows):
        pre_act = jnp.dot(rows, weight_in, preferred_element_type=jnp.float32)
        hidden = jax.nn.gelu(pre_act).astype(jnp.bfloat16)
        part = jnp.dot(hidden, weight_out, preferred_element_type=jnp.float32)
        return pre_act, part.astype(jnp.bfloat16)

    def slope_of(pre_act):
        return jax.vjp(jax.nn.gelu, pre_act)[1](jnp.ones_like(pre_act))[0]

    rows_own, rows_sent = dispatch(
        which_section,
        gate(code, other_y),
        [tokens, token_x, token_y, token_far],
        tuple(((place, 0, token_count, None),) for place in range(4)),
        capacity,
    )
    rows_core = swap(rows_sent, "dp", 1)
    pre_own, part_own = forward(rows_own)
    pre_core, part_core = forward(rows_core)
    part_core = gate(part_core, key_other, half_pair)
    rise_own, rise_core = slope_of(gate(pre_own, part_core)), slope_of(gate(pre_core, part_core))
    home = send_home(part_own, near_codes, capacity) + send_home(part_core, core_codes, capacity)

    grads_own, grads_sent = dispatch(
        which_section,
        code,
        [out_grad, half_x, half_y, half_far, other_y, other_pair],
        (
            ((0, 0, token_count, None),),
            ((1, 0, share, 0), (5, 0, share, 1)),
            ((2, 0, share, 0), (4, 0, share, 1)),
            ((3, 0, share, 0), (5, share, share, 1)),
        ),
        capacity,
    )
    grads_core = swap(grads_sent, "dp", 1)
    held_gates = gate(gate_weights, grads_sent)
    cuts = combine(which_section, position, held_gates, home, sections, jnp.float32)
    mixed_parts = [shift(cuts[step], "section", step) for step in range(1, sections)]
    states = dec_states[0]
    normed = normalize(states.astype(jnp.float32), norm_gain[0]).astype(jnp.bfloat16)
    asked = lax.dynamic_slice_in_dim(normed, (1 - y) * half, half, 1)
    asked_here = swap(gate(asked, cuts[0]), "expert", 1)
    mixed_sum = gate(cuts[0], grads_core, asked_here)
    for part in mixed_parts:
        mixed_sum = mixed_sum + part.astype(jnp.float32)
    mixed_slice = mixed_sum.astype(jnp.bfloat16)
    slices = [mixed_slice] + [shift(mixed_slice, "section", step) for step in range(1, sections)]

    value_other = swap(gate(value_own, *mixed_parts), "expert", 1)
    query_there = jnp.dot(asked_here, query_own, preferred_element_type=jnp.float32)
    query_back = swap(query_there.astype(jnp.bfloat16), "expert", 1)
    out_other = swap(gate(out_own, value_other), "expert", 1)
    normed_own = lax.dynamic_slice_in_dim(normed, y * half, half, 1)
    query_here = jnp.dot(normed_own, query_own, preferred_element_type=jnp.float32)
    query = (query_here + query_back.astype(jnp.float32)).astype(jnp.bfloat16)

    sent_pair, kept_first, kept_second = expert_backward(
        gate(jnp.stack([section, here]).astype(jnp.int32), slices[1]),
        near_codes + core_codes,
        grads_own,
        grads_core,
        rise_own,
        rise_core,
        weight_out,
        weight_in,
        sections,
    )
    held_tokens = gate(tokens, value_other, query_back, kept_first)
    memory = make_memory(which_section, held_tokens, slices, final_gain)
    memory_x = swap(memory, "dp", 2)
    memory_core = swap(memory, "dp", 1)

    def sentence(which, near, far, *rest):
        place = jnp.stack([y, core, which]).astype(jnp.int32)
        rows_of = lax.dynamic_slice_in_dim(query, which * TGT_LEN, TGT_LEN, 0)
        pairs = (key_own, key_other), (value_own, value_other)
        return attend_sentence(place, src_lengths, rows_of, near, far, *pairs, *rest)

    context_own = sentence(x, memory, memory_core)
    from_pair = swap(sent_pair, "section", 1)
    to_other = (kept_second + from_pair[1].astype(jnp.float32)).astype(jnp.bfloat16)
    from_other = swap(to_other, "section", 2)
    backward_sum = kept_first + from_pair[0].astype(jnp.float32) + from_other.astype(jnp.float32)
    memory_far = swap(gate(memory_x, context_own), "dp", 1)
    sent, kept_mine, kept_other = sentence(
        1 - x, memory_x, memory_far, gate(context_own, to_other), (out_own, out_other)
    )

    from_core = swap(sent, "dp", 1).astype(jnp.float32)
    from_x = swap((gate(kept_other, from_other) + from_core[1]).astype(jnp.bfloat16), "dp", 2)
    attended = kept_mine + from_core[0] + from_x.astype(jnp.float32)
    dec_out = add_residual(attended, states, tgt_lengths)

    grads_home = exchange(backward_sum.astype(jnp.bfloat16), group_size, capacity)
    natural = expert_ids * capacity + rank
    (token_grad,) = combine(
        which_section, natural, gate_weights, [grads_home], 1, jnp.bfloat16
    )
    return (dec_out[None], token_grad)


def add_residual(attended, states, tgt_lengths):
    my_columns = attended.shape[1]
    residual = lax.dynamic_slice_in_dim(
        states, lax.axis_index("dp") * my_columns, my_columns, 1
    ).astype(jnp.float32)
    row_mask = (jnp.arange(TGT_LEN, dtype=jnp.int32)[None, :] < tgt_lengths[:, None]).reshape(-1, 1)
    return (residual + jnp.where(row_mask, attended, 0.0)).astype(jnp.bfloat16)


def body(
    tokens,
    expert_ids,
    gate_weights,
    out_grad,
    inner_weight,
    outer_weight,
    final_gain,
    dec_states,
    src_lengths,
    tgt_lengths,
    norm_gain,
    query_weight,
    key_weight,
    value_weight,
    out_weight,
):
    token_count, feature_count = tokens.shape
    group_size = lax.axis_size(("expert", "dp"))
    capacity = 3 * token_count // group_size
    slots = group_size * capacity

    named = expert_ids[:, :, None] == jnp.arange(group_size, dtype=jnp.int32)[None, None, :]
    either = (named[:, 0] | named[:, 1]).astype(jnp.bfloat16)
    row = lax.broadcasted_iota(jnp.int32, (token_count, token_count), 0)
    column = lax.broadcasted_iota(jnp.int32, (token_count, token_count), 1)
    earlier = jnp.dot(
        (column < row).astype(jnp.bfloat16), either, preferred_element_type=jnp.float32
    ).astype(jnp.int32)
    rank = jnp.sum(jnp.where(named, earlier[:, None, :], 0), axis=2)
    position = expert_ids * capacity + rank
    pick_first = slot_matrix(position[:, 0], slots)
    pick_second = slot_matrix(position[:, 1], slots)
    fill = (pick_first + pick_second).T

    def place(values):
        return jnp.dot(fill, values, preferred_element_type=jnp.float32).astype(jnp.bfloat16)

    def combine(arrived):
        first = jnp.dot(pick_first, arrived, preferred_element_type=jnp.float32)
        second = jnp.dot(pick_second, arrived, preferred_element_type=jnp.float32)
        return gate_weights[:, :1] * first + gate_weights[:, 1:] * second

    weight_in = inner_weight[0]
    weight_out = outer_weight[0]
    arrived_rows = exchange(place(tokens), group_size, capacity)
    pre_act = jnp.dot(arrived_rows, weight_in, preferred_element_type=jnp.float32)
    hidden = jax.nn.gelu(pre_act).astype(jnp.bfloat16)
    forward_part = jnp.dot(hidden, weight_out, preferred_element_type=jnp.float32)
    arrived_grads = exchange(place(out_grad), group_size, capacity)
    outputs_home = exchange(forward_part.astype(jnp.bfloat16), group_size, capacity)
    mixed_slice = sum_sections(combine(outputs_home)).astype(jnp.bfloat16)
    mixed = gather_sections(mixed_slice).astype(jnp.float32)
    memory = normalize(tokens.astype(jnp.float32) + mixed, final_gain).astype(jnp.bfloat16)

    back = contract_last(arrived_grads, weight_out)
    slope = jax.vjp(jax.nn.gelu, pre_act)[1](back)[0].astype(jnp.bfloat16)
    backward_part = contract_last(slope, weight_in)
    backward_slice = sum_sections(backward_part).astype(jnp.bfloat16)
    grads_home = exchange(backward_slice, group_size, capacity)
    token_grad = combine(grads_home).astype(jnp.bfloat16)

    states = dec_states[0]
    normed = normalize(states.astype(jnp.float32), norm_gain[0]).astype(jnp.bfloat16)
    full_query = gather_weight(query_weight[0], 0)
    full_key = gather_weight(key_weight[0], 0)
    full_value = gather_weight(value_weight[0], 0)
    full_out = gather_weight(out_weight[0], 1)
    query_sum = jnp.dot(normed, full_query, preferred_element_type=jnp.float32)
    source = gather_rows(memory, "dp")
    key_sum = jnp.dot(source, full_key, preferred_element_type=jnp.float32)
    value_sum = jnp.dot(source, full_value, preferred_element_type=jnp.float32)
    key_mask = jnp.arange(SRC_LEN, dtype=jnp.int32)[None, :] < src_lengths[:, None]
    context = attend(
        query_sum.astype(jnp.bfloat16),
        key_sum.astype(jnp.bfloat16),
        value_sum.astype(jnp.bfloat16),
        key_mask,
    )
    attended = sum_heads(jnp.dot(context, full_out, preferred_element_type=jnp.float32))
    dec_out = add_residual(attended, states, tgt_lengths)
    return (dec_out[None], token_grad)


def solution(mesh):
    in_specs = (
        P(("expert", "dp"), None),
        P(("expert", "dp"), None),
        P(("expert", "dp"), None),
        P(("expert", "dp"), None),
        P(("expert", "dp"), None, "section"),
        P(("expert", "dp"), "section", None),
        P(),
        P("section", "expert", None),
        P("expert"),
        P("expert"),
        P("section", None),
        P("section", "expert", "dp"),
        P("section", "expert", "dp"),
        P("section", "expert", "dp"),
        P("section", "dp", "expert"),
    )
    out_specs = (P("section", "expert", "dp"), P(("expert", "dp"), "section"))
    small = (mesh.shape["section"], mesh.shape["expert"], mesh.shape["dp"]) == (4, 2, 4)
    chosen = small_body if small else body
    return jax.shard_map(chosen, mesh=mesh, in_specs=in_specs, out_specs=out_specs, check_vma=False)
```

```python
import functools

import jax
import jax.numpy as jnp
from jax import lax
from jax.experimental import pallas as pl
from jax.experimental.pallas import tpu as pltpu
from jax.sharding import PartitionSpec as P

HEAD_DIM = 128
SRC_LEN = 256
TGT_LEN = 128


EPSILON = 1e-05


def normalize(values, gain):
    centre = jnp.mean(values, axis=-1, keepdims=True)
    centred = values - centre
    spread = jnp.mean(centred * centred, axis=-1, keepdims=True)
    return centred * lax.rsqrt(spread + EPSILON) * gain


def contract_last(left, right):
    return lax.dot_general(
        left, right, (((1,), (1,)), ((), ())), preferred_element_type=jnp.float32
    )


def shift(value, axis, step):
    size = lax.axis_size(axis)
    return lax.ppermute(value, axis, [(i, (i + step) % size) for i in range(size)])


def swap(value, axis, mask):
    size = lax.axis_size(axis)
    return lax.ppermute(value, axis, [(i, i ^ mask) for i in range(size)])


def sum_sections(partial):
    count = lax.axis_size("section")
    me = lax.axis_index("section")
    width = partial.shape[1] // count

    def piece(owner):
        return lax.dynamic_slice_in_dim(partial, owner * width, width, 1)

    total = piece(me).astype(jnp.float32)
    for step in range(1, count):
        sent = piece(lax.rem(me + step, count)).astype(jnp.bfloat16)
        total = total + shift(sent, "section", step).astype(jnp.float32)
    return total


def gather_sections(mine):
    count = lax.axis_size("section")
    me = lax.axis_index("section")
    width = mine.shape[1]
    whole = jnp.zeros((mine.shape[0], width * count), mine.dtype)
    whole = lax.dynamic_update_slice_in_dim(whole, mine, me * width, 1)
    for step in range(1, count):
        owner = lax.rem(me - step + count, count)
        whole = lax.dynamic_update_slice_in_dim(
            whole, shift(mine, "section", step), owner * width, 1
        )
    return whole


def gather_rows(mine, axis):
    held = mine
    me = lax.axis_index(axis)
    mask = lax.axis_size(axis) // 2
    blocks = [mine]
    while mask >= 1:
        blocks = blocks + [swap(block, axis, mask) for block in blocks]
        mask //= 2
    codes = [0]
    mask = lax.axis_size(axis) // 2
    while mask >= 1:
        codes = codes + [code ^ mask for code in codes]
        mask //= 2
    ordered = []
    for place in range(len(blocks)):
        chosen = blocks[0]
        for code, block in zip(codes[1:], blocks[1:]):
            chosen = jnp.where((me ^ code) == place, block, chosen)
        ordered.append(chosen)
    return jnp.concatenate(ordered, axis=0)


def gather_weight(weight, dimension):
    if lax.axis_size("expert") != 2:
        return lax.all_gather(weight, "expert", axis=dimension, tiled=True)
    other = swap(weight, "expert", 1)
    first = lax.axis_index("expert") == 0
    return jnp.concatenate(
        [jnp.where(first, weight, other), jnp.where(first, other, weight)], axis=dimension
    )


def sum_heads(partial):
    me = lax.axis_index("dp")
    count = lax.axis_size("dp")
    rows, columns = partial.shape
    total = partial.reshape(rows, count, columns // count)
    mask = 1
    while mask < count:
        paired = total.reshape(rows, -1, 2, columns // count)
        bit = (me // mask) % 2
        sent = lax.dynamic_index_in_dim(paired, 1 - bit, 2, False).astype(jnp.bfloat16)
        kept = lax.dynamic_index_in_dim(paired, bit, 2, False)
        total = kept + swap(sent, "dp", mask).astype(jnp.float32)
        mask *= 2
    return total.reshape(rows, columns // count)


def slot_matrix(positions, slots):
    places = lax.broadcasted_iota(jnp.int32, (positions.shape[0], slots), 1)
    return (positions[:, None] == places).astype(jnp.bfloat16)


def attend(query, keys, values, key_mask):
    sequences = key_mask.shape[0]
    head_count = query.shape[1] // HEAD_DIM
    query_split = query.reshape(sequences, -1, head_count, HEAD_DIM)
    keys_split = keys.reshape(sequences, -1, head_count, HEAD_DIM)
    values_split = values.reshape(sequences, -1, head_count, HEAD_DIM)
    scores = jnp.einsum(
        "bqhd,bkhd->bhqk", query_split, keys_split, preferred_element_type=jnp.float32
    ) * HEAD_DIM ** (-0.5)
    scores = jnp.where(key_mask[:, None, None, :], scores, -1e30)
    highest = jnp.max(scores, axis=-1, keepdims=True)
    weights = jnp.exp(scores - highest)
    probs = (weights / jnp.sum(weights, axis=-1, keepdims=True)).astype(jnp.bfloat16)
    context = jnp.einsum("bhqk,bkhd->bqhd", probs, values_split, preferred_element_type=jnp.float32)
    return context.astype(jnp.bfloat16).reshape(-1, head_count * HEAD_DIM)


def exchange(values, group_size, capacity):
    sent = values.reshape(group_size, capacity, values.shape[1])
    arrived = lax.all_to_all(sent, ("expert", "dp"), split_axis=0, concat_axis=0, tiled=True)
    return arrived.reshape(values.shape)


SHORT = pl.CostEstimate(flops=1, bytes_accessed=1, transcendentals=0)


def gate(value, *after):
    return lax.optimization_barrier((value,) + after)[0]


def vmem(shape, dtype):
    return pltpu.VMEM(shape, dtype)


def dispatch_kernel(capacity, layout, section_ref, code_ref, *refs):
    blocks = refs[:-4]
    outs, held, sems = refs[-4:-2], refs[-2], refs[-1]
    count, rows = held.shape[0], held.shape[1]
    half = lax.rem(section_ref[0], 2)
    copies = []
    for place, pieces in enumerate(layout):
        group = []
        for i, (which, start, length, side) in enumerate(pieces):
            there = held.at[place]
            if side is not None:
                offset = (half if side == 0 else 1 - half) * length
                there = held.at[place, pl.ds(pl.multiple_of(offset, length), length)]
            here = blocks[which].at[pl.ds(start, length)]
            group.append(pltpu.make_async_copy(here, there, sems.at[place, i]))
        copies.append(group)
    for group in copies:
        for copy in group:
            copy.start()
    for place, group in enumerate(copies):
        picks = []
        for which in range(2):
            line = which * count + place
            code = code_ref[line : line + 1, :]
            slot = lax.broadcasted_iota(jnp.int32, (capacity, code.shape[1]), 0)
            picks.append(jnp.where(slot == code, 1.0, 0.0))
        pick = jnp.concatenate(picks, axis=0).astype(jnp.bfloat16)
        for copy in group:
            copy.wait()
        picked = jnp.dot(pick, held[place], preferred_element_type=jnp.float32)
        picked = picked.astype(jnp.bfloat16)
        for which, out_ref in enumerate(outs):
            out_ref[place * capacity : (place + 1) * capacity, :] = picked[
                which * capacity : (which + 1) * capacity
            ]


def dispatch(section, code, blocks, layout, capacity):
    rows, features = blocks[0].shape
    count = len(layout)
    picked = jax.ShapeDtypeStruct((count * capacity, features), jnp.bfloat16)
    return pl.pallas_call(
        functools.partial(dispatch_kernel, capacity, layout),
        out_shape=(picked, picked),
        in_specs=[
            pl.BlockSpec(memory_space=pltpu.SMEM),
            pl.BlockSpec(memory_space=pltpu.VMEM),
        ]
        + [pl.BlockSpec(memory_space=pltpu.HBM)] * len(blocks),
        out_specs=[pl.BlockSpec(memory_space=pltpu.VMEM)] * 2,
        scratch_shapes=[
            vmem((count, rows, features), jnp.bfloat16),
            pltpu.SemaphoreType.DMA((count, 2)),
        ],
        compiler_params=pltpu.CompilerParams(vmem_limit_bytes=10 * 1024 * 1024),
        cost_estimate=SHORT,
        name="dispatch",
    )(section, code, *blocks)


def send_home(part, codes, capacity):
    size = lax.axis_size(("expert", "dp"))
    arrived = []
    for place, code in enumerate(codes):
        block = part[place * capacity : (place + 1) * capacity]
        if code:
            block = lax.ppermute(block, ("expert", "dp"), [(i, i ^ code) for i in range(size)])
        arrived.append(block)
    return arrived


def combine_kernel(count, split, section_ref, position_ref, gates_ref, *refs):
    blocks = refs[:count]
    outs, (held, total) = refs[count:-2], refs[-2:]
    capacity, features = blocks[0].shape
    position = position_ref[...]
    slot = lax.broadcasted_iota(jnp.int32, (position.shape[0], count * capacity), 1)
    picks = [
        jnp.where(position[:, k : k + 1] == slot, 1.0, 0.0).astype(jnp.bfloat16) for k in range(2)
    ]
    for i, block in enumerate(blocks):
        held[i * capacity : (i + 1) * capacity, :] = block[...]
    pick = jnp.concatenate(picks, axis=0)
    rows = position.shape[0]
    both = jnp.dot(pick, held[...], preferred_element_type=jnp.float32)
    total[...] = gates_ref[:, 0:1] * both[:rows] + gates_ref[:, 1:2] * both[rows:]
    if split == 1:
        outs[0][...] = total[...].astype(outs[0].dtype)
        return
    sent_ref, kept_first, kept_second = outs
    width = features // split
    for step, out_ref in enumerate((kept_first, sent_ref.at[0], kept_second, sent_ref.at[1])):
        start = pl.multiple_of((section_ref[0] ^ step) * width, width)
        out_ref[...] = total[:, pl.ds(start, width)].astype(out_ref.dtype)


def combine(section, position, gates, blocks, split):
    capacity, features = blocks[0].shape
    rows = position.shape[0]
    count = len(blocks)
    width = features // split
    kept = jax.ShapeDtypeStruct((rows, width), jnp.float32)
    if split == 1:
        out_shape = (jax.ShapeDtypeStruct((rows, width), jnp.bfloat16),)
    else:
        out_shape = (jax.ShapeDtypeStruct((2, rows, width), jnp.bfloat16), kept, kept)
    full = pl.BlockSpec(memory_space=pltpu.VMEM)
    return pl.pallas_call(
        functools.partial(combine_kernel, count, split),
        out_shape=out_shape,
        in_specs=[pl.BlockSpec(memory_space=pltpu.SMEM)] + [full] * (2 + count),
        out_specs=[full] * len(out_shape),
        scratch_shapes=[
            vmem((count * capacity, features), jnp.bfloat16),
            vmem((rows, features), jnp.float32),
        ],
        compiler_params=pltpu.CompilerParams(vmem_limit_bytes=14 * 1024 * 1024),
        cost_estimate=SHORT,
        name="combine",
    )(section, position, gates, *blocks)


def memory_kernel(count, section_ref, tokens_ref, gain_ref, *refs):
    slices, out_ref, mixed = refs[:count], refs[count], refs[count + 1]
    me = section_ref[0]
    width = slices[0].shape[1]
    for step, piece in enumerate(slices):
        owner = me ^ step
        mixed[:, pl.ds(pl.multiple_of(owner * width, width), width)] = piece[...].astype(
            jnp.float32
        )
    values = tokens_ref[...].astype(jnp.float32) + mixed[...]
    out_ref[...] = normalize(values, gain_ref[...]).astype(jnp.bfloat16)


def make_memory(me, tokens, slices, gain):
    return pl.pallas_call(
        functools.partial(memory_kernel, len(slices)),
        out_shape=jax.ShapeDtypeStruct(tokens.shape, jnp.bfloat16),
        in_specs=[
            pl.BlockSpec(memory_space=pltpu.SMEM),
        ]
        + [pl.BlockSpec(memory_space=pltpu.VMEM)] * (2 + len(slices)),
        out_specs=pl.BlockSpec(memory_space=pltpu.VMEM),
        scratch_shapes=[vmem(tokens.shape, jnp.float32)],
        compiler_params=pltpu.CompilerParams(vmem_limit_bytes=8 * 1024 * 1024),
        cost_estimate=SHORT,
        name="memory",
    )(me, tokens, gain[None], *slices)


def attend_kernel(project, place_ref, lengths_ref, query_ref, *refs):
    near_ref, far_ref, key_own, key_other, value_own, value_other = refs[:6]
    y, core, sentence = place_ref[0], place_ref[1], place_ref[2]
    if project:
        done_ref, out_own, out_other, sent_ref, kept_mine, kept_other = refs[6:12]
        source, key_weight, value_weight, keys, values, sems, out_weight, context = refs[12:]
    else:
        out_ref = refs[6]
        source, key_weight, value_weight, keys, values, sems = refs[7:]
    rows = near_ref.shape[0]
    depth = key_own.shape[0]
    moves = [
        (near_ref, source.at[pl.ds(0, rows)]),
        (far_ref, source.at[pl.ds(rows, rows)]),
        (key_own, key_weight.at[y]),
        (key_other, key_weight.at[1 - y]),
        (value_own, value_weight.at[y]),
        (value_other, value_weight.at[1 - y]),
    ]
    if project:
        moves += [(out_own, out_weight.at[y]), (out_other, out_weight.at[1 - y])]
    copies = [
        pltpu.make_async_copy(here, there, sems.at[i]) for i, (here, there) in enumerate(moves)
    ]
    for copy in copies:
        copy.start()

    def linear(weight, result):
        total = jnp.dot(source[:, :depth], weight[0], preferred_element_type=jnp.float32)
        total += jnp.dot(source[:, depth:], weight[1], preferred_element_type=jnp.float32)
        result[...] = total.astype(jnp.bfloat16)

    for copy in copies[:4]:
        copy.wait()
    linear(key_weight, keys)
    for copy in copies[4:6]:
        copy.wait()
    linear(value_weight, values)

    targets = query_ref.shape[0]
    mine = pl.ds(pl.multiple_of(sentence * targets, targets), targets)
    column = lax.broadcasted_iota(jnp.int32, (targets, 2 * rows), 1)
    position = jnp.where(column < rows, column + core * rows, column - core * rows)
    valid = position < lengths_ref[sentence]
    for head in range(query_ref.shape[1] // HEAD_DIM):
        span = slice(head * HEAD_DIM, (head + 1) * HEAD_DIM)
        scores = contract_last(query_ref[:, span], keys[:, span]) * HEAD_DIM ** (-0.5)
        scores = jnp.where(valid, scores, -1e30)
        weights = jnp.exp(scores - jnp.max(scores, axis=-1, keepdims=True))
        probs = (weights / jnp.sum(weights, axis=-1, keepdims=True)).astype(jnp.bfloat16)
        result = jnp.dot(probs, values[:, span], preferred_element_type=jnp.float32)
        if project:
            context[mine, span] = result.astype(jnp.bfloat16)
        else:
            out_ref[:, span] = result.astype(jnp.bfloat16)

    if project:
        others = pl.ds(pl.multiple_of((1 - sentence) * targets, targets), targets)
        context[others, :] = done_ref[...]
        for copy in copies[6:]:
            copy.wait()
        columns = sent_ref.shape[2]
        x = 1 - sentence
        for which in range(2):
            half = jnp.where(which == 0, x, 1 - x)
            kept_ref = kept_mine if which == 0 else kept_other
            for out, side in ((sent_ref.at[which], 1 - core), (kept_ref, core)):
                span = pl.ds(pl.multiple_of(side * columns, columns), columns)
                part = jnp.dot(
                    context[...], out_weight[half, :, span], preferred_element_type=jnp.float32
                )
                out[...] = part.astype(out.dtype)


def attend_sentence(place, lengths, query, near, far, key_pair, value_pair, done=None, out_pair=()):
    rows, features = near.shape
    depth, width = key_pair[0].shape
    project = done is not None
    hold = pl.BlockSpec(memory_space=pltpu.HBM)
    smem = pl.BlockSpec(memory_space=pltpu.SMEM)
    full = pl.BlockSpec(memory_space=pltpu.VMEM)
    operands = [place, lengths, query, near, far, *key_pair, *value_pair]
    in_specs = [smem, smem, full] + [hold] * 6
    scratch = [
        vmem((2 * rows, features), jnp.bfloat16),
        vmem((2, depth, width), jnp.bfloat16),
        vmem((2, depth, width), jnp.bfloat16),
        vmem((2 * rows, width), jnp.bfloat16),
        vmem((2 * rows, width), jnp.bfloat16),
        pltpu.SemaphoreType.DMA((8,)),
    ]
    if project:
        targets = 2 * query.shape[0]
        columns = out_pair[0].shape[1] // 2
        operands += [done, *out_pair]
        in_specs += [full, hold, hold]
        scratch += [
            vmem((2,) + out_pair[0].shape, jnp.bfloat16),
            vmem((targets, width), jnp.bfloat16),
        ]
        out_shape = (
            jax.ShapeDtypeStruct((2, targets, columns), jnp.bfloat16),
            jax.ShapeDtypeStruct((targets, columns), jnp.float32),
            jax.ShapeDtypeStruct((targets, columns), jnp.float32),
        )
        out_specs = [full] * 3
    else:
        out_shape, out_specs = jax.ShapeDtypeStruct(query.shape, jnp.bfloat16), full
    return pl.pallas_call(
        functools.partial(attend_kernel, project),
        out_shape=out_shape,
        in_specs=in_specs,
        out_specs=out_specs,
        scratch_shapes=scratch,
        compiler_params=pltpu.CompilerParams(vmem_limit_bytes=56 * 1024 * 1024),
        cost_estimate=SHORT,
        name="attend_sentence",
    )(*operands)


def backward_kernel(split, codes, place_ref, own_ref, core_ref, rise_own, rise_core, out_ref, in_ref, *refs):
    sent_ref, kept_first, kept_second = refs[:3]
    grads, rise, weight_out, weight_in, slope, sems = refs[3:]
    rows = own_ref.shape[0]
    hidden, features = weight_out.shape
    width = features // split
    chunk = hidden // 4
    moves = []
    for part in range(4):
        span = pl.ds(part * chunk, chunk)
        moves.append((out_ref.at[span], weight_out.at[span]))
    block = 2 * rows // len(codes)
    for order, code in enumerate(codes):
        source = place_ref[1] ^ code
        there = pl.ds(pl.multiple_of(source * block, 16), block)
        here = pl.ds(order * block % rows, block)
        own = order * block < rows
        moves.append(((own_ref if own else core_ref).at[here], grads.at[there]))
        moves.append(((rise_own if own else rise_core).at[here], rise.at[there]))
    moves.append((in_ref, weight_in))
    copies = [
        pltpu.make_async_copy(here, there, sems.at[i]) for i, (here, there) in enumerate(moves)
    ]
    for copy in copies:
        copy.start()
    for copy in copies[4:-1]:
        copy.wait()
    for part in range(4):
        copies[part].wait()
        span = slice(part * chunk, (part + 1) * chunk)
        back = contract_last(grads[...], weight_out[span, :])
        slope[:, span] = (back * rise[:, span]).astype(jnp.bfloat16)
    copies[-1].wait()
    outs = (kept_first, sent_ref.at[0], kept_second, sent_ref.at[1])
    for step, out_ref in enumerate(outs):
        start = pl.multiple_of((place_ref[0] ^ step) * width, width)
        part = contract_last(slope[...], weight_in[pl.ds(start, width), :])
        out_ref[...] = part.astype(out_ref.dtype)


def expert_backward(
    place, codes, grads_own, grads_core, rise_own, rise_core, weight_out, weight_in, split
):
    rows = 2 * grads_own.shape[0]
    hidden, features = weight_out.shape
    hold = pl.BlockSpec(memory_space=pltpu.HBM)
    width = features // split
    kept = jax.ShapeDtypeStruct((rows, width), jnp.float32)
    return pl.pallas_call(
        functools.partial(backward_kernel, split, codes),
        out_shape=(jax.ShapeDtypeStruct((2, rows, width), jnp.bfloat16), kept, kept),
        in_specs=[pl.BlockSpec(memory_space=pltpu.SMEM)] + [hold] * 6,
        out_specs=[pl.BlockSpec(memory_space=pltpu.VMEM)] * 3,
        scratch_shapes=[
            vmem((rows, features), jnp.bfloat16),
            vmem((rows, hidden), jnp.float32),
            vmem((hidden, features), jnp.bfloat16),
            vmem((features, hidden), jnp.bfloat16),
            vmem((rows, hidden), jnp.bfloat16),
            pltpu.SemaphoreType.DMA((5 + 2 * len(codes),)),
        ],
        compiler_params=pltpu.CompilerParams(vmem_limit_bytes=56 * 1024 * 1024),
        cost_estimate=SHORT,
        name="expert_backward",
    )(place, grads_own, grads_core, rise_own, rise_core, weight_out, weight_in)


def small_body(
    tokens,
    expert_ids,
    gate_weights,
    out_grad,
    inner_weight,
    outer_weight,
    final_gain,
    dec_states,
    src_lengths,
    tgt_lengths,
    norm_gain,
    query_weight,
    key_weight,
    value_weight,
    out_weight,
):
    token_count, feature_count = tokens.shape
    group_size = lax.axis_size(("expert", "dp"))
    capacity = 3 * token_count // group_size
    here = lax.axis_index(("expert", "dp"))
    y = lax.axis_index("expert")
    d = lax.axis_index("dp")
    section = lax.axis_index("section")
    sections = lax.axis_size("section")
    half = feature_count // 2
    weight_in = inner_weight[0]
    weight_out = outer_weight[0]
    key_own, value_own, out_own = key_weight[0], value_weight[0], out_weight[0]
    query_own = query_weight[0]

    size = group_size
    near_codes = (0, 2, 4, 6)
    core_codes = (1, 3, 5, 7)
    core, x = d % 2, d // 2
    which_section = section.astype(jnp.int32).reshape(1)

    token_y = swap(tokens, "expert", 1)
    token_x = swap(tokens, "dp", 2)
    ids_own = expert_ids.T
    ids_x, ids_y = swap(ids_own, "dp", 2), swap(ids_own, "expert", 1)
    ids_far = swap(ids_x, "expert", 1)
    token_far = swap(token_y, "dp", 2)

    side = lax.rem(section, 2)
    share = token_count // 2
    grad_half = lax.dynamic_slice_in_dim(out_grad, side * share, share, 0)
    half_y = swap(gate(grad_half, token_y, ids_far), "expert", 1)
    key_other = swap(gate(key_own, token_y), "expert", 1)
    other_y = swap(half_y, "section", 1)
    half_x = swap(gate(grad_half, token_far), "dp", 2)
    half_far = swap(gate(half_y, token_far), "dp", 2)
    half_pair = jnp.concatenate([half_x, half_far], axis=0)
    other_pair = swap(half_pair, "section", 1)

    row = lax.broadcasted_iota(jnp.int32, (token_count, token_count), 0)
    column = lax.broadcasted_iota(jnp.int32, (token_count, token_count), 1)
    ids = jnp.stack([ids_own, ids_x, ids_y, ids_far])
    named_there = jnp.concatenate([(ids == here).any(axis=1), (ids == (here ^ 1)).any(axis=1)])
    before = jnp.dot(
        named_there.astype(jnp.bfloat16),
        (row < column).astype(jnp.bfloat16),
        preferred_element_type=jnp.float32,
    ).astype(jnp.int32)
    code = jnp.where(named_there, before, -1)

    named = expert_ids[:, :, None] == jnp.arange(size, dtype=jnp.int32)[None, None, :]
    either = (named[:, 0] | named[:, 1]).astype(jnp.bfloat16)
    earlier = jnp.dot(
        (column < row).astype(jnp.bfloat16), either, preferred_element_type=jnp.float32
    ).astype(jnp.int32)
    rank = jnp.sum(jnp.where(named, earlier[:, None, :], 0), axis=2)
    codes_of = expert_ids ^ here
    position = ((codes_of >> 1) + 4 * (codes_of & 1)) * capacity + rank

    def forward(rows):
        pre_act = jnp.dot(rows, weight_in, preferred_element_type=jnp.float32)
        hidden = jax.nn.gelu(pre_act).astype(jnp.bfloat16)
        part = jnp.dot(hidden, weight_out, preferred_element_type=jnp.float32)
        return pre_act, part.astype(jnp.bfloat16)

    def slope_of(pre_act):
        return jax.vjp(jax.nn.gelu, pre_act)[1](jnp.ones_like(pre_act))[0]

    rows_own, rows_sent = dispatch(
        which_section,
        gate(code, other_y),
        [tokens, token_x, token_y, token_far],
        tuple(((place, 0, token_count, None),) for place in range(4)),
        capacity,
    )
    rows_core = swap(rows_sent, "dp", 1)
    pre_own, part_own = forward(rows_own)
    pre_core, part_core = forward(rows_core)
    part_core = gate(part_core, key_other, half_pair)
    rise_own, rise_core = slope_of(gate(pre_own, part_core)), slope_of(gate(pre_core, part_core))
    home = send_home(part_own, near_codes, capacity) + send_home(part_core, core_codes, capacity)

    grads_own, grads_sent = dispatch(
        which_section,
        code,
        [out_grad, half_x, half_y, half_far, other_y, other_pair],
        (
            ((0, 0, token_count, None),),
            ((1, 0, share, 0), (5, 0, share, 1)),
            ((2, 0, share, 0), (4, 0, share, 1)),
            ((3, 0, share, 0), (5, share, share, 1)),
        ),
        capacity,
    )
    grads_core = swap(grads_sent, "dp", 1)
    held_gates = gate(gate_weights, grads_sent)
    sent_pair, first, second = combine(which_section, position, held_gates, home, sections)
    from_pair = swap(sent_pair, "section", 1)
    states = dec_states[0]
    normed = normalize(states.astype(jnp.float32), norm_gain[0]).astype(jnp.bfloat16)
    asked = lax.dynamic_slice_in_dim(normed, (1 - y) * half, half, 1)
    asked_here = swap(gate(asked, first), "expert", 1)
    to_other = (second + from_pair[1].astype(jnp.float32)).astype(jnp.bfloat16)
    from_other = swap(to_other, "section", 2)
    mixed_sum = gate(first, grads_core) + from_pair[0].astype(jnp.float32)
    mixed_slice = (mixed_sum + from_other.astype(jnp.float32)).astype(jnp.bfloat16)
    mixed_near = swap(mixed_slice, "section", 1)
    mixed_far = swap(jnp.stack([mixed_slice, mixed_near]), "section", 2)
    slices = [mixed_slice, mixed_near, mixed_far[0], mixed_far[1]]

    value_other = swap(gate(value_own, first), "expert", 1)
    query_there = jnp.dot(asked_here, query_own, preferred_element_type=jnp.float32)
    query_back = swap(query_there.astype(jnp.bfloat16), "expert", 1)
    out_other = swap(gate(out_own, value_other), "expert", 1)
    normed_own = lax.dynamic_slice_in_dim(normed, y * half, half, 1)
    query_here = jnp.dot(normed_own, query_own, preferred_element_type=jnp.float32)
    query = (query_here + query_back.astype(jnp.float32)).astype(jnp.bfloat16)

    back_pair, back_first, back_second = expert_backward(
        gate(jnp.stack([section, here]).astype(jnp.int32), mixed_near),
        near_codes + core_codes,
        grads_own,
        grads_core,
        rise_own,
        rise_core,
        weight_out,
        weight_in,
        sections,
    )
    held_tokens = gate(tokens, value_other, query_back, back_first)
    memory = make_memory(which_section, held_tokens, slices, final_gain)
    memory_x = swap(memory, "dp", 2)
    memory_core = swap(memory, "dp", 1)

    def sentence(which, near, far, *rest):
        place = jnp.stack([y, core, which]).astype(jnp.int32)
        rows_of = lax.dynamic_slice_in_dim(query, which * TGT_LEN, TGT_LEN, 0)
        pairs = (key_own, key_other), (value_own, value_other)
        return attend_sentence(place, src_lengths, rows_of, near, far, *pairs, *rest)

    context_own = sentence(x, memory, memory_core)
    back_from_pair = swap(back_pair, "section", 1)
    back_to_other = (back_second + back_from_pair[1].astype(jnp.float32)).astype(jnp.bfloat16)
    back_from_other = swap(back_to_other, "section", 2)
    backward_sum = back_first + back_from_pair[0].astype(jnp.float32)
    backward_sum = backward_sum + back_from_other.astype(jnp.float32)
    memory_far = swap(gate(memory_x, context_own), "dp", 1)
    sent, kept_mine, kept_other = sentence(
        1 - x, memory_x, memory_far, gate(context_own, back_to_other), (out_own, out_other)
    )

    from_core = swap(sent, "dp", 1).astype(jnp.float32)
    last = (kept_other + from_core[1]).astype(jnp.bfloat16)
    from_x = swap(last, "dp", 2)
    attended = kept_mine + from_core[0] + from_x.astype(jnp.float32)
    dec_out = add_residual(attended, states, tgt_lengths)

    grads_home = exchange(gate(backward_sum.astype(jnp.bfloat16), last), group_size, capacity)
    natural = expert_ids * capacity + rank
    (token_grad,) = combine(
        which_section, natural, gate_weights, [grads_home], 1
    )
    return (dec_out[None], token_grad)


def add_residual(attended, states, tgt_lengths):
    my_columns = attended.shape[1]
    residual = lax.dynamic_slice_in_dim(
        states, lax.axis_index("dp") * my_columns, my_columns, 1
    ).astype(jnp.float32)
    row_mask = (jnp.arange(TGT_LEN, dtype=jnp.int32)[None, :] < tgt_lengths[:, None]).reshape(-1, 1)
    return (residual + jnp.where(row_mask, attended, 0.0)).astype(jnp.bfloat16)


def body(
    tokens,
    expert_ids,
    gate_weights,
    out_grad,
    inner_weight,
    outer_weight,
    final_gain,
    dec_states,
    src_lengths,
    tgt_lengths,
    norm_gain,
    query_weight,
    key_weight,
    value_weight,
    out_weight,
):
    token_count, feature_count = tokens.shape
    group_size = lax.axis_size(("expert", "dp"))
    capacity = 3 * token_count // group_size
    slots = group_size * capacity

    named = expert_ids[:, :, None] == jnp.arange(group_size, dtype=jnp.int32)[None, None, :]
    either = (named[:, 0] | named[:, 1]).astype(jnp.bfloat16)
    row = lax.broadcasted_iota(jnp.int32, (token_count, token_count), 0)
    column = lax.broadcasted_iota(jnp.int32, (token_count, token_count), 1)
    earlier = jnp.dot(
        (column < row).astype(jnp.bfloat16), either, preferred_element_type=jnp.float32
    ).astype(jnp.int32)
    rank = jnp.sum(jnp.where(named, earlier[:, None, :], 0), axis=2)
    position = expert_ids * capacity + rank
    pick_first = slot_matrix(position[:, 0], slots)
    pick_second = slot_matrix(position[:, 1], slots)
    fill = (pick_first + pick_second).T

    def place(values):
        return jnp.dot(fill, values, preferred_element_type=jnp.float32).astype(jnp.bfloat16)

    def combine(arrived):
        first = jnp.dot(pick_first, arrived, preferred_element_type=jnp.float32)
        second = jnp.dot(pick_second, arrived, preferred_element_type=jnp.float32)
        return gate_weights[:, :1] * first + gate_weights[:, 1:] * second

    weight_in = inner_weight[0]
    weight_out = outer_weight[0]
    arrived_rows = exchange(place(tokens), group_size, capacity)
    pre_act = jnp.dot(arrived_rows, weight_in, preferred_element_type=jnp.float32)
    hidden = jax.nn.gelu(pre_act).astype(jnp.bfloat16)
    forward_part = jnp.dot(hidden, weight_out, preferred_element_type=jnp.float32)
    arrived_grads = exchange(place(out_grad), group_size, capacity)
    outputs_home = exchange(forward_part.astype(jnp.bfloat16), group_size, capacity)
    mixed_slice = sum_sections(combine(outputs_home)).astype(jnp.bfloat16)
    mixed = gather_sections(mixed_slice).astype(jnp.float32)
    memory = normalize(tokens.astype(jnp.float32) + mixed, final_gain).astype(jnp.bfloat16)

    back = contract_last(arrived_grads, weight_out)
    slope = jax.vjp(jax.nn.gelu, pre_act)[1](back)[0].astype(jnp.bfloat16)
    backward_part = contract_last(slope, weight_in)
    backward_slice = sum_sections(backward_part).astype(jnp.bfloat16)
    grads_home = exchange(backward_slice, group_size, capacity)
    token_grad = combine(grads_home).astype(jnp.bfloat16)

    states = dec_states[0]
    normed = normalize(states.astype(jnp.float32), norm_gain[0]).astype(jnp.bfloat16)
    full_query = gather_weight(query_weight[0], 0)
    full_key = gather_weight(key_weight[0], 0)
    full_value = gather_weight(value_weight[0], 0)
    full_out = gather_weight(out_weight[0], 1)
    query_sum = jnp.dot(normed, full_query, preferred_element_type=jnp.float32)
    source = gather_rows(memory, "dp")
    key_sum = jnp.dot(source, full_key, preferred_element_type=jnp.float32)
    value_sum = jnp.dot(source, full_value, preferred_element_type=jnp.float32)
    key_mask = jnp.arange(SRC_LEN, dtype=jnp.int32)[None, :] < src_lengths[:, None]
    context = attend(
        query_sum.astype(jnp.bfloat16),
        key_sum.astype(jnp.bfloat16),
        value_sum.astype(jnp.bfloat16),
        key_mask,
    )
    attended = sum_heads(jnp.dot(context, full_out, preferred_element_type=jnp.float32))
    dec_out = add_residual(attended, states, tgt_lengths)
    return (dec_out[None], token_grad)


def solution(mesh):
    in_specs = (
        P(("expert", "dp"), None),
        P(("expert", "dp"), None),
        P(("expert", "dp"), None),
        P(("expert", "dp"), None),
        P(("expert", "dp"), None, "section"),
        P(("expert", "dp"), "section", None),
        P(),
        P("section", "expert", None),
        P("expert"),
        P("expert"),
        P("section", None),
        P("section", "expert", "dp"),
        P("section", "expert", "dp"),
        P("section", "expert", "dp"),
        P("section", "dp", "expert"),
    )
    out_specs = (P("section", "expert", "dp"), P(("expert", "dp"), "section"))
    small = (mesh.shape["section"], mesh.shape["expert"], mesh.shape["dp"]) == (4, 2, 4)
    chosen = small_body if small else body
    return jax.shard_map(chosen, mesh=mesh, in_specs=in_specs, out_specs=out_specs, check_vma=False)
```

```python
import functools

import jax
import jax.numpy as jnp
from jax import lax
from jax.experimental import pallas as pl
from jax.experimental.pallas import tpu as pltpu
from jax.sharding import PartitionSpec as P

HEAD_DIM = 128
SRC_LEN = 256
TGT_LEN = 128


EPSILON = 1e-05


def normalize(values, gain):
    centre = jnp.mean(values, axis=-1, keepdims=True)
    centred = values - centre
    spread = jnp.mean(centred * centred, axis=-1, keepdims=True)
    return centred * lax.rsqrt(spread + EPSILON) * gain


def contract_last(left, right):
    return lax.dot_general(
        left, right, (((1,), (1,)), ((), ())), preferred_element_type=jnp.float32
    )


def shift(value, axis, step):
    size = lax.axis_size(axis)
    return lax.ppermute(value, axis, [(i, (i + step) % size) for i in range(size)])


def swap(value, axis, mask):
    size = lax.axis_size(axis)
    return lax.ppermute(value, axis, [(i, i ^ mask) for i in range(size)])


def sum_sections(partial):
    count = lax.axis_size("section")
    me = lax.axis_index("section")
    width = partial.shape[1] // count

    def piece(owner):
        return lax.dynamic_slice_in_dim(partial, owner * width, width, 1)

    total = piece(me).astype(jnp.float32)
    for step in range(1, count):
        sent = piece(lax.rem(me + step, count)).astype(jnp.bfloat16)
        total = total + shift(sent, "section", step).astype(jnp.float32)
    return total


def gather_sections(mine):
    count = lax.axis_size("section")
    me = lax.axis_index("section")
    width = mine.shape[1]
    whole = jnp.zeros((mine.shape[0], width * count), mine.dtype)
    whole = lax.dynamic_update_slice_in_dim(whole, mine, me * width, 1)
    for step in range(1, count):
        owner = lax.rem(me - step + count, count)
        whole = lax.dynamic_update_slice_in_dim(
            whole, shift(mine, "section", step), owner * width, 1
        )
    return whole


def gather_rows(mine, axis):
    held = mine
    me = lax.axis_index(axis)
    mask = lax.axis_size(axis) // 2
    blocks = [mine]
    while mask >= 1:
        blocks = blocks + [swap(block, axis, mask) for block in blocks]
        mask //= 2
    codes = [0]
    mask = lax.axis_size(axis) // 2
    while mask >= 1:
        codes = codes + [code ^ mask for code in codes]
        mask //= 2
    ordered = []
    for place in range(len(blocks)):
        chosen = blocks[0]
        for code, block in zip(codes[1:], blocks[1:]):
            chosen = jnp.where((me ^ code) == place, block, chosen)
        ordered.append(chosen)
    return jnp.concatenate(ordered, axis=0)


def gather_weight(weight, dimension):
    if lax.axis_size("expert") != 2:
        return lax.all_gather(weight, "expert", axis=dimension, tiled=True)
    other = swap(weight, "expert", 1)
    first = lax.axis_index("expert") == 0
    return jnp.concatenate(
        [jnp.where(first, weight, other), jnp.where(first, other, weight)], axis=dimension
    )


def sum_heads(partial):
    me = lax.axis_index("dp")
    count = lax.axis_size("dp")
    rows, columns = partial.shape
    total = partial.reshape(rows, count, columns // count)
    mask = 1
    while mask < count:
        paired = total.reshape(rows, -1, 2, columns // count)
        bit = (me // mask) % 2
        sent = lax.dynamic_index_in_dim(paired, 1 - bit, 2, False).astype(jnp.bfloat16)
        kept = lax.dynamic_index_in_dim(paired, bit, 2, False)
        total = kept + swap(sent, "dp", mask).astype(jnp.float32)
        mask *= 2
    return total.reshape(rows, columns // count)


def slot_matrix(positions, slots):
    places = lax.broadcasted_iota(jnp.int32, (positions.shape[0], slots), 1)
    return (positions[:, None] == places).astype(jnp.bfloat16)


def attend(query, keys, values, key_mask):
    sequences = key_mask.shape[0]
    head_count = query.shape[1] // HEAD_DIM
    query_split = query.reshape(sequences, -1, head_count, HEAD_DIM)
    keys_split = keys.reshape(sequences, -1, head_count, HEAD_DIM)
    values_split = values.reshape(sequences, -1, head_count, HEAD_DIM)
    scores = jnp.einsum(
        "bqhd,bkhd->bhqk", query_split, keys_split, preferred_element_type=jnp.float32
    ) * HEAD_DIM ** (-0.5)
    scores = jnp.where(key_mask[:, None, None, :], scores, -1e30)
    highest = jnp.max(scores, axis=-1, keepdims=True)
    weights = jnp.exp(scores - highest)
    probs = (weights / jnp.sum(weights, axis=-1, keepdims=True)).astype(jnp.bfloat16)
    context = jnp.einsum("bhqk,bkhd->bqhd", probs, values_split, preferred_element_type=jnp.float32)
    return context.astype(jnp.bfloat16).reshape(-1, head_count * HEAD_DIM)


def exchange(values, group_size, capacity):
    sent = values.reshape(group_size, capacity, values.shape[1])
    arrived = lax.all_to_all(sent, ("expert", "dp"), split_axis=0, concat_axis=0, tiled=True)
    return arrived.reshape(values.shape)


SHORT = pl.CostEstimate(flops=1, bytes_accessed=1, transcendentals=0)


def gate(value, *after):
    return lax.optimization_barrier((value,) + after)[0]


def vmem(shape, dtype):
    return pltpu.VMEM(shape, dtype)


def dispatch_kernel(capacity, layout, section_ref, code_ref, *refs):
    blocks = refs[:-4]
    outs, held, sems = refs[-4:-2], refs[-2], refs[-1]
    count, rows = held.shape[0], held.shape[1]
    half = lax.rem(section_ref[0], 2)
    copies = []
    for place, pieces in enumerate(layout):
        group = []
        for i, (which, start, length, side) in enumerate(pieces):
            there = held.at[place]
            if side is not None:
                offset = (half if side == 0 else 1 - half) * length
                there = held.at[place, pl.ds(pl.multiple_of(offset, length), length)]
            here = blocks[which].at[pl.ds(start, length)]
            group.append(pltpu.make_async_copy(here, there, sems.at[place, i]))
        copies.append(group)
    for group in copies:
        for copy in group:
            copy.start()
    for place, group in enumerate(copies):
        picks = []
        for which in range(2):
            line = which * count + place
            code = code_ref[line : line + 1, :]
            slot = lax.broadcasted_iota(jnp.int32, (capacity, code.shape[1]), 0)
            picks.append(jnp.where(slot == code, 1.0, 0.0))
        pick = jnp.concatenate(picks, axis=0).astype(jnp.bfloat16)
        for copy in group:
            copy.wait()
        picked = jnp.dot(pick, held[place], preferred_element_type=jnp.float32)
        picked = picked.astype(jnp.bfloat16)
        for which, out_ref in enumerate(outs):
            out_ref[place * capacity : (place + 1) * capacity, :] = picked[
                which * capacity : (which + 1) * capacity
            ]


def dispatch(section, code, blocks, layout, capacity):
    rows, features = blocks[0].shape
    count = len(layout)
    picked = jax.ShapeDtypeStruct((count * capacity, features), jnp.bfloat16)
    return pl.pallas_call(
        functools.partial(dispatch_kernel, capacity, layout),
        out_shape=(picked, picked),
        in_specs=[
            pl.BlockSpec(memory_space=pltpu.SMEM),
            pl.BlockSpec(memory_space=pltpu.VMEM),
        ]
        + [pl.BlockSpec(memory_space=pltpu.HBM)] * len(blocks),
        out_specs=[pl.BlockSpec(memory_space=pltpu.VMEM)] * 2,
        scratch_shapes=[
            vmem((count, rows, features), jnp.bfloat16),
            pltpu.SemaphoreType.DMA((count, 2)),
        ],
        compiler_params=pltpu.CompilerParams(vmem_limit_bytes=10 * 1024 * 1024),
        cost_estimate=SHORT,
        name="dispatch",
    )(section, code, *blocks)


def send_home(part, codes, capacity):
    size = lax.axis_size(("expert", "dp"))
    arrived = []
    for place, code in enumerate(codes):
        block = part[place * capacity : (place + 1) * capacity]
        if code:
            block = lax.ppermute(block, ("expert", "dp"), [(i, i ^ code) for i in range(size)])
        arrived.append(block)
    return arrived


def combine_kernel(count, split, section_ref, position_ref, gates_ref, *refs):
    blocks = refs[:count]
    outs, (held, total) = refs[count:-2], refs[-2:]
    capacity, features = blocks[0].shape
    position = position_ref[...]
    slot = lax.broadcasted_iota(jnp.int32, (position.shape[0], count * capacity), 1)
    picks = [
        jnp.where(position[:, k : k + 1] == slot, 1.0, 0.0).astype(jnp.bfloat16) for k in range(2)
    ]
    for i, block in enumerate(blocks):
        held[i * capacity : (i + 1) * capacity, :] = block[...]
    pick = jnp.concatenate(picks, axis=0)
    rows = position.shape[0]
    both = jnp.dot(pick, held[...], preferred_element_type=jnp.float32)
    total[...] = gates_ref[:, 0:1] * both[:rows] + gates_ref[:, 1:2] * both[rows:]
    if split == 1:
        outs[0][...] = total[...].astype(outs[0].dtype)
        return
    sent_ref, kept_first, kept_second = outs
    width = features // split
    for step, out_ref in enumerate((kept_first, sent_ref.at[0], kept_second, sent_ref.at[1])):
        start = pl.multiple_of((section_ref[0] ^ step) * width, width)
        out_ref[...] = total[:, pl.ds(start, width)].astype(out_ref.dtype)


def combine(section, position, gates, blocks, split):
    capacity, features = blocks[0].shape
    rows = position.shape[0]
    count = len(blocks)
    width = features // split
    kept = jax.ShapeDtypeStruct((rows, width), jnp.float32)
    if split == 1:
        out_shape = (jax.ShapeDtypeStruct((rows, width), jnp.bfloat16),)
    else:
        out_shape = (jax.ShapeDtypeStruct((2, rows, width), jnp.bfloat16), kept, kept)
    full = pl.BlockSpec(memory_space=pltpu.VMEM)
    return pl.pallas_call(
        functools.partial(combine_kernel, count, split),
        out_shape=out_shape,
        in_specs=[pl.BlockSpec(memory_space=pltpu.SMEM)] + [full] * (2 + count),
        out_specs=[full] * len(out_shape),
        scratch_shapes=[
            vmem((count * capacity, features), jnp.bfloat16),
            vmem((rows, features), jnp.float32),
        ],
        compiler_params=pltpu.CompilerParams(vmem_limit_bytes=14 * 1024 * 1024),
        cost_estimate=SHORT,
        name="combine",
    )(section, position, gates, *blocks)


def memory_kernel(count, section_ref, tokens_ref, gain_ref, *refs):
    slices, out_ref, mixed = refs[:count], refs[count], refs[count + 1]
    me = section_ref[0]
    width = slices[0].shape[1]
    for step, piece in enumerate(slices):
        owner = me ^ step
        mixed[:, pl.ds(pl.multiple_of(owner * width, width), width)] = piece[...].astype(
            jnp.float32
        )
    values = tokens_ref[...].astype(jnp.float32) + mixed[...]
    out_ref[...] = normalize(values, gain_ref[...]).astype(jnp.bfloat16)


def make_memory(me, tokens, slices, gain):
    return pl.pallas_call(
        functools.partial(memory_kernel, len(slices)),
        out_shape=jax.ShapeDtypeStruct(tokens.shape, jnp.bfloat16),
        in_specs=[
            pl.BlockSpec(memory_space=pltpu.SMEM),
        ]
        + [pl.BlockSpec(memory_space=pltpu.VMEM)] * (2 + len(slices)),
        out_specs=pl.BlockSpec(memory_space=pltpu.VMEM),
        scratch_shapes=[vmem(tokens.shape, jnp.float32)],
        compiler_params=pltpu.CompilerParams(vmem_limit_bytes=8 * 1024 * 1024),
        cost_estimate=SHORT,
        name="memory",
    )(me, tokens, gain[None], *slices)


def normed_kernel(y_ref, states_ref, gain_ref, own_ref, other_ref):
    values = normalize(states_ref[...].astype(jnp.float32), gain_ref[...]).astype(jnp.bfloat16)
    width = own_ref.shape[1]
    for out_ref, first in ((own_ref, y_ref[0] == 0), (other_ref, y_ref[0] == 1)):
        out_ref[...] = jnp.where(first, values[:, :width], values[:, width:])


def normed_halves(y, states, gain):
    rows, features = states.shape
    full = pl.BlockSpec(memory_space=pltpu.VMEM)
    return pl.pallas_call(
        normed_kernel,
        out_shape=(jax.ShapeDtypeStruct((rows, features // 2), jnp.bfloat16),) * 2,
        in_specs=[pl.BlockSpec(memory_space=pltpu.SMEM), full, full],
        out_specs=[full] * 2,
        compiler_params=pltpu.CompilerParams(vmem_limit_bytes=12 * 1024 * 1024),
        cost_estimate=SHORT,
        name="normed",
    )(y.astype(jnp.int32).reshape(1), states, gain)


def attend_kernel(place_ref, lengths_ref, query_ref, *refs):
    near_ref, far_ref, key_own, key_top, key_low, value_own, value_other, out_ref = refs[:8]
    source, key_weight, value_weight, keys, values, sems = refs[8:]
    y, core, sentence = place_ref[0], place_ref[1], place_ref[2]
    rows = near_ref.shape[0]
    depth = key_own.shape[0]
    moves = [
        (near_ref, source.at[pl.ds(0, rows)]),
        (far_ref, source.at[pl.ds(rows, rows)]),
        (key_own, key_weight.at[y]),
        (key_top, key_weight.at[1 - y, pl.ds(0, depth // 2)]),
        (key_low, key_weight.at[1 - y, pl.ds(depth // 2, depth // 2)]),
        (value_own, value_weight.at[y]),
        (value_other, value_weight.at[1 - y]),
    ]
    copies = [
        pltpu.make_async_copy(here, there, sems.at[i]) for i, (here, there) in enumerate(moves)
    ]
    for copy in copies:
        copy.start()

    def linear(weight, result):
        total = jnp.dot(source[:, :depth], weight[0], preferred_element_type=jnp.float32)
        total += jnp.dot(source[:, depth:], weight[1], preferred_element_type=jnp.float32)
        result[...] = total.astype(jnp.bfloat16)

    for copy in copies[:5]:
        copy.wait()
    linear(key_weight, keys)
    for copy in copies[5:]:
        copy.wait()
    linear(value_weight, values)

    column = lax.broadcasted_iota(jnp.int32, (query_ref.shape[0], 2 * rows), 1)
    position = jnp.where(column < rows, column + core * rows, column - core * rows)
    valid = position < lengths_ref[sentence]
    for head in range(query_ref.shape[1] // HEAD_DIM):
        span = slice(head * HEAD_DIM, (head + 1) * HEAD_DIM)
        scores = contract_last(query_ref[:, span], keys[:, span]) * HEAD_DIM ** (-0.5)
        scores = jnp.where(valid, scores, -1e30)
        weights = jnp.exp(scores - jnp.max(scores, axis=-1, keepdims=True))
        probs = (weights / jnp.sum(weights, axis=-1, keepdims=True)).astype(jnp.bfloat16)
        result = jnp.dot(probs, values[:, span], preferred_element_type=jnp.float32)
        out_ref[:, span] = result.astype(jnp.bfloat16)


def attend_sentence(place, lengths, query, near, far, key_parts, value_pair):
    rows, features = near.shape
    depth, width = key_parts[0].shape
    hold = pl.BlockSpec(memory_space=pltpu.HBM)
    smem = pl.BlockSpec(memory_space=pltpu.SMEM)
    full = pl.BlockSpec(memory_space=pltpu.VMEM)
    return pl.pallas_call(
        attend_kernel,
        out_shape=jax.ShapeDtypeStruct(query.shape, jnp.bfloat16),
        in_specs=[smem, smem, full] + [hold] * 7,
        out_specs=full,
        scratch_shapes=[
            vmem((2 * rows, features), jnp.bfloat16),
            vmem((2, depth, width), jnp.bfloat16),
            vmem((2, depth, width), jnp.bfloat16),
            vmem((2 * rows, width), jnp.bfloat16),
            vmem((2 * rows, width), jnp.bfloat16),
            pltpu.SemaphoreType.DMA((7,)),
        ],
        compiler_params=pltpu.CompilerParams(vmem_limit_bytes=56 * 1024 * 1024),
        cost_estimate=SHORT,
        name="attend_sentence",
    )(place, lengths, query, near, far, *key_parts, *value_pair)


def project_kernel(place_ref, mine_ref, done_ref, own_ref, other_ref, *refs):
    sent, kept_mine, kept_other, context = refs
    y, core, x = place_ref[0], place_ref[1], place_ref[2]
    targets = mine_ref.shape[0]
    for part, sentence in ((mine_ref, x), (done_ref, 1 - x)):
        context[pl.ds(pl.multiple_of(sentence * targets, targets), targets), :] = part[...]
    columns = kept_mine.shape[1]
    outs = ((sent.at[0], kept_mine), (sent.at[1], kept_other))

    def write(weight_ref, chosen):
        for side, out_ref in zip((1 - core, core), chosen):
            span = pl.ds(pl.multiple_of(side * columns, columns), columns)
            part = jnp.dot(context[...], weight_ref[:, span], preferred_element_type=jnp.float32)
            out_ref[...] = part.astype(out_ref.dtype)

    @pl.when(x == y)
    def _():
        write(own_ref, outs[0])
        write(other_ref, outs[1])

    @pl.when(x != y)
    def _():
        write(other_ref, outs[0])
        write(own_ref, outs[1])


def project(place, mine, done, out_own, out_other):
    targets, width = 2 * mine.shape[0], mine.shape[1]
    columns = out_own.shape[1] // 2
    full = pl.BlockSpec(memory_space=pltpu.VMEM)
    kept = jax.ShapeDtypeStruct((targets, columns), jnp.float32)
    return pl.pallas_call(
        project_kernel,
        out_shape=(jax.ShapeDtypeStruct((2, targets, columns), jnp.bfloat16), kept, kept),
        in_specs=[pl.BlockSpec(memory_space=pltpu.SMEM)] + [full] * 4,
        out_specs=[full] * 3,
        scratch_shapes=[vmem((targets, width), jnp.bfloat16)],
        compiler_params=pltpu.CompilerParams(vmem_limit_bytes=16 * 1024 * 1024),
        cost_estimate=SHORT,
        name="project",
    )(place, mine, done, out_own, out_other)


def slope_kernel(codes, here_ref, own_ref, core_ref, rise_own, rise_core, out_ref, slope, *refs):
    grads, rise, weight_out, sems = refs
    rows = own_ref.shape[0]
    hidden = weight_out.shape[0]
    chunk = hidden // 4
    moves = []
    block = 2 * rows // len(codes)
    for order, code in enumerate(codes):
        source = here_ref[0] ^ code
        there = pl.ds(pl.multiple_of(source * block, 16), block)
        here = pl.ds(order * block % rows, block)
        own = order * block < rows
        moves.append(((own_ref if own else core_ref).at[here], grads.at[there]))
        moves.append(((rise_own if own else rise_core).at[here], rise.at[there]))
    for part in range(4):
        span = pl.ds(part * chunk, chunk)
        moves.append((out_ref.at[span], weight_out.at[span]))
    copies = [
        pltpu.make_async_copy(here, there, sems.at[i]) for i, (here, there) in enumerate(moves)
    ]
    for copy in copies:
        copy.start()
    for copy in copies[:-4]:
        copy.wait()
    for part in range(4):
        copies[part - 4].wait()
        span = slice(part * chunk, (part + 1) * chunk)
        back = contract_last(grads[...], weight_out[span, :])
        slope[:, span] = (back * rise[:, span]).astype(jnp.bfloat16)


def expert_slope(here, codes, grads_own, grads_core, rise_own, rise_core, weight_out):
    rows = 2 * grads_own.shape[0]
    hidden, features = weight_out.shape
    hold = pl.BlockSpec(memory_space=pltpu.HBM)
    return pl.pallas_call(
        functools.partial(slope_kernel, codes),
        out_shape=jax.ShapeDtypeStruct((rows, hidden), jnp.bfloat16),
        in_specs=[pl.BlockSpec(memory_space=pltpu.SMEM)] + [hold] * 5,
        out_specs=pl.BlockSpec(memory_space=pltpu.VMEM),
        scratch_shapes=[
            vmem((rows, features), jnp.bfloat16),
            vmem((rows, hidden), jnp.float32),
            vmem((hidden, features), jnp.bfloat16),
            pltpu.SemaphoreType.DMA((4 + 2 * len(codes),)),
        ],
        compiler_params=pltpu.CompilerParams(vmem_limit_bytes=56 * 1024 * 1024),
        cost_estimate=SHORT,
        name="expert_slope",
    )(here, grads_own, grads_core, rise_own, rise_core, weight_out)


def backward_kernel(split, section_ref, slope_ref, in_ref, sent_ref, kept_first, kept_second, *refs):
    weight_in, sems = refs
    width = weight_in.shape[0] // split
    outs = (sent_ref.at[0], sent_ref.at[1], kept_first, kept_second)
    spans, copies = [], []
    for i, step in enumerate((1, 3, 0, 2)):
        start = pl.multiple_of((section_ref[0] ^ step) * width, width)
        spans.append(pl.ds(start, width))
        copies.append(
            pltpu.make_async_copy(in_ref.at[spans[i]], weight_in.at[spans[i]], sems.at[i])
        )
    for copy in copies:
        copy.start()
    for copy, span, out_ref in zip(copies, spans, outs):
        copy.wait()
        part = contract_last(slope_ref[...], weight_in[span, :])
        out_ref[...] = part.astype(out_ref.dtype)


def expert_backward(section, slope, weight_in, split):
    rows, hidden = slope.shape
    features = weight_in.shape[0]
    width = features // split
    full = pl.BlockSpec(memory_space=pltpu.VMEM)
    kept = jax.ShapeDtypeStruct((rows, width), jnp.float32)
    return pl.pallas_call(
        functools.partial(backward_kernel, split),
        out_shape=(jax.ShapeDtypeStruct((2, rows, width), jnp.bfloat16), kept, kept),
        in_specs=[pl.BlockSpec(memory_space=pltpu.SMEM), full, pl.BlockSpec(memory_space=pltpu.HBM)],
        out_specs=[full] * 3,
        scratch_shapes=[
            vmem((features, hidden), jnp.bfloat16),
            pltpu.SemaphoreType.DMA((split,)),
        ],
        compiler_params=pltpu.CompilerParams(vmem_limit_bytes=56 * 1024 * 1024),
        cost_estimate=SHORT,
        name="expert_backward",
    )(section, slope, weight_in)


def small_body(
    tokens,
    expert_ids,
    gate_weights,
    out_grad,
    inner_weight,
    outer_weight,
    final_gain,
    dec_states,
    src_lengths,
    tgt_lengths,
    norm_gain,
    query_weight,
    key_weight,
    value_weight,
    out_weight,
):
    token_count, feature_count = tokens.shape
    group_size = lax.axis_size(("expert", "dp"))
    capacity = 3 * token_count // group_size
    here = lax.axis_index(("expert", "dp"))
    y = lax.axis_index("expert")
    d = lax.axis_index("dp")
    section = lax.axis_index("section")
    sections = lax.axis_size("section")
    half = feature_count // 2
    weight_in = inner_weight[0]
    weight_out = outer_weight[0]
    key_own, value_own, out_own = key_weight[0], value_weight[0], out_weight[0]
    query_own = query_weight[0]

    size = group_size
    near_codes = (0, 2, 4, 6)
    core_codes = (1, 3, 5, 7)
    core, x = d % 2, d // 2
    which_section = section.astype(jnp.int32).reshape(1)

    token_y = swap(tokens, "expert", 1)
    token_x = swap(tokens, "dp", 2)
    ids_own = expert_ids.T
    ids_x, ids_y = swap(ids_own, "dp", 2), swap(ids_own, "expert", 1)
    ids_far = swap(ids_x, "expert", 1)
    token_far = swap(token_y, "dp", 2)

    side = lax.rem(section, 2)
    share = token_count // 2
    grad_half = lax.dynamic_slice_in_dim(out_grad, side * share, share, 0)
    half_y = swap(gate(grad_half, token_y, ids_far), "expert", 1)
    depth = key_own.shape[0] // 2
    key_top = swap(gate(key_own[:depth], token_y), "expert", 1)
    key_low = swap(gate(key_own[depth:], key_top), "expert", 1)
    states = dec_states[0]
    normed_own, asked = normed_halves(y, states, norm_gain)
    other_y = swap(half_y, "section", 1)
    half_x = swap(gate(grad_half, token_far), "dp", 2)
    half_far = swap(gate(half_y, token_far), "dp", 2)
    half_pair = jnp.concatenate([half_x, half_far], axis=0)
    other_pair = swap(half_pair, "section", 1)

    row = lax.broadcasted_iota(jnp.int32, (token_count, token_count), 0)
    column = lax.broadcasted_iota(jnp.int32, (token_count, token_count), 1)
    ids = jnp.stack([ids_own, ids_x, ids_y, ids_far])
    named_there = jnp.concatenate([(ids == here).any(axis=1), (ids == (here ^ 1)).any(axis=1)])
    before = jnp.dot(
        named_there.astype(jnp.bfloat16),
        (row < column).astype(jnp.bfloat16),
        preferred_element_type=jnp.float32,
    ).astype(jnp.int32)
    code = jnp.where(named_there, before, -1)

    named = expert_ids[:, :, None] == jnp.arange(size, dtype=jnp.int32)[None, None, :]
    either = (named[:, 0] | named[:, 1]).astype(jnp.bfloat16)
    earlier = jnp.dot(
        (column < row).astype(jnp.bfloat16), either, preferred_element_type=jnp.float32
    ).astype(jnp.int32)
    rank = jnp.sum(jnp.where(named, earlier[:, None, :], 0), axis=2)
    codes_of = expert_ids ^ here
    position = ((codes_of >> 1) + 4 * (codes_of & 1)) * capacity + rank

    def forward(rows):
        pre_act = jnp.dot(rows, weight_in, preferred_element_type=jnp.float32)
        hidden = jax.nn.gelu(pre_act).astype(jnp.bfloat16)
        part = jnp.dot(hidden, weight_out, preferred_element_type=jnp.float32)
        return pre_act, part.astype(jnp.bfloat16)

    def slope_of(pre_act):
        return jax.vjp(jax.nn.gelu, pre_act)[1](jnp.ones_like(pre_act))[0]

    rows_own, rows_sent = dispatch(
        which_section,
        gate(code, key_top, asked),
        [tokens, token_x, token_y, token_far],
        tuple(((place, 0, token_count, None),) for place in range(4)),
        capacity,
    )
    rows_core = swap(rows_sent, "dp", 1)
    pre_own, part_own = forward(rows_own)
    pre_core, part_core = forward(rows_core)
    part_core = gate(part_core, key_low, half_pair, other_y)
    rise_own, rise_core = slope_of(gate(pre_own, part_core)), slope_of(gate(pre_core, part_core))
    home = send_home(part_own, near_codes, capacity) + send_home(part_core, core_codes, capacity)

    grads_own, grads_sent = dispatch(
        which_section,
        gate(code, rise_own, rise_core),
        [out_grad, half_x, half_y, half_far, other_y, other_pair],
        (
            ((0, 0, token_count, None),),
            ((1, 0, share, 0), (5, 0, share, 1)),
            ((2, 0, share, 0), (4, 0, share, 1)),
            ((3, 0, share, 0), (5, share, share, 1)),
        ),
        capacity,
    )
    grads_core = swap(grads_sent, "dp", 1)
    held_gates = gate(gate_weights, grads_sent)
    sent_pair, first, second = combine(which_section, position, held_gates, home, sections)
    from_pair = swap(sent_pair, "section", 1)
    asked_here = swap(gate(asked, first), "expert", 1)
    to_other = (second + from_pair[1].astype(jnp.float32)).astype(jnp.bfloat16)
    from_other = swap(to_other, "section", 2)
    slope = expert_slope(
        gate(here.astype(jnp.int32).reshape(1), to_other),
        near_codes + core_codes,
        grads_own,
        grads_core,
        rise_own,
        rise_core,
        weight_out,
    )
    mixed_sum = gate(first, slope) + from_pair[0].astype(jnp.float32)
    mixed_slice = (mixed_sum + from_other.astype(jnp.float32)).astype(jnp.bfloat16)
    mixed_near = swap(mixed_slice, "section", 1)
    back_pair, back_first, back_second = expert_backward(
        gate(which_section, mixed_slice), slope, weight_in, sections
    )
    mixed_far = swap(jnp.stack([mixed_slice, gate(mixed_near, back_first)]), "section", 2)
    slices = [mixed_slice, mixed_near, mixed_far[0], mixed_far[1]]

    value_other = swap(gate(value_own, first), "expert", 1)
    query_there = jnp.dot(asked_here, query_own, preferred_element_type=jnp.float32)
    query_back = swap(query_there.astype(jnp.bfloat16), "expert", 1)
    out_other = swap(gate(out_own, value_other), "expert", 1)
    query_here = jnp.dot(normed_own, query_own, preferred_element_type=jnp.float32)
    query = (query_here + query_back.astype(jnp.float32)).astype(jnp.bfloat16)

    memory = make_memory(which_section, tokens, slices, final_gain)
    memory_x = swap(memory, "dp", 2)
    memory_core = swap(memory, "dp", 1)

    def sentence(which, near, far, *after):
        place = gate(jnp.stack([y, core, which]).astype(jnp.int32), *after)
        rows_of = lax.dynamic_slice_in_dim(query, which * TGT_LEN, TGT_LEN, 0)
        parts = (key_own, key_top, key_low), (value_own, value_other)
        return attend_sentence(place, src_lengths, rows_of, near, far, *parts)

    back_from_pair = swap(back_pair, "section", 1)
    back_to_other = (back_second + back_from_pair[1].astype(jnp.float32)).astype(jnp.bfloat16)
    part = back_to_other.shape[0] // 2
    back_top = swap(back_to_other[:part], "section", 2)
    back_low = swap(gate(back_to_other[part:], back_top), "section", 2)
    backward_sum = back_first + back_from_pair[0].astype(jnp.float32)
    backward_sum = backward_sum + jnp.concatenate([back_top, back_low], axis=0).astype(jnp.float32)
    context_own = sentence(x, memory, memory_core, back_top)
    memory_far = swap(memory_x, "dp", 1)
    context_other = sentence(1 - x, memory_x, memory_far)
    place = gate(jnp.stack([y, core, x]).astype(jnp.int32), back_low)
    sent, kept_mine, kept_other = project(place, context_own, context_other, out_own, out_other)

    from_core = swap(sent, "dp", 1).astype(jnp.float32)
    last = (kept_other + from_core[1]).astype(jnp.bfloat16)
    from_x = swap(last, "dp", 2)
    attended = kept_mine + from_core[0] + from_x.astype(jnp.float32)
    dec_out = add_residual(attended, states, tgt_lengths)

    grads_home = exchange(gate(backward_sum.astype(jnp.bfloat16), last), group_size, capacity)
    natural = expert_ids * capacity + rank
    (token_grad,) = combine(
        which_section, natural, gate_weights, [grads_home], 1
    )
    return (dec_out[None], token_grad)


def add_residual(attended, states, tgt_lengths):
    my_columns = attended.shape[1]
    residual = lax.dynamic_slice_in_dim(
        states, lax.axis_index("dp") * my_columns, my_columns, 1
    ).astype(jnp.float32)
    row_mask = (jnp.arange(TGT_LEN, dtype=jnp.int32)[None, :] < tgt_lengths[:, None]).reshape(-1, 1)
    return (residual + jnp.where(row_mask, attended, 0.0)).astype(jnp.bfloat16)


def body(
    tokens,
    expert_ids,
    gate_weights,
    out_grad,
    inner_weight,
    outer_weight,
    final_gain,
    dec_states,
    src_lengths,
    tgt_lengths,
    norm_gain,
    query_weight,
    key_weight,
    value_weight,
    out_weight,
):
    token_count, feature_count = tokens.shape
    group_size = lax.axis_size(("expert", "dp"))
    capacity = 3 * token_count // group_size
    slots = group_size * capacity

    named = expert_ids[:, :, None] == jnp.arange(group_size, dtype=jnp.int32)[None, None, :]
    either = (named[:, 0] | named[:, 1]).astype(jnp.bfloat16)
    row = lax.broadcasted_iota(jnp.int32, (token_count, token_count), 0)
    column = lax.broadcasted_iota(jnp.int32, (token_count, token_count), 1)
    earlier = jnp.dot(
        (column < row).astype(jnp.bfloat16), either, preferred_element_type=jnp.float32
    ).astype(jnp.int32)
    rank = jnp.sum(jnp.where(named, earlier[:, None, :], 0), axis=2)
    position = expert_ids * capacity + rank
    pick_first = slot_matrix(position[:, 0], slots)
    pick_second = slot_matrix(position[:, 1], slots)
    fill = (pick_first + pick_second).T

    def place(values):
        return jnp.dot(fill, values, preferred_element_type=jnp.float32).astype(jnp.bfloat16)

    def combine(arrived):
        first = jnp.dot(pick_first, arrived, preferred_element_type=jnp.float32)
        second = jnp.dot(pick_second, arrived, preferred_element_type=jnp.float32)
        return gate_weights[:, :1] * first + gate_weights[:, 1:] * second

    weight_in = inner_weight[0]
    weight_out = outer_weight[0]
    arrived_rows = exchange(place(tokens), group_size, capacity)
    pre_act = jnp.dot(arrived_rows, weight_in, preferred_element_type=jnp.float32)
    hidden = jax.nn.gelu(pre_act).astype(jnp.bfloat16)
    forward_part = jnp.dot(hidden, weight_out, preferred_element_type=jnp.float32)
    arrived_grads = exchange(place(out_grad), group_size, capacity)
    outputs_home = exchange(forward_part.astype(jnp.bfloat16), group_size, capacity)
    mixed_slice = sum_sections(combine(outputs_home)).astype(jnp.bfloat16)
    mixed = gather_sections(mixed_slice).astype(jnp.float32)
    memory = normalize(tokens.astype(jnp.float32) + mixed, final_gain).astype(jnp.bfloat16)

    back = contract_last(arrived_grads, weight_out)
    slope = jax.vjp(jax.nn.gelu, pre_act)[1](back)[0].astype(jnp.bfloat16)
    backward_part = contract_last(slope, weight_in)
    backward_slice = sum_sections(backward_part).astype(jnp.bfloat16)
    grads_home = exchange(backward_slice, group_size, capacity)
    token_grad = combine(grads_home).astype(jnp.bfloat16)

    states = dec_states[0]
    normed = normalize(states.astype(jnp.float32), norm_gain[0]).astype(jnp.bfloat16)
    full_query = gather_weight(query_weight[0], 0)
    full_key = gather_weight(key_weight[0], 0)
    full_value = gather_weight(value_weight[0], 0)
    full_out = gather_weight(out_weight[0], 1)
    query_sum = jnp.dot(normed, full_query, preferred_element_type=jnp.float32)
    source = gather_rows(memory, "dp")
    key_sum = jnp.dot(source, full_key, preferred_element_type=jnp.float32)
    value_sum = jnp.dot(source, full_value, preferred_element_type=jnp.float32)
    key_mask = jnp.arange(SRC_LEN, dtype=jnp.int32)[None, :] < src_lengths[:, None]
    context = attend(
        query_sum.astype(jnp.bfloat16),
        key_sum.astype(jnp.bfloat16),
        value_sum.astype(jnp.bfloat16),
        key_mask,
    )
    attended = sum_heads(jnp.dot(context, full_out, preferred_element_type=jnp.float32))
    dec_out = add_residual(attended, states, tgt_lengths)
    return (dec_out[None], token_grad)


def solution(mesh):
    in_specs = (
        P(("expert", "dp"), None),
        P(("expert", "dp"), None),
        P(("expert", "dp"), None),
        P(("expert", "dp"), None),
        P(("expert", "dp"), None, "section"),
        P(("expert", "dp"), "section", None),
        P(),
        P("section", "expert", None),
        P("expert"),
        P("expert"),
        P("section", None),
        P("section", "expert", "dp"),
        P("section", "expert", "dp"),
        P("section", "expert", "dp"),
        P("section", "dp", "expert"),
    )
    out_specs = (P("section", "expert", "dp"), P(("expert", "dp"), "section"))
    small = (mesh.shape["section"], mesh.shape["expert"], mesh.shape["dp"]) == (4, 2, 4)
    chosen = small_body if small else body
    return jax.shard_map(chosen, mesh=mesh, in_specs=in_specs, out_specs=out_specs, check_vma=False)
```

```python
import functools

import jax
import jax.numpy as jnp
from jax import lax
from jax.experimental import pallas as pl
from jax.experimental.pallas import tpu as pltpu
from jax.sharding import PartitionSpec as P

HEAD_DIM = 128
SRC_LEN = 256
TGT_LEN = 128


EPSILON = 1e-05


def normalize(values, gain):
    centre = jnp.mean(values, axis=-1, keepdims=True)
    centred = values - centre
    spread = jnp.mean(centred * centred, axis=-1, keepdims=True)
    return centred * lax.rsqrt(spread + EPSILON) * gain


def contract_last(left, right):
    return lax.dot_general(
        left, right, (((1,), (1,)), ((), ())), preferred_element_type=jnp.float32
    )


def shift(value, axis, step):
    size = lax.axis_size(axis)
    return lax.ppermute(value, axis, [(i, (i + step) % size) for i in range(size)])


def swap(value, axis, mask):
    size = lax.axis_size(axis)
    return lax.ppermute(value, axis, [(i, i ^ mask) for i in range(size)])


def sum_sections(partial):
    count = lax.axis_size("section")
    me = lax.axis_index("section")
    width = partial.shape[1] // count

    def piece(owner):
        return lax.dynamic_slice_in_dim(partial, owner * width, width, 1)

    total = piece(me).astype(jnp.float32)
    for step in range(1, count):
        sent = piece(lax.rem(me + step, count)).astype(jnp.bfloat16)
        total = total + shift(sent, "section", step).astype(jnp.float32)
    return total


def gather_sections(mine):
    count = lax.axis_size("section")
    me = lax.axis_index("section")
    width = mine.shape[1]
    whole = jnp.zeros((mine.shape[0], width * count), mine.dtype)
    whole = lax.dynamic_update_slice_in_dim(whole, mine, me * width, 1)
    for step in range(1, count):
        owner = lax.rem(me - step + count, count)
        whole = lax.dynamic_update_slice_in_dim(
            whole, shift(mine, "section", step), owner * width, 1
        )
    return whole


def gather_rows(mine, axis):
    held = mine
    me = lax.axis_index(axis)
    mask = lax.axis_size(axis) // 2
    blocks = [mine]
    while mask >= 1:
        blocks = blocks + [swap(block, axis, mask) for block in blocks]
        mask //= 2
    codes = [0]
    mask = lax.axis_size(axis) // 2
    while mask >= 1:
        codes = codes + [code ^ mask for code in codes]
        mask //= 2
    ordered = []
    for place in range(len(blocks)):
        chosen = blocks[0]
        for code, block in zip(codes[1:], blocks[1:]):
            chosen = jnp.where((me ^ code) == place, block, chosen)
        ordered.append(chosen)
    return jnp.concatenate(ordered, axis=0)


def gather_weight(weight, dimension):
    if lax.axis_size("expert") != 2:
        return lax.all_gather(weight, "expert", axis=dimension, tiled=True)
    other = swap(weight, "expert", 1)
    first = lax.axis_index("expert") == 0
    return jnp.concatenate(
        [jnp.where(first, weight, other), jnp.where(first, other, weight)], axis=dimension
    )


def sum_heads(partial):
    me = lax.axis_index("dp")
    count = lax.axis_size("dp")
    rows, columns = partial.shape
    total = partial.reshape(rows, count, columns // count)
    mask = 1
    while mask < count:
        paired = total.reshape(rows, -1, 2, columns // count)
        bit = (me // mask) % 2
        sent = lax.dynamic_index_in_dim(paired, 1 - bit, 2, False).astype(jnp.bfloat16)
        kept = lax.dynamic_index_in_dim(paired, bit, 2, False)
        total = kept + swap(sent, "dp", mask).astype(jnp.float32)
        mask *= 2
    return total.reshape(rows, columns // count)


def slot_matrix(positions, slots):
    places = lax.broadcasted_iota(jnp.int32, (positions.shape[0], slots), 1)
    return (positions[:, None] == places).astype(jnp.bfloat16)


def attend(query, keys, values, key_mask):
    sequences = key_mask.shape[0]
    head_count = query.shape[1] // HEAD_DIM
    query_split = query.reshape(sequences, -1, head_count, HEAD_DIM)
    keys_split = keys.reshape(sequences, -1, head_count, HEAD_DIM)
    values_split = values.reshape(sequences, -1, head_count, HEAD_DIM)
    scores = jnp.einsum(
        "bqhd,bkhd->bhqk", query_split, keys_split, preferred_element_type=jnp.float32
    ) * HEAD_DIM ** (-0.5)
    scores = jnp.where(key_mask[:, None, None, :], scores, -1e30)
    highest = jnp.max(scores, axis=-1, keepdims=True)
    weights = jnp.exp(scores - highest)
    probs = (weights / jnp.sum(weights, axis=-1, keepdims=True)).astype(jnp.bfloat16)
    context = jnp.einsum("bhqk,bkhd->bqhd", probs, values_split, preferred_element_type=jnp.float32)
    return context.astype(jnp.bfloat16).reshape(-1, head_count * HEAD_DIM)


def exchange(values, group_size, capacity):
    sent = values.reshape(group_size, capacity, values.shape[1])
    arrived = lax.all_to_all(sent, ("expert", "dp"), split_axis=0, concat_axis=0, tiled=True)
    return arrived.reshape(values.shape)


SHORT = pl.CostEstimate(flops=1, bytes_accessed=1, transcendentals=0)


def gate(value, *after):
    return lax.optimization_barrier((value,) + after)[0]


def vmem(shape, dtype):
    return pltpu.VMEM(shape, dtype)


def dispatch_kernel(capacity, layout, section_ref, code_ref, *refs):
    blocks = refs[:-4]
    outs, held, sems = refs[-4:-2], refs[-2], refs[-1]
    count, rows = held.shape[0], held.shape[1]
    half = lax.rem(section_ref[0], 2)
    copies = []
    for place, pieces in enumerate(layout):
        group = []
        for i, (which, start, length, side) in enumerate(pieces):
            there = held.at[place]
            if side is not None:
                offset = (half if side == 0 else 1 - half) * length
                there = held.at[place, pl.ds(pl.multiple_of(offset, length), length)]
            here = blocks[which].at[pl.ds(start, length)]
            group.append(pltpu.make_async_copy(here, there, sems.at[place, i]))
        copies.append(group)
    for group in copies:
        for copy in group:
            copy.start()
    for place, group in enumerate(copies):
        picks = []
        for which in range(2):
            line = which * count + place
            code = code_ref[line : line + 1, :]
            slot = lax.broadcasted_iota(jnp.int32, (capacity, code.shape[1]), 0)
            picks.append(jnp.where(slot == code, 1.0, 0.0))
        pick = jnp.concatenate(picks, axis=0).astype(jnp.bfloat16)
        for copy in group:
            copy.wait()
        picked = jnp.dot(pick, held[place], preferred_element_type=jnp.float32)
        picked = picked.astype(jnp.bfloat16)
        for which, out_ref in enumerate(outs):
            out_ref[place * capacity : (place + 1) * capacity, :] = picked[
                which * capacity : (which + 1) * capacity
            ]


def dispatch(section, code, blocks, layout, capacity):
    rows, features = blocks[0].shape
    count = len(layout)
    picked = jax.ShapeDtypeStruct((count * capacity, features), jnp.bfloat16)
    return pl.pallas_call(
        functools.partial(dispatch_kernel, capacity, layout),
        out_shape=(picked, picked),
        in_specs=[
            pl.BlockSpec(memory_space=pltpu.SMEM),
            pl.BlockSpec(memory_space=pltpu.VMEM),
        ]
        + [pl.BlockSpec(memory_space=pltpu.HBM)] * len(blocks),
        out_specs=[pl.BlockSpec(memory_space=pltpu.VMEM)] * 2,
        scratch_shapes=[
            vmem((count, rows, features), jnp.bfloat16),
            pltpu.SemaphoreType.DMA((count, 2)),
        ],
        compiler_params=pltpu.CompilerParams(vmem_limit_bytes=10 * 1024 * 1024),
        cost_estimate=SHORT,
        name="dispatch",
    )(section, code, *blocks)


def send_home(part, codes, capacity):
    size = lax.axis_size(("expert", "dp"))
    arrived = []
    for place, code in enumerate(codes):
        block = part[place * capacity : (place + 1) * capacity]
        if code:
            block = lax.ppermute(block, ("expert", "dp"), [(i, i ^ code) for i in range(size)])
        arrived.append(block)
    return arrived


def combine_kernel(count, split, section_ref, position_ref, gates_ref, *refs):
    blocks = refs[:count]
    outs, (held, total) = refs[count:-2], refs[-2:]
    capacity, features = blocks[0].shape
    position = position_ref[...]
    slot = lax.broadcasted_iota(jnp.int32, (position.shape[0], count * capacity), 1)
    picks = [
        jnp.where(position[:, k : k + 1] == slot, 1.0, 0.0).astype(jnp.bfloat16) for k in range(2)
    ]
    for i, block in enumerate(blocks):
        held[i * capacity : (i + 1) * capacity, :] = block[...]
    pick = jnp.concatenate(picks, axis=0)
    rows = position.shape[0]
    both = jnp.dot(pick, held[...], preferred_element_type=jnp.float32)
    total[...] = gates_ref[:, 0:1] * both[:rows] + gates_ref[:, 1:2] * both[rows:]
    if split == 1:
        outs[0][...] = total[...].astype(outs[0].dtype)
        return
    sent_ref, kept_first, kept_second = outs
    width = features // split
    for step, out_ref in enumerate((kept_first, sent_ref.at[0], kept_second, sent_ref.at[1])):
        start = pl.multiple_of((section_ref[0] ^ step) * width, width)
        out_ref[...] = total[:, pl.ds(start, width)].astype(out_ref.dtype)


def combine(section, position, gates, blocks, split):
    capacity, features = blocks[0].shape
    rows = position.shape[0]
    count = len(blocks)
    width = features // split
    kept = jax.ShapeDtypeStruct((rows, width), jnp.float32)
    if split == 1:
        out_shape = (jax.ShapeDtypeStruct((rows, width), jnp.bfloat16),)
    else:
        out_shape = (jax.ShapeDtypeStruct((2, rows, width), jnp.bfloat16), kept, kept)
    full = pl.BlockSpec(memory_space=pltpu.VMEM)
    return pl.pallas_call(
        functools.partial(combine_kernel, count, split),
        out_shape=out_shape,
        in_specs=[pl.BlockSpec(memory_space=pltpu.SMEM)] + [full] * (2 + count),
        out_specs=[full] * len(out_shape),
        scratch_shapes=[
            vmem((count * capacity, features), jnp.bfloat16),
            vmem((rows, features), jnp.float32),
        ],
        compiler_params=pltpu.CompilerParams(vmem_limit_bytes=14 * 1024 * 1024),
        cost_estimate=SHORT,
        name="combine",
    )(section, position, gates, *blocks)


def memory_kernel(count, section_ref, tokens_ref, gain_ref, *refs):
    slices, out_ref, mixed = refs[:count], refs[count], refs[count + 1]
    me = section_ref[0]
    width = slices[0].shape[1]
    for step, piece in enumerate(slices):
        owner = me ^ step
        mixed[:, pl.ds(pl.multiple_of(owner * width, width), width)] = piece[...].astype(
            jnp.float32
        )
    values = tokens_ref[...].astype(jnp.float32) + mixed[...]
    out_ref[...] = normalize(values, gain_ref[...]).astype(jnp.bfloat16)


def make_memory(me, tokens, slices, gain):
    return pl.pallas_call(
        functools.partial(memory_kernel, len(slices)),
        out_shape=jax.ShapeDtypeStruct(tokens.shape, jnp.bfloat16),
        in_specs=[
            pl.BlockSpec(memory_space=pltpu.SMEM),
        ]
        + [pl.BlockSpec(memory_space=pltpu.VMEM)] * (2 + len(slices)),
        out_specs=pl.BlockSpec(memory_space=pltpu.VMEM),
        scratch_shapes=[vmem(tokens.shape, jnp.float32)],
        compiler_params=pltpu.CompilerParams(vmem_limit_bytes=8 * 1024 * 1024),
        cost_estimate=SHORT,
        name="memory",
    )(me, tokens, gain[None], *slices)


def normed_kernel(y_ref, states_ref, gain_ref, own_ref, other_ref):
    values = normalize(states_ref[...].astype(jnp.float32), gain_ref[...]).astype(jnp.bfloat16)
    width = own_ref.shape[1]
    for out_ref, first in ((own_ref, y_ref[0] == 0), (other_ref, y_ref[0] == 1)):
        out_ref[...] = jnp.where(first, values[:, :width], values[:, width:])


def normed_halves(y, states, gain):
    rows, features = states.shape
    full = pl.BlockSpec(memory_space=pltpu.VMEM)
    return pl.pallas_call(
        normed_kernel,
        out_shape=(jax.ShapeDtypeStruct((rows, features // 2), jnp.bfloat16),) * 2,
        in_specs=[pl.BlockSpec(memory_space=pltpu.SMEM), full, full],
        out_specs=[full] * 2,
        compiler_params=pltpu.CompilerParams(vmem_limit_bytes=12 * 1024 * 1024),
        cost_estimate=SHORT,
        name="normed",
    )(y.astype(jnp.int32).reshape(1), states, gain)


def attend_kernel(place_ref, lengths_ref, query_ref, *refs):
    near_ref, far_ref, key_own, key_other, value_own, value_other, out_ref = refs[:7]
    source, key_weight, value_weight, keys, values, sems = refs[7:]
    y, core, sentence = place_ref[0], place_ref[1], place_ref[2]
    rows = near_ref.shape[0]
    depth = key_own.shape[0]
    moves = [
        (near_ref, source.at[pl.ds(0, rows)]),
        (far_ref, source.at[pl.ds(rows, rows)]),
        (key_own, key_weight.at[y]),
        (key_other, key_weight.at[1 - y]),
        (value_own, value_weight.at[y]),
        (value_other, value_weight.at[1 - y]),
    ]
    copies = [
        pltpu.make_async_copy(here, there, sems.at[i]) for i, (here, there) in enumerate(moves)
    ]
    for copy in copies:
        copy.start()

    def linear(weight, result):
        total = jnp.dot(source[:, :depth], weight[0], preferred_element_type=jnp.float32)
        total += jnp.dot(source[:, depth:], weight[1], preferred_element_type=jnp.float32)
        result[...] = total.astype(jnp.bfloat16)

    for copy in copies[:4]:
        copy.wait()
    linear(key_weight, keys)
    for copy in copies[4:]:
        copy.wait()
    linear(value_weight, values)

    column = lax.broadcasted_iota(jnp.int32, (query_ref.shape[0], 2 * rows), 1)
    position = jnp.where(column < rows, column + core * rows, column - core * rows)
    valid = position < lengths_ref[sentence]
    for head in range(query_ref.shape[1] // HEAD_DIM):
        span = slice(head * HEAD_DIM, (head + 1) * HEAD_DIM)
        scores = contract_last(query_ref[:, span], keys[:, span]) * HEAD_DIM ** (-0.5)
        scores = jnp.where(valid, scores, -1e30)
        weights = jnp.exp(scores - jnp.max(scores, axis=-1, keepdims=True))
        probs = (weights / jnp.sum(weights, axis=-1, keepdims=True)).astype(jnp.bfloat16)
        result = jnp.dot(probs, values[:, span], preferred_element_type=jnp.float32)
        out_ref[:, span] = result.astype(jnp.bfloat16)


def attend_sentence(place, lengths, query, near, far, key_parts, value_pair):
    rows, features = near.shape
    depth, width = key_parts[0].shape
    hold = pl.BlockSpec(memory_space=pltpu.HBM)
    smem = pl.BlockSpec(memory_space=pltpu.SMEM)
    full = pl.BlockSpec(memory_space=pltpu.VMEM)
    return pl.pallas_call(
        attend_kernel,
        out_shape=jax.ShapeDtypeStruct(query.shape, jnp.bfloat16),
        in_specs=[smem, smem, full] + [hold] * 6,
        out_specs=full,
        scratch_shapes=[
            vmem((2 * rows, features), jnp.bfloat16),
            vmem((2, depth, width), jnp.bfloat16),
            vmem((2, depth, width), jnp.bfloat16),
            vmem((2 * rows, width), jnp.bfloat16),
            vmem((2 * rows, width), jnp.bfloat16),
            pltpu.SemaphoreType.DMA((6,)),
        ],
        compiler_params=pltpu.CompilerParams(vmem_limit_bytes=56 * 1024 * 1024),
        cost_estimate=SHORT,
        name="attend_sentence",
    )(place, lengths, query, near, far, *key_parts, *value_pair)


def project_kernel(place_ref, mine_ref, done_ref, own_ref, other_ref, *refs):
    sent, kept_mine, kept_other, context = refs
    y, core, x = place_ref[0], place_ref[1], place_ref[2]
    targets = mine_ref.shape[0]
    for part, sentence in ((mine_ref, x), (done_ref, 1 - x)):
        context[pl.ds(pl.multiple_of(sentence * targets, targets), targets), :] = part[...]
    columns = kept_mine.shape[1]
    outs = ((sent.at[0], kept_mine), (sent.at[1], kept_other))

    def write(weight_ref, chosen):
        for side, out_ref in zip((1 - core, core), chosen):
            span = pl.ds(pl.multiple_of(side * columns, columns), columns)
            part = jnp.dot(context[...], weight_ref[:, span], preferred_element_type=jnp.float32)
            out_ref[...] = part.astype(out_ref.dtype)

    @pl.when(x == y)
    def _():
        write(own_ref, outs[0])
        write(other_ref, outs[1])

    @pl.when(x != y)
    def _():
        write(other_ref, outs[0])
        write(own_ref, outs[1])


def project(place, mine, done, out_own, out_other):
    targets, width = 2 * mine.shape[0], mine.shape[1]
    columns = out_own.shape[1] // 2
    full = pl.BlockSpec(memory_space=pltpu.VMEM)
    kept = jax.ShapeDtypeStruct((targets, columns), jnp.float32)
    return pl.pallas_call(
        project_kernel,
        out_shape=(jax.ShapeDtypeStruct((2, targets, columns), jnp.bfloat16), kept, kept),
        in_specs=[pl.BlockSpec(memory_space=pltpu.SMEM)] + [full] * 4,
        out_specs=[full] * 3,
        scratch_shapes=[vmem((targets, width), jnp.bfloat16)],
        compiler_params=pltpu.CompilerParams(vmem_limit_bytes=16 * 1024 * 1024),
        cost_estimate=SHORT,
        name="project",
    )(place, mine, done, out_own, out_other)


def slope_kernel(codes, here_ref, own_ref, core_ref, rise_own, rise_core, out_ref, slope, *refs):
    grads, rise, weight_out, sems = refs
    rows = own_ref.shape[0]
    hidden = weight_out.shape[0]
    chunk = hidden // 4
    moves = []
    block = 2 * rows // len(codes)
    for order, code in enumerate(codes):
        source = here_ref[0] ^ code
        there = pl.ds(pl.multiple_of(source * block, 16), block)
        here = pl.ds(order * block % rows, block)
        own = order * block < rows
        moves.append(((own_ref if own else core_ref).at[here], grads.at[there]))
        moves.append(((rise_own if own else rise_core).at[here], rise.at[there]))
    for part in range(4):
        span = pl.ds(part * chunk, chunk)
        moves.append((out_ref.at[span], weight_out.at[span]))
    copies = [
        pltpu.make_async_copy(here, there, sems.at[i]) for i, (here, there) in enumerate(moves)
    ]
    for copy in copies:
        copy.start()
    for copy in copies[:-4]:
        copy.wait()
    for part in range(4):
        copies[part - 4].wait()
        span = slice(part * chunk, (part + 1) * chunk)
        back = contract_last(grads[...], weight_out[span, :])
        slope[:, span] = (back * rise[:, span]).astype(jnp.bfloat16)


def expert_slope(here, codes, grads_own, grads_core, rise_own, rise_core, weight_out):
    rows = 2 * grads_own.shape[0]
    hidden, features = weight_out.shape
    hold = pl.BlockSpec(memory_space=pltpu.HBM)
    return pl.pallas_call(
        functools.partial(slope_kernel, codes),
        out_shape=jax.ShapeDtypeStruct((rows, hidden), jnp.bfloat16),
        in_specs=[pl.BlockSpec(memory_space=pltpu.SMEM)] + [hold] * 5,
        out_specs=pl.BlockSpec(memory_space=pltpu.VMEM),
        scratch_shapes=[
            vmem((rows, features), jnp.bfloat16),
            vmem((rows, hidden), jnp.float32),
            vmem((hidden, features), jnp.bfloat16),
            pltpu.SemaphoreType.DMA((4 + 2 * len(codes),)),
        ],
        compiler_params=pltpu.CompilerParams(vmem_limit_bytes=56 * 1024 * 1024),
        cost_estimate=SHORT,
        name="expert_slope",
    )(here, grads_own, grads_core, rise_own, rise_core, weight_out)


def backward_kernel(split, section_ref, slope_ref, in_ref, sent_ref, kept_first, kept_second, *refs):
    weight_in, sems = refs
    width = weight_in.shape[0] // split
    outs = (sent_ref.at[0], sent_ref.at[1], kept_first, kept_second)
    spans, copies = [], []
    for i, step in enumerate((1, 3, 0, 2)):
        start = pl.multiple_of((section_ref[0] ^ step) * width, width)
        spans.append(pl.ds(start, width))
        copies.append(
            pltpu.make_async_copy(in_ref.at[spans[i]], weight_in.at[spans[i]], sems.at[i])
        )
    for copy in copies:
        copy.start()
    for copy, span, out_ref in zip(copies, spans, outs):
        copy.wait()
        part = contract_last(slope_ref[...], weight_in[span, :])
        out_ref[...] = part.astype(out_ref.dtype)


def expert_backward(section, slope, weight_in, split):
    rows, hidden = slope.shape
    features = weight_in.shape[0]
    width = features // split
    full = pl.BlockSpec(memory_space=pltpu.VMEM)
    kept = jax.ShapeDtypeStruct((rows, width), jnp.float32)
    return pl.pallas_call(
        functools.partial(backward_kernel, split),
        out_shape=(jax.ShapeDtypeStruct((2, rows, width), jnp.bfloat16), kept, kept),
        in_specs=[pl.BlockSpec(memory_space=pltpu.SMEM), full, pl.BlockSpec(memory_space=pltpu.HBM)],
        out_specs=[full] * 3,
        scratch_shapes=[
            vmem((features, hidden), jnp.bfloat16),
            pltpu.SemaphoreType.DMA((split,)),
        ],
        compiler_params=pltpu.CompilerParams(vmem_limit_bytes=56 * 1024 * 1024),
        cost_estimate=SHORT,
        name="expert_backward",
    )(section, slope, weight_in)


def small_body(
    tokens,
    expert_ids,
    gate_weights,
    out_grad,
    inner_weight,
    outer_weight,
    final_gain,
    dec_states,
    src_lengths,
    tgt_lengths,
    norm_gain,
    query_weight,
    key_weight,
    value_weight,
    out_weight,
):
    token_count, feature_count = tokens.shape
    group_size = lax.axis_size(("expert", "dp"))
    capacity = 3 * token_count // group_size
    here = lax.axis_index(("expert", "dp"))
    y = lax.axis_index("expert")
    d = lax.axis_index("dp")
    section = lax.axis_index("section")
    sections = lax.axis_size("section")
    half = feature_count // 2
    weight_in = inner_weight[0]
    weight_out = outer_weight[0]
    key_own, value_own, out_own = key_weight[0], value_weight[0], out_weight[0]
    query_own = query_weight[0]

    size = group_size
    near_codes = (0, 2, 4, 6)
    core_codes = (1, 3, 5, 7)
    core, x = d % 2, d // 2
    which_section = section.astype(jnp.int32).reshape(1)

    token_y = swap(tokens, "expert", 1)
    token_x = swap(tokens, "dp", 2)
    ids_own = expert_ids.T
    ids_x, ids_y = swap(ids_own, "dp", 2), swap(ids_own, "expert", 1)
    ids_far = swap(ids_x, "expert", 1)
    token_far = swap(token_y, "dp", 2)

    side = lax.rem(section, 2)
    share = token_count // 2
    grad_half = lax.dynamic_slice_in_dim(out_grad, side * share, share, 0)
    half_y = swap(gate(grad_half, token_y, ids_far), "expert", 1)
    key_other = swap(gate(key_own, half_y), "expert", 1)
    states = dec_states[0]
    normed_own, asked = normed_halves(y, states, norm_gain)
    other_y = swap(half_y, "section", 1)
    half_x = swap(gate(grad_half, token_far), "dp", 2)
    half_far = swap(gate(half_y, token_far), "dp", 2)
    half_pair = jnp.concatenate([half_x, half_far], axis=0)
    other_pair = swap(half_pair, "section", 1)

    row = lax.broadcasted_iota(jnp.int32, (token_count, token_count), 0)
    column = lax.broadcasted_iota(jnp.int32, (token_count, token_count), 1)
    ids = jnp.stack([ids_own, ids_x, ids_y, ids_far])
    named_there = jnp.concatenate([(ids == here).any(axis=1), (ids == (here ^ 1)).any(axis=1)])
    before = jnp.dot(
        named_there.astype(jnp.bfloat16),
        (row < column).astype(jnp.bfloat16),
        preferred_element_type=jnp.float32,
    ).astype(jnp.int32)
    code = jnp.where(named_there, before, -1)

    named = expert_ids[:, :, None] == jnp.arange(size, dtype=jnp.int32)[None, None, :]
    either = (named[:, 0] | named[:, 1]).astype(jnp.bfloat16)
    earlier = jnp.dot(
        (column < row).astype(jnp.bfloat16), either, preferred_element_type=jnp.float32
    ).astype(jnp.int32)
    rank = jnp.sum(jnp.where(named, earlier[:, None, :], 0), axis=2)
    codes_of = expert_ids ^ here
    position = ((codes_of >> 1) + 4 * (codes_of & 1)) * capacity + rank

    def forward(rows):
        pre_act = jnp.dot(rows, weight_in, preferred_element_type=jnp.float32)
        hidden = jax.nn.gelu(pre_act).astype(jnp.bfloat16)
        part = jnp.dot(hidden, weight_out, preferred_element_type=jnp.float32)
        return pre_act, part.astype(jnp.bfloat16)

    def slope_of(pre_act):
        return jax.vjp(jax.nn.gelu, pre_act)[1](jnp.ones_like(pre_act))[0]

    rows_own, rows_sent = dispatch(
        which_section,
        gate(code, asked),
        [tokens, token_x, token_y, token_far],
        tuple(((place, 0, token_count, None),) for place in range(4)),
        capacity,
    )
    rows_core = swap(rows_sent, "dp", 1)
    pre_own, part_own = forward(rows_own)
    pre_core, part_core = forward(rows_core)
    part_core = gate(part_core, key_other)
    rise_own, rise_core = slope_of(gate(pre_own, part_core)), slope_of(gate(pre_core, part_core))
    home = send_home(part_own, near_codes, capacity) + send_home(part_core, core_codes, capacity)

    grads_own, grads_sent = dispatch(
        which_section,
        gate(code, home[2], rise_own, rise_core),
        [out_grad, half_x, half_y, half_far, other_y, other_pair],
        (
            ((0, 0, token_count, None),),
            ((1, 0, share, 0), (5, 0, share, 1)),
            ((2, 0, share, 0), (4, 0, share, 1)),
            ((3, 0, share, 0), (5, share, share, 1)),
        ),
        capacity,
    )
    held_gates = gate(gate_weights, grads_sent)
    sent_pair, first, second = combine(which_section, position, held_gates, home, sections)
    from_pair = swap(sent_pair, "section", 1)
    grads_core = swap(grads_sent, "dp", 1)
    asked_here = swap(gate(asked, first), "expert", 1)
    to_other = (second + from_pair[1].astype(jnp.float32)).astype(jnp.bfloat16)
    from_other = swap(to_other, "section", 2)
    slope = expert_slope(
        gate(here.astype(jnp.int32).reshape(1), to_other),
        near_codes + core_codes,
        grads_own,
        grads_core,
        rise_own,
        rise_core,
        weight_out,
    )
    mixed_sum = gate(first, slope) + from_pair[0].astype(jnp.float32)
    mixed_slice = (mixed_sum + from_other.astype(jnp.float32)).astype(jnp.bfloat16)
    mixed_near = swap(mixed_slice, "section", 1)
    back_pair, back_first, back_second = expert_backward(
        gate(which_section, mixed_near), slope, weight_in, sections
    )
    mixed_far = swap(jnp.stack([mixed_slice, mixed_near]), "section", 2)
    slices = [mixed_slice, mixed_near, mixed_far[0], mixed_far[1]]

    value_other = swap(gate(value_own, first), "expert", 1)
    query_there = jnp.dot(asked_here, query_own, preferred_element_type=jnp.float32)
    query_back = swap(query_there.astype(jnp.bfloat16), "expert", 1)
    out_other = swap(gate(out_own, value_other, query_back), "expert", 1)
    query_here = jnp.dot(normed_own, query_own, preferred_element_type=jnp.float32)
    query = (query_here + query_back.astype(jnp.float32)).astype(jnp.bfloat16)

    memory = make_memory(which_section, gate(tokens, value_other, query_back), slices, final_gain)
    memory_x = swap(memory, "dp", 2)
    memory_core = swap(memory, "dp", 1)

    def sentence(which, near, far, *after):
        place = gate(jnp.stack([y, core, which]).astype(jnp.int32), *after)
        rows_of = lax.dynamic_slice_in_dim(query, which * TGT_LEN, TGT_LEN, 0)
        parts = (key_own, key_other), (value_own, value_other)
        return attend_sentence(place, src_lengths, rows_of, near, far, *parts)

    back_from_pair = swap(back_pair, "section", 1)
    back_to_other = (back_second + back_from_pair[1].astype(jnp.float32)).astype(jnp.bfloat16)
    part = back_to_other.shape[0] // 2
    back_top = swap(back_to_other[:part], "section", 2)
    back_low = swap(gate(back_to_other[part:], back_top), "section", 2)
    backward_sum = back_first + back_from_pair[0].astype(jnp.float32)
    backward_sum = backward_sum + jnp.concatenate([back_top, back_low], axis=0).astype(jnp.float32)
    context_own = sentence(x, memory, memory_core)
    memory_far = swap(gate(memory_x, context_own), "dp", 1)
    context_other = sentence(1 - x, memory_x, memory_far)
    place = gate(jnp.stack([y, core, x]).astype(jnp.int32), back_top)
    sent, kept_mine, kept_other = project(place, context_own, context_other, out_own, out_other)

    from_core = swap(sent, "dp", 1).astype(jnp.float32)
    last = (gate(kept_other, back_low) + from_core[1]).astype(jnp.bfloat16)
    from_x = swap(last, "dp", 2)
    attended = kept_mine + from_core[0] + from_x.astype(jnp.float32)
    dec_out = add_residual(attended, states, tgt_lengths)

    grads_home = exchange(gate(backward_sum.astype(jnp.bfloat16), sent), group_size, capacity)
    natural = expert_ids * capacity + rank
    (token_grad,) = combine(
        which_section, natural, gate_weights, [grads_home], 1
    )
    return (dec_out[None], token_grad)


def add_residual(attended, states, tgt_lengths):
    my_columns = attended.shape[1]
    residual = lax.dynamic_slice_in_dim(
        states, lax.axis_index("dp") * my_columns, my_columns, 1
    ).astype(jnp.float32)
    row_mask = (jnp.arange(TGT_LEN, dtype=jnp.int32)[None, :] < tgt_lengths[:, None]).reshape(-1, 1)
    return (residual + jnp.where(row_mask, attended, 0.0)).astype(jnp.bfloat16)


def body(
    tokens,
    expert_ids,
    gate_weights,
    out_grad,
    inner_weight,
    outer_weight,
    final_gain,
    dec_states,
    src_lengths,
    tgt_lengths,
    norm_gain,
    query_weight,
    key_weight,
    value_weight,
    out_weight,
):
    token_count, feature_count = tokens.shape
    group_size = lax.axis_size(("expert", "dp"))
    capacity = 3 * token_count // group_size
    slots = group_size * capacity

    named = expert_ids[:, :, None] == jnp.arange(group_size, dtype=jnp.int32)[None, None, :]
    either = (named[:, 0] | named[:, 1]).astype(jnp.bfloat16)
    row = lax.broadcasted_iota(jnp.int32, (token_count, token_count), 0)
    column = lax.broadcasted_iota(jnp.int32, (token_count, token_count), 1)
    earlier = jnp.dot(
        (column < row).astype(jnp.bfloat16), either, preferred_element_type=jnp.float32
    ).astype(jnp.int32)
    rank = jnp.sum(jnp.where(named, earlier[:, None, :], 0), axis=2)
    position = expert_ids * capacity + rank
    pick_first = slot_matrix(position[:, 0], slots)
    pick_second = slot_matrix(position[:, 1], slots)
    fill = (pick_first + pick_second).T

    def place(values):
        return jnp.dot(fill, values, preferred_element_type=jnp.float32).astype(jnp.bfloat16)

    def combine(arrived):
        first = jnp.dot(pick_first, arrived, preferred_element_type=jnp.float32)
        second = jnp.dot(pick_second, arrived, preferred_element_type=jnp.float32)
        return gate_weights[:, :1] * first + gate_weights[:, 1:] * second

    weight_in = inner_weight[0]
    weight_out = outer_weight[0]
    arrived_rows = exchange(place(tokens), group_size, capacity)
    pre_act = jnp.dot(arrived_rows, weight_in, preferred_element_type=jnp.float32)
    hidden = jax.nn.gelu(pre_act).astype(jnp.bfloat16)
    forward_part = jnp.dot(hidden, weight_out, preferred_element_type=jnp.float32)
    arrived_grads = exchange(place(out_grad), group_size, capacity)
    outputs_home = exchange(forward_part.astype(jnp.bfloat16), group_size, capacity)
    mixed_slice = sum_sections(combine(outputs_home)).astype(jnp.bfloat16)
    mixed = gather_sections(mixed_slice).astype(jnp.float32)
    memory = normalize(tokens.astype(jnp.float32) + mixed, final_gain).astype(jnp.bfloat16)

    back = contract_last(arrived_grads, weight_out)
    slope = jax.vjp(jax.nn.gelu, pre_act)[1](back)[0].astype(jnp.bfloat16)
    backward_part = contract_last(slope, weight_in)
    backward_slice = sum_sections(backward_part).astype(jnp.bfloat16)
    grads_home = exchange(backward_slice, group_size, capacity)
    token_grad = combine(grads_home).astype(jnp.bfloat16)

    states = dec_states[0]
    normed = normalize(states.astype(jnp.float32), norm_gain[0]).astype(jnp.bfloat16)
    full_query = gather_weight(query_weight[0], 0)
    full_key = gather_weight(key_weight[0], 0)
    full_value = gather_weight(value_weight[0], 0)
    full_out = gather_weight(out_weight[0], 1)
    query_sum = jnp.dot(normed, full_query, preferred_element_type=jnp.float32)
    source = gather_rows(memory, "dp")
    key_sum = jnp.dot(source, full_key, preferred_element_type=jnp.float32)
    value_sum = jnp.dot(source, full_value, preferred_element_type=jnp.float32)
    key_mask = jnp.arange(SRC_LEN, dtype=jnp.int32)[None, :] < src_lengths[:, None]
    context = attend(
        query_sum.astype(jnp.bfloat16),
        key_sum.astype(jnp.bfloat16),
        value_sum.astype(jnp.bfloat16),
        key_mask,
    )
    attended = sum_heads(jnp.dot(context, full_out, preferred_element_type=jnp.float32))
    dec_out = add_residual(attended, states, tgt_lengths)
    return (dec_out[None], token_grad)


def solution(mesh):
    in_specs = (
        P(("expert", "dp"), None),
        P(("expert", "dp"), None),
        P(("expert", "dp"), None),
        P(("expert", "dp"), None),
        P(("expert", "dp"), None, "section"),
        P(("expert", "dp"), "section", None),
        P(),
        P("section", "expert", None),
        P("expert"),
        P("expert"),
        P("section", None),
        P("section", "expert", "dp"),
        P("section", "expert", "dp"),
        P("section", "expert", "dp"),
        P("section", "dp", "expert"),
    )
    out_specs = (P("section", "expert", "dp"), P(("expert", "dp"), "section"))
    small = (mesh.shape["section"], mesh.shape["expert"], mesh.shape["dp"]) == (4, 2, 4)
    chosen = small_body if small else body
    return jax.shard_map(chosen, mesh=mesh, in_specs=in_specs, out_specs=out_specs, check_vma=False)
```

```python
import functools

import jax
import jax.numpy as jnp
from jax import lax
from jax.experimental import pallas as pl
from jax.experimental.pallas import tpu as pltpu
from jax.sharding import PartitionSpec as P

HEAD_DIM = 128
SRC_LEN = 256
TGT_LEN = 128


EPSILON = 1e-05


def normalize(values, gain):
    centre = jnp.mean(values, axis=-1, keepdims=True)
    centred = values - centre
    spread = jnp.mean(centred * centred, axis=-1, keepdims=True)
    return centred * lax.rsqrt(spread + EPSILON) * gain


def contract_last(left, right):
    return lax.dot_general(
        left, right, (((1,), (1,)), ((), ())), preferred_element_type=jnp.float32
    )


def shift(value, axis, step):
    size = lax.axis_size(axis)
    return lax.ppermute(value, axis, [(i, (i + step) % size) for i in range(size)])


def swap(value, axis, mask):
    size = lax.axis_size(axis)
    return lax.ppermute(value, axis, [(i, i ^ mask) for i in range(size)])


def sum_sections(partial):
    count = lax.axis_size("section")
    me = lax.axis_index("section")
    width = partial.shape[1] // count

    def piece(owner):
        return lax.dynamic_slice_in_dim(partial, owner * width, width, 1)

    total = piece(me).astype(jnp.float32)
    for step in range(1, count):
        sent = piece(lax.rem(me + step, count)).astype(jnp.bfloat16)
        total = total + shift(sent, "section", step).astype(jnp.float32)
    return total


def gather_sections(mine):
    count = lax.axis_size("section")
    me = lax.axis_index("section")
    width = mine.shape[1]
    whole = jnp.zeros((mine.shape[0], width * count), mine.dtype)
    whole = lax.dynamic_update_slice_in_dim(whole, mine, me * width, 1)
    for step in range(1, count):
        owner = lax.rem(me - step + count, count)
        whole = lax.dynamic_update_slice_in_dim(
            whole, shift(mine, "section", step), owner * width, 1
        )
    return whole


def gather_rows(mine, axis):
    held = mine
    me = lax.axis_index(axis)
    mask = lax.axis_size(axis) // 2
    blocks = [mine]
    while mask >= 1:
        blocks = blocks + [swap(block, axis, mask) for block in blocks]
        mask //= 2
    codes = [0]
    mask = lax.axis_size(axis) // 2
    while mask >= 1:
        codes = codes + [code ^ mask for code in codes]
        mask //= 2
    ordered = []
    for place in range(len(blocks)):
        chosen = blocks[0]
        for code, block in zip(codes[1:], blocks[1:]):
            chosen = jnp.where((me ^ code) == place, block, chosen)
        ordered.append(chosen)
    return jnp.concatenate(ordered, axis=0)


def gather_weight(weight, dimension):
    if lax.axis_size("expert") != 2:
        return lax.all_gather(weight, "expert", axis=dimension, tiled=True)
    other = swap(weight, "expert", 1)
    first = lax.axis_index("expert") == 0
    return jnp.concatenate(
        [jnp.where(first, weight, other), jnp.where(first, other, weight)], axis=dimension
    )


def sum_heads(partial):
    me = lax.axis_index("dp")
    count = lax.axis_size("dp")
    rows, columns = partial.shape
    total = partial.reshape(rows, count, columns // count)
    mask = 1
    while mask < count:
        paired = total.reshape(rows, -1, 2, columns // count)
        bit = (me // mask) % 2
        sent = lax.dynamic_index_in_dim(paired, 1 - bit, 2, False).astype(jnp.bfloat16)
        kept = lax.dynamic_index_in_dim(paired, bit, 2, False)
        total = kept + swap(sent, "dp", mask).astype(jnp.float32)
        mask *= 2
    return total.reshape(rows, columns // count)


def slot_matrix(positions, slots):
    places = lax.broadcasted_iota(jnp.int32, (positions.shape[0], slots), 1)
    return (positions[:, None] == places).astype(jnp.bfloat16)


def attend(query, keys, values, key_mask):
    sequences = key_mask.shape[0]
    head_count = query.shape[1] // HEAD_DIM
    query_split = query.reshape(sequences, -1, head_count, HEAD_DIM)
    keys_split = keys.reshape(sequences, -1, head_count, HEAD_DIM)
    values_split = values.reshape(sequences, -1, head_count, HEAD_DIM)
    scores = jnp.einsum(
        "bqhd,bkhd->bhqk", query_split, keys_split, preferred_element_type=jnp.float32
    ) * HEAD_DIM ** (-0.5)
    scores = jnp.where(key_mask[:, None, None, :], scores, -1e30)
    highest = jnp.max(scores, axis=-1, keepdims=True)
    weights = jnp.exp(scores - highest)
    probs = (weights / jnp.sum(weights, axis=-1, keepdims=True)).astype(jnp.bfloat16)
    context = jnp.einsum("bhqk,bkhd->bqhd", probs, values_split, preferred_element_type=jnp.float32)
    return context.astype(jnp.bfloat16).reshape(-1, head_count * HEAD_DIM)


def exchange(values, group_size, capacity):
    sent = values.reshape(group_size, capacity, values.shape[1])
    arrived = lax.all_to_all(sent, ("expert", "dp"), split_axis=0, concat_axis=0, tiled=True)
    return arrived.reshape(values.shape)


SHORT = pl.CostEstimate(flops=1, bytes_accessed=1, transcendentals=0)


def gate(value, *after):
    return lax.optimization_barrier((value,) + after)[0]


def vmem(shape, dtype):
    return pltpu.VMEM(shape, dtype)


def dispatch_kernel(capacity, layout, section_ref, code_ref, *refs):
    blocks = refs[:-4]
    outs, held, sems = refs[-4:-2], refs[-2], refs[-1]
    count, rows = held.shape[0], held.shape[1]
    half = lax.rem(section_ref[0], 2)
    copies = []
    for place, pieces in enumerate(layout):
        group = []
        for i, (which, start, length, side) in enumerate(pieces):
            there = held.at[place]
            if side is not None:
                offset = (half if side == 0 else 1 - half) * length
                there = held.at[place, pl.ds(pl.multiple_of(offset, length), length)]
            here = blocks[which].at[pl.ds(start, length)]
            group.append(pltpu.make_async_copy(here, there, sems.at[place, i]))
        copies.append(group)
    for group in copies:
        for copy in group:
            copy.start()
    for place, group in enumerate(copies):
        picks = []
        for which in range(2):
            line = which * count + place
            code = code_ref[line : line + 1, :]
            slot = lax.broadcasted_iota(jnp.int32, (capacity, code.shape[1]), 0)
            picks.append(jnp.where(slot == code, 1.0, 0.0))
        pick = jnp.concatenate(picks, axis=0).astype(jnp.bfloat16)
        for copy in group:
            copy.wait()
        picked = jnp.dot(pick, held[place], preferred_element_type=jnp.float32)
        picked = picked.astype(jnp.bfloat16)
        for which, out_ref in enumerate(outs):
            out_ref[place * capacity : (place + 1) * capacity, :] = picked[
                which * capacity : (which + 1) * capacity
            ]


def dispatch(section, code, blocks, layout, capacity):
    rows, features = blocks[0].shape
    count = len(layout)
    picked = jax.ShapeDtypeStruct((count * capacity, features), jnp.bfloat16)
    return pl.pallas_call(
        functools.partial(dispatch_kernel, capacity, layout),
        out_shape=(picked, picked),
        in_specs=[
            pl.BlockSpec(memory_space=pltpu.SMEM),
            pl.BlockSpec(memory_space=pltpu.VMEM),
        ]
        + [pl.BlockSpec(memory_space=pltpu.HBM)] * len(blocks),
        out_specs=[pl.BlockSpec(memory_space=pltpu.VMEM)] * 2,
        scratch_shapes=[
            vmem((count, rows, features), jnp.bfloat16),
            pltpu.SemaphoreType.DMA((count, 2)),
        ],
        compiler_params=pltpu.CompilerParams(vmem_limit_bytes=10 * 1024 * 1024),
        cost_estimate=SHORT,
        name="dispatch",
    )(section, code, *blocks)


def send_home(part, codes, capacity):
    size = lax.axis_size(("expert", "dp"))
    arrived = []
    for place, code in enumerate(codes):
        block = part[place * capacity : (place + 1) * capacity]
        if code:
            block = lax.ppermute(block, ("expert", "dp"), [(i, i ^ code) for i in range(size)])
        arrived.append(block)
    return arrived


def combine_kernel(count, split, section_ref, position_ref, gates_ref, *refs):
    blocks = refs[:count]
    outs, (held, total) = refs[count:-2], refs[-2:]
    capacity, features = blocks[0].shape
    position = position_ref[...]
    slot = lax.broadcasted_iota(jnp.int32, (position.shape[0], count * capacity), 1)
    picks = [
        jnp.where(position[:, k : k + 1] == slot, 1.0, 0.0).astype(jnp.bfloat16) for k in range(2)
    ]
    for i, block in enumerate(blocks):
        held[i * capacity : (i + 1) * capacity, :] = block[...]
    pick = jnp.concatenate(picks, axis=0)
    rows = position.shape[0]
    both = jnp.dot(pick, held[...], preferred_element_type=jnp.float32)
    total[...] = gates_ref[:, 0:1] * both[:rows] + gates_ref[:, 1:2] * both[rows:]
    if split == 1:
        outs[0][...] = total[...].astype(outs[0].dtype)
        return
    sent_ref, kept_first, kept_second = outs
    width = features // split
    for step, out_ref in enumerate((kept_first, sent_ref.at[0], kept_second, sent_ref.at[1])):
        start = pl.multiple_of((section_ref[0] ^ step) * width, width)
        out_ref[...] = total[:, pl.ds(start, width)].astype(out_ref.dtype)


def combine(section, position, gates, blocks, split):
    capacity, features = blocks[0].shape
    rows = position.shape[0]
    count = len(blocks)
    width = features // split
    kept = jax.ShapeDtypeStruct((rows, width), jnp.float32)
    if split == 1:
        out_shape = (jax.ShapeDtypeStruct((rows, width), jnp.bfloat16),)
    else:
        out_shape = (jax.ShapeDtypeStruct((2, rows, width), jnp.bfloat16), kept, kept)
    full = pl.BlockSpec(memory_space=pltpu.VMEM)
    return pl.pallas_call(
        functools.partial(combine_kernel, count, split),
        out_shape=out_shape,
        in_specs=[pl.BlockSpec(memory_space=pltpu.SMEM)] + [full] * (2 + count),
        out_specs=[full] * len(out_shape),
        scratch_shapes=[
            vmem((count * capacity, features), jnp.bfloat16),
            vmem((rows, features), jnp.float32),
        ],
        compiler_params=pltpu.CompilerParams(vmem_limit_bytes=14 * 1024 * 1024),
        cost_estimate=SHORT,
        name="combine",
    )(section, position, gates, *blocks)


def memory_kernel(count, section_ref, tokens_ref, gain_ref, *refs):
    slices, out_ref, mixed = refs[:count], refs[count], refs[count + 1]
    me = section_ref[0]
    width = slices[0].shape[1]
    for step, piece in enumerate(slices):
        owner = me ^ step
        mixed[:, pl.ds(pl.multiple_of(owner * width, width), width)] = piece[...].astype(
            jnp.float32
        )
    values = tokens_ref[...].astype(jnp.float32) + mixed[...]
    out_ref[...] = normalize(values, gain_ref[...]).astype(jnp.bfloat16)


def make_memory(me, tokens, slices, gain):
    return pl.pallas_call(
        functools.partial(memory_kernel, len(slices)),
        out_shape=jax.ShapeDtypeStruct(tokens.shape, jnp.bfloat16),
        in_specs=[
            pl.BlockSpec(memory_space=pltpu.SMEM),
        ]
        + [pl.BlockSpec(memory_space=pltpu.VMEM)] * (2 + len(slices)),
        out_specs=pl.BlockSpec(memory_space=pltpu.VMEM),
        scratch_shapes=[vmem(tokens.shape, jnp.float32)],
        compiler_params=pltpu.CompilerParams(vmem_limit_bytes=8 * 1024 * 1024),
        cost_estimate=SHORT,
        name="memory",
    )(me, tokens, gain[None], *slices)


def normed_kernel(y_ref, states_ref, gain_ref, own_ref, other_ref):
    values = normalize(states_ref[...].astype(jnp.float32), gain_ref[...]).astype(jnp.bfloat16)
    width = own_ref.shape[1]
    for out_ref, first in ((own_ref, y_ref[0] == 0), (other_ref, y_ref[0] == 1)):
        out_ref[...] = jnp.where(first, values[:, :width], values[:, width:])


def normed_halves(y, states, gain):
    rows, features = states.shape
    full = pl.BlockSpec(memory_space=pltpu.VMEM)
    return pl.pallas_call(
        normed_kernel,
        out_shape=(jax.ShapeDtypeStruct((rows, features // 2), jnp.bfloat16),) * 2,
        in_specs=[pl.BlockSpec(memory_space=pltpu.SMEM), full, full],
        out_specs=[full] * 2,
        compiler_params=pltpu.CompilerParams(vmem_limit_bytes=12 * 1024 * 1024),
        cost_estimate=SHORT,
        name="normed",
    )(y.astype(jnp.int32).reshape(1), states, gain)


def attend_kernel(place_ref, lengths_ref, query_ref, *refs):
    near_ref, far_ref, key_own, key_other, value_own, value_other, out_ref = refs[:7]
    source, key_weight, value_weight, keys, values, sems = refs[7:]
    y, core, sentence = place_ref[0], place_ref[1], place_ref[2]
    rows = near_ref.shape[0]
    depth = key_own.shape[0]
    moves = [
        (near_ref, source.at[pl.ds(0, rows)]),
        (far_ref, source.at[pl.ds(rows, rows)]),
        (key_own, key_weight.at[y]),
        (key_other, key_weight.at[1 - y]),
        (value_own, value_weight.at[y]),
        (value_other, value_weight.at[1 - y]),
    ]
    copies = [
        pltpu.make_async_copy(here, there, sems.at[i]) for i, (here, there) in enumerate(moves)
    ]
    for copy in copies:
        copy.start()

    def linear(weight, result):
        total = jnp.dot(source[:, :depth], weight[0], preferred_element_type=jnp.float32)
        total += jnp.dot(source[:, depth:], weight[1], preferred_element_type=jnp.float32)
        result[...] = total.astype(jnp.bfloat16)

    for copy in copies[:4]:
        copy.wait()
    linear(key_weight, keys)
    for copy in copies[4:]:
        copy.wait()
    linear(value_weight, values)

    column = lax.broadcasted_iota(jnp.int32, (query_ref.shape[0], 2 * rows), 1)
    position = jnp.where(column < rows, column + core * rows, column - core * rows)
    valid = position < lengths_ref[sentence]
    for head in range(query_ref.shape[1] // HEAD_DIM):
        span = slice(head * HEAD_DIM, (head + 1) * HEAD_DIM)
        scores = contract_last(query_ref[:, span], keys[:, span]) * HEAD_DIM ** (-0.5)
        scores = jnp.where(valid, scores, -1e30)
        weights = jnp.exp(scores - jnp.max(scores, axis=-1, keepdims=True))
        probs = (weights / jnp.sum(weights, axis=-1, keepdims=True)).astype(jnp.bfloat16)
        result = jnp.dot(probs, values[:, span], preferred_element_type=jnp.float32)
        out_ref[:, span] = result.astype(jnp.bfloat16)


def attend_sentence(place, lengths, query, near, far, key_parts, value_pair):
    rows, features = near.shape
    depth, width = key_parts[0].shape
    hold = pl.BlockSpec(memory_space=pltpu.HBM)
    smem = pl.BlockSpec(memory_space=pltpu.SMEM)
    full = pl.BlockSpec(memory_space=pltpu.VMEM)
    return pl.pallas_call(
        attend_kernel,
        out_shape=jax.ShapeDtypeStruct(query.shape, jnp.bfloat16),
        in_specs=[smem, smem, full] + [hold] * 6,
        out_specs=full,
        scratch_shapes=[
            vmem((2 * rows, features), jnp.bfloat16),
            vmem((2, depth, width), jnp.bfloat16),
            vmem((2, depth, width), jnp.bfloat16),
            vmem((2 * rows, width), jnp.bfloat16),
            vmem((2 * rows, width), jnp.bfloat16),
            pltpu.SemaphoreType.DMA((6,)),
        ],
        compiler_params=pltpu.CompilerParams(vmem_limit_bytes=56 * 1024 * 1024),
        cost_estimate=SHORT,
        name="attend_sentence",
    )(place, lengths, query, near, far, *key_parts, *value_pair)


def project_kernel(place_ref, mine_ref, done_ref, own_ref, other_ref, *refs):
    sent_mine, sent_other, kept_mine, kept_other, context = refs
    y, core, x = place_ref[0], place_ref[1], place_ref[2]
    targets = mine_ref.shape[0]
    for part, sentence in ((mine_ref, x), (done_ref, 1 - x)):
        context[pl.ds(pl.multiple_of(sentence * targets, targets), targets), :] = part[...]
    columns = kept_mine.shape[1]
    outs = ((sent_mine, kept_mine), (sent_other, kept_other))

    def write(weight_ref, chosen):
        for side, out_ref in zip((1 - core, core), chosen):
            span = pl.ds(pl.multiple_of(side * columns, columns), columns)
            part = jnp.dot(context[...], weight_ref[:, span], preferred_element_type=jnp.float32)
            out_ref[...] = part.astype(out_ref.dtype)

    @pl.when(x == y)
    def _():
        write(own_ref, outs[0])
        write(other_ref, outs[1])

    @pl.when(x != y)
    def _():
        write(other_ref, outs[0])
        write(own_ref, outs[1])


def project(place, mine, done, out_own, out_other):
    targets, width = 2 * mine.shape[0], mine.shape[1]
    columns = out_own.shape[1] // 2
    full = pl.BlockSpec(memory_space=pltpu.VMEM)
    sent = jax.ShapeDtypeStruct((targets, columns), jnp.bfloat16)
    kept = jax.ShapeDtypeStruct((targets, columns), jnp.float32)
    return pl.pallas_call(
        project_kernel,
        out_shape=(sent, sent, kept, kept),
        in_specs=[pl.BlockSpec(memory_space=pltpu.SMEM)] + [full] * 4,
        out_specs=[full] * 4,
        scratch_shapes=[vmem((targets, width), jnp.bfloat16)],
        compiler_params=pltpu.CompilerParams(vmem_limit_bytes=16 * 1024 * 1024),
        cost_estimate=SHORT,
        name="project",
    )(place, mine, done, out_own, out_other)


def slope_kernel(codes, here_ref, own_ref, core_ref, rise_own, rise_core, out_ref, slope, *refs):
    grads, rise, weight_out, sems = refs
    rows = own_ref.shape[0]
    hidden = weight_out.shape[0]
    chunk = hidden // 4
    moves = []
    block = 2 * rows // len(codes)
    for order, code in enumerate(codes):
        source = here_ref[0] ^ code
        there = pl.ds(pl.multiple_of(source * block, 16), block)
        here = pl.ds(order * block % rows, block)
        own = order * block < rows
        moves.append(((own_ref if own else core_ref).at[here], grads.at[there]))
        moves.append(((rise_own if own else rise_core).at[here], rise.at[there]))
    for part in range(4):
        span = pl.ds(part * chunk, chunk)
        moves.append((out_ref.at[span], weight_out.at[span]))
    copies = [
        pltpu.make_async_copy(here, there, sems.at[i]) for i, (here, there) in enumerate(moves)
    ]
    for copy in copies:
        copy.start()
    for copy in copies[:-4]:
        copy.wait()
    for part in range(4):
        copies[part - 4].wait()
        span = slice(part * chunk, (part + 1) * chunk)
        back = contract_last(grads[...], weight_out[span, :])
        slope[:, span] = (back * rise[:, span]).astype(jnp.bfloat16)


def expert_slope(here, codes, grads_own, grads_core, rise_own, rise_core, weight_out):
    rows = 2 * grads_own.shape[0]
    hidden, features = weight_out.shape
    hold = pl.BlockSpec(memory_space=pltpu.HBM)
    return pl.pallas_call(
        functools.partial(slope_kernel, codes),
        out_shape=jax.ShapeDtypeStruct((rows, hidden), jnp.bfloat16),
        in_specs=[pl.BlockSpec(memory_space=pltpu.SMEM)] + [hold] * 5,
        out_specs=pl.BlockSpec(memory_space=pltpu.VMEM),
        scratch_shapes=[
            vmem((rows, features), jnp.bfloat16),
            vmem((rows, hidden), jnp.float32),
            vmem((hidden, features), jnp.bfloat16),
            pltpu.SemaphoreType.DMA((4 + 2 * len(codes),)),
        ],
        compiler_params=pltpu.CompilerParams(vmem_limit_bytes=56 * 1024 * 1024),
        cost_estimate=SHORT,
        name="expert_slope",
    )(here, grads_own, grads_core, rise_own, rise_core, weight_out)


def backward_kernel(split, section_ref, slope_ref, in_ref, sent_ref, kept_first, kept_second, *refs):
    weight_in, sems = refs
    width = weight_in.shape[0] // split
    outs = (sent_ref.at[0], sent_ref.at[1], kept_first, kept_second)
    spans, copies = [], []
    for i, step in enumerate((1, 3, 0, 2)):
        start = pl.multiple_of((section_ref[0] ^ step) * width, width)
        spans.append(pl.ds(start, width))
        copies.append(
            pltpu.make_async_copy(in_ref.at[spans[i]], weight_in.at[spans[i]], sems.at[i])
        )
    for copy in copies:
        copy.start()
    for copy, span, out_ref in zip(copies, spans, outs):
        copy.wait()
        part = contract_last(slope_ref[...], weight_in[span, :])
        out_ref[...] = part.astype(out_ref.dtype)


def expert_backward(section, slope, weight_in, split):
    rows, hidden = slope.shape
    features = weight_in.shape[0]
    width = features // split
    full = pl.BlockSpec(memory_space=pltpu.VMEM)
    kept = jax.ShapeDtypeStruct((rows, width), jnp.float32)
    return pl.pallas_call(
        functools.partial(backward_kernel, split),
        out_shape=(jax.ShapeDtypeStruct((2, rows, width), jnp.bfloat16), kept, kept),
        in_specs=[pl.BlockSpec(memory_space=pltpu.SMEM), full, pl.BlockSpec(memory_space=pltpu.HBM)],
        out_specs=[full] * 3,
        scratch_shapes=[
            vmem((features, hidden), jnp.bfloat16),
            pltpu.SemaphoreType.DMA((split,)),
        ],
        compiler_params=pltpu.CompilerParams(vmem_limit_bytes=56 * 1024 * 1024),
        cost_estimate=SHORT,
        name="expert_backward",
    )(section, slope, weight_in)


def small_body(
    tokens,
    expert_ids,
    gate_weights,
    out_grad,
    inner_weight,
    outer_weight,
    final_gain,
    dec_states,
    src_lengths,
    tgt_lengths,
    norm_gain,
    query_weight,
    key_weight,
    value_weight,
    out_weight,
):
    token_count, feature_count = tokens.shape
    group_size = lax.axis_size(("expert", "dp"))
    capacity = 3 * token_count // group_size
    here = lax.axis_index(("expert", "dp"))
    y = lax.axis_index("expert")
    d = lax.axis_index("dp")
    section = lax.axis_index("section")
    sections = lax.axis_size("section")
    half = feature_count // 2
    weight_in = inner_weight[0]
    weight_out = outer_weight[0]
    key_own, value_own, out_own = key_weight[0], value_weight[0], out_weight[0]
    query_own = query_weight[0]

    size = group_size
    near_codes = (0, 2, 4, 6)
    core_codes = (1, 3, 5, 7)
    core, x = d % 2, d // 2
    which_section = section.astype(jnp.int32).reshape(1)

    token_y = swap(tokens, "expert", 1)
    token_x = swap(tokens, "dp", 2)
    ids_own = expert_ids.T
    ids_x, ids_y = swap(ids_own, "dp", 2), swap(ids_own, "expert", 1)
    ids_far = swap(ids_x, "expert", 1)
    token_far = swap(token_y, "dp", 2)

    side = lax.rem(section, 2)
    share = token_count // 2
    grad_half = lax.dynamic_slice_in_dim(out_grad, side * share, share, 0)
    half_y = swap(gate(grad_half, token_y, ids_far), "expert", 1)
    states = dec_states[0]
    normed_own, asked = normed_halves(y, states, norm_gain)
    asked_here = swap(gate(asked, half_y), "expert", 1)
    query_there = jnp.dot(asked_here, query_own, preferred_element_type=jnp.float32)
    query_back = swap(query_there.astype(jnp.bfloat16), "expert", 1)
    other_y = swap(half_y, "section", 1)
    half_x = swap(gate(grad_half, token_far), "dp", 2)
    half_far = swap(gate(half_y, token_far), "dp", 2)
    half_pair = jnp.concatenate([half_x, half_far], axis=0)
    other_pair = swap(half_pair, "section", 1)

    row = lax.broadcasted_iota(jnp.int32, (token_count, token_count), 0)
    column = lax.broadcasted_iota(jnp.int32, (token_count, token_count), 1)
    ids = jnp.stack([ids_own, ids_x, ids_y, ids_far])
    named_there = jnp.concatenate([(ids == here).any(axis=1), (ids == (here ^ 1)).any(axis=1)])
    before = jnp.dot(
        named_there.astype(jnp.bfloat16),
        (row < column).astype(jnp.bfloat16),
        preferred_element_type=jnp.float32,
    ).astype(jnp.int32)
    code = jnp.where(named_there, before, -1)

    named = expert_ids[:, :, None] == jnp.arange(size, dtype=jnp.int32)[None, None, :]
    either = (named[:, 0] | named[:, 1]).astype(jnp.bfloat16)
    earlier = jnp.dot(
        (column < row).astype(jnp.bfloat16), either, preferred_element_type=jnp.float32
    ).astype(jnp.int32)
    rank = jnp.sum(jnp.where(named, earlier[:, None, :], 0), axis=2)
    codes_of = expert_ids ^ here
    position = ((codes_of >> 1) + 4 * (codes_of & 1)) * capacity + rank

    def forward(rows, after):
        pre_act = jnp.dot(rows, weight_in, preferred_element_type=jnp.float32)
        hidden = jax.nn.gelu(gate(pre_act, after)).astype(jnp.bfloat16)
        part = jnp.dot(hidden, weight_out, preferred_element_type=jnp.float32)
        return pre_act, part.astype(jnp.bfloat16)

    def slope_of(pre_act):
        return jax.vjp(jax.nn.gelu, pre_act)[1](jnp.ones_like(pre_act))[0]

    rows_own, rows_sent = dispatch(
        which_section,
        code,
        [tokens, token_x, token_y, token_far],
        tuple(((place, 0, token_count, None),) for place in range(4)),
        capacity,
    )
    rows_core = swap(rows_sent, "dp", 1)
    pre_own, part_own = forward(rows_own, rows_core)
    pre_core, part_core = forward(gate(rows_core, asked_here), half_pair)
    home = send_home(part_own, near_codes, capacity) + send_home(part_core, core_codes, capacity)

    rise_own, rise_core = slope_of(gate(pre_own, home[1])), slope_of(gate(pre_core, home[1]))
    grads_own, grads_sent = dispatch(
        which_section,
        gate(code, home[2], rise_own, rise_core),
        [out_grad, half_x, half_y, half_far, other_y, other_pair],
        (
            ((0, 0, token_count, None),),
            ((1, 0, share, 0), (5, 0, share, 1)),
            ((2, 0, share, 0), (4, 0, share, 1)),
            ((3, 0, share, 0), (5, share, share, 1)),
        ),
        capacity,
    )
    held_gates = gate(gate_weights, grads_sent, query_back)
    sent_pair, first, second = combine(which_section, position, held_gates, home, sections)
    from_pair = swap(sent_pair, "section", 1)
    grads_core = swap(grads_sent, "dp", 1)
    to_other = (second + from_pair[1].astype(jnp.float32)).astype(jnp.bfloat16)
    from_other = swap(to_other, "section", 2)
    slope = expert_slope(
        gate(here.astype(jnp.int32).reshape(1), to_other),
        near_codes + core_codes,
        grads_own,
        grads_core,
        rise_own,
        rise_core,
        weight_out,
    )
    mixed_sum = gate(first, slope) + from_pair[0].astype(jnp.float32)
    mixed_slice = (mixed_sum + from_other.astype(jnp.float32)).astype(jnp.bfloat16)
    key_other = swap(gate(key_own, first), "expert", 1)
    mixed_near = swap(mixed_slice, "section", 1)
    back_pair, back_first, back_second = expert_backward(
        gate(which_section, mixed_near), slope, weight_in, sections
    )
    mixed_far = swap(jnp.stack([mixed_slice, gate(mixed_near, key_other)]), "section", 2)
    slices = [mixed_slice, mixed_near, mixed_far[0], mixed_far[1]]

    value_other = swap(gate(value_own, mixed_slice), "expert", 1)

    query_here = jnp.dot(normed_own, query_own, preferred_element_type=jnp.float32)
    query = (query_here + query_back.astype(jnp.float32)).astype(jnp.bfloat16)

    memory = make_memory(which_section, gate(tokens, value_other), slices, final_gain)
    out_other = swap(gate(out_own, memory), "expert", 1)
    memory_x = swap(memory, "dp", 2)
    memory_core = swap(memory, "dp", 1)

    def sentence(which, near, far, *after):
        place = gate(jnp.stack([y, core, which]).astype(jnp.int32), *after)
        rows_of = lax.dynamic_slice_in_dim(query, which * TGT_LEN, TGT_LEN, 0)
        parts = (key_own, key_other), (value_own, value_other)
        return attend_sentence(place, src_lengths, rows_of, near, far, *parts)

    back_from_pair = swap(back_pair, "section", 1)
    back_to_other = (back_second + back_from_pair[1].astype(jnp.float32)).astype(jnp.bfloat16)
    back_from_other = swap(back_to_other, "section", 2)
    backward_sum = back_first + back_from_pair[0].astype(jnp.float32)
    backward_sum = backward_sum + back_from_other.astype(jnp.float32)
    context_own = sentence(x, memory, memory_core)
    memory_far = swap(gate(memory_x, context_own), "dp", 1)
    context_other = sentence(1 - x, memory_x, memory_far)
    place = jnp.stack([y, core, x]).astype(jnp.int32)
    sent_mine, sent_other, kept_mine, kept_other = project(
        place, context_own, context_other, out_own, out_other
    )

    core_other = swap(sent_other, "dp", 1)
    core_mine = swap(sent_mine, "dp", 1)
    last = gate(kept_other, back_from_other) + core_other.astype(jnp.float32)
    from_x = swap(last.astype(jnp.bfloat16), "dp", 2)
    attended = kept_mine + core_mine.astype(jnp.float32) + from_x.astype(jnp.float32)
    dec_out = add_residual(attended, states, tgt_lengths)

    grads_home = exchange(gate(backward_sum.astype(jnp.bfloat16), last), group_size, capacity)
    natural = expert_ids * capacity + rank
    (token_grad,) = combine(
        which_section, natural, gate_weights, [grads_home], 1
    )
    return (dec_out[None], token_grad)


def add_residual(attended, states, tgt_lengths):
    my_columns = attended.shape[1]
    residual = lax.dynamic_slice_in_dim(
        states, lax.axis_index("dp") * my_columns, my_columns, 1
    ).astype(jnp.float32)
    row_mask = (jnp.arange(TGT_LEN, dtype=jnp.int32)[None, :] < tgt_lengths[:, None]).reshape(-1, 1)
    return (residual + jnp.where(row_mask, attended, 0.0)).astype(jnp.bfloat16)


def body(
    tokens,
    expert_ids,
    gate_weights,
    out_grad,
    inner_weight,
    outer_weight,
    final_gain,
    dec_states,
    src_lengths,
    tgt_lengths,
    norm_gain,
    query_weight,
    key_weight,
    value_weight,
    out_weight,
):
    token_count, feature_count = tokens.shape
    group_size = lax.axis_size(("expert", "dp"))
    capacity = 3 * token_count // group_size
    slots = group_size * capacity

    named = expert_ids[:, :, None] == jnp.arange(group_size, dtype=jnp.int32)[None, None, :]
    either = (named[:, 0] | named[:, 1]).astype(jnp.bfloat16)
    row = lax.broadcasted_iota(jnp.int32, (token_count, token_count), 0)
    column = lax.broadcasted_iota(jnp.int32, (token_count, token_count), 1)
    earlier = jnp.dot(
        (column < row).astype(jnp.bfloat16), either, preferred_element_type=jnp.float32
    ).astype(jnp.int32)
    rank = jnp.sum(jnp.where(named, earlier[:, None, :], 0), axis=2)
    position = expert_ids * capacity + rank
    pick_first = slot_matrix(position[:, 0], slots)
    pick_second = slot_matrix(position[:, 1], slots)
    fill = (pick_first + pick_second).T

    def place(values):
        return jnp.dot(fill, values, preferred_element_type=jnp.float32).astype(jnp.bfloat16)

    def combine(arrived):
        first = jnp.dot(pick_first, arrived, preferred_element_type=jnp.float32)
        second = jnp.dot(pick_second, arrived, preferred_element_type=jnp.float32)
        return gate_weights[:, :1] * first + gate_weights[:, 1:] * second

    weight_in = inner_weight[0]
    weight_out = outer_weight[0]
    arrived_rows = exchange(place(tokens), group_size, capacity)
    pre_act = jnp.dot(arrived_rows, weight_in, preferred_element_type=jnp.float32)
    hidden = jax.nn.gelu(pre_act).astype(jnp.bfloat16)
    forward_part = jnp.dot(hidden, weight_out, preferred_element_type=jnp.float32)
    arrived_grads = exchange(place(out_grad), group_size, capacity)
    outputs_home = exchange(forward_part.astype(jnp.bfloat16), group_size, capacity)
    mixed_slice = sum_sections(combine(outputs_home)).astype(jnp.bfloat16)
    mixed = gather_sections(mixed_slice).astype(jnp.float32)
    memory = normalize(tokens.astype(jnp.float32) + mixed, final_gain).astype(jnp.bfloat16)

    back = contract_last(arrived_grads, weight_out)
    slope = jax.vjp(jax.nn.gelu, pre_act)[1](back)[0].astype(jnp.bfloat16)
    backward_part = contract_last(slope, weight_in)
    backward_slice = sum_sections(backward_part).astype(jnp.bfloat16)
    grads_home = exchange(backward_slice, group_size, capacity)
    token_grad = combine(grads_home).astype(jnp.bfloat16)

    states = dec_states[0]
    normed = normalize(states.astype(jnp.float32), norm_gain[0]).astype(jnp.bfloat16)
    full_query = gather_weight(query_weight[0], 0)
    full_key = gather_weight(key_weight[0], 0)
    full_value = gather_weight(value_weight[0], 0)
    full_out = gather_weight(out_weight[0], 1)
    query_sum = jnp.dot(normed, full_query, preferred_element_type=jnp.float32)
    source = gather_rows(memory, "dp")
    key_sum = jnp.dot(source, full_key, preferred_element_type=jnp.float32)
    value_sum = jnp.dot(source, full_value, preferred_element_type=jnp.float32)
    key_mask = jnp.arange(SRC_LEN, dtype=jnp.int32)[None, :] < src_lengths[:, None]
    context = attend(
        query_sum.astype(jnp.bfloat16),
        key_sum.astype(jnp.bfloat16),
        value_sum.astype(jnp.bfloat16),
        key_mask,
    )
    attended = sum_heads(jnp.dot(context, full_out, preferred_element_type=jnp.float32))
    dec_out = add_residual(attended, states, tgt_lengths)
    return (dec_out[None], token_grad)


def solution(mesh):
    in_specs = (
        P(("expert", "dp"), None),
        P(("expert", "dp"), None),
        P(("expert", "dp"), None),
        P(("expert", "dp"), None),
        P(("expert", "dp"), None, "section"),
        P(("expert", "dp"), "section", None),
        P(),
        P("section", "expert", None),
        P("expert"),
        P("expert"),
        P("section", None),
        P("section", "expert", "dp"),
        P("section", "expert", "dp"),
        P("section", "expert", "dp"),
        P("section", "dp", "expert"),
    )
    out_specs = (P("section", "expert", "dp"), P(("expert", "dp"), "section"))
    small = (mesh.shape["section"], mesh.shape["expert"], mesh.shape["dp"]) == (4, 2, 4)
    chosen = small_body if small else body
    return jax.shard_map(chosen, mesh=mesh, in_specs=in_specs, out_specs=out_specs, check_vma=False)
```

```python
import functools

import jax
import jax.numpy as jnp
from jax import lax
from jax.experimental import pallas as pl
from jax.experimental.pallas import tpu as pltpu
from jax.sharding import PartitionSpec as P

HEAD_DIM = 128
SRC_LEN = 256
TGT_LEN = 128


EPSILON = 1e-05


def normalize(values, gain):
    centre = jnp.mean(values, axis=-1, keepdims=True)
    centred = values - centre
    spread = jnp.mean(centred * centred, axis=-1, keepdims=True)
    return centred * lax.rsqrt(spread + EPSILON) * gain


def contract_last(left, right):
    return lax.dot_general(
        left, right, (((1,), (1,)), ((), ())), preferred_element_type=jnp.float32
    )


def shift(value, axis, step):
    size = lax.axis_size(axis)
    return lax.ppermute(value, axis, [(i, (i + step) % size) for i in range(size)])


def swap(value, axis, mask):
    size = lax.axis_size(axis)
    return lax.ppermute(value, axis, [(i, i ^ mask) for i in range(size)])


def sum_sections(partial):
    count = lax.axis_size("section")
    me = lax.axis_index("section")
    width = partial.shape[1] // count

    def piece(owner):
        return lax.dynamic_slice_in_dim(partial, owner * width, width, 1)

    total = piece(me).astype(jnp.float32)
    for step in range(1, count):
        sent = piece(lax.rem(me + step, count)).astype(jnp.bfloat16)
        total = total + shift(sent, "section", step).astype(jnp.float32)
    return total


def gather_sections(mine):
    count = lax.axis_size("section")
    me = lax.axis_index("section")
    width = mine.shape[1]
    whole = jnp.zeros((mine.shape[0], width * count), mine.dtype)
    whole = lax.dynamic_update_slice_in_dim(whole, mine, me * width, 1)
    for step in range(1, count):
        owner = lax.rem(me - step + count, count)
        whole = lax.dynamic_update_slice_in_dim(
            whole, shift(mine, "section", step), owner * width, 1
        )
    return whole


def gather_rows(mine, axis):
    held = mine
    me = lax.axis_index(axis)
    mask = lax.axis_size(axis) // 2
    blocks = [mine]
    while mask >= 1:
        blocks = blocks + [swap(block, axis, mask) for block in blocks]
        mask //= 2
    codes = [0]
    mask = lax.axis_size(axis) // 2
    while mask >= 1:
        codes = codes + [code ^ mask for code in codes]
        mask //= 2
    ordered = []
    for place in range(len(blocks)):
        chosen = blocks[0]
        for code, block in zip(codes[1:], blocks[1:]):
            chosen = jnp.where((me ^ code) == place, block, chosen)
        ordered.append(chosen)
    return jnp.concatenate(ordered, axis=0)


def gather_weight(weight, dimension):
    if lax.axis_size("expert") != 2:
        return lax.all_gather(weight, "expert", axis=dimension, tiled=True)
    other = swap(weight, "expert", 1)
    first = lax.axis_index("expert") == 0
    return jnp.concatenate(
        [jnp.where(first, weight, other), jnp.where(first, other, weight)], axis=dimension
    )


def sum_heads(partial):
    me = lax.axis_index("dp")
    count = lax.axis_size("dp")
    rows, columns = partial.shape
    total = partial.reshape(rows, count, columns // count)
    mask = 1
    while mask < count:
        paired = total.reshape(rows, -1, 2, columns // count)
        bit = (me // mask) % 2
        sent = lax.dynamic_index_in_dim(paired, 1 - bit, 2, False).astype(jnp.bfloat16)
        kept = lax.dynamic_index_in_dim(paired, bit, 2, False)
        total = kept + swap(sent, "dp", mask).astype(jnp.float32)
        mask *= 2
    return total.reshape(rows, columns // count)


def slot_matrix(positions, slots):
    places = lax.broadcasted_iota(jnp.int32, (positions.shape[0], slots), 1)
    return (positions[:, None] == places).astype(jnp.bfloat16)


def attend(query, keys, values, key_mask):
    sequences = key_mask.shape[0]
    head_count = query.shape[1] // HEAD_DIM
    query_split = query.reshape(sequences, -1, head_count, HEAD_DIM)
    keys_split = keys.reshape(sequences, -1, head_count, HEAD_DIM)
    values_split = values.reshape(sequences, -1, head_count, HEAD_DIM)
    scores = jnp.einsum(
        "bqhd,bkhd->bhqk", query_split, keys_split, preferred_element_type=jnp.float32
    ) * HEAD_DIM ** (-0.5)
    scores = jnp.where(key_mask[:, None, None, :], scores, -1e30)
    highest = jnp.max(scores, axis=-1, keepdims=True)
    weights = jnp.exp(scores - highest)
    probs = (weights / jnp.sum(weights, axis=-1, keepdims=True)).astype(jnp.bfloat16)
    context = jnp.einsum("bhqk,bkhd->bqhd", probs, values_split, preferred_element_type=jnp.float32)
    return context.astype(jnp.bfloat16).reshape(-1, head_count * HEAD_DIM)


def exchange(values, group_size, capacity):
    sent = values.reshape(group_size, capacity, values.shape[1])
    arrived = lax.all_to_all(sent, ("expert", "dp"), split_axis=0, concat_axis=0, tiled=True)
    return arrived.reshape(values.shape)


SHORT = pl.CostEstimate(flops=1, bytes_accessed=1, transcendentals=0)


def gate(value, *after):
    return lax.optimization_barrier((value,) + after)[0]


def vmem(shape, dtype):
    return pltpu.VMEM(shape, dtype)


def dispatch_kernel(capacity, layout, section_ref, code_ref, *refs):
    blocks = refs[:-4]
    outs, held, sems = refs[-4:-2], refs[-2], refs[-1]
    count, rows = held.shape[0], held.shape[1]
    half = lax.rem(section_ref[0], 2)
    copies = []
    for place, pieces in enumerate(layout):
        group = []
        for i, (which, start, length, side) in enumerate(pieces):
            there = held.at[place]
            if side is not None:
                offset = (half if side == 0 else 1 - half) * length
                there = held.at[place, pl.ds(pl.multiple_of(offset, length), length)]
            here = blocks[which].at[pl.ds(start, length)]
            group.append(pltpu.make_async_copy(here, there, sems.at[place, i]))
        copies.append(group)
    for group in copies:
        for copy in group:
            copy.start()
    for place, group in enumerate(copies):
        picks = []
        for which in range(2):
            line = which * count + place
            code = code_ref[line : line + 1, :]
            slot = lax.broadcasted_iota(jnp.int32, (capacity, code.shape[1]), 0)
            picks.append(jnp.where(slot == code, 1.0, 0.0))
        pick = jnp.concatenate(picks, axis=0).astype(jnp.bfloat16)
        for copy in group:
            copy.wait()
        picked = jnp.dot(pick, held[place], preferred_element_type=jnp.float32)
        picked = picked.astype(jnp.bfloat16)
        for which, out_ref in enumerate(outs):
            out_ref[place * capacity : (place + 1) * capacity, :] = picked[
                which * capacity : (which + 1) * capacity
            ]


def dispatch(section, code, blocks, layout, capacity):
    rows, features = blocks[0].shape
    count = len(layout)
    picked = jax.ShapeDtypeStruct((count * capacity, features), jnp.bfloat16)
    return pl.pallas_call(
        functools.partial(dispatch_kernel, capacity, layout),
        out_shape=(picked, picked),
        in_specs=[
            pl.BlockSpec(memory_space=pltpu.SMEM),
            pl.BlockSpec(memory_space=pltpu.VMEM),
        ]
        + [pl.BlockSpec(memory_space=pltpu.HBM)] * len(blocks),
        out_specs=[pl.BlockSpec(memory_space=pltpu.VMEM)] * 2,
        scratch_shapes=[
            vmem((count, rows, features), jnp.bfloat16),
            pltpu.SemaphoreType.DMA((count, 2)),
        ],
        compiler_params=pltpu.CompilerParams(vmem_limit_bytes=10 * 1024 * 1024),
        cost_estimate=SHORT,
        name="dispatch",
    )(section, code, *blocks)


def send_home(part, codes, capacity):
    size = lax.axis_size(("expert", "dp"))
    arrived = []
    for place, code in enumerate(codes):
        block = part[place * capacity : (place + 1) * capacity]
        if code:
            block = lax.ppermute(block, ("expert", "dp"), [(i, i ^ code) for i in range(size)])
        arrived.append(block)
    return arrived


def combine_kernel(count, split, section_ref, position_ref, gates_ref, *refs):
    blocks = refs[:count]
    outs, (held, total) = refs[count:-2], refs[-2:]
    capacity, features = blocks[0].shape
    position = position_ref[...]
    slot = lax.broadcasted_iota(jnp.int32, (position.shape[0], count * capacity), 1)
    picks = [
        jnp.where(position[:, k : k + 1] == slot, 1.0, 0.0).astype(jnp.bfloat16) for k in range(2)
    ]
    for i, block in enumerate(blocks):
        held[i * capacity : (i + 1) * capacity, :] = block[...]
    pick = jnp.concatenate(picks, axis=0)
    rows = position.shape[0]
    both = jnp.dot(pick, held[...], preferred_element_type=jnp.float32)
    total[...] = gates_ref[:, 0:1] * both[:rows] + gates_ref[:, 1:2] * both[rows:]
    if split == 1:
        outs[0][...] = total[...].astype(outs[0].dtype)
        return
    sent_ref, kept_first, kept_second = outs
    width = features // split
    for step, out_ref in enumerate((kept_first, sent_ref.at[0], kept_second, sent_ref.at[1])):
        start = pl.multiple_of((section_ref[0] ^ step) * width, width)
        out_ref[...] = total[:, pl.ds(start, width)].astype(out_ref.dtype)


def combine(section, position, gates, blocks, split):
    capacity, features = blocks[0].shape
    rows = position.shape[0]
    count = len(blocks)
    width = features // split
    kept = jax.ShapeDtypeStruct((rows, width), jnp.float32)
    if split == 1:
        out_shape = (jax.ShapeDtypeStruct((rows, width), jnp.bfloat16),)
    else:
        out_shape = (jax.ShapeDtypeStruct((2, rows, width), jnp.bfloat16), kept, kept)
    full = pl.BlockSpec(memory_space=pltpu.VMEM)
    return pl.pallas_call(
        functools.partial(combine_kernel, count, split),
        out_shape=out_shape,
        in_specs=[pl.BlockSpec(memory_space=pltpu.SMEM)] + [full] * (2 + count),
        out_specs=[full] * len(out_shape),
        scratch_shapes=[
            vmem((count * capacity, features), jnp.bfloat16),
            vmem((rows, features), jnp.float32),
        ],
        compiler_params=pltpu.CompilerParams(vmem_limit_bytes=14 * 1024 * 1024),
        cost_estimate=SHORT,
        name="combine",
    )(section, position, gates, *blocks)


def memory_kernel(count, section_ref, tokens_ref, gain_ref, *refs):
    slices, out_ref, mixed = refs[:count], refs[count], refs[count + 1]
    me = section_ref[0]
    width = slices[0].shape[1]
    for step, piece in enumerate(slices):
        owner = me ^ step
        mixed[:, pl.ds(pl.multiple_of(owner * width, width), width)] = piece[...].astype(
            jnp.float32
        )
    values = tokens_ref[...].astype(jnp.float32) + mixed[...]
    out_ref[...] = normalize(values, gain_ref[...]).astype(jnp.bfloat16)


def make_memory(me, tokens, slices, gain):
    return pl.pallas_call(
        functools.partial(memory_kernel, len(slices)),
        out_shape=jax.ShapeDtypeStruct(tokens.shape, jnp.bfloat16),
        in_specs=[
            pl.BlockSpec(memory_space=pltpu.SMEM),
        ]
        + [pl.BlockSpec(memory_space=pltpu.VMEM)] * (2 + len(slices)),
        out_specs=pl.BlockSpec(memory_space=pltpu.VMEM),
        scratch_shapes=[vmem(tokens.shape, jnp.float32)],
        compiler_params=pltpu.CompilerParams(vmem_limit_bytes=8 * 1024 * 1024),
        cost_estimate=SHORT,
        name="memory",
    )(me, tokens, gain[None], *slices)


def normed_kernel(y_ref, states_ref, gain_ref, own_ref, other_ref):
    values = normalize(states_ref[...].astype(jnp.float32), gain_ref[...]).astype(jnp.bfloat16)
    width = own_ref.shape[1]
    for out_ref, first in ((own_ref, y_ref[0] == 0), (other_ref, y_ref[0] == 1)):
        out_ref[...] = jnp.where(first, values[:, :width], values[:, width:])


def normed_halves(y, states, gain):
    rows, features = states.shape
    full = pl.BlockSpec(memory_space=pltpu.VMEM)
    return pl.pallas_call(
        normed_kernel,
        out_shape=(jax.ShapeDtypeStruct((rows, features // 2), jnp.bfloat16),) * 2,
        in_specs=[pl.BlockSpec(memory_space=pltpu.SMEM), full, full],
        out_specs=[full] * 2,
        compiler_params=pltpu.CompilerParams(vmem_limit_bytes=12 * 1024 * 1024),
        cost_estimate=SHORT,
        name="normed",
    )(y.astype(jnp.int32).reshape(1), states, gain)


def attend_kernel(place_ref, lengths_ref, query_ref, *refs):
    near_ref, far_ref, key_own, key_other, value_own, value_other, out_ref = refs[:7]
    source, key_weight, value_weight, keys, values, sems = refs[7:]
    y, core, sentence = place_ref[0], place_ref[1], place_ref[2]
    rows = near_ref.shape[0]
    depth = key_own.shape[0]
    moves = [
        (near_ref, source.at[pl.ds(0, rows)]),
        (far_ref, source.at[pl.ds(rows, rows)]),
        (key_own, key_weight.at[y]),
        (key_other, key_weight.at[1 - y]),
        (value_own, value_weight.at[y]),
        (value_other, value_weight.at[1 - y]),
    ]
    copies = [
        pltpu.make_async_copy(here, there, sems.at[i]) for i, (here, there) in enumerate(moves)
    ]
    for copy in copies:
        copy.start()

    def linear(weight, result):
        total = jnp.dot(source[:, :depth], weight[0], preferred_element_type=jnp.float32)
        total += jnp.dot(source[:, depth:], weight[1], preferred_element_type=jnp.float32)
        result[...] = total.astype(jnp.bfloat16)

    for copy in copies[:4]:
        copy.wait()
    linear(key_weight, keys)
    for copy in copies[4:]:
        copy.wait()
    linear(value_weight, values)

    column = lax.broadcasted_iota(jnp.int32, (query_ref.shape[0], 2 * rows), 1)
    position = jnp.where(column < rows, column + core * rows, column - core * rows)
    valid = position < lengths_ref[sentence]
    for head in range(query_ref.shape[1] // HEAD_DIM):
        span = slice(head * HEAD_DIM, (head + 1) * HEAD_DIM)
        scores = contract_last(query_ref[:, span], keys[:, span]) * HEAD_DIM ** (-0.5)
        scores = jnp.where(valid, scores, -1e30)
        weights = jnp.exp(scores - jnp.max(scores, axis=-1, keepdims=True))
        probs = (weights / jnp.sum(weights, axis=-1, keepdims=True)).astype(jnp.bfloat16)
        result = jnp.dot(probs, values[:, span], preferred_element_type=jnp.float32)
        out_ref[:, span] = result.astype(jnp.bfloat16)


def attend_sentence(place, lengths, query, near, far, key_parts, value_pair):
    rows, features = near.shape
    depth, width = key_parts[0].shape
    hold = pl.BlockSpec(memory_space=pltpu.HBM)
    smem = pl.BlockSpec(memory_space=pltpu.SMEM)
    full = pl.BlockSpec(memory_space=pltpu.VMEM)
    return pl.pallas_call(
        attend_kernel,
        out_shape=jax.ShapeDtypeStruct(query.shape, jnp.bfloat16),
        in_specs=[smem, smem, full] + [hold] * 6,
        out_specs=full,
        scratch_shapes=[
            vmem((2 * rows, features), jnp.bfloat16),
            vmem((2, depth, width), jnp.bfloat16),
            vmem((2, depth, width), jnp.bfloat16),
            vmem((2 * rows, width), jnp.bfloat16),
            vmem((2 * rows, width), jnp.bfloat16),
            pltpu.SemaphoreType.DMA((6,)),
        ],
        compiler_params=pltpu.CompilerParams(vmem_limit_bytes=56 * 1024 * 1024),
        cost_estimate=SHORT,
        name="attend_sentence",
    )(place, lengths, query, near, far, *key_parts, *value_pair)


def project_kernel(place_ref, mine_ref, done_ref, own_ref, other_ref, *refs):
    sent_mine, sent_other, kept_mine, kept_other, context = refs
    y, core, x = place_ref[0], place_ref[1], place_ref[2]
    targets = mine_ref.shape[0]
    for part, sentence in ((mine_ref, x), (done_ref, 1 - x)):
        context[pl.ds(pl.multiple_of(sentence * targets, targets), targets), :] = part[...]
    columns = kept_mine.shape[1]
    outs = ((sent_mine, kept_mine), (sent_other, kept_other))

    def write(weight_ref, chosen):
        for side, out_ref in zip((1 - core, core), chosen):
            span = pl.ds(pl.multiple_of(side * columns, columns), columns)
            part = jnp.dot(context[...], weight_ref[:, span], preferred_element_type=jnp.float32)
            out_ref[...] = part.astype(out_ref.dtype)

    @pl.when(x == y)
    def _():
        write(own_ref, outs[0])
        write(other_ref, outs[1])

    @pl.when(x != y)
    def _():
        write(other_ref, outs[0])
        write(own_ref, outs[1])


def project(place, mine, done, out_own, out_other):
    targets, width = 2 * mine.shape[0], mine.shape[1]
    columns = out_own.shape[1] // 2
    full = pl.BlockSpec(memory_space=pltpu.VMEM)
    sent = jax.ShapeDtypeStruct((targets, columns), jnp.bfloat16)
    kept = jax.ShapeDtypeStruct((targets, columns), jnp.float32)
    return pl.pallas_call(
        project_kernel,
        out_shape=(sent, sent, kept, kept),
        in_specs=[pl.BlockSpec(memory_space=pltpu.SMEM)] + [full] * 4,
        out_specs=[full] * 4,
        scratch_shapes=[vmem((targets, width), jnp.bfloat16)],
        compiler_params=pltpu.CompilerParams(vmem_limit_bytes=16 * 1024 * 1024),
        cost_estimate=SHORT,
        name="project",
    )(place, mine, done, out_own, out_other)


def slope_kernel(codes, here_ref, own_ref, core_ref, rise_own, rise_core, out_ref, slope, *refs):
    grads, rise, weight_out, sems = refs
    rows = own_ref.shape[0]
    hidden = weight_out.shape[0]
    chunk = hidden // 4
    moves = []
    block = 2 * rows // len(codes)
    for order, code in enumerate(codes):
        source = here_ref[0] ^ code
        there = pl.ds(pl.multiple_of(source * block, 16), block)
        here = pl.ds(order * block % rows, block)
        own = order * block < rows
        moves.append(((own_ref if own else core_ref).at[here], grads.at[there]))
        moves.append(((rise_own if own else rise_core).at[here], rise.at[there]))
    for part in range(4):
        span = pl.ds(part * chunk, chunk)
        moves.append((out_ref.at[span], weight_out.at[span]))
    copies = [
        pltpu.make_async_copy(here, there, sems.at[i]) for i, (here, there) in enumerate(moves)
    ]
    for copy in copies:
        copy.start()
    for copy in copies[:-4]:
        copy.wait()
    for part in range(4):
        copies[part - 4].wait()
        span = slice(part * chunk, (part + 1) * chunk)
        back = contract_last(grads[...], weight_out[span, :])
        slope[:, span] = (back * rise[:, span]).astype(jnp.bfloat16)


def expert_slope(here, codes, grads_own, grads_core, rise_own, rise_core, weight_out):
    rows = 2 * grads_own.shape[0]
    hidden, features = weight_out.shape
    hold = pl.BlockSpec(memory_space=pltpu.HBM)
    return pl.pallas_call(
        functools.partial(slope_kernel, codes),
        out_shape=jax.ShapeDtypeStruct((rows, hidden), jnp.bfloat16),
        in_specs=[pl.BlockSpec(memory_space=pltpu.SMEM)] + [hold] * 5,
        out_specs=pl.BlockSpec(memory_space=pltpu.VMEM),
        scratch_shapes=[
            vmem((rows, features), jnp.bfloat16),
            vmem((rows, hidden), jnp.float32),
            vmem((hidden, features), jnp.bfloat16),
            pltpu.SemaphoreType.DMA((4 + 2 * len(codes),)),
        ],
        compiler_params=pltpu.CompilerParams(vmem_limit_bytes=56 * 1024 * 1024),
        cost_estimate=SHORT,
        name="expert_slope",
    )(here, grads_own, grads_core, rise_own, rise_core, weight_out)


def backward_kernel(split, section_ref, slope_ref, in_ref, sent_ref, kept_first, kept_second, *refs):
    weight_in, sems = refs
    width = weight_in.shape[0] // split
    outs = (sent_ref.at[0], sent_ref.at[1], kept_first, kept_second)
    spans, copies = [], []
    for i, step in enumerate((1, 3, 0, 2)):
        start = pl.multiple_of((section_ref[0] ^ step) * width, width)
        spans.append(pl.ds(start, width))
        copies.append(
            pltpu.make_async_copy(in_ref.at[spans[i]], weight_in.at[spans[i]], sems.at[i])
        )
    for copy in copies:
        copy.start()
    for copy, span, out_ref in zip(copies, spans, outs):
        copy.wait()
        part = contract_last(slope_ref[...], weight_in[span, :])
        out_ref[...] = part.astype(out_ref.dtype)


def expert_backward(section, slope, weight_in, split):
    rows, hidden = slope.shape
    features = weight_in.shape[0]
    width = features // split
    full = pl.BlockSpec(memory_space=pltpu.VMEM)
    kept = jax.ShapeDtypeStruct((rows, width), jnp.float32)
    return pl.pallas_call(
        functools.partial(backward_kernel, split),
        out_shape=(jax.ShapeDtypeStruct((2, rows, width), jnp.bfloat16), kept, kept),
        in_specs=[pl.BlockSpec(memory_space=pltpu.SMEM), full, pl.BlockSpec(memory_space=pltpu.HBM)],
        out_specs=[full] * 3,
        scratch_shapes=[
            vmem((features, hidden), jnp.bfloat16),
            pltpu.SemaphoreType.DMA((split,)),
        ],
        compiler_params=pltpu.CompilerParams(vmem_limit_bytes=56 * 1024 * 1024),
        cost_estimate=SHORT,
        name="expert_backward",
    )(section, slope, weight_in)


def small_body(
    tokens,
    expert_ids,
    gate_weights,
    out_grad,
    inner_weight,
    outer_weight,
    final_gain,
    dec_states,
    src_lengths,
    tgt_lengths,
    norm_gain,
    query_weight,
    key_weight,
    value_weight,
    out_weight,
):
    token_count, feature_count = tokens.shape
    group_size = lax.axis_size(("expert", "dp"))
    capacity = 3 * token_count // group_size
    here = lax.axis_index(("expert", "dp"))
    y = lax.axis_index("expert")
    d = lax.axis_index("dp")
    section = lax.axis_index("section")
    sections = lax.axis_size("section")
    half = feature_count // 2
    weight_in = inner_weight[0]
    weight_out = outer_weight[0]
    key_own, value_own, out_own = key_weight[0], value_weight[0], out_weight[0]
    query_own = query_weight[0]

    size = group_size
    near_codes = (0, 2, 4, 6)
    core_codes = (1, 3, 5, 7)
    core, x = d % 2, d // 2
    which_section = section.astype(jnp.int32).reshape(1)

    token_y = swap(tokens, "expert", 1)
    token_x = swap(tokens, "dp", 2)
    ids_own = expert_ids.T
    ids_x, ids_y = swap(ids_own, "dp", 2), swap(ids_own, "expert", 1)
    ids_far = swap(ids_x, "expert", 1)
    token_far = swap(token_y, "dp", 2)

    side = lax.rem(section, 2)
    share = token_count // 2
    grad_half = lax.dynamic_slice_in_dim(out_grad, side * share, share, 0)
    half_y = swap(gate(grad_half, token_y, ids_far), "expert", 1)
    states = dec_states[0]
    normed_own, asked = normed_halves(y, states, norm_gain)
    asked_here = swap(gate(asked, half_y), "expert", 1)
    query_there = jnp.dot(asked_here, query_own, preferred_element_type=jnp.float32)
    query_back = swap(query_there.astype(jnp.bfloat16), "expert", 1)
    other_y = swap(half_y, "section", 1)
    grad_y = jnp.concatenate([half_y, other_y], axis=0)
    half_x = swap(gate(grad_half, token_far), "dp", 2)
    other_x = swap(half_x, "section", 1)

    row = lax.broadcasted_iota(jnp.int32, (token_count, token_count), 0)
    column = lax.broadcasted_iota(jnp.int32, (token_count, token_count), 1)
    ids = jnp.stack([ids_own, ids_x, ids_y, ids_far])
    named_there = jnp.concatenate([(ids == here).any(axis=1), (ids == (here ^ 1)).any(axis=1)])
    before = jnp.dot(
        named_there.astype(jnp.bfloat16),
        (row < column).astype(jnp.bfloat16),
        preferred_element_type=jnp.float32,
    ).astype(jnp.int32)
    code = jnp.where(named_there, before, -1)

    named = expert_ids[:, :, None] == jnp.arange(size, dtype=jnp.int32)[None, None, :]
    either = (named[:, 0] | named[:, 1]).astype(jnp.bfloat16)
    earlier = jnp.dot(
        (column < row).astype(jnp.bfloat16), either, preferred_element_type=jnp.float32
    ).astype(jnp.int32)
    rank = jnp.sum(jnp.where(named, earlier[:, None, :], 0), axis=2)
    codes_of = expert_ids ^ here
    position = ((codes_of >> 1) + 4 * (codes_of & 1)) * capacity + rank

    def forward(rows, *after):
        pre_act = jnp.dot(rows, weight_in, preferred_element_type=jnp.float32)
        hidden = jax.nn.gelu(gate(pre_act, *after)).astype(jnp.bfloat16)
        part = jnp.dot(hidden, weight_out, preferred_element_type=jnp.float32)
        return pre_act, part.astype(jnp.bfloat16)

    def slope_of(pre_act):
        return jax.vjp(jax.nn.gelu, pre_act)[1](jnp.ones_like(pre_act))[0]

    rows_own, rows_sent = dispatch(
        which_section,
        code,
        [tokens, token_x, token_y, token_far],
        tuple(((place, 0, token_count, None),) for place in range(4)),
        capacity,
    )
    rows_core = swap(rows_sent, "dp", 1)
    pre_own, part_own = forward(rows_own, rows_core, half_x)
    pre_core, part_core = forward(rows_core, asked_here)
    home = send_home(part_own, near_codes, capacity) + send_home(part_core, core_codes, capacity)

    rise_own, rise_core = slope_of(gate(pre_own, home[1])), slope_of(gate(pre_core, home[1]))
    held_gates = gate(gate_weights, rise_own, rise_core, query_back, other_x, other_y)
    sent_pair, first, second = combine(which_section, position, held_gates, home, sections)
    from_pair = swap(sent_pair, "section", 1)
    grad_far = swap(gate(grad_y, first), "dp", 2)
    grads_own, grads_sent = dispatch(
        which_section,
        code,
        [out_grad, half_x, other_x, grad_y, grad_far],
        (
            ((0, 0, token_count, None),),
            ((1, 0, share, 0), (2, 0, share, 1)),
            ((3, 0, share, 0), (3, share, share, 1)),
            ((4, 0, share, 0), (4, share, share, 1)),
        ),
        capacity,
    )
    grads_core = swap(grads_sent, "dp", 1)
    grads_core = swap(grads_sent, "dp", 1)
    to_other = (second + from_pair[1].astype(jnp.float32)).astype(jnp.bfloat16)
    from_other = swap(to_other, "section", 2)
    mixed_sum = gate(first, grads_sent) + from_pair[0].astype(jnp.float32)
    mixed_slice = (mixed_sum + from_other.astype(jnp.float32)).astype(jnp.bfloat16)
    key_other = swap(gate(key_own, first), "expert", 1)
    mixed_near = swap(mixed_slice, "section", 1)
    slope = expert_slope(
        gate(here.astype(jnp.int32).reshape(1), mixed_near),
        near_codes + core_codes,
        grads_own,
        grads_core,
        rise_own,
        rise_core,
        weight_out,
    )
    back_pair, back_first, back_second = expert_backward(
        which_section, slope, weight_in, sections
    )
    mixed_far = swap(jnp.stack([mixed_slice, gate(mixed_near, key_other)]), "section", 2)
    slices = [mixed_slice, mixed_near, mixed_far[0], mixed_far[1]]

    value_other = swap(gate(value_own, mixed_slice), "expert", 1)

    query_here = jnp.dot(normed_own, query_own, preferred_element_type=jnp.float32)
    query = (query_here + query_back.astype(jnp.float32)).astype(jnp.bfloat16)

    memory = make_memory(which_section, tokens, slices, final_gain)
    out_other = swap(gate(out_own, memory), "expert", 1)
    memory_x = swap(memory, "dp", 2)
    memory_core = swap(memory, "dp", 1)

    def sentence(which, near, far, *after):
        place = gate(jnp.stack([y, core, which]).astype(jnp.int32), *after)
        rows_of = lax.dynamic_slice_in_dim(query, which * TGT_LEN, TGT_LEN, 0)
        parts = (key_own, key_other), (value_own, value_other)
        return attend_sentence(place, src_lengths, rows_of, near, far, *parts)

    back_from_pair = swap(back_pair, "section", 1)
    back_to_other = (back_second + back_from_pair[1].astype(jnp.float32)).astype(jnp.bfloat16)
    back_from_other = swap(back_to_other, "section", 2)
    backward_sum = back_first + back_from_pair[0].astype(jnp.float32)
    backward_sum = backward_sum + back_from_other.astype(jnp.float32)
    context_own = sentence(x, memory, memory_core)
    memory_far = swap(gate(memory_x, context_own), "dp", 1)
    context_other = sentence(1 - x, memory_x, memory_far)
    place = jnp.stack([y, core, x]).astype(jnp.int32)
    sent_mine, sent_other, kept_mine, kept_other = project(
        place, context_own, context_other, out_own, out_other
    )

    core_other = swap(sent_other, "dp", 1)
    core_mine = swap(sent_mine, "dp", 1)
    last = gate(kept_other, back_from_other) + core_other.astype(jnp.float32)
    from_x = swap(last.astype(jnp.bfloat16), "dp", 2)
    attended = kept_mine + core_mine.astype(jnp.float32) + from_x.astype(jnp.float32)
    dec_out = add_residual(attended, states, tgt_lengths)

    grads_home = exchange(gate(backward_sum.astype(jnp.bfloat16), last), group_size, capacity)
    natural = expert_ids * capacity + rank
    (token_grad,) = combine(
        which_section, natural, gate_weights, [grads_home], 1
    )
    return (dec_out[None], token_grad)


def add_residual(attended, states, tgt_lengths):
    my_columns = attended.shape[1]
    residual = lax.dynamic_slice_in_dim(
        states, lax.axis_index("dp") * my_columns, my_columns, 1
    ).astype(jnp.float32)
    row_mask = (jnp.arange(TGT_LEN, dtype=jnp.int32)[None, :] < tgt_lengths[:, None]).reshape(-1, 1)
    return (residual + jnp.where(row_mask, attended, 0.0)).astype(jnp.bfloat16)


def body(
    tokens,
    expert_ids,
    gate_weights,
    out_grad,
    inner_weight,
    outer_weight,
    final_gain,
    dec_states,
    src_lengths,
    tgt_lengths,
    norm_gain,
    query_weight,
    key_weight,
    value_weight,
    out_weight,
):
    token_count, feature_count = tokens.shape
    group_size = lax.axis_size(("expert", "dp"))
    capacity = 3 * token_count // group_size
    slots = group_size * capacity

    named = expert_ids[:, :, None] == jnp.arange(group_size, dtype=jnp.int32)[None, None, :]
    either = (named[:, 0] | named[:, 1]).astype(jnp.bfloat16)
    row = lax.broadcasted_iota(jnp.int32, (token_count, token_count), 0)
    column = lax.broadcasted_iota(jnp.int32, (token_count, token_count), 1)
    earlier = jnp.dot(
        (column < row).astype(jnp.bfloat16), either, preferred_element_type=jnp.float32
    ).astype(jnp.int32)
    rank = jnp.sum(jnp.where(named, earlier[:, None, :], 0), axis=2)
    position = expert_ids * capacity + rank
    pick_first = slot_matrix(position[:, 0], slots)
    pick_second = slot_matrix(position[:, 1], slots)
    fill = (pick_first + pick_second).T

    def place(values):
        return jnp.dot(fill, values, preferred_element_type=jnp.float32).astype(jnp.bfloat16)

    def combine(arrived):
        first = jnp.dot(pick_first, arrived, preferred_element_type=jnp.float32)
        second = jnp.dot(pick_second, arrived, preferred_element_type=jnp.float32)
        return gate_weights[:, :1] * first + gate_weights[:, 1:] * second

    weight_in = inner_weight[0]
    weight_out = outer_weight[0]
    arrived_rows = exchange(place(tokens), group_size, capacity)
    pre_act = jnp.dot(arrived_rows, weight_in, preferred_element_type=jnp.float32)
    hidden = jax.nn.gelu(pre_act).astype(jnp.bfloat16)
    forward_part = jnp.dot(hidden, weight_out, preferred_element_type=jnp.float32)
    arrived_grads = exchange(place(out_grad), group_size, capacity)
    outputs_home = exchange(forward_part.astype(jnp.bfloat16), group_size, capacity)
    mixed_slice = sum_sections(combine(outputs_home)).astype(jnp.bfloat16)
    mixed = gather_sections(mixed_slice).astype(jnp.float32)
    memory = normalize(tokens.astype(jnp.float32) + mixed, final_gain).astype(jnp.bfloat16)

    back = contract_last(arrived_grads, weight_out)
    slope = jax.vjp(jax.nn.gelu, pre_act)[1](back)[0].astype(jnp.bfloat16)
    backward_part = contract_last(slope, weight_in)
    backward_slice = sum_sections(backward_part).astype(jnp.bfloat16)
    grads_home = exchange(backward_slice, group_size, capacity)
    token_grad = combine(grads_home).astype(jnp.bfloat16)

    states = dec_states[0]
    normed = normalize(states.astype(jnp.float32), norm_gain[0]).astype(jnp.bfloat16)
    full_query = gather_weight(query_weight[0], 0)
    full_key = gather_weight(key_weight[0], 0)
    full_value = gather_weight(value_weight[0], 0)
    full_out = gather_weight(out_weight[0], 1)
    query_sum = jnp.dot(normed, full_query, preferred_element_type=jnp.float32)
    source = gather_rows(memory, "dp")
    key_sum = jnp.dot(source, full_key, preferred_element_type=jnp.float32)
    value_sum = jnp.dot(source, full_value, preferred_element_type=jnp.float32)
    key_mask = jnp.arange(SRC_LEN, dtype=jnp.int32)[None, :] < src_lengths[:, None]
    context = attend(
        query_sum.astype(jnp.bfloat16),
        key_sum.astype(jnp.bfloat16),
        value_sum.astype(jnp.bfloat16),
        key_mask,
    )
    attended = sum_heads(jnp.dot(context, full_out, preferred_element_type=jnp.float32))
    dec_out = add_residual(attended, states, tgt_lengths)
    return (dec_out[None], token_grad)


def solution(mesh):
    in_specs = (
        P(("expert", "dp"), None),
        P(("expert", "dp"), None),
        P(("expert", "dp"), None),
        P(("expert", "dp"), None),
        P(("expert", "dp"), None, "section"),
        P(("expert", "dp"), "section", None),
        P(),
        P("section", "expert", None),
        P("expert"),
        P("expert"),
        P("section", None),
        P("section", "expert", "dp"),
        P("section", "expert", "dp"),
        P("section", "expert", "dp"),
        P("section", "dp", "expert"),
    )
    out_specs = (P("section", "expert", "dp"), P(("expert", "dp"), "section"))
    small = (mesh.shape["section"], mesh.shape["expert"], mesh.shape["dp"]) == (4, 2, 4)
    chosen = small_body if small else body
    return jax.shard_map(chosen, mesh=mesh, in_specs=in_specs, out_specs=out_specs, check_vma=False)
```

```python
import functools

import jax
import jax.numpy as jnp
from jax import lax
from jax.experimental import pallas as pl
from jax.experimental.pallas import tpu as pltpu
from jax.sharding import PartitionSpec as P

HEAD_DIM = 128
SRC_LEN = 256
TGT_LEN = 128


EPSILON = 1e-05


def normalize(values, gain):
    centre = jnp.mean(values, axis=-1, keepdims=True)
    centred = values - centre
    spread = jnp.mean(centred * centred, axis=-1, keepdims=True)
    return centred * lax.rsqrt(spread + EPSILON) * gain


def contract_last(left, right):
    return lax.dot_general(
        left, right, (((1,), (1,)), ((), ())), preferred_element_type=jnp.float32
    )


def shift(value, axis, step):
    size = lax.axis_size(axis)
    return lax.ppermute(value, axis, [(i, (i + step) % size) for i in range(size)])


def swap(value, axis, mask):
    size = lax.axis_size(axis)
    return lax.ppermute(value, axis, [(i, i ^ mask) for i in range(size)])


def sum_sections(partial):
    count = lax.axis_size("section")
    me = lax.axis_index("section")
    width = partial.shape[1] // count

    def piece(owner):
        return lax.dynamic_slice_in_dim(partial, owner * width, width, 1)

    total = piece(me).astype(jnp.float32)
    for step in range(1, count):
        sent = piece(lax.rem(me + step, count)).astype(jnp.bfloat16)
        total = total + shift(sent, "section", step).astype(jnp.float32)
    return total


def gather_sections(mine):
    count = lax.axis_size("section")
    me = lax.axis_index("section")
    width = mine.shape[1]
    whole = jnp.zeros((mine.shape[0], width * count), mine.dtype)
    whole = lax.dynamic_update_slice_in_dim(whole, mine, me * width, 1)
    for step in range(1, count):
        owner = lax.rem(me - step + count, count)
        whole = lax.dynamic_update_slice_in_dim(
            whole, shift(mine, "section", step), owner * width, 1
        )
    return whole


def gather_rows(mine, axis):
    held = mine
    me = lax.axis_index(axis)
    mask = lax.axis_size(axis) // 2
    blocks = [mine]
    while mask >= 1:
        blocks = blocks + [swap(block, axis, mask) for block in blocks]
        mask //= 2
    codes = [0]
    mask = lax.axis_size(axis) // 2
    while mask >= 1:
        codes = codes + [code ^ mask for code in codes]
        mask //= 2
    ordered = []
    for place in range(len(blocks)):
        chosen = blocks[0]
        for code, block in zip(codes[1:], blocks[1:]):
            chosen = jnp.where((me ^ code) == place, block, chosen)
        ordered.append(chosen)
    return jnp.concatenate(ordered, axis=0)


def gather_weight(weight, dimension):
    if lax.axis_size("expert") != 2:
        return lax.all_gather(weight, "expert", axis=dimension, tiled=True)
    other = swap(weight, "expert", 1)
    first = lax.axis_index("expert") == 0
    return jnp.concatenate(
        [jnp.where(first, weight, other), jnp.where(first, other, weight)], axis=dimension
    )


def sum_heads(partial):
    me = lax.axis_index("dp")
    count = lax.axis_size("dp")
    rows, columns = partial.shape
    total = partial.reshape(rows, count, columns // count)
    mask = 1
    while mask < count:
        paired = total.reshape(rows, -1, 2, columns // count)
        bit = (me // mask) % 2
        sent = lax.dynamic_index_in_dim(paired, 1 - bit, 2, False).astype(jnp.bfloat16)
        kept = lax.dynamic_index_in_dim(paired, bit, 2, False)
        total = kept + swap(sent, "dp", mask).astype(jnp.float32)
        mask *= 2
    return total.reshape(rows, columns // count)


def slot_matrix(positions, slots):
    places = lax.broadcasted_iota(jnp.int32, (positions.shape[0], slots), 1)
    return (positions[:, None] == places).astype(jnp.bfloat16)


def attend(query, keys, values, key_mask):
    sequences = key_mask.shape[0]
    head_count = query.shape[1] // HEAD_DIM
    query_split = query.reshape(sequences, -1, head_count, HEAD_DIM)
    keys_split = keys.reshape(sequences, -1, head_count, HEAD_DIM)
    values_split = values.reshape(sequences, -1, head_count, HEAD_DIM)
    scores = jnp.einsum(
        "bqhd,bkhd->bhqk", query_split, keys_split, preferred_element_type=jnp.float32
    ) * HEAD_DIM ** (-0.5)
    scores = jnp.where(key_mask[:, None, None, :], scores, -1e30)
    highest = jnp.max(scores, axis=-1, keepdims=True)
    weights = jnp.exp(scores - highest)
    probs = (weights / jnp.sum(weights, axis=-1, keepdims=True)).astype(jnp.bfloat16)
    context = jnp.einsum("bhqk,bkhd->bqhd", probs, values_split, preferred_element_type=jnp.float32)
    return context.astype(jnp.bfloat16).reshape(-1, head_count * HEAD_DIM)


def exchange(values, group_size, capacity):
    sent = values.reshape(group_size, capacity, values.shape[1])
    arrived = lax.all_to_all(sent, ("expert", "dp"), split_axis=0, concat_axis=0, tiled=True)
    return arrived.reshape(values.shape)


SHORT = pl.CostEstimate(flops=1, bytes_accessed=1, transcendentals=0)


def gate(value, *after):
    return lax.optimization_barrier((value,) + after)[0]


def vmem(shape, dtype):
    return pltpu.VMEM(shape, dtype)


def dispatch_kernel(capacity, layout, section_ref, code_ref, *refs):
    blocks = refs[:-4]
    outs, held, sems = refs[-4:-2], refs[-2], refs[-1]
    count, rows = held.shape[0], held.shape[1]
    half = lax.rem(section_ref[0], 2)
    copies = []
    for place, pieces in enumerate(layout):
        group = []
        for i, (which, start, length, side) in enumerate(pieces):
            there = held.at[place]
            if side is not None:
                offset = (half if side == 0 else 1 - half) * length
                there = held.at[place, pl.ds(pl.multiple_of(offset, length), length)]
            here = blocks[which].at[pl.ds(start, length)]
            group.append(pltpu.make_async_copy(here, there, sems.at[place, i]))
        copies.append(group)
    for group in copies:
        for copy in group:
            copy.start()
    for place, group in enumerate(copies):
        picks = []
        for which in range(2):
            line = which * count + place
            code = code_ref[line : line + 1, :]
            slot = lax.broadcasted_iota(jnp.int32, (capacity, code.shape[1]), 0)
            picks.append(jnp.where(slot == code, 1.0, 0.0))
        pick = jnp.concatenate(picks, axis=0).astype(jnp.bfloat16)
        for copy in group:
            copy.wait()
        picked = jnp.dot(pick, held[place], preferred_element_type=jnp.float32)
        picked = picked.astype(jnp.bfloat16)
        for which, out_ref in enumerate(outs):
            out_ref[place * capacity : (place + 1) * capacity, :] = picked[
                which * capacity : (which + 1) * capacity
            ]


def dispatch(section, code, blocks, layout, capacity):
    rows, features = blocks[0].shape
    count = len(layout)
    picked = jax.ShapeDtypeStruct((count * capacity, features), jnp.bfloat16)
    return pl.pallas_call(
        functools.partial(dispatch_kernel, capacity, layout),
        out_shape=(picked, picked),
        in_specs=[
            pl.BlockSpec(memory_space=pltpu.SMEM),
            pl.BlockSpec(memory_space=pltpu.VMEM),
        ]
        + [pl.BlockSpec(memory_space=pltpu.HBM)] * len(blocks),
        out_specs=[pl.BlockSpec(memory_space=pltpu.VMEM)] * 2,
        scratch_shapes=[
            vmem((count, rows, features), jnp.bfloat16),
            pltpu.SemaphoreType.DMA((count, 2)),
        ],
        compiler_params=pltpu.CompilerParams(vmem_limit_bytes=10 * 1024 * 1024),
        cost_estimate=SHORT,
        name="dispatch",
    )(section, code, *blocks)


def send_home(part, codes, capacity):
    size = lax.axis_size(("expert", "dp"))
    arrived = []
    for place, code in enumerate(codes):
        block = part[place * capacity : (place + 1) * capacity]
        if code:
            block = lax.ppermute(block, ("expert", "dp"), [(i, i ^ code) for i in range(size)])
        arrived.append(block)
    return arrived


def combine_kernel(count, split, section_ref, position_ref, gates_ref, *refs):
    blocks = refs[:count]
    outs, (held, total) = refs[count:-2], refs[-2:]
    capacity, features = blocks[0].shape
    position = position_ref[...]
    slot = lax.broadcasted_iota(jnp.int32, (position.shape[0], count * capacity), 1)
    picks = [
        jnp.where(position[:, k : k + 1] == slot, 1.0, 0.0).astype(jnp.bfloat16) for k in range(2)
    ]
    for i, block in enumerate(blocks):
        held[i * capacity : (i + 1) * capacity, :] = block[...]
    pick = jnp.concatenate(picks, axis=0)
    rows = position.shape[0]
    both = jnp.dot(pick, held[...], preferred_element_type=jnp.float32)
    total[...] = gates_ref[:, 0:1] * both[:rows] + gates_ref[:, 1:2] * both[rows:]
    if split == 1:
        outs[0][...] = total[...].astype(outs[0].dtype)
        return
    sent_ref, kept_first, kept_second = outs
    width = features // split
    for step, out_ref in enumerate((kept_first, sent_ref.at[0], kept_second, sent_ref.at[1])):
        start = pl.multiple_of((section_ref[0] ^ step) * width, width)
        out_ref[...] = total[:, pl.ds(start, width)].astype(out_ref.dtype)


def combine(section, position, gates, blocks, split):
    capacity, features = blocks[0].shape
    rows = position.shape[0]
    count = len(blocks)
    width = features // split
    kept = jax.ShapeDtypeStruct((rows, width), jnp.float32)
    if split == 1:
        out_shape = (jax.ShapeDtypeStruct((rows, width), jnp.bfloat16),)
    else:
        out_shape = (jax.ShapeDtypeStruct((2, rows, width), jnp.bfloat16), kept, kept)
    full = pl.BlockSpec(memory_space=pltpu.VMEM)
    return pl.pallas_call(
        functools.partial(combine_kernel, count, split),
        out_shape=out_shape,
        in_specs=[pl.BlockSpec(memory_space=pltpu.SMEM)] + [full] * (2 + count),
        out_specs=[full] * len(out_shape),
        scratch_shapes=[
            vmem((count * capacity, features), jnp.bfloat16),
            vmem((rows, features), jnp.float32),
        ],
        compiler_params=pltpu.CompilerParams(vmem_limit_bytes=14 * 1024 * 1024),
        cost_estimate=SHORT,
        name="combine",
    )(section, position, gates, *blocks)


def memory_kernel(count, section_ref, tokens_ref, gain_ref, *refs):
    slices, out_ref, mixed = refs[:count], refs[count], refs[count + 1]
    me = section_ref[0]
    width = slices[0].shape[1]
    for step, piece in enumerate(slices):
        owner = me ^ step
        mixed[:, pl.ds(pl.multiple_of(owner * width, width), width)] = piece[...].astype(
            jnp.float32
        )
    values = tokens_ref[...].astype(jnp.float32) + mixed[...]
    out_ref[...] = normalize(values, gain_ref[...]).astype(jnp.bfloat16)


def make_memory(me, tokens, slices, gain):
    return pl.pallas_call(
        functools.partial(memory_kernel, len(slices)),
        out_shape=jax.ShapeDtypeStruct(tokens.shape, jnp.bfloat16),
        in_specs=[
            pl.BlockSpec(memory_space=pltpu.SMEM),
        ]
        + [pl.BlockSpec(memory_space=pltpu.VMEM)] * (2 + len(slices)),
        out_specs=pl.BlockSpec(memory_space=pltpu.VMEM),
        scratch_shapes=[vmem(tokens.shape, jnp.float32)],
        compiler_params=pltpu.CompilerParams(vmem_limit_bytes=8 * 1024 * 1024),
        cost_estimate=SHORT,
        name="memory",
    )(me, tokens, gain[None], *slices)


def normed_kernel(y_ref, states_ref, gain_ref, own_ref, other_ref):
    values = normalize(states_ref[...].astype(jnp.float32), gain_ref[...]).astype(jnp.bfloat16)
    width = own_ref.shape[1]
    for out_ref, first in ((own_ref, y_ref[0] == 0), (other_ref, y_ref[0] == 1)):
        out_ref[...] = jnp.where(first, values[:, :width], values[:, width:])


def normed_halves(y, states, gain):
    rows, features = states.shape
    full = pl.BlockSpec(memory_space=pltpu.VMEM)
    return pl.pallas_call(
        normed_kernel,
        out_shape=(jax.ShapeDtypeStruct((rows, features // 2), jnp.bfloat16),) * 2,
        in_specs=[pl.BlockSpec(memory_space=pltpu.SMEM), full, full],
        out_specs=[full] * 2,
        compiler_params=pltpu.CompilerParams(vmem_limit_bytes=12 * 1024 * 1024),
        cost_estimate=SHORT,
        name="normed",
    )(y.astype(jnp.int32).reshape(1), states, gain)


def attend_kernel(place_ref, lengths_ref, query_ref, *refs):
    near_ref, far_ref, key_own, key_other, value_own, value_other, out_ref = refs[:7]
    source, key_weight, value_weight, keys, values, sems = refs[7:]
    y, core, sentence = place_ref[0], place_ref[1], place_ref[2]
    rows = near_ref.shape[0]
    depth = key_own.shape[0]
    moves = [
        (near_ref, source.at[pl.ds(0, rows)]),
        (far_ref, source.at[pl.ds(rows, rows)]),
        (key_own, key_weight.at[y]),
        (key_other, key_weight.at[1 - y]),
        (value_own, value_weight.at[y]),
        (value_other, value_weight.at[1 - y]),
    ]
    copies = [
        pltpu.make_async_copy(here, there, sems.at[i]) for i, (here, there) in enumerate(moves)
    ]
    for copy in copies:
        copy.start()

    def linear(weight, result):
        total = jnp.dot(source[:, :depth], weight[0], preferred_element_type=jnp.float32)
        total += jnp.dot(source[:, depth:], weight[1], preferred_element_type=jnp.float32)
        result[...] = total.astype(jnp.bfloat16)

    for copy in copies[:4]:
        copy.wait()
    linear(key_weight, keys)
    for copy in copies[4:]:
        copy.wait()
    linear(value_weight, values)

    column = lax.broadcasted_iota(jnp.int32, (query_ref.shape[0], 2 * rows), 1)
    position = jnp.where(column < rows, column + core * rows, column - core * rows)
    valid = position < lengths_ref[sentence]
    for head in range(query_ref.shape[1] // HEAD_DIM):
        span = slice(head * HEAD_DIM, (head + 1) * HEAD_DIM)
        scores = contract_last(query_ref[:, span], keys[:, span]) * HEAD_DIM ** (-0.5)
        scores = jnp.where(valid, scores, -1e30)
        weights = jnp.exp(scores - jnp.max(scores, axis=-1, keepdims=True))
        probs = (weights / jnp.sum(weights, axis=-1, keepdims=True)).astype(jnp.bfloat16)
        result = jnp.dot(probs, values[:, span], preferred_element_type=jnp.float32)
        out_ref[:, span] = result.astype(jnp.bfloat16)


def attend_sentence(place, lengths, query, near, far, key_parts, value_pair):
    rows, features = near.shape
    depth, width = key_parts[0].shape
    hold = pl.BlockSpec(memory_space=pltpu.HBM)
    smem = pl.BlockSpec(memory_space=pltpu.SMEM)
    full = pl.BlockSpec(memory_space=pltpu.VMEM)
    return pl.pallas_call(
        attend_kernel,
        out_shape=jax.ShapeDtypeStruct(query.shape, jnp.bfloat16),
        in_specs=[smem, smem, full] + [hold] * 6,
        out_specs=full,
        scratch_shapes=[
            vmem((2 * rows, features), jnp.bfloat16),
            vmem((2, depth, width), jnp.bfloat16),
            vmem((2, depth, width), jnp.bfloat16),
            vmem((2 * rows, width), jnp.bfloat16),
            vmem((2 * rows, width), jnp.bfloat16),
            pltpu.SemaphoreType.DMA((6,)),
        ],
        compiler_params=pltpu.CompilerParams(vmem_limit_bytes=56 * 1024 * 1024),
        cost_estimate=SHORT,
        name="attend_sentence",
    )(place, lengths, query, near, far, *key_parts, *value_pair)


def project_kernel(place_ref, mine_ref, done_ref, own_ref, other_ref, *refs):
    sent_mine, sent_other, kept_mine, kept_other, context = refs
    y, core, x = place_ref[0], place_ref[1], place_ref[2]
    targets = mine_ref.shape[0]
    for part, sentence in ((mine_ref, x), (done_ref, 1 - x)):
        context[pl.ds(pl.multiple_of(sentence * targets, targets), targets), :] = part[...]
    columns = kept_mine.shape[1]
    outs = ((sent_mine, kept_mine), (sent_other, kept_other))

    def write(weight_ref, chosen):
        for side, out_ref in zip((1 - core, core), chosen):
            span = pl.ds(pl.multiple_of(side * columns, columns), columns)
            part = jnp.dot(context[...], weight_ref[:, span], preferred_element_type=jnp.float32)
            out_ref[...] = part.astype(out_ref.dtype)

    @pl.when(x == y)
    def _():
        write(own_ref, outs[0])
        write(other_ref, outs[1])

    @pl.when(x != y)
    def _():
        write(other_ref, outs[0])
        write(own_ref, outs[1])


def project(place, mine, done, out_own, out_other):
    targets, width = 2 * mine.shape[0], mine.shape[1]
    columns = out_own.shape[1] // 2
    full = pl.BlockSpec(memory_space=pltpu.VMEM)
    sent = jax.ShapeDtypeStruct((targets, columns), jnp.bfloat16)
    kept = jax.ShapeDtypeStruct((targets, columns), jnp.float32)
    return pl.pallas_call(
        project_kernel,
        out_shape=(sent, sent, kept, kept),
        in_specs=[pl.BlockSpec(memory_space=pltpu.SMEM)] + [full] * 4,
        out_specs=[full] * 4,
        scratch_shapes=[vmem((targets, width), jnp.bfloat16)],
        compiler_params=pltpu.CompilerParams(vmem_limit_bytes=16 * 1024 * 1024),
        cost_estimate=SHORT,
        name="project",
    )(place, mine, done, out_own, out_other)


def slope_kernel(codes, here_ref, own_ref, core_ref, rise_own, rise_core, out_ref, slope, *refs):
    grads, rise, weight_out, sems = refs
    rows = own_ref.shape[0]
    hidden = weight_out.shape[0]
    chunk = hidden // 4
    moves = []
    block = 2 * rows // len(codes)
    for order, code in enumerate(codes):
        source = here_ref[0] ^ code
        there = pl.ds(pl.multiple_of(source * block, 16), block)
        here = pl.ds(order * block % rows, block)
        own = order * block < rows
        moves.append(((own_ref if own else core_ref).at[here], grads.at[there]))
        moves.append(((rise_own if own else rise_core).at[here], rise.at[there]))
    for part in range(4):
        span = pl.ds(part * chunk, chunk)
        moves.append((out_ref.at[span], weight_out.at[span]))
    copies = [
        pltpu.make_async_copy(here, there, sems.at[i]) for i, (here, there) in enumerate(moves)
    ]
    for copy in copies:
        copy.start()
    for copy in copies[:-4]:
        copy.wait()
    for part in range(4):
        copies[part - 4].wait()
        span = slice(part * chunk, (part + 1) * chunk)
        back = contract_last(grads[...], weight_out[span, :])
        slope[:, span] = (back * rise[:, span]).astype(jnp.bfloat16)


def expert_slope(here, codes, grads_own, grads_core, rise_own, rise_core, weight_out):
    rows = 2 * grads_own.shape[0]
    hidden, features = weight_out.shape
    hold = pl.BlockSpec(memory_space=pltpu.HBM)
    return pl.pallas_call(
        functools.partial(slope_kernel, codes),
        out_shape=jax.ShapeDtypeStruct((rows, hidden), jnp.bfloat16),
        in_specs=[pl.BlockSpec(memory_space=pltpu.SMEM)] + [hold] * 5,
        out_specs=pl.BlockSpec(memory_space=pltpu.VMEM),
        scratch_shapes=[
            vmem((rows, features), jnp.bfloat16),
            vmem((rows, hidden), jnp.float32),
            vmem((hidden, features), jnp.bfloat16),
            pltpu.SemaphoreType.DMA((4 + 2 * len(codes),)),
        ],
        compiler_params=pltpu.CompilerParams(vmem_limit_bytes=56 * 1024 * 1024),
        cost_estimate=SHORT,
        name="expert_slope",
    )(here, grads_own, grads_core, rise_own, rise_core, weight_out)


def backward_kernel(split, section_ref, slope_ref, in_ref, sent_ref, kept_first, kept_second, *refs):
    weight_in, sems = refs
    width = weight_in.shape[0] // split
    outs = (sent_ref.at[0], sent_ref.at[1], kept_first, kept_second)
    spans, copies = [], []
    for i, step in enumerate((1, 3, 0, 2)):
        start = pl.multiple_of((section_ref[0] ^ step) * width, width)
        spans.append(pl.ds(start, width))
        copies.append(
            pltpu.make_async_copy(in_ref.at[spans[i]], weight_in.at[spans[i]], sems.at[i])
        )
    for copy in copies:
        copy.start()
    for copy, span, out_ref in zip(copies, spans, outs):
        copy.wait()
        part = contract_last(slope_ref[...], weight_in[span, :])
        out_ref[...] = part.astype(out_ref.dtype)


def expert_backward(section, slope, weight_in, split):
    rows, hidden = slope.shape
    features = weight_in.shape[0]
    width = features // split
    full = pl.BlockSpec(memory_space=pltpu.VMEM)
    kept = jax.ShapeDtypeStruct((rows, width), jnp.float32)
    return pl.pallas_call(
        functools.partial(backward_kernel, split),
        out_shape=(jax.ShapeDtypeStruct((2, rows, width), jnp.bfloat16), kept, kept),
        in_specs=[pl.BlockSpec(memory_space=pltpu.SMEM), full, pl.BlockSpec(memory_space=pltpu.HBM)],
        out_specs=[full] * 3,
        scratch_shapes=[
            vmem((features, hidden), jnp.bfloat16),
            pltpu.SemaphoreType.DMA((split,)),
        ],
        compiler_params=pltpu.CompilerParams(vmem_limit_bytes=56 * 1024 * 1024),
        cost_estimate=SHORT,
        name="expert_backward",
    )(section, slope, weight_in)


def small_body(
    tokens,
    expert_ids,
    gate_weights,
    out_grad,
    inner_weight,
    outer_weight,
    final_gain,
    dec_states,
    src_lengths,
    tgt_lengths,
    norm_gain,
    query_weight,
    key_weight,
    value_weight,
    out_weight,
):
    token_count, feature_count = tokens.shape
    group_size = lax.axis_size(("expert", "dp"))
    capacity = 3 * token_count // group_size
    here = lax.axis_index(("expert", "dp"))
    y = lax.axis_index("expert")
    d = lax.axis_index("dp")
    section = lax.axis_index("section")
    sections = lax.axis_size("section")
    half = feature_count // 2
    weight_in = inner_weight[0]
    weight_out = outer_weight[0]
    key_own, value_own, out_own = key_weight[0], value_weight[0], out_weight[0]
    query_own = query_weight[0]

    size = group_size
    near_codes = (0, 2, 4, 6)
    core_codes = (1, 3, 5, 7)
    core, x = d % 2, d // 2
    which_section = section.astype(jnp.int32).reshape(1)

    token_y = swap(tokens, "expert", 1)
    token_x = swap(tokens, "dp", 2)
    row = lax.broadcasted_iota(jnp.int32, (token_count, token_count), 0)
    column = lax.broadcasted_iota(jnp.int32, (token_count, token_count), 1)
    named = expert_ids[:, :, None] == jnp.arange(size, dtype=jnp.int32)[None, None, :]
    either = (named[:, 0] | named[:, 1]).astype(jnp.bfloat16)
    earlier = jnp.dot(
        (column < row).astype(jnp.bfloat16), either, preferred_element_type=jnp.float32
    ).astype(jnp.int32)
    rank = jnp.sum(jnp.where(named, earlier[:, None, :], 0), axis=2)
    codes_of = expert_ids ^ here
    position = ((codes_of >> 1) + 4 * (codes_of & 1)) * capacity + rank

    states = dec_states[0]
    normed_own, asked = normed_halves(y, states, norm_gain)
    ids_own = gate(expert_ids, asked).T
    ids_x, ids_y = swap(ids_own, "dp", 2), swap(ids_own, "expert", 1)
    ids_far = swap(ids_x, "expert", 1)
    token_far = swap(gate(token_y, ids_x, ids_y, asked), "dp", 2)

    side = lax.rem(section, 2)
    share = token_count // 2
    grad_half = lax.dynamic_slice_in_dim(out_grad, side * share, share, 0)
    asked_here = swap(gate(asked, token_y), "expert", 1)
    half_y = swap(gate(grad_half, asked_here), "expert", 1)
    other_y = swap(half_y, "section", 1)
    query_there = jnp.dot(asked_here, query_own, preferred_element_type=jnp.float32)
    query_back = swap(query_there.astype(jnp.bfloat16), "expert", 1)

    ids = jnp.stack([ids_own, ids_x, ids_y, ids_far])
    named_there = jnp.concatenate([(ids == here).any(axis=1), (ids == (here ^ 1)).any(axis=1)])
    before = jnp.dot(
        named_there.astype(jnp.bfloat16),
        (row < column).astype(jnp.bfloat16),
        preferred_element_type=jnp.float32,
    ).astype(jnp.int32)
    code = jnp.where(named_there, before, -1)

    def forward(rows, *after):
        pre_act = jnp.dot(rows, weight_in, preferred_element_type=jnp.float32)
        hidden = jax.nn.gelu(gate(pre_act, *after)).astype(jnp.bfloat16)
        part = jnp.dot(hidden, weight_out, preferred_element_type=jnp.float32)
        return pre_act, part.astype(jnp.bfloat16)

    def slope_of(pre_act):
        return jax.vjp(jax.nn.gelu, pre_act)[1](jnp.ones_like(pre_act))[0]

    rows_own, rows_sent = dispatch(
        which_section,
        gate(code, asked),
        [tokens, token_x, token_y, token_far],
        tuple(((place, 0, token_count, None),) for place in range(4)),
        capacity,
    )
    rows_core = swap(rows_sent, "dp", 1)
    pre_own, part_own = forward(rows_own)
    pre_core, part_core = forward(gate(rows_core, part_own))
    part_core = gate(part_core, query_back)
    home = send_home(part_own, near_codes, capacity) + send_home(part_core, core_codes, capacity)
    grad_y = jnp.concatenate([gate(half_y, home[4]), other_y], axis=0)

    rise_own, rise_core = slope_of(gate(pre_own, home[1])), slope_of(gate(pre_core, home[1]))
    held_gates = gate(gate_weights, rise_own, rise_core, grad_y)
    sent_pair, first, second = combine(which_section, position, held_gates, home, sections)
    from_pair = swap(sent_pair, "section", 1)
    grad_x = swap(gate(out_grad, home[5]), "dp", 2)
    grad_far = swap(gate(grad_y, first), "dp", 2)
    to_other = (second + from_pair[1].astype(jnp.float32)).astype(jnp.bfloat16)
    from_other = swap(to_other, "section", 2)
    mixed_sum = first + from_pair[0].astype(jnp.float32)
    mixed_slice = (mixed_sum + from_other.astype(jnp.float32)).astype(jnp.bfloat16)
    key_other = swap(gate(key_own, first), "expert", 1)
    mixed_near = swap(mixed_slice, "section", 1)
    grads_own, grads_sent = dispatch(
        which_section,
        gate(code, mixed_near),
        [out_grad, grad_x, grad_y, grad_far],
        (
            ((0, 0, token_count, None),),
            ((1, 0, token_count, None),),
            ((2, 0, share, 0), (2, share, share, 1)),
            ((3, 0, share, 0), (3, share, share, 1)),
        ),
        capacity,
    )
    grads_core = swap(grads_sent, "dp", 1)
    grads_core = swap(grads_sent, "dp", 1)
    slope = expert_slope(
        here.astype(jnp.int32).reshape(1),
        near_codes + core_codes,
        grads_own,
        grads_core,
        rise_own,
        rise_core,
        weight_out,
    )
    mixed_far = swap(jnp.stack([mixed_slice, gate(mixed_near, key_other)]), "section", 2)
    back_pair, back_first, back_second = expert_backward(
        which_section, slope, weight_in, sections
    )
    slices = [mixed_slice, mixed_near, mixed_far[0], mixed_far[1]]

    value_other = swap(gate(value_own, mixed_near), "expert", 1)

    query_here = jnp.dot(normed_own, query_own, preferred_element_type=jnp.float32)
    query = (query_here + query_back.astype(jnp.float32)).astype(jnp.bfloat16)

    memory = make_memory(which_section, tokens, slices, final_gain)
    out_other = swap(gate(out_own, memory), "expert", 1)
    memory_x = swap(memory, "dp", 2)
    memory_core = swap(memory, "dp", 1)

    def sentence(which, near, far, *after):
        place = gate(jnp.stack([y, core, which]).astype(jnp.int32), *after)
        rows_of = lax.dynamic_slice_in_dim(query, which * TGT_LEN, TGT_LEN, 0)
        parts = (key_own, key_other), (value_own, value_other)
        return attend_sentence(place, src_lengths, rows_of, near, far, *parts)

    back_from_pair = swap(back_pair, "section", 1)
    back_to_other = (back_second + back_from_pair[1].astype(jnp.float32)).astype(jnp.bfloat16)
    back_from_other = swap(back_to_other, "section", 2)
    backward_sum = back_first + back_from_pair[0].astype(jnp.float32)
    backward_sum = backward_sum + back_from_other.astype(jnp.float32)
    context_own = sentence(x, memory, memory_core)
    memory_far = swap(gate(memory_x, context_own), "dp", 1)
    context_other = sentence(1 - x, memory_x, memory_far)
    place = jnp.stack([y, core, x]).astype(jnp.int32)
    sent_mine, sent_other, kept_mine, kept_other = project(
        place, context_own, context_other, out_own, out_other
    )

    core_other = swap(sent_other, "dp", 1)
    core_mine = swap(sent_mine, "dp", 1)
    last = gate(kept_other, back_from_other) + core_other.astype(jnp.float32)
    from_x = swap(last.astype(jnp.bfloat16), "dp", 2)
    attended = kept_mine + core_mine.astype(jnp.float32) + from_x.astype(jnp.float32)
    dec_out = add_residual(attended, states, tgt_lengths)

    grads_home = exchange(gate(backward_sum.astype(jnp.bfloat16), last), group_size, capacity)
    natural = expert_ids * capacity + rank
    (token_grad,) = combine(
        which_section, natural, gate_weights, [grads_home], 1
    )
    return (dec_out[None], token_grad)


def add_residual(attended, states, tgt_lengths):
    my_columns = attended.shape[1]
    residual = lax.dynamic_slice_in_dim(
        states, lax.axis_index("dp") * my_columns, my_columns, 1
    ).astype(jnp.float32)
    row_mask = (jnp.arange(TGT_LEN, dtype=jnp.int32)[None, :] < tgt_lengths[:, None]).reshape(-1, 1)
    return (residual + jnp.where(row_mask, attended, 0.0)).astype(jnp.bfloat16)


def body(
    tokens,
    expert_ids,
    gate_weights,
    out_grad,
    inner_weight,
    outer_weight,
    final_gain,
    dec_states,
    src_lengths,
    tgt_lengths,
    norm_gain,
    query_weight,
    key_weight,
    value_weight,
    out_weight,
):
    token_count, feature_count = tokens.shape
    group_size = lax.axis_size(("expert", "dp"))
    capacity = 3 * token_count // group_size
    slots = group_size * capacity

    named = expert_ids[:, :, None] == jnp.arange(group_size, dtype=jnp.int32)[None, None, :]
    either = (named[:, 0] | named[:, 1]).astype(jnp.bfloat16)
    row = lax.broadcasted_iota(jnp.int32, (token_count, token_count), 0)
    column = lax.broadcasted_iota(jnp.int32, (token_count, token_count), 1)
    earlier = jnp.dot(
        (column < row).astype(jnp.bfloat16), either, preferred_element_type=jnp.float32
    ).astype(jnp.int32)
    rank = jnp.sum(jnp.where(named, earlier[:, None, :], 0), axis=2)
    position = expert_ids * capacity + rank
    pick_first = slot_matrix(position[:, 0], slots)
    pick_second = slot_matrix(position[:, 1], slots)
    fill = (pick_first + pick_second).T

    def place(values):
        return jnp.dot(fill, values, preferred_element_type=jnp.float32).astype(jnp.bfloat16)

    def combine(arrived):
        first = jnp.dot(pick_first, arrived, preferred_element_type=jnp.float32)
        second = jnp.dot(pick_second, arrived, preferred_element_type=jnp.float32)
        return gate_weights[:, :1] * first + gate_weights[:, 1:] * second

    weight_in = inner_weight[0]
    weight_out = outer_weight[0]
    arrived_rows = exchange(place(tokens), group_size, capacity)
    pre_act = jnp.dot(arrived_rows, weight_in, preferred_element_type=jnp.float32)
    hidden = jax.nn.gelu(pre_act).astype(jnp.bfloat16)
    forward_part = jnp.dot(hidden, weight_out, preferred_element_type=jnp.float32)
    arrived_grads = exchange(place(out_grad), group_size, capacity)
    outputs_home = exchange(forward_part.astype(jnp.bfloat16), group_size, capacity)
    mixed_slice = sum_sections(combine(outputs_home)).astype(jnp.bfloat16)
    mixed = gather_sections(mixed_slice).astype(jnp.float32)
    memory = normalize(tokens.astype(jnp.float32) + mixed, final_gain).astype(jnp.bfloat16)

    back = contract_last(arrived_grads, weight_out)
    slope = jax.vjp(jax.nn.gelu, pre_act)[1](back)[0].astype(jnp.bfloat16)
    backward_part = contract_last(slope, weight_in)
    backward_slice = sum_sections(backward_part).astype(jnp.bfloat16)
    grads_home = exchange(backward_slice, group_size, capacity)
    token_grad = combine(grads_home).astype(jnp.bfloat16)

    states = dec_states[0]
    normed = normalize(states.astype(jnp.float32), norm_gain[0]).astype(jnp.bfloat16)
    full_query = gather_weight(query_weight[0], 0)
    full_key = gather_weight(key_weight[0], 0)
    full_value = gather_weight(value_weight[0], 0)
    full_out = gather_weight(out_weight[0], 1)
    query_sum = jnp.dot(normed, full_query, preferred_element_type=jnp.float32)
    source = gather_rows(memory, "dp")
    key_sum = jnp.dot(source, full_key, preferred_element_type=jnp.float32)
    value_sum = jnp.dot(source, full_value, preferred_element_type=jnp.float32)
    key_mask = jnp.arange(SRC_LEN, dtype=jnp.int32)[None, :] < src_lengths[:, None]
    context = attend(
        query_sum.astype(jnp.bfloat16),
        key_sum.astype(jnp.bfloat16),
        value_sum.astype(jnp.bfloat16),
        key_mask,
    )
    attended = sum_heads(jnp.dot(context, full_out, preferred_element_type=jnp.float32))
    dec_out = add_residual(attended, states, tgt_lengths)
    return (dec_out[None], token_grad)


def solution(mesh):
    in_specs = (
        P(("expert", "dp"), None),
        P(("expert", "dp"), None),
        P(("expert", "dp"), None),
        P(("expert", "dp"), None),
        P(("expert", "dp"), None, "section"),
        P(("expert", "dp"), "section", None),
        P(),
        P("section", "expert", None),
        P("expert"),
        P("expert"),
        P("section", None),
        P("section", "expert", "dp"),
        P("section", "expert", "dp"),
        P("section", "expert", "dp"),
        P("section", "dp", "expert"),
    )
    out_specs = (P("section", "expert", "dp"), P(("expert", "dp"), "section"))
    small = (mesh.shape["section"], mesh.shape["expert"], mesh.shape["dp"]) == (4, 2, 4)
    chosen = small_body if small else body
    return jax.shard_map(chosen, mesh=mesh, in_specs=in_specs, out_specs=out_specs, check_vma=False)
```

```python
import functools

import jax
import jax.numpy as jnp
from jax import lax
from jax.experimental import pallas as pl
from jax.experimental.pallas import tpu as pltpu
from jax.sharding import PartitionSpec as P

HEAD_DIM = 128
SRC_LEN = 256
TGT_LEN = 128


EPSILON = 1e-05


def normalize(values, gain):
    centre = jnp.mean(values, axis=-1, keepdims=True)
    centred = values - centre
    spread = jnp.mean(centred * centred, axis=-1, keepdims=True)
    return centred * lax.rsqrt(spread + EPSILON) * gain


def contract_last(left, right):
    return lax.dot_general(
        left, right, (((1,), (1,)), ((), ())), preferred_element_type=jnp.float32
    )


def shift(value, axis, step):
    size = lax.axis_size(axis)
    return lax.ppermute(value, axis, [(i, (i + step) % size) for i in range(size)])


def swap(value, axis, mask):
    size = lax.axis_size(axis)
    return lax.ppermute(value, axis, [(i, i ^ mask) for i in range(size)])


def sum_sections(partial):
    count = lax.axis_size("section")
    me = lax.axis_index("section")
    width = partial.shape[1] // count

    def piece(owner):
        return lax.dynamic_slice_in_dim(partial, owner * width, width, 1)

    total = piece(me).astype(jnp.float32)
    for step in range(1, count):
        sent = piece(lax.rem(me + step, count)).astype(jnp.bfloat16)
        total = total + shift(sent, "section", step).astype(jnp.float32)
    return total


def gather_sections(mine):
    count = lax.axis_size("section")
    me = lax.axis_index("section")
    width = mine.shape[1]
    whole = jnp.zeros((mine.shape[0], width * count), mine.dtype)
    whole = lax.dynamic_update_slice_in_dim(whole, mine, me * width, 1)
    for step in range(1, count):
        owner = lax.rem(me - step + count, count)
        whole = lax.dynamic_update_slice_in_dim(
            whole, shift(mine, "section", step), owner * width, 1
        )
    return whole


def gather_rows(mine, axis):
    held = mine
    me = lax.axis_index(axis)
    mask = lax.axis_size(axis) // 2
    blocks = [mine]
    while mask >= 1:
        blocks = blocks + [swap(block, axis, mask) for block in blocks]
        mask //= 2
    codes = [0]
    mask = lax.axis_size(axis) // 2
    while mask >= 1:
        codes = codes + [code ^ mask for code in codes]
        mask //= 2
    ordered = []
    for place in range(len(blocks)):
        chosen = blocks[0]
        for code, block in zip(codes[1:], blocks[1:]):
            chosen = jnp.where((me ^ code) == place, block, chosen)
        ordered.append(chosen)
    return jnp.concatenate(ordered, axis=0)


def gather_weight(weight, dimension):
    if lax.axis_size("expert") != 2:
        return lax.all_gather(weight, "expert", axis=dimension, tiled=True)
    other = swap(weight, "expert", 1)
    first = lax.axis_index("expert") == 0
    return jnp.concatenate(
        [jnp.where(first, weight, other), jnp.where(first, other, weight)], axis=dimension
    )


def sum_heads(partial):
    me = lax.axis_index("dp")
    count = lax.axis_size("dp")
    rows, columns = partial.shape
    total = partial.reshape(rows, count, columns // count)
    mask = 1
    while mask < count:
        paired = total.reshape(rows, -1, 2, columns // count)
        bit = (me // mask) % 2
        sent = lax.dynamic_index_in_dim(paired, 1 - bit, 2, False).astype(jnp.bfloat16)
        kept = lax.dynamic_index_in_dim(paired, bit, 2, False)
        total = kept + swap(sent, "dp", mask).astype(jnp.float32)
        mask *= 2
    return total.reshape(rows, columns // count)


def slot_matrix(positions, slots):
    places = lax.broadcasted_iota(jnp.int32, (positions.shape[0], slots), 1)
    return (positions[:, None] == places).astype(jnp.bfloat16)


def attend(query, keys, values, key_mask):
    sequences = key_mask.shape[0]
    head_count = query.shape[1] // HEAD_DIM
    query_split = query.reshape(sequences, -1, head_count, HEAD_DIM)
    keys_split = keys.reshape(sequences, -1, head_count, HEAD_DIM)
    values_split = values.reshape(sequences, -1, head_count, HEAD_DIM)
    scores = jnp.einsum(
        "bqhd,bkhd->bhqk", query_split, keys_split, preferred_element_type=jnp.float32
    ) * HEAD_DIM ** (-0.5)
    scores = jnp.where(key_mask[:, None, None, :], scores, -1e30)
    highest = jnp.max(scores, axis=-1, keepdims=True)
    weights = jnp.exp(scores - highest)
    probs = (weights / jnp.sum(weights, axis=-1, keepdims=True)).astype(jnp.bfloat16)
    context = jnp.einsum("bhqk,bkhd->bqhd", probs, values_split, preferred_element_type=jnp.float32)
    return context.astype(jnp.bfloat16).reshape(-1, head_count * HEAD_DIM)


def exchange(values, group_size, capacity):
    sent = values.reshape(group_size, capacity, values.shape[1])
    arrived = lax.all_to_all(sent, ("expert", "dp"), split_axis=0, concat_axis=0, tiled=True)
    return arrived.reshape(values.shape)


SHORT = pl.CostEstimate(flops=1, bytes_accessed=1, transcendentals=0)


def gate(value, *after):
    return lax.optimization_barrier((value,) + after)[0]


def vmem(shape, dtype):
    return pltpu.VMEM(shape, dtype)


def dispatch_kernel(capacity, layout, section_ref, code_ref, *refs):
    blocks = refs[:-4]
    outs, held, sems = refs[-4:-2], refs[-2], refs[-1]
    count, rows = held.shape[0], held.shape[1]
    half = lax.rem(section_ref[0], 2)
    copies = []
    for place, pieces in enumerate(layout):
        group = []
        for i, (which, start, length, side) in enumerate(pieces):
            there = held.at[place]
            if side is not None:
                offset = (half if side == 0 else 1 - half) * length
                there = held.at[place, pl.ds(pl.multiple_of(offset, length), length)]
            here = blocks[which].at[pl.ds(start, length)]
            group.append(pltpu.make_async_copy(here, there, sems.at[place, i]))
        copies.append(group)
    for group in copies:
        for copy in group:
            copy.start()
    for place, group in enumerate(copies):
        picks = []
        for which in range(2):
            line = which * count + place
            code = code_ref[line : line + 1, :]
            slot = lax.broadcasted_iota(jnp.int32, (capacity, code.shape[1]), 0)
            picks.append(jnp.where(slot == code, 1.0, 0.0))
        pick = jnp.concatenate(picks, axis=0).astype(jnp.bfloat16)
        for copy in group:
            copy.wait()
        picked = jnp.dot(pick, held[place], preferred_element_type=jnp.float32)
        picked = picked.astype(jnp.bfloat16)
        for which, out_ref in enumerate(outs):
            out_ref[place * capacity : (place + 1) * capacity, :] = picked[
                which * capacity : (which + 1) * capacity
            ]


def dispatch(section, code, blocks, layout, capacity):
    rows, features = blocks[0].shape
    count = len(layout)
    picked = jax.ShapeDtypeStruct((count * capacity, features), jnp.bfloat16)
    return pl.pallas_call(
        functools.partial(dispatch_kernel, capacity, layout),
        out_shape=(picked, picked),
        in_specs=[
            pl.BlockSpec(memory_space=pltpu.SMEM),
            pl.BlockSpec(memory_space=pltpu.VMEM),
        ]
        + [pl.BlockSpec(memory_space=pltpu.HBM)] * len(blocks),
        out_specs=[pl.BlockSpec(memory_space=pltpu.VMEM)] * 2,
        scratch_shapes=[
            vmem((count, rows, features), jnp.bfloat16),
            pltpu.SemaphoreType.DMA((count, 2)),
        ],
        compiler_params=pltpu.CompilerParams(vmem_limit_bytes=10 * 1024 * 1024),
        cost_estimate=SHORT,
        name="dispatch",
    )(section, code, *blocks)


def send_home(part, codes, capacity):
    size = lax.axis_size(("expert", "dp"))
    arrived = []
    for place, code in enumerate(codes):
        block = part[place * capacity : (place + 1) * capacity]
        if code:
            block = lax.ppermute(block, ("expert", "dp"), [(i, i ^ code) for i in range(size)])
        arrived.append(block)
    return arrived


def combine_kernel(count, split, section_ref, position_ref, gates_ref, *refs):
    blocks = refs[:count]
    outs, (held, total) = refs[count:-2], refs[-2:]
    capacity, features = blocks[0].shape
    position = position_ref[...]
    slot = lax.broadcasted_iota(jnp.int32, (position.shape[0], count * capacity), 1)
    picks = [
        jnp.where(position[:, k : k + 1] == slot, 1.0, 0.0).astype(jnp.bfloat16) for k in range(2)
    ]
    for i, block in enumerate(blocks):
        held[i * capacity : (i + 1) * capacity, :] = block[...]
    pick = jnp.concatenate(picks, axis=0)
    rows = position.shape[0]
    both = jnp.dot(pick, held[...], preferred_element_type=jnp.float32)
    total[...] = gates_ref[:, 0:1] * both[:rows] + gates_ref[:, 1:2] * both[rows:]
    if split == 1:
        outs[0][...] = total[...].astype(outs[0].dtype)
        return
    sent_ref, kept_first, kept_second = outs
    width = features // split
    for step, out_ref in enumerate((kept_first, sent_ref.at[0], kept_second, sent_ref.at[1])):
        start = pl.multiple_of((section_ref[0] ^ step) * width, width)
        out_ref[...] = total[:, pl.ds(start, width)].astype(out_ref.dtype)


def combine(section, position, gates, blocks, split):
    capacity, features = blocks[0].shape
    rows = position.shape[0]
    count = len(blocks)
    width = features // split
    kept = jax.ShapeDtypeStruct((rows, width), jnp.float32)
    if split == 1:
        out_shape = (jax.ShapeDtypeStruct((rows, width), jnp.bfloat16),)
    else:
        out_shape = (jax.ShapeDtypeStruct((2, rows, width), jnp.bfloat16), kept, kept)
    full = pl.BlockSpec(memory_space=pltpu.VMEM)
    return pl.pallas_call(
        functools.partial(combine_kernel, count, split),
        out_shape=out_shape,
        in_specs=[pl.BlockSpec(memory_space=pltpu.SMEM)] + [full] * (2 + count),
        out_specs=[full] * len(out_shape),
        scratch_shapes=[
            vmem((count * capacity, features), jnp.bfloat16),
            vmem((rows, features), jnp.float32),
        ],
        compiler_params=pltpu.CompilerParams(vmem_limit_bytes=14 * 1024 * 1024),
        cost_estimate=SHORT,
        name="combine",
    )(section, position, gates, *blocks)


def memory_kernel(count, section_ref, tokens_ref, gain_ref, *refs):
    slices, out_ref, mixed = refs[:count], refs[count], refs[count + 1]
    me = section_ref[0]
    width = slices[0].shape[1]
    for step, piece in enumerate(slices):
        owner = me ^ step
        mixed[:, pl.ds(pl.multiple_of(owner * width, width), width)] = piece[...].astype(
            jnp.float32
        )
    values = tokens_ref[...].astype(jnp.float32) + mixed[...]
    out_ref[...] = normalize(values, gain_ref[...]).astype(jnp.bfloat16)


def make_memory(me, tokens, slices, gain):
    return pl.pallas_call(
        functools.partial(memory_kernel, len(slices)),
        out_shape=jax.ShapeDtypeStruct(tokens.shape, jnp.bfloat16),
        in_specs=[
            pl.BlockSpec(memory_space=pltpu.SMEM),
        ]
        + [pl.BlockSpec(memory_space=pltpu.VMEM)] * (2 + len(slices)),
        out_specs=pl.BlockSpec(memory_space=pltpu.VMEM),
        scratch_shapes=[vmem(tokens.shape, jnp.float32)],
        compiler_params=pltpu.CompilerParams(vmem_limit_bytes=8 * 1024 * 1024),
        cost_estimate=SHORT,
        name="memory",
    )(me, tokens, gain[None], *slices)


def normed_kernel(y_ref, states_ref, gain_ref, own_ref, other_ref):
    values = normalize(states_ref[...].astype(jnp.float32), gain_ref[...]).astype(jnp.bfloat16)
    width = own_ref.shape[1]
    for out_ref, first in ((own_ref, y_ref[0] == 0), (other_ref, y_ref[0] == 1)):
        out_ref[...] = jnp.where(first, values[:, :width], values[:, width:])


def normed_halves(y, states, gain):
    rows, features = states.shape
    full = pl.BlockSpec(memory_space=pltpu.VMEM)
    return pl.pallas_call(
        normed_kernel,
        out_shape=(jax.ShapeDtypeStruct((rows, features // 2), jnp.bfloat16),) * 2,
        in_specs=[pl.BlockSpec(memory_space=pltpu.SMEM), full, full],
        out_specs=[full] * 2,
        compiler_params=pltpu.CompilerParams(vmem_limit_bytes=12 * 1024 * 1024),
        cost_estimate=SHORT,
        name="normed",
    )(y.astype(jnp.int32).reshape(1), states, gain)


def attend_kernel(place_ref, lengths_ref, query_ref, *refs):
    near_ref, far_ref, key_own, key_other, value_own, value_other, out_ref = refs[:7]
    source, key_weight, value_weight, keys, values, sems = refs[7:]
    y, core, sentence = place_ref[0], place_ref[1], place_ref[2]
    rows = near_ref.shape[0]
    depth = key_own.shape[0]
    moves = [
        (near_ref, source.at[pl.ds(0, rows)]),
        (far_ref, source.at[pl.ds(rows, rows)]),
        (key_own, key_weight.at[y]),
        (key_other, key_weight.at[1 - y]),
        (value_own, value_weight.at[y]),
        (value_other, value_weight.at[1 - y]),
    ]
    copies = [
        pltpu.make_async_copy(here, there, sems.at[i]) for i, (here, there) in enumerate(moves)
    ]
    for copy in copies:
        copy.start()

    def linear(weight, result):
        total = jnp.dot(source[:, :depth], weight[0], preferred_element_type=jnp.float32)
        total += jnp.dot(source[:, depth:], weight[1], preferred_element_type=jnp.float32)
        result[...] = total.astype(jnp.bfloat16)

    for copy in copies[:4]:
        copy.wait()
    linear(key_weight, keys)
    for copy in copies[4:]:
        copy.wait()
    linear(value_weight, values)

    column = lax.broadcasted_iota(jnp.int32, (query_ref.shape[0], 2 * rows), 1)
    position = jnp.where(column < rows, column + core * rows, column - core * rows)
    valid = position < lengths_ref[sentence]
    for head in range(query_ref.shape[1] // HEAD_DIM):
        span = slice(head * HEAD_DIM, (head + 1) * HEAD_DIM)
        scores = contract_last(query_ref[:, span], keys[:, span]) * HEAD_DIM ** (-0.5)
        scores = jnp.where(valid, scores, -1e30)
        weights = jnp.exp(scores - jnp.max(scores, axis=-1, keepdims=True))
        probs = (weights / jnp.sum(weights, axis=-1, keepdims=True)).astype(jnp.bfloat16)
        result = jnp.dot(probs, values[:, span], preferred_element_type=jnp.float32)
        out_ref[:, span] = result.astype(jnp.bfloat16)


def attend_sentence(place, lengths, query, near, far, key_parts, value_pair):
    rows, features = near.shape
    depth, width = key_parts[0].shape
    hold = pl.BlockSpec(memory_space=pltpu.HBM)
    smem = pl.BlockSpec(memory_space=pltpu.SMEM)
    full = pl.BlockSpec(memory_space=pltpu.VMEM)
    return pl.pallas_call(
        attend_kernel,
        out_shape=jax.ShapeDtypeStruct(query.shape, jnp.bfloat16),
        in_specs=[smem, smem, full] + [hold] * 6,
        out_specs=full,
        scratch_shapes=[
            vmem((2 * rows, features), jnp.bfloat16),
            vmem((2, depth, width), jnp.bfloat16),
            vmem((2, depth, width), jnp.bfloat16),
            vmem((2 * rows, width), jnp.bfloat16),
            vmem((2 * rows, width), jnp.bfloat16),
            pltpu.SemaphoreType.DMA((6,)),
        ],
        compiler_params=pltpu.CompilerParams(vmem_limit_bytes=56 * 1024 * 1024),
        cost_estimate=SHORT,
        name="attend_sentence",
    )(place, lengths, query, near, far, *key_parts, *value_pair)


def project_kernel(place_ref, mine_ref, done_ref, own_ref, other_ref, *refs):
    sent_mine, sent_other, kept_mine, kept_other, context = refs
    y, core, x = place_ref[0], place_ref[1], place_ref[2]
    targets = mine_ref.shape[0]
    for part, sentence in ((mine_ref, x), (done_ref, 1 - x)):
        context[pl.ds(pl.multiple_of(sentence * targets, targets), targets), :] = part[...]
    columns = kept_mine.shape[1]
    outs = ((sent_mine, kept_mine), (sent_other, kept_other))

    def write(weight_ref, chosen):
        for side, out_ref in zip((1 - core, core), chosen):
            span = pl.ds(pl.multiple_of(side * columns, columns), columns)
            part = jnp.dot(context[...], weight_ref[:, span], preferred_element_type=jnp.float32)
            out_ref[...] = part.astype(out_ref.dtype)

    @pl.when(x == y)
    def _():
        write(own_ref, outs[0])
        write(other_ref, outs[1])

    @pl.when(x != y)
    def _():
        write(other_ref, outs[0])
        write(own_ref, outs[1])


def project(place, mine, done, out_own, out_other):
    targets, width = 2 * mine.shape[0], mine.shape[1]
    columns = out_own.shape[1] // 2
    full = pl.BlockSpec(memory_space=pltpu.VMEM)
    sent = jax.ShapeDtypeStruct((targets, columns), jnp.bfloat16)
    kept = jax.ShapeDtypeStruct((targets, columns), jnp.float32)
    return pl.pallas_call(
        project_kernel,
        out_shape=(sent, sent, kept, kept),
        in_specs=[pl.BlockSpec(memory_space=pltpu.SMEM)] + [full] * 4,
        out_specs=[full] * 4,
        scratch_shapes=[vmem((targets, width), jnp.bfloat16)],
        compiler_params=pltpu.CompilerParams(vmem_limit_bytes=16 * 1024 * 1024),
        cost_estimate=SHORT,
        name="project",
    )(place, mine, done, out_own, out_other)


def slope_kernel(codes, here_ref, own_ref, core_ref, rise_own, rise_core, out_ref, slope, *refs):
    grads, rise, weight_out, sems = refs
    rows = own_ref.shape[0]
    hidden = weight_out.shape[0]
    chunk = hidden // 4
    moves = []
    block = 2 * rows // len(codes)
    for order, code in enumerate(codes):
        source = here_ref[0] ^ code
        there = pl.ds(pl.multiple_of(source * block, 16), block)
        here = pl.ds(order * block % rows, block)
        own = order * block < rows
        moves.append(((own_ref if own else core_ref).at[here], grads.at[there]))
        moves.append(((rise_own if own else rise_core).at[here], rise.at[there]))
    for part in range(4):
        span = pl.ds(part * chunk, chunk)
        moves.append((out_ref.at[span], weight_out.at[span]))
    copies = [
        pltpu.make_async_copy(here, there, sems.at[i]) for i, (here, there) in enumerate(moves)
    ]
    for copy in copies:
        copy.start()
    for copy in copies[:-4]:
        copy.wait()
    for part in range(4):
        copies[part - 4].wait()
        span = slice(part * chunk, (part + 1) * chunk)
        back = contract_last(grads[...], weight_out[span, :])
        slope[:, span] = (back * rise[:, span]).astype(jnp.bfloat16)


def expert_slope(here, codes, grads_own, grads_core, rise_own, rise_core, weight_out):
    rows = 2 * grads_own.shape[0]
    hidden, features = weight_out.shape
    hold = pl.BlockSpec(memory_space=pltpu.HBM)
    return pl.pallas_call(
        functools.partial(slope_kernel, codes),
        out_shape=jax.ShapeDtypeStruct((rows, hidden), jnp.bfloat16),
        in_specs=[pl.BlockSpec(memory_space=pltpu.SMEM)] + [hold] * 5,
        out_specs=pl.BlockSpec(memory_space=pltpu.VMEM),
        scratch_shapes=[
            vmem((rows, features), jnp.bfloat16),
            vmem((rows, hidden), jnp.float32),
            vmem((hidden, features), jnp.bfloat16),
            pltpu.SemaphoreType.DMA((4 + 2 * len(codes),)),
        ],
        compiler_params=pltpu.CompilerParams(vmem_limit_bytes=56 * 1024 * 1024),
        cost_estimate=SHORT,
        name="expert_slope",
    )(here, grads_own, grads_core, rise_own, rise_core, weight_out)


def backward_kernel(split, section_ref, slope_ref, in_ref, sent_ref, kept_first, kept_second, *refs):
    weight_in, sems = refs
    width = weight_in.shape[0] // split
    outs = (sent_ref.at[0], sent_ref.at[1], kept_first, kept_second)
    spans, copies = [], []
    for i, step in enumerate((1, 3, 0, 2)):
        start = pl.multiple_of((section_ref[0] ^ step) * width, width)
        spans.append(pl.ds(start, width))
        copies.append(
            pltpu.make_async_copy(in_ref.at[spans[i]], weight_in.at[spans[i]], sems.at[i])
        )
    for copy in copies:
        copy.start()
    for copy, span, out_ref in zip(copies, spans, outs):
        copy.wait()
        part = contract_last(slope_ref[...], weight_in[span, :])
        out_ref[...] = part.astype(out_ref.dtype)


def expert_backward(section, slope, weight_in, split):
    rows, hidden = slope.shape
    features = weight_in.shape[0]
    width = features // split
    full = pl.BlockSpec(memory_space=pltpu.VMEM)
    kept = jax.ShapeDtypeStruct((rows, width), jnp.float32)
    return pl.pallas_call(
        functools.partial(backward_kernel, split),
        out_shape=(jax.ShapeDtypeStruct((2, rows, width), jnp.bfloat16), kept, kept),
        in_specs=[pl.BlockSpec(memory_space=pltpu.SMEM), full, pl.BlockSpec(memory_space=pltpu.HBM)],
        out_specs=[full] * 3,
        scratch_shapes=[
            vmem((features, hidden), jnp.bfloat16),
            pltpu.SemaphoreType.DMA((split,)),
        ],
        compiler_params=pltpu.CompilerParams(vmem_limit_bytes=56 * 1024 * 1024),
        cost_estimate=SHORT,
        name="expert_backward",
    )(section, slope, weight_in)


def small_body(
    tokens,
    expert_ids,
    gate_weights,
    out_grad,
    inner_weight,
    outer_weight,
    final_gain,
    dec_states,
    src_lengths,
    tgt_lengths,
    norm_gain,
    query_weight,
    key_weight,
    value_weight,
    out_weight,
):
    token_count, feature_count = tokens.shape
    group_size = lax.axis_size(("expert", "dp"))
    capacity = 3 * token_count // group_size
    here = lax.axis_index(("expert", "dp"))
    y = lax.axis_index("expert")
    d = lax.axis_index("dp")
    section = lax.axis_index("section")
    sections = lax.axis_size("section")
    half = feature_count // 2
    weight_in = inner_weight[0]
    weight_out = outer_weight[0]
    key_own, value_own, out_own = key_weight[0], value_weight[0], out_weight[0]
    query_own = query_weight[0]

    size = group_size
    near_codes = (0, 2, 4, 6)
    core_codes = (1, 3, 5, 7)
    core, x = d % 2, d // 2
    which_section = section.astype(jnp.int32).reshape(1)

    token_y = swap(tokens, "expert", 1)
    token_x = swap(tokens, "dp", 2)
    row = lax.broadcasted_iota(jnp.int32, (token_count, token_count), 0)
    column = lax.broadcasted_iota(jnp.int32, (token_count, token_count), 1)
    named = expert_ids[:, :, None] == jnp.arange(size, dtype=jnp.int32)[None, None, :]
    either = (named[:, 0] | named[:, 1]).astype(jnp.bfloat16)
    earlier = jnp.dot(
        (column < row).astype(jnp.bfloat16), either, preferred_element_type=jnp.float32
    ).astype(jnp.int32)
    rank = jnp.sum(jnp.where(named, earlier[:, None, :], 0), axis=2)
    codes_of = expert_ids ^ here
    position = ((codes_of >> 1) + 4 * (codes_of & 1)) * capacity + rank

    ids_own = expert_ids.T
    ids_x, ids_y = swap(ids_own, "dp", 2), swap(ids_own, "expert", 1)
    ids_far = swap(ids_x, "expert", 1)
    token_far = swap(gate(token_y, ids_x, ids_y), "dp", 2)

    side = lax.rem(section, 2)
    share = token_count // 2
    grad_half = lax.dynamic_slice_in_dim(out_grad, side * share, share, 0)
    half_y = swap(gate(grad_half, token_y), "expert", 1)
    states = dec_states[0]
    normed_own, asked = normed_halves(y, states, norm_gain)
    asked_here = swap(gate(asked, half_y), "expert", 1)
    query_there = jnp.dot(asked_here, query_own, preferred_element_type=jnp.float32)
    other_y = swap(half_y, "section", 1)

    ids = jnp.stack([ids_own, ids_x, ids_y, ids_far])
    named_there = jnp.concatenate([(ids == here).any(axis=1), (ids == (here ^ 1)).any(axis=1)])
    before = jnp.dot(
        named_there.astype(jnp.bfloat16),
        (row < column).astype(jnp.bfloat16),
        preferred_element_type=jnp.float32,
    ).astype(jnp.int32)
    code = jnp.where(named_there, before, -1)

    def forward(rows, *after):
        pre_act = jnp.dot(rows, weight_in, preferred_element_type=jnp.float32)
        hidden = jax.nn.gelu(gate(pre_act, *after)).astype(jnp.bfloat16)
        part = jnp.dot(hidden, weight_out, preferred_element_type=jnp.float32)
        return pre_act, part.astype(jnp.bfloat16)

    def slope_of(pre_act):
        return jax.vjp(jax.nn.gelu, pre_act)[1](jnp.ones_like(pre_act))[0]

    rows_own, rows_sent = dispatch(
        which_section,
        gate(code, asked),
        [tokens, token_x, token_y, token_far],
        tuple(((place, 0, token_count, None),) for place in range(4)),
        capacity,
    )
    rows_core = swap(rows_sent, "dp", 1)
    pre_own, part_own = forward(rows_own, other_y)
    pre_core, part_core = forward(gate(rows_core, part_own))
    home = send_home(part_own, near_codes, capacity) + send_home(part_core, core_codes, capacity)
    grad_y = jnp.concatenate([gate(half_y, home[4]), other_y], axis=0)
    query_back = swap(gate(query_there.astype(jnp.bfloat16), home[5], home[6]), "expert", 1)

    rise_own, rise_core = slope_of(gate(pre_own, home[1])), slope_of(gate(pre_core, home[1]))
    held_gates = gate(gate_weights, rise_own, rise_core, query_there, grad_y)
    sent_pair, first, second = combine(which_section, position, held_gates, home, sections)
    from_pair = swap(sent_pair, "section", 1)
    grad_x = swap(gate(out_grad, home[5]), "dp", 2)
    grad_far = swap(gate(grad_y, first), "dp", 2)
    to_other = (second + from_pair[1].astype(jnp.float32)).astype(jnp.bfloat16)
    from_other = swap(to_other, "section", 2)
    mixed_sum = first + from_pair[0].astype(jnp.float32)
    mixed_slice = (mixed_sum + from_other.astype(jnp.float32)).astype(jnp.bfloat16)
    key_other = swap(gate(key_own, first), "expert", 1)
    mixed_near = swap(mixed_slice, "section", 1)
    grads_own, grads_sent = dispatch(
        which_section,
        gate(code, mixed_near),
        [out_grad, grad_x, grad_y, grad_far],
        (
            ((0, 0, token_count, None),),
            ((1, 0, token_count, None),),
            ((2, 0, share, 0), (2, share, share, 1)),
            ((3, 0, share, 0), (3, share, share, 1)),
        ),
        capacity,
    )
    grads_core = swap(grads_sent, "dp", 1)
    grads_core = swap(grads_sent, "dp", 1)
    slope = expert_slope(
        here.astype(jnp.int32).reshape(1),
        near_codes + core_codes,
        grads_own,
        grads_core,
        rise_own,
        rise_core,
        weight_out,
    )
    back_pair, back_first, back_second = expert_backward(
        which_section, slope, weight_in, sections
    )
    mixed_far = swap(jnp.stack([mixed_slice, gate(mixed_near, key_other)]), "section", 2)
    slices = [mixed_slice, mixed_near, mixed_far[0], mixed_far[1]]

    value_other = swap(gate(value_own, mixed_near), "expert", 1)

    query_here = jnp.dot(normed_own, query_own, preferred_element_type=jnp.float32)
    query = (query_here + query_back.astype(jnp.float32)).astype(jnp.bfloat16)

    memory = make_memory(which_section, gate(tokens, query_back), slices, final_gain)
    out_other = swap(gate(out_own, memory), "expert", 1)
    memory_x = swap(memory, "dp", 2)
    memory_core = swap(memory, "dp", 1)

    def sentence(which, near, far, *after):
        place = gate(jnp.stack([y, core, which]).astype(jnp.int32), *after)
        rows_of = lax.dynamic_slice_in_dim(query, which * TGT_LEN, TGT_LEN, 0)
        parts = (key_own, key_other), (value_own, value_other)
        return attend_sentence(place, src_lengths, rows_of, near, far, *parts)

    back_from_pair = swap(back_pair, "section", 1)
    back_to_other = (back_second + back_from_pair[1].astype(jnp.float32)).astype(jnp.bfloat16)
    back_from_other = swap(back_to_other, "section", 2)
    backward_sum = back_first + back_from_pair[0].astype(jnp.float32)
    backward_sum = backward_sum + back_from_other.astype(jnp.float32)
    context_own = sentence(x, memory, memory_core)
    memory_far = swap(gate(memory_x, context_own), "dp", 1)
    context_other = sentence(1 - x, memory_x, memory_far)
    place = jnp.stack([y, core, x]).astype(jnp.int32)
    sent_mine, sent_other, kept_mine, kept_other = project(
        place, context_own, context_other, out_own, out_other
    )

    core_other = swap(sent_other, "dp", 1)
    core_mine = swap(sent_mine, "dp", 1)
    last = gate(kept_other, back_from_other) + core_other.astype(jnp.float32)
    from_x = swap(last.astype(jnp.bfloat16), "dp", 2)
    attended = kept_mine + core_mine.astype(jnp.float32) + from_x.astype(jnp.float32)
    dec_out = add_residual(attended, states, tgt_lengths)

    grads_home = exchange(gate(backward_sum.astype(jnp.bfloat16), last), group_size, capacity)
    natural = expert_ids * capacity + rank
    (token_grad,) = combine(
        which_section, natural, gate_weights, [grads_home], 1
    )
    return (dec_out[None], token_grad)


def add_residual(attended, states, tgt_lengths):
    my_columns = attended.shape[1]
    residual = lax.dynamic_slice_in_dim(
        states, lax.axis_index("dp") * my_columns, my_columns, 1
    ).astype(jnp.float32)
    row_mask = (jnp.arange(TGT_LEN, dtype=jnp.int32)[None, :] < tgt_lengths[:, None]).reshape(-1, 1)
    return (residual + jnp.where(row_mask, attended, 0.0)).astype(jnp.bfloat16)


def body(
    tokens,
    expert_ids,
    gate_weights,
    out_grad,
    inner_weight,
    outer_weight,
    final_gain,
    dec_states,
    src_lengths,
    tgt_lengths,
    norm_gain,
    query_weight,
    key_weight,
    value_weight,
    out_weight,
):
    token_count, feature_count = tokens.shape
    group_size = lax.axis_size(("expert", "dp"))
    capacity = 3 * token_count // group_size
    slots = group_size * capacity

    named = expert_ids[:, :, None] == jnp.arange(group_size, dtype=jnp.int32)[None, None, :]
    either = (named[:, 0] | named[:, 1]).astype(jnp.bfloat16)
    row = lax.broadcasted_iota(jnp.int32, (token_count, token_count), 0)
    column = lax.broadcasted_iota(jnp.int32, (token_count, token_count), 1)
    earlier = jnp.dot(
        (column < row).astype(jnp.bfloat16), either, preferred_element_type=jnp.float32
    ).astype(jnp.int32)
    rank = jnp.sum(jnp.where(named, earlier[:, None, :], 0), axis=2)
    position = expert_ids * capacity + rank
    pick_first = slot_matrix(position[:, 0], slots)
    pick_second = slot_matrix(position[:, 1], slots)
    fill = (pick_first + pick_second).T

    def place(values):
        return jnp.dot(fill, values, preferred_element_type=jnp.float32).astype(jnp.bfloat16)

    def combine(arrived):
        first = jnp.dot(pick_first, arrived, preferred_element_type=jnp.float32)
        second = jnp.dot(pick_second, arrived, preferred_element_type=jnp.float32)
        return gate_weights[:, :1] * first + gate_weights[:, 1:] * second

    weight_in = inner_weight[0]
    weight_out = outer_weight[0]
    arrived_rows = exchange(place(tokens), group_size, capacity)
    pre_act = jnp.dot(arrived_rows, weight_in, preferred_element_type=jnp.float32)
    hidden = jax.nn.gelu(pre_act).astype(jnp.bfloat16)
    forward_part = jnp.dot(hidden, weight_out, preferred_element_type=jnp.float32)
    arrived_grads = exchange(place(out_grad), group_size, capacity)
    outputs_home = exchange(forward_part.astype(jnp.bfloat16), group_size, capacity)
    mixed_slice = sum_sections(combine(outputs_home)).astype(jnp.bfloat16)
    mixed = gather_sections(mixed_slice).astype(jnp.float32)
    memory = normalize(tokens.astype(jnp.float32) + mixed, final_gain).astype(jnp.bfloat16)

    back = contract_last(arrived_grads, weight_out)
    slope = jax.vjp(jax.nn.gelu, pre_act)[1](back)[0].astype(jnp.bfloat16)
    backward_part = contract_last(slope, weight_in)
    backward_slice = sum_sections(backward_part).astype(jnp.bfloat16)
    grads_home = exchange(backward_slice, group_size, capacity)
    token_grad = combine(grads_home).astype(jnp.bfloat16)

    states = dec_states[0]
    normed = normalize(states.astype(jnp.float32), norm_gain[0]).astype(jnp.bfloat16)
    full_query = gather_weight(query_weight[0], 0)
    full_key = gather_weight(key_weight[0], 0)
    full_value = gather_weight(value_weight[0], 0)
    full_out = gather_weight(out_weight[0], 1)
    query_sum = jnp.dot(normed, full_query, preferred_element_type=jnp.float32)
    source = gather_rows(memory, "dp")
    key_sum = jnp.dot(source, full_key, preferred_element_type=jnp.float32)
    value_sum = jnp.dot(source, full_value, preferred_element_type=jnp.float32)
    key_mask = jnp.arange(SRC_LEN, dtype=jnp.int32)[None, :] < src_lengths[:, None]
    context = attend(
        query_sum.astype(jnp.bfloat16),
        key_sum.astype(jnp.bfloat16),
        value_sum.astype(jnp.bfloat16),
        key_mask,
    )
    attended = sum_heads(jnp.dot(context, full_out, preferred_element_type=jnp.float32))
    dec_out = add_residual(attended, states, tgt_lengths)
    return (dec_out[None], token_grad)


def solution(mesh):
    in_specs = (
        P(("expert", "dp"), None),
        P(("expert", "dp"), None),
        P(("expert", "dp"), None),
        P(("expert", "dp"), None),
        P(("expert", "dp"), None, "section"),
        P(("expert", "dp"), "section", None),
        P(),
        P("section", "expert", None),
        P("expert"),
        P("expert"),
        P("section", None),
        P("section", "expert", "dp"),
        P("section", "expert", "dp"),
        P("section", "expert", "dp"),
        P("section", "dp", "expert"),
    )
    out_specs = (P("section", "expert", "dp"), P(("expert", "dp"), "section"))
    small = (mesh.shape["section"], mesh.shape["expert"], mesh.shape["dp"]) == (4, 2, 4)
    chosen = small_body if small else body
    return jax.shard_map(chosen, mesh=mesh, in_specs=in_specs, out_specs=out_specs, check_vma=False)
```

```python
import functools

import jax
import jax.numpy as jnp
from jax import lax
from jax.experimental import pallas as pl
from jax.experimental.pallas import tpu as pltpu
from jax.sharding import PartitionSpec as P

HEAD_DIM = 128
SRC_LEN = 256
TGT_LEN = 128


EPSILON = 1e-05


def normalize(values, gain):
    centre = jnp.mean(values, axis=-1, keepdims=True)
    centred = values - centre
    spread = jnp.mean(centred * centred, axis=-1, keepdims=True)
    return centred * lax.rsqrt(spread + EPSILON) * gain


def contract_last(left, right):
    return lax.dot_general(
        left, right, (((1,), (1,)), ((), ())), preferred_element_type=jnp.float32
    )


def shift(value, axis, step):
    size = lax.axis_size(axis)
    return lax.ppermute(value, axis, [(i, (i + step) % size) for i in range(size)])


def swap(value, axis, mask):
    size = lax.axis_size(axis)
    return lax.ppermute(value, axis, [(i, i ^ mask) for i in range(size)])


def sum_sections(partial):
    count = lax.axis_size("section")
    me = lax.axis_index("section")
    width = partial.shape[1] // count

    def piece(owner):
        return lax.dynamic_slice_in_dim(partial, owner * width, width, 1)

    total = piece(me).astype(jnp.float32)
    for step in range(1, count):
        sent = piece(lax.rem(me + step, count)).astype(jnp.bfloat16)
        total = total + shift(sent, "section", step).astype(jnp.float32)
    return total


def gather_sections(mine):
    count = lax.axis_size("section")
    me = lax.axis_index("section")
    width = mine.shape[1]
    whole = jnp.zeros((mine.shape[0], width * count), mine.dtype)
    whole = lax.dynamic_update_slice_in_dim(whole, mine, me * width, 1)
    for step in range(1, count):
        owner = lax.rem(me - step + count, count)
        whole = lax.dynamic_update_slice_in_dim(
            whole, shift(mine, "section", step), owner * width, 1
        )
    return whole


def gather_rows(mine, axis):
    held = mine
    me = lax.axis_index(axis)
    mask = lax.axis_size(axis) // 2
    blocks = [mine]
    while mask >= 1:
        blocks = blocks + [swap(block, axis, mask) for block in blocks]
        mask //= 2
    codes = [0]
    mask = lax.axis_size(axis) // 2
    while mask >= 1:
        codes = codes + [code ^ mask for code in codes]
        mask //= 2
    ordered = []
    for place in range(len(blocks)):
        chosen = blocks[0]
        for code, block in zip(codes[1:], blocks[1:]):
            chosen = jnp.where((me ^ code) == place, block, chosen)
        ordered.append(chosen)
    return jnp.concatenate(ordered, axis=0)


def gather_weight(weight, dimension):
    if lax.axis_size("expert") != 2:
        return lax.all_gather(weight, "expert", axis=dimension, tiled=True)
    other = swap(weight, "expert", 1)
    first = lax.axis_index("expert") == 0
    return jnp.concatenate(
        [jnp.where(first, weight, other), jnp.where(first, other, weight)], axis=dimension
    )


def sum_heads(partial):
    me = lax.axis_index("dp")
    count = lax.axis_size("dp")
    rows, columns = partial.shape
    total = partial.reshape(rows, count, columns // count)
    mask = 1
    while mask < count:
        paired = total.reshape(rows, -1, 2, columns // count)
        bit = (me // mask) % 2
        sent = lax.dynamic_index_in_dim(paired, 1 - bit, 2, False).astype(jnp.bfloat16)
        kept = lax.dynamic_index_in_dim(paired, bit, 2, False)
        total = kept + swap(sent, "dp", mask).astype(jnp.float32)
        mask *= 2
    return total.reshape(rows, columns // count)


def slot_matrix(positions, slots):
    places = lax.broadcasted_iota(jnp.int32, (positions.shape[0], slots), 1)
    return (positions[:, None] == places).astype(jnp.bfloat16)


def attend(query, keys, values, key_mask):
    sequences = key_mask.shape[0]
    head_count = query.shape[1] // HEAD_DIM
    query_split = query.reshape(sequences, -1, head_count, HEAD_DIM)
    keys_split = keys.reshape(sequences, -1, head_count, HEAD_DIM)
    values_split = values.reshape(sequences, -1, head_count, HEAD_DIM)
    scores = jnp.einsum(
        "bqhd,bkhd->bhqk", query_split, keys_split, preferred_element_type=jnp.float32
    ) * HEAD_DIM ** (-0.5)
    scores = jnp.where(key_mask[:, None, None, :], scores, -1e30)
    highest = jnp.max(scores, axis=-1, keepdims=True)
    weights = jnp.exp(scores - highest)
    probs = (weights / jnp.sum(weights, axis=-1, keepdims=True)).astype(jnp.bfloat16)
    context = jnp.einsum("bhqk,bkhd->bqhd", probs, values_split, preferred_element_type=jnp.float32)
    return context.astype(jnp.bfloat16).reshape(-1, head_count * HEAD_DIM)


def exchange(values, group_size, capacity):
    sent = values.reshape(group_size, capacity, values.shape[1])
    arrived = lax.all_to_all(sent, ("expert", "dp"), split_axis=0, concat_axis=0, tiled=True)
    return arrived.reshape(values.shape)


SHORT = pl.CostEstimate(flops=1, bytes_accessed=1, transcendentals=0)


def gate(value, *after):
    return lax.optimization_barrier((value,) + after)[0]


def vmem(shape, dtype):
    return pltpu.VMEM(shape, dtype)


def dispatch_kernel(capacity, layout, section_ref, code_ref, *refs):
    blocks = refs[:-4]
    outs, held, sems = refs[-4:-2], refs[-2], refs[-1]
    count, rows = held.shape[0], held.shape[1]
    half = lax.rem(section_ref[0], 2)
    copies = []
    for place, pieces in enumerate(layout):
        group = []
        for i, (which, start, length, side) in enumerate(pieces):
            there = held.at[place]
            if side is not None:
                offset = (half if side == 0 else 1 - half) * length
                there = held.at[place, pl.ds(pl.multiple_of(offset, length), length)]
            here = blocks[which].at[pl.ds(start, length)]
            group.append(pltpu.make_async_copy(here, there, sems.at[place, i]))
        copies.append(group)
    for group in copies:
        for copy in group:
            copy.start()
    for place, group in enumerate(copies):
        picks = []
        for which in range(2):
            line = which * count + place
            code = code_ref[line : line + 1, :]
            slot = lax.broadcasted_iota(jnp.int32, (capacity, code.shape[1]), 0)
            picks.append(jnp.where(slot == code, 1.0, 0.0))
        pick = jnp.concatenate(picks, axis=0).astype(jnp.bfloat16)
        for copy in group:
            copy.wait()
        picked = jnp.dot(pick, held[place], preferred_element_type=jnp.float32)
        picked = picked.astype(jnp.bfloat16)
        for which, out_ref in enumerate(outs):
            out_ref[place * capacity : (place + 1) * capacity, :] = picked[
                which * capacity : (which + 1) * capacity
            ]


def dispatch(section, code, blocks, layout, capacity):
    rows, features = blocks[0].shape
    count = len(layout)
    picked = jax.ShapeDtypeStruct((count * capacity, features), jnp.bfloat16)
    return pl.pallas_call(
        functools.partial(dispatch_kernel, capacity, layout),
        out_shape=(picked, picked),
        in_specs=[
            pl.BlockSpec(memory_space=pltpu.SMEM),
            pl.BlockSpec(memory_space=pltpu.VMEM),
        ]
        + [pl.BlockSpec(memory_space=pltpu.HBM)] * len(blocks),
        out_specs=[pl.BlockSpec(memory_space=pltpu.VMEM)] * 2,
        scratch_shapes=[
            vmem((count, rows, features), jnp.bfloat16),
            pltpu.SemaphoreType.DMA((count, 2)),
        ],
        compiler_params=pltpu.CompilerParams(vmem_limit_bytes=10 * 1024 * 1024),
        cost_estimate=SHORT,
        name="dispatch",
    )(section, code, *blocks)


def send_home(part, codes, capacity):
    size = lax.axis_size(("expert", "dp"))
    arrived = []
    for place, code in enumerate(codes):
        block = part[place * capacity : (place + 1) * capacity]
        if code:
            block = lax.ppermute(block, ("expert", "dp"), [(i, i ^ code) for i in range(size)])
        arrived.append(block)
    return arrived


def combine_kernel(count, split, section_ref, position_ref, gates_ref, *refs):
    blocks = refs[:count]
    outs, (held, total) = refs[count:-2], refs[-2:]
    capacity, features = blocks[0].shape
    position = position_ref[...]
    slot = lax.broadcasted_iota(jnp.int32, (position.shape[0], count * capacity), 1)
    picks = [
        jnp.where(position[:, k : k + 1] == slot, 1.0, 0.0).astype(jnp.bfloat16) for k in range(2)
    ]
    for i, block in enumerate(blocks):
        held[i * capacity : (i + 1) * capacity, :] = block[...]
    pick = jnp.concatenate(picks, axis=0)
    rows = position.shape[0]
    both = jnp.dot(pick, held[...], preferred_element_type=jnp.float32)
    total[...] = gates_ref[:, 0:1] * both[:rows] + gates_ref[:, 1:2] * both[rows:]
    if split == 1:
        outs[0][...] = total[...].astype(outs[0].dtype)
        return
    sent_ref, kept_first, kept_second = outs
    width = features // split
    for step, out_ref in enumerate((kept_first, sent_ref.at[0], kept_second, sent_ref.at[1])):
        start = pl.multiple_of((section_ref[0] ^ step) * width, width)
        out_ref[...] = total[:, pl.ds(start, width)].astype(out_ref.dtype)


def combine(section, position, gates, blocks, split):
    capacity, features = blocks[0].shape
    rows = position.shape[0]
    count = len(blocks)
    width = features // split
    kept = jax.ShapeDtypeStruct((rows, width), jnp.float32)
    if split == 1:
        out_shape = (jax.ShapeDtypeStruct((rows, width), jnp.bfloat16),)
    else:
        out_shape = (jax.ShapeDtypeStruct((2, rows, width), jnp.bfloat16), kept, kept)
    full = pl.BlockSpec(memory_space=pltpu.VMEM)
    return pl.pallas_call(
        functools.partial(combine_kernel, count, split),
        out_shape=out_shape,
        in_specs=[pl.BlockSpec(memory_space=pltpu.SMEM)] + [full] * (2 + count),
        out_specs=[full] * len(out_shape),
        scratch_shapes=[
            vmem((count * capacity, features), jnp.bfloat16),
            vmem((rows, features), jnp.float32),
        ],
        compiler_params=pltpu.CompilerParams(vmem_limit_bytes=14 * 1024 * 1024),
        cost_estimate=SHORT,
        name="combine",
    )(section, position, gates, *blocks)


def memory_kernel(count, section_ref, tokens_ref, gain_ref, *refs):
    slices, out_ref, mixed = refs[:count], refs[count], refs[count + 1]
    me = section_ref[0]
    width = slices[0].shape[1]
    for step, piece in enumerate(slices):
        owner = me ^ step
        mixed[:, pl.ds(pl.multiple_of(owner * width, width), width)] = piece[...].astype(
            jnp.float32
        )
    values = tokens_ref[...].astype(jnp.float32) + mixed[...]
    out_ref[...] = normalize(values, gain_ref[...]).astype(jnp.bfloat16)


def make_memory(me, tokens, slices, gain):
    return pl.pallas_call(
        functools.partial(memory_kernel, len(slices)),
        out_shape=jax.ShapeDtypeStruct(tokens.shape, jnp.bfloat16),
        in_specs=[
            pl.BlockSpec(memory_space=pltpu.SMEM),
        ]
        + [pl.BlockSpec(memory_space=pltpu.VMEM)] * (2 + len(slices)),
        out_specs=pl.BlockSpec(memory_space=pltpu.VMEM),
        scratch_shapes=[vmem(tokens.shape, jnp.float32)],
        compiler_params=pltpu.CompilerParams(vmem_limit_bytes=8 * 1024 * 1024),
        cost_estimate=SHORT,
        name="memory",
    )(me, tokens, gain[None], *slices)


def normed_kernel(y_ref, states_ref, gain_ref, own_ref, other_ref):
    values = normalize(states_ref[...].astype(jnp.float32), gain_ref[...]).astype(jnp.bfloat16)
    width = own_ref.shape[1]
    for out_ref, first in ((own_ref, y_ref[0] == 0), (other_ref, y_ref[0] == 1)):
        out_ref[...] = jnp.where(first, values[:, :width], values[:, width:])


def normed_halves(y, states, gain):
    rows, features = states.shape
    full = pl.BlockSpec(memory_space=pltpu.VMEM)
    return pl.pallas_call(
        normed_kernel,
        out_shape=(jax.ShapeDtypeStruct((rows, features // 2), jnp.bfloat16),) * 2,
        in_specs=[pl.BlockSpec(memory_space=pltpu.SMEM), full, full],
        out_specs=[full] * 2,
        compiler_params=pltpu.CompilerParams(vmem_limit_bytes=12 * 1024 * 1024),
        cost_estimate=SHORT,
        name="normed",
    )(y.astype(jnp.int32).reshape(1), states, gain)


def attend_kernel(place_ref, lengths_ref, query_ref, *refs):
    near_ref, far_ref, key_own, key_other, value_own, value_other, out_ref = refs[:7]
    source, key_weight, value_weight, keys, values, sems = refs[7:]
    y, core, sentence = place_ref[0], place_ref[1], place_ref[2]
    rows = near_ref.shape[0]
    depth = key_own.shape[0]
    moves = [
        (near_ref, source.at[pl.ds(0, rows)]),
        (far_ref, source.at[pl.ds(rows, rows)]),
        (key_own, key_weight.at[y]),
        (key_other, key_weight.at[1 - y]),
        (value_own, value_weight.at[y]),
        (value_other, value_weight.at[1 - y]),
    ]
    copies = [
        pltpu.make_async_copy(here, there, sems.at[i]) for i, (here, there) in enumerate(moves)
    ]
    for copy in copies:
        copy.start()

    def linear(weight, result):
        total = jnp.dot(source[:, :depth], weight[0], preferred_element_type=jnp.float32)
        total += jnp.dot(source[:, depth:], weight[1], preferred_element_type=jnp.float32)
        result[...] = total.astype(jnp.bfloat16)

    for copy in copies[:4]:
        copy.wait()
    linear(key_weight, keys)
    for copy in copies[4:]:
        copy.wait()
    linear(value_weight, values)

    column = lax.broadcasted_iota(jnp.int32, (query_ref.shape[0], 2 * rows), 1)
    position = jnp.where(column < rows, column + core * rows, column - core * rows)
    valid = position < lengths_ref[sentence]
    for head in range(query_ref.shape[1] // HEAD_DIM):
        span = slice(head * HEAD_DIM, (head + 1) * HEAD_DIM)
        scores = contract_last(query_ref[:, span], keys[:, span]) * HEAD_DIM ** (-0.5)
        scores = jnp.where(valid, scores, -1e30)
        weights = jnp.exp(scores - jnp.max(scores, axis=-1, keepdims=True))
        probs = (weights / jnp.sum(weights, axis=-1, keepdims=True)).astype(jnp.bfloat16)
        result = jnp.dot(probs, values[:, span], preferred_element_type=jnp.float32)
        out_ref[:, span] = result.astype(jnp.bfloat16)


def attend_sentence(place, lengths, query, near, far, key_parts, value_pair):
    rows, features = near.shape
    depth, width = key_parts[0].shape
    hold = pl.BlockSpec(memory_space=pltpu.HBM)
    smem = pl.BlockSpec(memory_space=pltpu.SMEM)
    full = pl.BlockSpec(memory_space=pltpu.VMEM)
    return pl.pallas_call(
        attend_kernel,
        out_shape=jax.ShapeDtypeStruct(query.shape, jnp.bfloat16),
        in_specs=[smem, smem, full] + [hold] * 6,
        out_specs=full,
        scratch_shapes=[
            vmem((2 * rows, features), jnp.bfloat16),
            vmem((2, depth, width), jnp.bfloat16),
            vmem((2, depth, width), jnp.bfloat16),
            vmem((2 * rows, width), jnp.bfloat16),
            vmem((2 * rows, width), jnp.bfloat16),
            pltpu.SemaphoreType.DMA((6,)),
        ],
        compiler_params=pltpu.CompilerParams(vmem_limit_bytes=56 * 1024 * 1024),
        cost_estimate=SHORT,
        name="attend_sentence",
    )(place, lengths, query, near, far, *key_parts, *value_pair)


def project_kernel(place_ref, mine_ref, done_ref, own_ref, other_ref, *refs):
    sent_mine, sent_other, kept_mine, kept_other, context = refs
    y, core, x = place_ref[0], place_ref[1], place_ref[2]
    targets = mine_ref.shape[0]
    for part, sentence in ((mine_ref, x), (done_ref, 1 - x)):
        context[pl.ds(pl.multiple_of(sentence * targets, targets), targets), :] = part[...]
    columns = kept_mine.shape[1]
    outs = ((sent_mine, kept_mine), (sent_other, kept_other))

    def write(weight_ref, chosen):
        for side, out_ref in zip((1 - core, core), chosen):
            span = pl.ds(pl.multiple_of(side * columns, columns), columns)
            part = jnp.dot(context[...], weight_ref[:, span], preferred_element_type=jnp.float32)
            out_ref[...] = part.astype(out_ref.dtype)

    @pl.when(x == y)
    def _():
        write(own_ref, outs[0])
        write(other_ref, outs[1])

    @pl.when(x != y)
    def _():
        write(other_ref, outs[0])
        write(own_ref, outs[1])


def project(place, mine, done, out_own, out_other):
    targets, width = 2 * mine.shape[0], mine.shape[1]
    columns = out_own.shape[1] // 2
    full = pl.BlockSpec(memory_space=pltpu.VMEM)
    sent = jax.ShapeDtypeStruct((targets, columns), jnp.bfloat16)
    kept = jax.ShapeDtypeStruct((targets, columns), jnp.float32)
    return pl.pallas_call(
        project_kernel,
        out_shape=(sent, sent, kept, kept),
        in_specs=[pl.BlockSpec(memory_space=pltpu.SMEM)] + [full] * 4,
        out_specs=[full] * 4,
        scratch_shapes=[vmem((targets, width), jnp.bfloat16)],
        compiler_params=pltpu.CompilerParams(vmem_limit_bytes=16 * 1024 * 1024),
        cost_estimate=SHORT,
        name="project",
    )(place, mine, done, out_own, out_other)


def slope_kernel(codes, here_ref, own_ref, core_ref, rise_own, rise_core, out_ref, slope, *refs):
    grads, rise, weight_out, sems = refs
    rows = own_ref.shape[0]
    hidden = weight_out.shape[0]
    chunk = hidden // 4
    moves = []
    block = 2 * rows // len(codes)
    for order, code in enumerate(codes):
        source = here_ref[0] ^ code
        there = pl.ds(pl.multiple_of(source * block, 16), block)
        here = pl.ds(order * block % rows, block)
        own = order * block < rows
        moves.append(((own_ref if own else core_ref).at[here], grads.at[there]))
        moves.append(((rise_own if own else rise_core).at[here], rise.at[there]))
    for part in range(4):
        span = pl.ds(part * chunk, chunk)
        moves.append((out_ref.at[span], weight_out.at[span]))
    copies = [
        pltpu.make_async_copy(here, there, sems.at[i]) for i, (here, there) in enumerate(moves)
    ]
    for copy in copies:
        copy.start()
    for copy in copies[:-4]:
        copy.wait()
    for part in range(4):
        copies[part - 4].wait()
        span = slice(part * chunk, (part + 1) * chunk)
        back = contract_last(grads[...], weight_out[span, :])
        slope[:, span] = (back * rise[:, span]).astype(jnp.bfloat16)


def expert_slope(here, codes, grads_own, grads_core, rise_own, rise_core, weight_out):
    rows = 2 * grads_own.shape[0]
    hidden, features = weight_out.shape
    hold = pl.BlockSpec(memory_space=pltpu.HBM)
    return pl.pallas_call(
        functools.partial(slope_kernel, codes),
        out_shape=jax.ShapeDtypeStruct((rows, hidden), jnp.bfloat16),
        in_specs=[pl.BlockSpec(memory_space=pltpu.SMEM)] + [hold] * 5,
        out_specs=pl.BlockSpec(memory_space=pltpu.VMEM),
        scratch_shapes=[
            vmem((rows, features), jnp.bfloat16),
            vmem((rows, hidden), jnp.float32),
            vmem((hidden, features), jnp.bfloat16),
            pltpu.SemaphoreType.DMA((4 + 2 * len(codes),)),
        ],
        compiler_params=pltpu.CompilerParams(vmem_limit_bytes=56 * 1024 * 1024),
        cost_estimate=SHORT,
        name="expert_slope",
    )(here, grads_own, grads_core, rise_own, rise_core, weight_out)


def backward_kernel(split, section_ref, slope_ref, in_ref, sent_ref, kept_first, kept_second, *refs):
    weight_in, sems = refs
    width = weight_in.shape[0] // split
    outs = (sent_ref.at[0], sent_ref.at[1], kept_first, kept_second)
    spans, copies = [], []
    for i, step in enumerate((1, 3, 0, 2)):
        start = pl.multiple_of((section_ref[0] ^ step) * width, width)
        spans.append(pl.ds(start, width))
        copies.append(
            pltpu.make_async_copy(in_ref.at[spans[i]], weight_in.at[spans[i]], sems.at[i])
        )
    for copy in copies:
        copy.start()
    for copy, span, out_ref in zip(copies, spans, outs):
        copy.wait()
        part = contract_last(slope_ref[...], weight_in[span, :])
        out_ref[...] = part.astype(out_ref.dtype)


def expert_backward(section, slope, weight_in, split):
    rows, hidden = slope.shape
    features = weight_in.shape[0]
    width = features // split
    full = pl.BlockSpec(memory_space=pltpu.VMEM)
    kept = jax.ShapeDtypeStruct((rows, width), jnp.float32)
    return pl.pallas_call(
        functools.partial(backward_kernel, split),
        out_shape=(jax.ShapeDtypeStruct((2, rows, width), jnp.bfloat16), kept, kept),
        in_specs=[pl.BlockSpec(memory_space=pltpu.SMEM), full, pl.BlockSpec(memory_space=pltpu.HBM)],
        out_specs=[full] * 3,
        scratch_shapes=[
            vmem((features, hidden), jnp.bfloat16),
            pltpu.SemaphoreType.DMA((split,)),
        ],
        compiler_params=pltpu.CompilerParams(vmem_limit_bytes=56 * 1024 * 1024),
        cost_estimate=SHORT,
        name="expert_backward",
    )(section, slope, weight_in)


def small_body(
    tokens,
    expert_ids,
    gate_weights,
    out_grad,
    inner_weight,
    outer_weight,
    final_gain,
    dec_states,
    src_lengths,
    tgt_lengths,
    norm_gain,
    query_weight,
    key_weight,
    value_weight,
    out_weight,
):
    token_count, feature_count = tokens.shape
    group_size = lax.axis_size(("expert", "dp"))
    capacity = 3 * token_count // group_size
    here = lax.axis_index(("expert", "dp"))
    y = lax.axis_index("expert")
    d = lax.axis_index("dp")
    section = lax.axis_index("section")
    sections = lax.axis_size("section")
    half = feature_count // 2
    weight_in = inner_weight[0]
    weight_out = outer_weight[0]
    key_own, value_own, out_own = key_weight[0], value_weight[0], out_weight[0]
    query_own = query_weight[0]

    size = group_size
    near_codes = (0, 2, 4, 6)
    core_codes = (1, 3, 5, 7)
    core, x = d % 2, d // 2
    which_section = section.astype(jnp.int32).reshape(1)

    token_y = swap(tokens, "expert", 1)
    token_x = swap(tokens, "dp", 2)
    row = lax.broadcasted_iota(jnp.int32, (token_count, token_count), 0)
    column = lax.broadcasted_iota(jnp.int32, (token_count, token_count), 1)
    named = expert_ids[:, :, None] == jnp.arange(size, dtype=jnp.int32)[None, None, :]
    either = (named[:, 0] | named[:, 1]).astype(jnp.bfloat16)
    earlier = jnp.dot(
        (column < row).astype(jnp.bfloat16), either, preferred_element_type=jnp.float32
    ).astype(jnp.int32)
    rank = jnp.sum(jnp.where(named, earlier[:, None, :], 0), axis=2)
    codes_of = expert_ids ^ here
    position = ((codes_of >> 1) + 4 * (codes_of & 1)) * capacity + rank

    ids_own = expert_ids.T
    ids_x, ids_y = swap(ids_own, "dp", 2), swap(ids_own, "expert", 1)
    ids_far = swap(ids_x, "expert", 1)
    token_far = swap(gate(token_y, ids_x, ids_y), "dp", 2)

    side = lax.rem(section, 2)
    share = token_count // 2
    grad_half = lax.dynamic_slice_in_dim(out_grad, side * share, share, 0)
    half_y = swap(gate(grad_half, token_y), "expert", 1)
    states = dec_states[0]
    normed_own, asked = normed_halves(y, states, norm_gain)
    asked_here = swap(gate(asked, half_y), "expert", 1)
    query_there = jnp.dot(asked_here, query_own, preferred_element_type=jnp.float32)
    other_y = swap(half_y, "section", 1)
    half_x = swap(gate(grad_half, token_far), "dp", 2)

    ids = jnp.stack([ids_own, ids_x, ids_y, ids_far])
    named_there = jnp.concatenate([(ids == here).any(axis=1), (ids == (here ^ 1)).any(axis=1)])
    before = jnp.dot(
        named_there.astype(jnp.bfloat16),
        (row < column).astype(jnp.bfloat16),
        preferred_element_type=jnp.float32,
    ).astype(jnp.int32)
    code = jnp.where(named_there, before, -1)

    def forward(rows, *after):
        pre_act = jnp.dot(rows, weight_in, preferred_element_type=jnp.float32)
        hidden = jax.nn.gelu(gate(pre_act, *after)).astype(jnp.bfloat16)
        part = jnp.dot(hidden, weight_out, preferred_element_type=jnp.float32)
        return pre_act, part.astype(jnp.bfloat16)

    def slope_of(pre_act):
        return jax.vjp(jax.nn.gelu, pre_act)[1](jnp.ones_like(pre_act))[0]

    rows_own, rows_sent = dispatch(
        which_section,
        gate(code, asked),
        [tokens, token_x, token_y, token_far],
        tuple(((place, 0, token_count, None),) for place in range(4)),
        capacity,
    )
    rows_core = swap(rows_sent, "dp", 1)
    pre_own, part_own = forward(rows_own, other_y, half_x)
    pre_core, part_core = forward(gate(rows_core, part_own))
    home = send_home(part_own, near_codes, capacity) + send_home(part_core, core_codes, capacity)
    other_x = swap(gate(half_x, home[1], home[2], home[3]), "section", 1)
    grad_y = jnp.concatenate([gate(half_y, home[4]), other_y], axis=0)
    query_back = swap(gate(query_there.astype(jnp.bfloat16), home[5], home[6]), "expert", 1)

    rise_own, rise_core = slope_of(gate(pre_own, home[5])), slope_of(gate(pre_core, home[5]))
    held_gates = gate(gate_weights, rise_own, rise_core, query_there, grad_y, other_x)
    sent_pair, first, second = combine(which_section, position, held_gates, home, sections)
    from_pair = swap(sent_pair, "section", 1)
    grad_far = swap(gate(grad_y, first), "dp", 2)
    to_other = (second + from_pair[1].astype(jnp.float32)).astype(jnp.bfloat16)
    from_other = swap(to_other, "section", 2)
    grads_own, grads_sent = dispatch(
        which_section,
        gate(code, to_other),
        [out_grad, half_x, other_x, grad_y, grad_far],
        (
            ((0, 0, token_count, None),),
            ((1, 0, share, 0), (2, 0, share, 1)),
            ((3, 0, share, 0), (3, share, share, 1)),
            ((4, 0, share, 0), (4, share, share, 1)),
        ),
        capacity,
    )
    grads_core = swap(grads_sent, "dp", 1)
    grads_core = swap(grads_sent, "dp", 1)
    mixed_sum = gate(first, query_back, grads_sent) + from_pair[0].astype(jnp.float32)
    mixed_slice = (mixed_sum + from_other.astype(jnp.float32)).astype(jnp.bfloat16)
    key_other = swap(gate(key_own, first), "expert", 1)
    mixed_near = swap(mixed_slice, "section", 1)
    slope = expert_slope(
        gate(here.astype(jnp.int32).reshape(1), mixed_near, key_other),
        near_codes + core_codes,
        grads_own,
        grads_core,
        rise_own,
        rise_core,
        weight_out,
    )
    back_pair, back_first, back_second = expert_backward(
        which_section, slope, weight_in, sections
    )
    mixed_far = swap(jnp.stack([mixed_slice, mixed_near]), "section", 2)
    slices = [mixed_slice, mixed_near, mixed_far[0], mixed_far[1]]

    value_other = swap(gate(value_own, mixed_near), "expert", 1)

    query_here = jnp.dot(normed_own, query_own, preferred_element_type=jnp.float32)
    query = (query_here + query_back.astype(jnp.float32)).astype(jnp.bfloat16)

    memory = make_memory(which_section, tokens, slices, final_gain)
    out_other = swap(gate(out_own, memory), "expert", 1)
    memory_x = swap(memory, "dp", 2)
    memory_core = swap(memory, "dp", 1)

    def sentence(which, near, far, *after):
        place = gate(jnp.stack([y, core, which]).astype(jnp.int32), *after)
        rows_of = lax.dynamic_slice_in_dim(query, which * TGT_LEN, TGT_LEN, 0)
        parts = (key_own, key_other), (value_own, value_other)
        return attend_sentence(place, src_lengths, rows_of, near, far, *parts)

    back_from_pair = swap(back_pair, "section", 1)
    back_to_other = (back_second + back_from_pair[1].astype(jnp.float32)).astype(jnp.bfloat16)
    back_from_other = swap(back_to_other, "section", 2)
    backward_sum = back_first + back_from_pair[0].astype(jnp.float32)
    backward_sum = backward_sum + back_from_other.astype(jnp.float32)
    context_own = sentence(x, memory, memory_core)
    memory_far = swap(gate(memory_x, context_own), "dp", 1)
    context_other = sentence(1 - x, memory_x, memory_far)
    place = jnp.stack([y, core, x]).astype(jnp.int32)
    sent_mine, sent_other, kept_mine, kept_other = project(
        place, context_own, context_other, out_own, out_other
    )

    core_other = swap(sent_other, "dp", 1)
    core_mine = swap(sent_mine, "dp", 1)
    last = gate(kept_other, back_from_other) + core_other.astype(jnp.float32)
    from_x = swap(last.astype(jnp.bfloat16), "dp", 2)
    attended = kept_mine + core_mine.astype(jnp.float32) + from_x.astype(jnp.float32)
    dec_out = add_residual(attended, states, tgt_lengths)

    grads_home = exchange(gate(backward_sum.astype(jnp.bfloat16), last), group_size, capacity)
    natural = expert_ids * capacity + rank
    (token_grad,) = combine(
        which_section, natural, gate_weights, [grads_home], 1
    )
    return (dec_out[None], token_grad)


def add_residual(attended, states, tgt_lengths):
    my_columns = attended.shape[1]
    residual = lax.dynamic_slice_in_dim(
        states, lax.axis_index("dp") * my_columns, my_columns, 1
    ).astype(jnp.float32)
    row_mask = (jnp.arange(TGT_LEN, dtype=jnp.int32)[None, :] < tgt_lengths[:, None]).reshape(-1, 1)
    return (residual + jnp.where(row_mask, attended, 0.0)).astype(jnp.bfloat16)


def body(
    tokens,
    expert_ids,
    gate_weights,
    out_grad,
    inner_weight,
    outer_weight,
    final_gain,
    dec_states,
    src_lengths,
    tgt_lengths,
    norm_gain,
    query_weight,
    key_weight,
    value_weight,
    out_weight,
):
    token_count, feature_count = tokens.shape
    group_size = lax.axis_size(("expert", "dp"))
    capacity = 3 * token_count // group_size
    slots = group_size * capacity

    named = expert_ids[:, :, None] == jnp.arange(group_size, dtype=jnp.int32)[None, None, :]
    either = (named[:, 0] | named[:, 1]).astype(jnp.bfloat16)
    row = lax.broadcasted_iota(jnp.int32, (token_count, token_count), 0)
    column = lax.broadcasted_iota(jnp.int32, (token_count, token_count), 1)
    earlier = jnp.dot(
        (column < row).astype(jnp.bfloat16), either, preferred_element_type=jnp.float32
    ).astype(jnp.int32)
    rank = jnp.sum(jnp.where(named, earlier[:, None, :], 0), axis=2)
    position = expert_ids * capacity + rank
    pick_first = slot_matrix(position[:, 0], slots)
    pick_second = slot_matrix(position[:, 1], slots)
    fill = (pick_first + pick_second).T

    def place(values):
        return jnp.dot(fill, values, preferred_element_type=jnp.float32).astype(jnp.bfloat16)

    def combine(arrived):
        first = jnp.dot(pick_first, arrived, preferred_element_type=jnp.float32)
        second = jnp.dot(pick_second, arrived, preferred_element_type=jnp.float32)
        return gate_weights[:, :1] * first + gate_weights[:, 1:] * second

    weight_in = inner_weight[0]
    weight_out = outer_weight[0]
    arrived_rows = exchange(place(tokens), group_size, capacity)
    pre_act = jnp.dot(arrived_rows, weight_in, preferred_element_type=jnp.float32)
    hidden = jax.nn.gelu(pre_act).astype(jnp.bfloat16)
    forward_part = jnp.dot(hidden, weight_out, preferred_element_type=jnp.float32)
    arrived_grads = exchange(place(out_grad), group_size, capacity)
    outputs_home = exchange(forward_part.astype(jnp.bfloat16), group_size, capacity)
    mixed_slice = sum_sections(combine(outputs_home)).astype(jnp.bfloat16)
    mixed = gather_sections(mixed_slice).astype(jnp.float32)
    memory = normalize(tokens.astype(jnp.float32) + mixed, final_gain).astype(jnp.bfloat16)

    back = contract_last(arrived_grads, weight_out)
    slope = jax.vjp(jax.nn.gelu, pre_act)[1](back)[0].astype(jnp.bfloat16)
    backward_part = contract_last(slope, weight_in)
    backward_slice = sum_sections(backward_part).astype(jnp.bfloat16)
    grads_home = exchange(backward_slice, group_size, capacity)
    token_grad = combine(grads_home).astype(jnp.bfloat16)

    states = dec_states[0]
    normed = normalize(states.astype(jnp.float32), norm_gain[0]).astype(jnp.bfloat16)
    full_query = gather_weight(query_weight[0], 0)
    full_key = gather_weight(key_weight[0], 0)
    full_value = gather_weight(value_weight[0], 0)
    full_out = gather_weight(out_weight[0], 1)
    query_sum = jnp.dot(normed, full_query, preferred_element_type=jnp.float32)
    source = gather_rows(memory, "dp")
    key_sum = jnp.dot(source, full_key, preferred_element_type=jnp.float32)
    value_sum = jnp.dot(source, full_value, preferred_element_type=jnp.float32)
    key_mask = jnp.arange(SRC_LEN, dtype=jnp.int32)[None, :] < src_lengths[:, None]
    context = attend(
        query_sum.astype(jnp.bfloat16),
        key_sum.astype(jnp.bfloat16),
        value_sum.astype(jnp.bfloat16),
        key_mask,
    )
    attended = sum_heads(jnp.dot(context, full_out, preferred_element_type=jnp.float32))
    dec_out = add_residual(attended, states, tgt_lengths)
    return (dec_out[None], token_grad)


def solution(mesh):
    in_specs = (
        P(("expert", "dp"), None),
        P(("expert", "dp"), None),
        P(("expert", "dp"), None),
        P(("expert", "dp"), None),
        P(("expert", "dp"), None, "section"),
        P(("expert", "dp"), "section", None),
        P(),
        P("section", "expert", None),
        P("expert"),
        P("expert"),
        P("section", None),
        P("section", "expert", "dp"),
        P("section", "expert", "dp"),
        P("section", "expert", "dp"),
        P("section", "dp", "expert"),
    )
    out_specs = (P("section", "expert", "dp"), P(("expert", "dp"), "section"))
    small = (mesh.shape["section"], mesh.shape["expert"], mesh.shape["dp"]) == (4, 2, 4)
    chosen = small_body if small else body
    return jax.shard_map(chosen, mesh=mesh, in_specs=in_specs, out_specs=out_specs, check_vma=False)
```

```python
import functools

import jax
import jax.numpy as jnp
from jax import lax
from jax.experimental import pallas as pl
from jax.experimental.pallas import tpu as pltpu
from jax.sharding import PartitionSpec as P

HEAD_DIM = 128
SRC_LEN = 256
TGT_LEN = 128


EPSILON = 1e-05


def normalize(values, gain):
    centre = jnp.mean(values, axis=-1, keepdims=True)
    centred = values - centre
    spread = jnp.mean(centred * centred, axis=-1, keepdims=True)
    return centred * lax.rsqrt(spread + EPSILON) * gain


def contract_last(left, right):
    return lax.dot_general(
        left, right, (((1,), (1,)), ((), ())), preferred_element_type=jnp.float32
    )


def shift(value, axis, step):
    size = lax.axis_size(axis)
    return lax.ppermute(value, axis, [(i, (i + step) % size) for i in range(size)])


def swap(value, axis, mask):
    size = lax.axis_size(axis)
    return lax.ppermute(value, axis, [(i, i ^ mask) for i in range(size)])


def sum_sections(partial):
    count = lax.axis_size("section")
    me = lax.axis_index("section")
    width = partial.shape[1] // count

    def piece(owner):
        return lax.dynamic_slice_in_dim(partial, owner * width, width, 1)

    total = piece(me).astype(jnp.float32)
    for step in range(1, count):
        sent = piece(lax.rem(me + step, count)).astype(jnp.bfloat16)
        total = total + shift(sent, "section", step).astype(jnp.float32)
    return total


def gather_sections(mine):
    count = lax.axis_size("section")
    me = lax.axis_index("section")
    width = mine.shape[1]
    whole = jnp.zeros((mine.shape[0], width * count), mine.dtype)
    whole = lax.dynamic_update_slice_in_dim(whole, mine, me * width, 1)
    for step in range(1, count):
        owner = lax.rem(me - step + count, count)
        whole = lax.dynamic_update_slice_in_dim(
            whole, shift(mine, "section", step), owner * width, 1
        )
    return whole


def gather_rows(mine, axis):
    held = mine
    me = lax.axis_index(axis)
    mask = lax.axis_size(axis) // 2
    blocks = [mine]
    while mask >= 1:
        blocks = blocks + [swap(block, axis, mask) for block in blocks]
        mask //= 2
    codes = [0]
    mask = lax.axis_size(axis) // 2
    while mask >= 1:
        codes = codes + [code ^ mask for code in codes]
        mask //= 2
    ordered = []
    for place in range(len(blocks)):
        chosen = blocks[0]
        for code, block in zip(codes[1:], blocks[1:]):
            chosen = jnp.where((me ^ code) == place, block, chosen)
        ordered.append(chosen)
    return jnp.concatenate(ordered, axis=0)


def gather_weight(weight, dimension):
    if lax.axis_size("expert") != 2:
        return lax.all_gather(weight, "expert", axis=dimension, tiled=True)
    other = swap(weight, "expert", 1)
    first = lax.axis_index("expert") == 0
    return jnp.concatenate(
        [jnp.where(first, weight, other), jnp.where(first, other, weight)], axis=dimension
    )


def sum_heads(partial):
    me = lax.axis_index("dp")
    count = lax.axis_size("dp")
    rows, columns = partial.shape
    total = partial.reshape(rows, count, columns // count)
    mask = 1
    while mask < count:
        paired = total.reshape(rows, -1, 2, columns // count)
        bit = (me // mask) % 2
        sent = lax.dynamic_index_in_dim(paired, 1 - bit, 2, False).astype(jnp.bfloat16)
        kept = lax.dynamic_index_in_dim(paired, bit, 2, False)
        total = kept + swap(sent, "dp", mask).astype(jnp.float32)
        mask *= 2
    return total.reshape(rows, columns // count)


def slot_matrix(positions, slots):
    places = lax.broadcasted_iota(jnp.int32, (positions.shape[0], slots), 1)
    return (positions[:, None] == places).astype(jnp.bfloat16)


def attend(query, keys, values, key_mask):
    sequences = key_mask.shape[0]
    head_count = query.shape[1] // HEAD_DIM
    query_split = query.reshape(sequences, -1, head_count, HEAD_DIM)
    keys_split = keys.reshape(sequences, -1, head_count, HEAD_DIM)
    values_split = values.reshape(sequences, -1, head_count, HEAD_DIM)
    scores = jnp.einsum(
        "bqhd,bkhd->bhqk", query_split, keys_split, preferred_element_type=jnp.float32
    ) * HEAD_DIM ** (-0.5)
    scores = jnp.where(key_mask[:, None, None, :], scores, -1e30)
    highest = jnp.max(scores, axis=-1, keepdims=True)
    weights = jnp.exp(scores - highest)
    probs = (weights / jnp.sum(weights, axis=-1, keepdims=True)).astype(jnp.bfloat16)
    context = jnp.einsum("bhqk,bkhd->bqhd", probs, values_split, preferred_element_type=jnp.float32)
    return context.astype(jnp.bfloat16).reshape(-1, head_count * HEAD_DIM)


def exchange(values, group_size, capacity):
    sent = values.reshape(group_size, capacity, values.shape[1])
    arrived = lax.all_to_all(sent, ("expert", "dp"), split_axis=0, concat_axis=0, tiled=True)
    return arrived.reshape(values.shape)


SHORT = pl.CostEstimate(flops=1, bytes_accessed=1, transcendentals=0)


def gate(value, *after):
    return lax.optimization_barrier((value,) + after)[0]


def vmem(shape, dtype):
    return pltpu.VMEM(shape, dtype)


def dispatch_kernel(capacity, layout, section_ref, code_ref, *refs):
    blocks = refs[:-4]
    outs, held, sems = refs[-4:-2], refs[-2], refs[-1]
    count, rows = held.shape[0], held.shape[1]
    half = lax.rem(section_ref[0], 2)
    copies = []
    for place, pieces in enumerate(layout):
        group = []
        for i, (which, start, length, side) in enumerate(pieces):
            there = held.at[place]
            if side is not None:
                offset = (half if side == 0 else 1 - half) * length
                there = held.at[place, pl.ds(pl.multiple_of(offset, length), length)]
            here = blocks[which].at[pl.ds(start, length)]
            group.append(pltpu.make_async_copy(here, there, sems.at[place, i]))
        copies.append(group)
    for group in copies:
        for copy in group:
            copy.start()
    for place, group in enumerate(copies):
        picks = []
        for which in range(2):
            line = which * count + place
            code = code_ref[line : line + 1, :]
            slot = lax.broadcasted_iota(jnp.int32, (capacity, code.shape[1]), 0)
            picks.append(jnp.where(slot == code, 1.0, 0.0))
        pick = jnp.concatenate(picks, axis=0).astype(jnp.bfloat16)
        for copy in group:
            copy.wait()
        picked = jnp.dot(pick, held[place], preferred_element_type=jnp.float32)
        picked = picked.astype(jnp.bfloat16)
        for which, out_ref in enumerate(outs):
            out_ref[place * capacity : (place + 1) * capacity, :] = picked[
                which * capacity : (which + 1) * capacity
            ]


def dispatch(section, code, blocks, layout, capacity):
    rows, features = blocks[0].shape
    count = len(layout)
    picked = jax.ShapeDtypeStruct((count * capacity, features), jnp.bfloat16)
    return pl.pallas_call(
        functools.partial(dispatch_kernel, capacity, layout),
        out_shape=(picked, picked),
        in_specs=[
            pl.BlockSpec(memory_space=pltpu.SMEM),
            pl.BlockSpec(memory_space=pltpu.VMEM),
        ]
        + [pl.BlockSpec(memory_space=pltpu.HBM)] * len(blocks),
        out_specs=[pl.BlockSpec(memory_space=pltpu.VMEM)] * 2,
        scratch_shapes=[
            vmem((count, rows, features), jnp.bfloat16),
            pltpu.SemaphoreType.DMA((count, 2)),
        ],
        compiler_params=pltpu.CompilerParams(vmem_limit_bytes=10 * 1024 * 1024),
        cost_estimate=SHORT,
        name="dispatch",
    )(section, code, *blocks)


def send_home(part, codes, capacity):
    size = lax.axis_size(("expert", "dp"))
    arrived = []
    for place, code in enumerate(codes):
        block = part[place * capacity : (place + 1) * capacity]
        if code:
            block = lax.ppermute(block, ("expert", "dp"), [(i, i ^ code) for i in range(size)])
        arrived.append(block)
    return arrived


def combine_kernel(count, split, section_ref, position_ref, gates_ref, *refs):
    blocks = refs[:count]
    outs, (held, total, sems) = refs[count:-3], refs[-3:]
    capacity, features = blocks[0].shape
    copies = [
        pltpu.make_async_copy(block, held.at[pl.ds(i * capacity, capacity)], sems.at[i])
        for i, block in enumerate(blocks)
    ]
    for copy in copies:
        copy.start()
    position = position_ref[...]
    slot = lax.broadcasted_iota(jnp.int32, (position.shape[0], count * capacity), 1)
    picks = [
        jnp.where(position[:, k : k + 1] == slot, 1.0, 0.0).astype(jnp.bfloat16) for k in range(2)
    ]
    for copy in copies:
        copy.wait()
    pick = jnp.concatenate(picks, axis=0)
    rows = position.shape[0]
    both = jnp.dot(pick, held[...], preferred_element_type=jnp.float32)
    total[...] = gates_ref[:, 0:1] * both[:rows] + gates_ref[:, 1:2] * both[rows:]
    if split == 1:
        outs[0][...] = total[...].astype(outs[0].dtype)
        return
    sent_ref, kept_first, kept_second = outs
    width = features // split
    for step, out_ref in enumerate((kept_first, sent_ref.at[0], kept_second, sent_ref.at[1])):
        start = pl.multiple_of((section_ref[0] ^ step) * width, width)
        out_ref[...] = total[:, pl.ds(start, width)].astype(out_ref.dtype)


def combine(section, position, gates, blocks, split):
    capacity, features = blocks[0].shape
    rows = position.shape[0]
    count = len(blocks)
    width = features // split
    kept = jax.ShapeDtypeStruct((rows, width), jnp.float32)
    if split == 1:
        out_shape = (jax.ShapeDtypeStruct((rows, width), jnp.bfloat16),)
    else:
        out_shape = (jax.ShapeDtypeStruct((2, rows, width), jnp.bfloat16), kept, kept)
    full = pl.BlockSpec(memory_space=pltpu.VMEM)
    return pl.pallas_call(
        functools.partial(combine_kernel, count, split),
        out_shape=out_shape,
        in_specs=[pl.BlockSpec(memory_space=pltpu.SMEM), full, full]
        + [pl.BlockSpec(memory_space=pltpu.HBM)] * count,
        out_specs=[full] * len(out_shape),
        scratch_shapes=[
            vmem((count * capacity, features), jnp.bfloat16),
            vmem((rows, features), jnp.float32),
            pltpu.SemaphoreType.DMA((count,)),
        ],
        compiler_params=pltpu.CompilerParams(vmem_limit_bytes=56 * 1024 * 1024),
        cost_estimate=SHORT,
        name="combine",
    )(section, position, gates, *blocks)


def memory_kernel(count, section_ref, tokens_ref, gain_ref, *refs):
    slices, out_ref, mixed = refs[:count], refs[count], refs[count + 1]
    me = section_ref[0]
    width = slices[0].shape[1]
    for step, piece in enumerate(slices):
        owner = me ^ step
        mixed[:, pl.ds(pl.multiple_of(owner * width, width), width)] = piece[...].astype(
            jnp.float32
        )
    values = tokens_ref[...].astype(jnp.float32) + mixed[...]
    out_ref[...] = normalize(values, gain_ref[...]).astype(jnp.bfloat16)


def make_memory(me, tokens, slices, gain):
    return pl.pallas_call(
        functools.partial(memory_kernel, len(slices)),
        out_shape=jax.ShapeDtypeStruct(tokens.shape, jnp.bfloat16),
        in_specs=[
            pl.BlockSpec(memory_space=pltpu.SMEM),
        ]
        + [pl.BlockSpec(memory_space=pltpu.VMEM)] * (2 + len(slices)),
        out_specs=pl.BlockSpec(memory_space=pltpu.VMEM),
        scratch_shapes=[vmem(tokens.shape, jnp.float32)],
        compiler_params=pltpu.CompilerParams(vmem_limit_bytes=8 * 1024 * 1024),
        cost_estimate=SHORT,
        name="memory",
    )(me, tokens, gain[None], *slices)


def normed_kernel(y_ref, states_ref, gain_ref, own_ref, other_ref):
    values = normalize(states_ref[...].astype(jnp.float32), gain_ref[...]).astype(jnp.bfloat16)
    width = own_ref.shape[1]
    for out_ref, first in ((own_ref, y_ref[0] == 0), (other_ref, y_ref[0] == 1)):
        out_ref[...] = jnp.where(first, values[:, :width], values[:, width:])


def normed_halves(y, states, gain):
    rows, features = states.shape
    full = pl.BlockSpec(memory_space=pltpu.VMEM)
    return pl.pallas_call(
        normed_kernel,
        out_shape=(jax.ShapeDtypeStruct((rows, features // 2), jnp.bfloat16),) * 2,
        in_specs=[pl.BlockSpec(memory_space=pltpu.SMEM), full, full],
        out_specs=[full] * 2,
        compiler_params=pltpu.CompilerParams(vmem_limit_bytes=12 * 1024 * 1024),
        cost_estimate=SHORT,
        name="normed",
    )(y.astype(jnp.int32).reshape(1), states, gain)


def attend_kernel(place_ref, lengths_ref, query_ref, *refs):
    near_ref, far_ref, key_own, key_other, value_own, value_other, out_ref = refs[:7]
    source, key_weight, value_weight, keys, values, sems = refs[7:]
    y, core, sentence = place_ref[0], place_ref[1], place_ref[2]
    rows = near_ref.shape[0]
    depth = key_own.shape[0]
    moves = [
        (near_ref, source.at[pl.ds(0, rows)]),
        (far_ref, source.at[pl.ds(rows, rows)]),
        (key_own, key_weight.at[y]),
        (key_other, key_weight.at[1 - y]),
        (value_own, value_weight.at[y]),
        (value_other, value_weight.at[1 - y]),
    ]
    copies = [
        pltpu.make_async_copy(here, there, sems.at[i]) for i, (here, there) in enumerate(moves)
    ]
    for copy in copies:
        copy.start()

    def linear(weight, result):
        total = jnp.dot(source[:, :depth], weight[0], preferred_element_type=jnp.float32)
        total += jnp.dot(source[:, depth:], weight[1], preferred_element_type=jnp.float32)
        result[...] = total.astype(jnp.bfloat16)

    for copy in copies[:4]:
        copy.wait()
    linear(key_weight, keys)
    for copy in copies[4:]:
        copy.wait()
    linear(value_weight, values)

    column = lax.broadcasted_iota(jnp.int32, (query_ref.shape[0], 2 * rows), 1)
    position = jnp.where(column < rows, column + core * rows, column - core * rows)
    valid = position < lengths_ref[sentence]
    for head in range(query_ref.shape[1] // HEAD_DIM):
        span = slice(head * HEAD_DIM, (head + 1) * HEAD_DIM)
        scores = contract_last(query_ref[:, span], keys[:, span]) * HEAD_DIM ** (-0.5)
        scores = jnp.where(valid, scores, -1e30)
        weights = jnp.exp(scores - jnp.max(scores, axis=-1, keepdims=True))
        probs = (weights / jnp.sum(weights, axis=-1, keepdims=True)).astype(jnp.bfloat16)
        result = jnp.dot(probs, values[:, span], preferred_element_type=jnp.float32)
        out_ref[:, span] = result.astype(jnp.bfloat16)


def attend_sentence(place, lengths, query, near, far, key_parts, value_pair):
    rows, features = near.shape
    depth, width = key_parts[0].shape
    hold = pl.BlockSpec(memory_space=pltpu.HBM)
    smem = pl.BlockSpec(memory_space=pltpu.SMEM)
    full = pl.BlockSpec(memory_space=pltpu.VMEM)
    return pl.pallas_call(
        attend_kernel,
        out_shape=jax.ShapeDtypeStruct(query.shape, jnp.bfloat16),
        in_specs=[smem, smem, full] + [hold] * 6,
        out_specs=full,
        scratch_shapes=[
            vmem((2 * rows, features), jnp.bfloat16),
            vmem((2, depth, width), jnp.bfloat16),
            vmem((2, depth, width), jnp.bfloat16),
            vmem((2 * rows, width), jnp.bfloat16),
            vmem((2 * rows, width), jnp.bfloat16),
            pltpu.SemaphoreType.DMA((6,)),
        ],
        compiler_params=pltpu.CompilerParams(vmem_limit_bytes=56 * 1024 * 1024),
        cost_estimate=SHORT,
        name="attend_sentence",
    )(place, lengths, query, near, far, *key_parts, *value_pair)


def project_kernel(place_ref, mine_ref, done_ref, own_ref, other_ref, *refs):
    sent_mine, sent_other, kept_mine, kept_other, context = refs
    y, core, x = place_ref[0], place_ref[1], place_ref[2]
    targets = mine_ref.shape[0]
    for part, sentence in ((mine_ref, x), (done_ref, 1 - x)):
        context[pl.ds(pl.multiple_of(sentence * targets, targets), targets), :] = part[...]
    columns = kept_mine.shape[1]
    outs = ((sent_mine, kept_mine), (sent_other, kept_other))

    def write(weight_ref, chosen):
        for side, out_ref in zip((1 - core, core), chosen):
            span = pl.ds(pl.multiple_of(side * columns, columns), columns)
            part = jnp.dot(context[...], weight_ref[:, span], preferred_element_type=jnp.float32)
            out_ref[...] = part.astype(out_ref.dtype)

    @pl.when(x == y)
    def _():
        write(own_ref, outs[0])
        write(other_ref, outs[1])

    @pl.when(x != y)
    def _():
        write(other_ref, outs[0])
        write(own_ref, outs[1])


def project(place, mine, done, out_own, out_other):
    targets, width = 2 * mine.shape[0], mine.shape[1]
    columns = out_own.shape[1] // 2
    full = pl.BlockSpec(memory_space=pltpu.VMEM)
    sent = jax.ShapeDtypeStruct((targets, columns), jnp.bfloat16)
    kept = jax.ShapeDtypeStruct((targets, columns), jnp.float32)
    return pl.pallas_call(
        project_kernel,
        out_shape=(sent, sent, kept, kept),
        in_specs=[pl.BlockSpec(memory_space=pltpu.SMEM)] + [full] * 4,
        out_specs=[full] * 4,
        scratch_shapes=[vmem((targets, width), jnp.bfloat16)],
        compiler_params=pltpu.CompilerParams(vmem_limit_bytes=16 * 1024 * 1024),
        cost_estimate=SHORT,
        name="project",
    )(place, mine, done, out_own, out_other)


def slope_kernel(codes, here_ref, own_ref, core_ref, rise_own, rise_core, out_ref, slope, *refs):
    grads, rise, weight_out, sems = refs
    rows = own_ref.shape[0]
    hidden = weight_out.shape[0]
    chunk = hidden // 4
    moves = []
    block = 2 * rows // len(codes)
    for order, code in enumerate(codes):
        source = here_ref[0] ^ code
        there = pl.ds(pl.multiple_of(source * block, 16), block)
        here = pl.ds(order * block % rows, block)
        own = order * block < rows
        moves.append(((own_ref if own else core_ref).at[here], grads.at[there]))
        moves.append(((rise_own if own else rise_core).at[here], rise.at[there]))
    for part in range(4):
        span = pl.ds(part * chunk, chunk)
        moves.append((out_ref.at[span], weight_out.at[span]))
    copies = [
        pltpu.make_async_copy(here, there, sems.at[i]) for i, (here, there) in enumerate(moves)
    ]
    for copy in copies:
        copy.start()
    for copy in copies[:-4]:
        copy.wait()
    for part in range(4):
        copies[part - 4].wait()
        span = slice(part * chunk, (part + 1) * chunk)
        back = contract_last(grads[...], weight_out[span, :])
        slope[:, span] = (back * rise[:, span]).astype(jnp.bfloat16)


def expert_slope(here, codes, grads_own, grads_core, rise_own, rise_core, weight_out):
    rows = 2 * grads_own.shape[0]
    hidden, features = weight_out.shape
    hold = pl.BlockSpec(memory_space=pltpu.HBM)
    return pl.pallas_call(
        functools.partial(slope_kernel, codes),
        out_shape=jax.ShapeDtypeStruct((rows, hidden), jnp.bfloat16),
        in_specs=[pl.BlockSpec(memory_space=pltpu.SMEM)] + [hold] * 5,
        out_specs=pl.BlockSpec(memory_space=pltpu.VMEM),
        scratch_shapes=[
            vmem((rows, features), jnp.bfloat16),
            vmem((rows, hidden), jnp.float32),
            vmem((hidden, features), jnp.bfloat16),
            pltpu.SemaphoreType.DMA((4 + 2 * len(codes),)),
        ],
        compiler_params=pltpu.CompilerParams(vmem_limit_bytes=56 * 1024 * 1024),
        cost_estimate=SHORT,
        name="expert_slope",
    )(here, grads_own, grads_core, rise_own, rise_core, weight_out)


def backward_kernel(split, section_ref, slope_ref, in_ref, sent_ref, kept_first, kept_second, *refs):
    weight_in, sems = refs
    width = weight_in.shape[0] // split
    outs = (sent_ref.at[0], sent_ref.at[1], kept_first, kept_second)
    spans, copies = [], []
    for i, step in enumerate((1, 3, 0, 2)):
        start = pl.multiple_of((section_ref[0] ^ step) * width, width)
        spans.append(pl.ds(start, width))
        copies.append(
            pltpu.make_async_copy(in_ref.at[spans[i]], weight_in.at[spans[i]], sems.at[i])
        )
    for copy in copies:
        copy.start()
    for copy, span, out_ref in zip(copies, spans, outs):
        copy.wait()
        part = contract_last(slope_ref[...], weight_in[span, :])
        out_ref[...] = part.astype(out_ref.dtype)


def expert_backward(section, slope, weight_in, split):
    rows, hidden = slope.shape
    features = weight_in.shape[0]
    width = features // split
    full = pl.BlockSpec(memory_space=pltpu.VMEM)
    kept = jax.ShapeDtypeStruct((rows, width), jnp.float32)
    return pl.pallas_call(
        functools.partial(backward_kernel, split),
        out_shape=(jax.ShapeDtypeStruct((2, rows, width), jnp.bfloat16), kept, kept),
        in_specs=[pl.BlockSpec(memory_space=pltpu.SMEM), full, pl.BlockSpec(memory_space=pltpu.HBM)],
        out_specs=[full] * 3,
        scratch_shapes=[
            vmem((features, hidden), jnp.bfloat16),
            pltpu.SemaphoreType.DMA((split,)),
        ],
        compiler_params=pltpu.CompilerParams(vmem_limit_bytes=56 * 1024 * 1024),
        cost_estimate=SHORT,
        name="expert_backward",
    )(section, slope, weight_in)


def small_body(
    tokens,
    expert_ids,
    gate_weights,
    out_grad,
    inner_weight,
    outer_weight,
    final_gain,
    dec_states,
    src_lengths,
    tgt_lengths,
    norm_gain,
    query_weight,
    key_weight,
    value_weight,
    out_weight,
):
    token_count, feature_count = tokens.shape
    group_size = lax.axis_size(("expert", "dp"))
    capacity = 3 * token_count // group_size
    here = lax.axis_index(("expert", "dp"))
    y = lax.axis_index("expert")
    d = lax.axis_index("dp")
    section = lax.axis_index("section")
    sections = lax.axis_size("section")
    half = feature_count // 2
    weight_in = inner_weight[0]
    weight_out = outer_weight[0]
    key_own, value_own, out_own = key_weight[0], value_weight[0], out_weight[0]
    query_own = query_weight[0]

    size = group_size
    near_codes = (0, 2, 4, 6)
    core_codes = (1, 3, 5, 7)
    core, x = d % 2, d // 2
    which_section = section.astype(jnp.int32).reshape(1)

    token_y = swap(tokens, "expert", 1)
    token_x = swap(tokens, "dp", 2)
    row = lax.broadcasted_iota(jnp.int32, (token_count, token_count), 0)
    column = lax.broadcasted_iota(jnp.int32, (token_count, token_count), 1)
    ids_own = expert_ids.T
    ids_x, ids_y = swap(ids_own, "dp", 2), swap(ids_own, "expert", 1)
    ids_far = swap(ids_x, "expert", 1)
    token_far = swap(gate(token_y, ids_x, ids_y, token_x), "dp", 2)

    later_ids = gate(expert_ids, token_far)
    named = later_ids[:, :, None] == jnp.arange(size, dtype=jnp.int32)[None, None, :]
    either = (named[:, 0] | named[:, 1]).astype(jnp.bfloat16)
    earlier = jnp.dot(
        (column < row).astype(jnp.bfloat16), either, preferred_element_type=jnp.float32
    ).astype(jnp.int32)
    rank = jnp.sum(jnp.where(named, earlier[:, None, :], 0), axis=2)
    codes_of = later_ids ^ here
    position = ((codes_of >> 1) + 4 * (codes_of & 1)) * capacity + rank

    side = lax.rem(section, 2)
    share = token_count // 2
    grad_half = lax.dynamic_slice_in_dim(out_grad, side * share, share, 0)
    half_y = swap(gate(grad_half, token_y), "expert", 1)
    states = dec_states[0]
    normed_own, asked = normed_halves(y, states, norm_gain)
    asked_here = swap(gate(asked, half_y), "expert", 1)
    query_there = jnp.dot(asked_here, query_own, preferred_element_type=jnp.float32)
    other_y = swap(half_y, "section", 1)
    half_x = swap(gate(grad_half, token_far), "dp", 2)

    ids = jnp.stack([ids_own, ids_x, ids_y, ids_far])
    named_there = jnp.concatenate([(ids == here).any(axis=1), (ids == (here ^ 1)).any(axis=1)])
    before = jnp.dot(
        named_there.astype(jnp.bfloat16),
        (row < column).astype(jnp.bfloat16),
        preferred_element_type=jnp.float32,
    ).astype(jnp.int32)
    code = jnp.where(named_there, before, -1)

    def forward(rows, *after):
        pre_act = jnp.dot(rows, weight_in, preferred_element_type=jnp.float32)
        hidden = jax.nn.gelu(gate(pre_act, *after)).astype(jnp.bfloat16)
        part = jnp.dot(hidden, weight_out, preferred_element_type=jnp.float32)
        return pre_act, part.astype(jnp.bfloat16)

    def slope_of(pre_act):
        return jax.vjp(jax.nn.gelu, pre_act)[1](jnp.ones_like(pre_act))[0]

    rows_own, rows_sent = dispatch(
        which_section,
        gate(code, asked),
        [tokens, token_x, token_y, token_far],
        tuple(((place, 0, token_count, None),) for place in range(4)),
        capacity,
    )
    rows_core = swap(rows_sent, "dp", 1)
    pre_own, part_own = forward(rows_own, other_y, half_x)
    pre_core, part_core = forward(gate(rows_core, part_own))
    home = send_home(part_own, near_codes, capacity) + send_home(part_core, core_codes, capacity)
    other_x = swap(gate(half_x, home[1], home[2], home[3]), "section", 1)
    grad_y = jnp.concatenate([gate(half_y, home[4]), other_y], axis=0)
    query_back = swap(gate(query_there.astype(jnp.bfloat16), home[5], home[6]), "expert", 1)

    rise_own, rise_core = slope_of(gate(pre_own, home[5])), slope_of(gate(pre_core, home[5]))
    held_gates = gate(gate_weights, rise_own, rise_core, query_there, grad_y, other_x)
    sent_pair, first, second = combine(which_section, position, held_gates, home, sections)
    from_pair = swap(sent_pair, "section", 1)
    grad_far = swap(gate(grad_y, first), "dp", 2)
    to_other = (second + from_pair[1].astype(jnp.float32)).astype(jnp.bfloat16)
    from_other = swap(to_other, "section", 2)
    grads_own, grads_sent = dispatch(
        which_section,
        gate(code, to_other),
        [out_grad, half_x, other_x, grad_y, grad_far],
        (
            ((0, 0, token_count, None),),
            ((1, 0, share, 0), (2, 0, share, 1)),
            ((3, 0, share, 0), (3, share, share, 1)),
            ((4, 0, share, 0), (4, share, share, 1)),
        ),
        capacity,
    )
    grads_core = swap(grads_sent, "dp", 1)
    grads_core = swap(grads_sent, "dp", 1)
    mixed_sum = gate(first, query_back, grads_sent) + from_pair[0].astype(jnp.float32)
    mixed_slice = (mixed_sum + from_other.astype(jnp.float32)).astype(jnp.bfloat16)
    key_other = swap(gate(key_own, first), "expert", 1)
    mixed_near = swap(mixed_slice, "section", 1)
    slope = expert_slope(
        gate(here.astype(jnp.int32).reshape(1), mixed_near),
        near_codes + core_codes,
        grads_own,
        grads_core,
        rise_own,
        rise_core,
        weight_out,
    )
    back_pair, back_first, back_second = expert_backward(
        which_section, slope, weight_in, sections
    )
    mixed_far = swap(jnp.stack([mixed_slice, mixed_near]), "section", 2)
    slices = [mixed_slice, mixed_near, mixed_far[0], mixed_far[1]]

    value_other = swap(gate(value_own, mixed_near), "expert", 1)

    query_here = jnp.dot(normed_own, query_own, preferred_element_type=jnp.float32)
    query = (query_here + query_back.astype(jnp.float32)).astype(jnp.bfloat16)

    memory = make_memory(which_section, gate(tokens, key_other), slices, final_gain)
    out_other = swap(gate(out_own, memory), "expert", 1)
    memory_x = swap(memory, "dp", 2)
    memory_core = swap(memory, "dp", 1)

    def sentence(which, near, far, *after):
        place = gate(jnp.stack([y, core, which]).astype(jnp.int32), *after)
        rows_of = lax.dynamic_slice_in_dim(query, which * TGT_LEN, TGT_LEN, 0)
        parts = (key_own, key_other), (value_own, value_other)
        return attend_sentence(place, src_lengths, rows_of, near, far, *parts)

    back_from_pair = swap(back_pair, "section", 1)
    back_to_other = (back_second + back_from_pair[1].astype(jnp.float32)).astype(jnp.bfloat16)
    back_from_other = swap(back_to_other, "section", 2)
    backward_sum = back_first + back_from_pair[0].astype(jnp.float32)
    backward_sum = backward_sum + back_from_other.astype(jnp.float32)
    context_own = sentence(x, memory, memory_core)
    memory_far = swap(gate(memory_x, context_own), "dp", 1)
    context_other = sentence(1 - x, memory_x, memory_far)
    place = jnp.stack([y, core, x]).astype(jnp.int32)
    sent_mine, sent_other, kept_mine, kept_other = project(
        place, context_own, context_other, out_own, out_other
    )

    core_other = swap(sent_other, "dp", 1)
    core_mine = swap(sent_mine, "dp", 1)
    last = gate(kept_other, back_from_other) + core_other.astype(jnp.float32)
    from_x = swap(last.astype(jnp.bfloat16), "dp", 2)
    attended = kept_mine + core_mine.astype(jnp.float32) + from_x.astype(jnp.float32)
    dec_out = add_residual(attended, states, tgt_lengths)

    grads_home = exchange(gate(backward_sum.astype(jnp.bfloat16), last), group_size, capacity)
    natural = later_ids * capacity + rank
    (token_grad,) = combine(
        which_section, natural, gate_weights, [grads_home], 1
    )
    return (dec_out[None], token_grad)


def add_residual(attended, states, tgt_lengths):
    my_columns = attended.shape[1]
    residual = lax.dynamic_slice_in_dim(
        states, lax.axis_index("dp") * my_columns, my_columns, 1
    ).astype(jnp.float32)
    row_mask = (jnp.arange(TGT_LEN, dtype=jnp.int32)[None, :] < tgt_lengths[:, None]).reshape(-1, 1)
    return (residual + jnp.where(row_mask, attended, 0.0)).astype(jnp.bfloat16)


def body(
    tokens,
    expert_ids,
    gate_weights,
    out_grad,
    inner_weight,
    outer_weight,
    final_gain,
    dec_states,
    src_lengths,
    tgt_lengths,
    norm_gain,
    query_weight,
    key_weight,
    value_weight,
    out_weight,
):
    token_count, feature_count = tokens.shape
    group_size = lax.axis_size(("expert", "dp"))
    capacity = 3 * token_count // group_size
    slots = group_size * capacity

    named = expert_ids[:, :, None] == jnp.arange(group_size, dtype=jnp.int32)[None, None, :]
    either = (named[:, 0] | named[:, 1]).astype(jnp.bfloat16)
    row = lax.broadcasted_iota(jnp.int32, (token_count, token_count), 0)
    column = lax.broadcasted_iota(jnp.int32, (token_count, token_count), 1)
    earlier = jnp.dot(
        (column < row).astype(jnp.bfloat16), either, preferred_element_type=jnp.float32
    ).astype(jnp.int32)
    rank = jnp.sum(jnp.where(named, earlier[:, None, :], 0), axis=2)
    position = expert_ids * capacity + rank
    pick_first = slot_matrix(position[:, 0], slots)
    pick_second = slot_matrix(position[:, 1], slots)
    fill = (pick_first + pick_second).T

    def place(values):
        return jnp.dot(fill, values, preferred_element_type=jnp.float32).astype(jnp.bfloat16)

    def combine(arrived):
        first = jnp.dot(pick_first, arrived, preferred_element_type=jnp.float32)
        second = jnp.dot(pick_second, arrived, preferred_element_type=jnp.float32)
        return gate_weights[:, :1] * first + gate_weights[:, 1:] * second

    weight_in = inner_weight[0]
    weight_out = outer_weight[0]
    arrived_rows = exchange(place(tokens), group_size, capacity)
    pre_act = jnp.dot(arrived_rows, weight_in, preferred_element_type=jnp.float32)
    hidden = jax.nn.gelu(pre_act).astype(jnp.bfloat16)
    forward_part = jnp.dot(hidden, weight_out, preferred_element_type=jnp.float32)
    arrived_grads = exchange(place(out_grad), group_size, capacity)
    outputs_home = exchange(forward_part.astype(jnp.bfloat16), group_size, capacity)
    mixed_slice = sum_sections(combine(outputs_home)).astype(jnp.bfloat16)
    mixed = gather_sections(mixed_slice).astype(jnp.float32)
    memory = normalize(tokens.astype(jnp.float32) + mixed, final_gain).astype(jnp.bfloat16)

    back = contract_last(arrived_grads, weight_out)
    slope = jax.vjp(jax.nn.gelu, pre_act)[1](back)[0].astype(jnp.bfloat16)
    backward_part = contract_last(slope, weight_in)
    backward_slice = sum_sections(backward_part).astype(jnp.bfloat16)
    grads_home = exchange(backward_slice, group_size, capacity)
    token_grad = combine(grads_home).astype(jnp.bfloat16)

    states = dec_states[0]
    normed = normalize(states.astype(jnp.float32), norm_gain[0]).astype(jnp.bfloat16)
    full_query = gather_weight(query_weight[0], 0)
    full_key = gather_weight(key_weight[0], 0)
    full_value = gather_weight(value_weight[0], 0)
    full_out = gather_weight(out_weight[0], 1)
    query_sum = jnp.dot(normed, full_query, preferred_element_type=jnp.float32)
    source = gather_rows(memory, "dp")
    key_sum = jnp.dot(source, full_key, preferred_element_type=jnp.float32)
    value_sum = jnp.dot(source, full_value, preferred_element_type=jnp.float32)
    key_mask = jnp.arange(SRC_LEN, dtype=jnp.int32)[None, :] < src_lengths[:, None]
    context = attend(
        query_sum.astype(jnp.bfloat16),
        key_sum.astype(jnp.bfloat16),
        value_sum.astype(jnp.bfloat16),
        key_mask,
    )
    attended = sum_heads(jnp.dot(context, full_out, preferred_element_type=jnp.float32))
    dec_out = add_residual(attended, states, tgt_lengths)
    return (dec_out[None], token_grad)


def solution(mesh):
    in_specs = (
        P(("expert", "dp"), None),
        P(("expert", "dp"), None),
        P(("expert", "dp"), None),
        P(("expert", "dp"), None),
        P(("expert", "dp"), None, "section"),
        P(("expert", "dp"), "section", None),
        P(),
        P("section", "expert", None),
        P("expert"),
        P("expert"),
        P("section", None),
        P("section", "expert", "dp"),
        P("section", "expert", "dp"),
        P("section", "expert", "dp"),
        P("section", "dp", "expert"),
    )
    out_specs = (P("section", "expert", "dp"), P(("expert", "dp"), "section"))
    small = (mesh.shape["section"], mesh.shape["expert"], mesh.shape["dp"]) == (4, 2, 4)
    chosen = small_body if small else body
    return jax.shard_map(chosen, mesh=mesh, in_specs=in_specs, out_specs=out_specs, check_vma=False)
```

```python
import functools

import jax
import jax.numpy as jnp
from jax import lax
from jax.experimental import pallas as pl
from jax.experimental.pallas import tpu as pltpu
from jax.sharding import PartitionSpec as P

HEAD_DIM = 128
SRC_LEN = 256
TGT_LEN = 128


EPSILON = 1e-05


def normalize(values, gain):
    centre = jnp.mean(values, axis=-1, keepdims=True)
    centred = values - centre
    spread = jnp.mean(centred * centred, axis=-1, keepdims=True)
    return centred * lax.rsqrt(spread + EPSILON) * gain


def contract_last(left, right):
    return lax.dot_general(
        left, right, (((1,), (1,)), ((), ())), preferred_element_type=jnp.float32
    )


def shift(value, axis, step):
    size = lax.axis_size(axis)
    return lax.ppermute(value, axis, [(i, (i + step) % size) for i in range(size)])


def swap(value, axis, mask):
    size = lax.axis_size(axis)
    return lax.ppermute(value, axis, [(i, i ^ mask) for i in range(size)])


def sum_sections(partial):
    count = lax.axis_size("section")
    me = lax.axis_index("section")
    width = partial.shape[1] // count

    def piece(owner):
        return lax.dynamic_slice_in_dim(partial, owner * width, width, 1)

    total = piece(me).astype(jnp.float32)
    for step in range(1, count):
        sent = piece(lax.rem(me + step, count)).astype(jnp.bfloat16)
        total = total + shift(sent, "section", step).astype(jnp.float32)
    return total


def gather_sections(mine):
    count = lax.axis_size("section")
    me = lax.axis_index("section")
    width = mine.shape[1]
    whole = jnp.zeros((mine.shape[0], width * count), mine.dtype)
    whole = lax.dynamic_update_slice_in_dim(whole, mine, me * width, 1)
    for step in range(1, count):
        owner = lax.rem(me - step + count, count)
        whole = lax.dynamic_update_slice_in_dim(
            whole, shift(mine, "section", step), owner * width, 1
        )
    return whole


def gather_rows(mine, axis):
    held = mine
    me = lax.axis_index(axis)
    mask = lax.axis_size(axis) // 2
    blocks = [mine]
    while mask >= 1:
        blocks = blocks + [swap(block, axis, mask) for block in blocks]
        mask //= 2
    codes = [0]
    mask = lax.axis_size(axis) // 2
    while mask >= 1:
        codes = codes + [code ^ mask for code in codes]
        mask //= 2
    ordered = []
    for place in range(len(blocks)):
        chosen = blocks[0]
        for code, block in zip(codes[1:], blocks[1:]):
            chosen = jnp.where((me ^ code) == place, block, chosen)
        ordered.append(chosen)
    return jnp.concatenate(ordered, axis=0)


def gather_weight(weight, dimension):
    if lax.axis_size("expert") != 2:
        return lax.all_gather(weight, "expert", axis=dimension, tiled=True)
    other = swap(weight, "expert", 1)
    first = lax.axis_index("expert") == 0
    return jnp.concatenate(
        [jnp.where(first, weight, other), jnp.where(first, other, weight)], axis=dimension
    )


def sum_heads(partial):
    me = lax.axis_index("dp")
    count = lax.axis_size("dp")
    rows, columns = partial.shape
    total = partial.reshape(rows, count, columns // count)
    mask = 1
    while mask < count:
        paired = total.reshape(rows, -1, 2, columns // count)
        bit = (me // mask) % 2
        sent = lax.dynamic_index_in_dim(paired, 1 - bit, 2, False).astype(jnp.bfloat16)
        kept = lax.dynamic_index_in_dim(paired, bit, 2, False)
        total = kept + swap(sent, "dp", mask).astype(jnp.float32)
        mask *= 2
    return total.reshape(rows, columns // count)


def slot_matrix(positions, slots):
    places = lax.broadcasted_iota(jnp.int32, (positions.shape[0], slots), 1)
    return (positions[:, None] == places).astype(jnp.bfloat16)


def attend(query, keys, values, key_mask):
    sequences = key_mask.shape[0]
    head_count = query.shape[1] // HEAD_DIM
    query_split = query.reshape(sequences, -1, head_count, HEAD_DIM)
    keys_split = keys.reshape(sequences, -1, head_count, HEAD_DIM)
    values_split = values.reshape(sequences, -1, head_count, HEAD_DIM)
    scores = jnp.einsum(
        "bqhd,bkhd->bhqk", query_split, keys_split, preferred_element_type=jnp.float32
    ) * HEAD_DIM ** (-0.5)
    scores = jnp.where(key_mask[:, None, None, :], scores, -1e30)
    highest = jnp.max(scores, axis=-1, keepdims=True)
    weights = jnp.exp(scores - highest)
    probs = (weights / jnp.sum(weights, axis=-1, keepdims=True)).astype(jnp.bfloat16)
    context = jnp.einsum("bhqk,bkhd->bqhd", probs, values_split, preferred_element_type=jnp.float32)
    return context.astype(jnp.bfloat16).reshape(-1, head_count * HEAD_DIM)


def exchange(values, group_size, capacity):
    sent = values.reshape(group_size, capacity, values.shape[1])
    arrived = lax.all_to_all(sent, ("expert", "dp"), split_axis=0, concat_axis=0, tiled=True)
    return arrived.reshape(values.shape)


SHORT = pl.CostEstimate(flops=1, bytes_accessed=1, transcendentals=0)


def gate(value, *after):
    return lax.optimization_barrier((value,) + after)[0]


def vmem(shape, dtype):
    return pltpu.VMEM(shape, dtype)


def dispatch_kernel(capacity, layout, section_ref, code_ref, *refs):
    blocks = refs[:-4]
    outs, held, sems = refs[-4:-2], refs[-2], refs[-1]
    count, rows = held.shape[0], held.shape[1]
    half = lax.rem(section_ref[0], 2)
    copies = []
    for place, pieces in enumerate(layout):
        group = []
        for i, (which, start, length, side) in enumerate(pieces):
            there = held.at[place]
            if side is not None:
                offset = (half if side == 0 else 1 - half) * length
                there = held.at[place, pl.ds(pl.multiple_of(offset, length), length)]
            here = blocks[which].at[pl.ds(start, length)]
            group.append(pltpu.make_async_copy(here, there, sems.at[place, i]))
        copies.append(group)
    for group in copies:
        for copy in group:
            copy.start()
    for place, group in enumerate(copies):
        picks = []
        for which in range(2):
            line = which * count + place
            code = code_ref[line : line + 1, :]
            slot = lax.broadcasted_iota(jnp.int32, (capacity, code.shape[1]), 0)
            picks.append(jnp.where(slot == code, 1.0, 0.0))
        pick = jnp.concatenate(picks, axis=0).astype(jnp.bfloat16)
        for copy in group:
            copy.wait()
        picked = jnp.dot(pick, held[place], preferred_element_type=jnp.float32)
        picked = picked.astype(jnp.bfloat16)
        for which, out_ref in enumerate(outs):
            out_ref[place * capacity : (place + 1) * capacity, :] = picked[
                which * capacity : (which + 1) * capacity
            ]


def dispatch(section, code, blocks, layout, capacity):
    rows, features = blocks[0].shape
    count = len(layout)
    picked = jax.ShapeDtypeStruct((count * capacity, features), jnp.bfloat16)
    return pl.pallas_call(
        functools.partial(dispatch_kernel, capacity, layout),
        out_shape=(picked, picked),
        in_specs=[
            pl.BlockSpec(memory_space=pltpu.SMEM),
            pl.BlockSpec(memory_space=pltpu.VMEM),
        ]
        + [pl.BlockSpec(memory_space=pltpu.HBM)] * len(blocks),
        out_specs=[pl.BlockSpec(memory_space=pltpu.VMEM)] * 2,
        scratch_shapes=[
            vmem((count, rows, features), jnp.bfloat16),
            pltpu.SemaphoreType.DMA((count, 2)),
        ],
        compiler_params=pltpu.CompilerParams(vmem_limit_bytes=10 * 1024 * 1024),
        cost_estimate=SHORT,
        name="dispatch",
    )(section, code, *blocks)


def send_home(part, codes, capacity):
    size = lax.axis_size(("expert", "dp"))
    arrived = []
    for place, code in enumerate(codes):
        block = part[place * capacity : (place + 1) * capacity]
        if code:
            block = lax.ppermute(block, ("expert", "dp"), [(i, i ^ code) for i in range(size)])
        arrived.append(block)
    return arrived


def combine_kernel(count, split, section_ref, position_ref, gates_ref, *refs):
    blocks = refs[:count]
    outs, (held, total) = refs[count:-2], refs[-2:]
    capacity, features = blocks[0].shape
    position = position_ref[...]
    slot = lax.broadcasted_iota(jnp.int32, (position.shape[0], count * capacity), 1)
    picks = [
        jnp.where(position[:, k : k + 1] == slot, 1.0, 0.0).astype(jnp.bfloat16) for k in range(2)
    ]
    for i, block in enumerate(blocks):
        held[i * capacity : (i + 1) * capacity, :] = block[...]
    pick = jnp.concatenate(picks, axis=0)
    rows = position.shape[0]
    both = jnp.dot(pick, held[...], preferred_element_type=jnp.float32)
    total[...] = gates_ref[:, 0:1] * both[:rows] + gates_ref[:, 1:2] * both[rows:]
    if split == 1:
        outs[0][...] = total[...].astype(outs[0].dtype)
        return
    sent_ref, kept_first, kept_second = outs
    width = features // split
    for step, out_ref in enumerate((kept_first, sent_ref.at[0], kept_second, sent_ref.at[1])):
        start = pl.multiple_of((section_ref[0] ^ step) * width, width)
        out_ref[...] = total[:, pl.ds(start, width)].astype(out_ref.dtype)


def combine(section, position, gates, blocks, split):
    capacity, features = blocks[0].shape
    rows = position.shape[0]
    count = len(blocks)
    width = features // split
    kept = jax.ShapeDtypeStruct((rows, width), jnp.float32)
    if split == 1:
        out_shape = (jax.ShapeDtypeStruct((rows, width), jnp.bfloat16),)
    else:
        out_shape = (jax.ShapeDtypeStruct((2, rows, width), jnp.bfloat16), kept, kept)
    full = pl.BlockSpec(memory_space=pltpu.VMEM)
    return pl.pallas_call(
        functools.partial(combine_kernel, count, split),
        out_shape=out_shape,
        in_specs=[pl.BlockSpec(memory_space=pltpu.SMEM)] + [full] * (2 + count),
        out_specs=[full] * len(out_shape),
        scratch_shapes=[
            vmem((count * capacity, features), jnp.bfloat16),
            vmem((rows, features), jnp.float32),
        ],
        compiler_params=pltpu.CompilerParams(vmem_limit_bytes=14 * 1024 * 1024),
        cost_estimate=SHORT,
        name="combine",
    )(section, position, gates, *blocks)


def memory_kernel(count, section_ref, tokens_ref, gain_ref, *refs):
    slices, out_ref, mixed = refs[:count], refs[count], refs[count + 1]
    me = section_ref[0]
    width = slices[0].shape[1]
    for step, piece in enumerate(slices):
        owner = me ^ step
        mixed[:, pl.ds(pl.multiple_of(owner * width, width), width)] = piece[...].astype(
            jnp.float32
        )
    values = tokens_ref[...].astype(jnp.float32) + mixed[...]
    out_ref[...] = normalize(values, gain_ref[...]).astype(jnp.bfloat16)


def make_memory(me, tokens, slices, gain):
    return pl.pallas_call(
        functools.partial(memory_kernel, len(slices)),
        out_shape=jax.ShapeDtypeStruct(tokens.shape, jnp.bfloat16),
        in_specs=[
            pl.BlockSpec(memory_space=pltpu.SMEM),
        ]
        + [pl.BlockSpec(memory_space=pltpu.VMEM)] * (2 + len(slices)),
        out_specs=pl.BlockSpec(memory_space=pltpu.VMEM),
        scratch_shapes=[vmem(tokens.shape, jnp.float32)],
        compiler_params=pltpu.CompilerParams(vmem_limit_bytes=8 * 1024 * 1024),
        cost_estimate=SHORT,
        name="memory",
    )(me, tokens, gain[None], *slices)


def normed_kernel(y_ref, states_ref, gain_ref, own_ref, other_ref):
    values = normalize(states_ref[...].astype(jnp.float32), gain_ref[...]).astype(jnp.bfloat16)
    width = own_ref.shape[1]
    for out_ref, first in ((own_ref, y_ref[0] == 0), (other_ref, y_ref[0] == 1)):
        out_ref[...] = jnp.where(first, values[:, :width], values[:, width:])


def normed_halves(y, states, gain):
    rows, features = states.shape
    full = pl.BlockSpec(memory_space=pltpu.VMEM)
    return pl.pallas_call(
        normed_kernel,
        out_shape=(jax.ShapeDtypeStruct((rows, features // 2), jnp.bfloat16),) * 2,
        in_specs=[pl.BlockSpec(memory_space=pltpu.SMEM), full, full],
        out_specs=[full] * 2,
        compiler_params=pltpu.CompilerParams(vmem_limit_bytes=12 * 1024 * 1024),
        cost_estimate=SHORT,
        name="normed",
    )(y.astype(jnp.int32).reshape(1), states, gain)


def attend_kernel(place_ref, lengths_ref, query_ref, *refs):
    near_ref, far_ref, key_own, key_other, value_own, value_other, out_ref = refs[:7]
    source, key_weight, value_weight, keys, values, sems = refs[7:]
    y, core, sentence = place_ref[0], place_ref[1], place_ref[2]
    rows = near_ref.shape[0]
    depth = key_own.shape[0]
    moves = [
        (near_ref, source.at[pl.ds(0, rows)]),
        (far_ref, source.at[pl.ds(rows, rows)]),
        (key_own, key_weight.at[y]),
        (key_other, key_weight.at[1 - y]),
        (value_own, value_weight.at[y]),
        (value_other, value_weight.at[1 - y]),
    ]
    copies = [
        pltpu.make_async_copy(here, there, sems.at[i]) for i, (here, there) in enumerate(moves)
    ]
    for copy in copies:
        copy.start()

    def linear(weight, result):
        total = jnp.dot(source[:, :depth], weight[0], preferred_element_type=jnp.float32)
        total += jnp.dot(source[:, depth:], weight[1], preferred_element_type=jnp.float32)
        result[...] = total.astype(jnp.bfloat16)

    for copy in copies[:4]:
        copy.wait()
    linear(key_weight, keys)
    for copy in copies[4:]:
        copy.wait()
    linear(value_weight, values)

    column = lax.broadcasted_iota(jnp.int32, (query_ref.shape[0], 2 * rows), 1)
    position = jnp.where(column < rows, column + core * rows, column - core * rows)
    valid = position < lengths_ref[sentence]
    for head in range(query_ref.shape[1] // HEAD_DIM):
        span = slice(head * HEAD_DIM, (head + 1) * HEAD_DIM)
        scores = contract_last(query_ref[:, span], keys[:, span]) * HEAD_DIM ** (-0.5)
        scores = jnp.where(valid, scores, -1e30)
        weights = jnp.exp(scores - jnp.max(scores, axis=-1, keepdims=True))
        probs = (weights / jnp.sum(weights, axis=-1, keepdims=True)).astype(jnp.bfloat16)
        result = jnp.dot(probs, values[:, span], preferred_element_type=jnp.float32)
        out_ref[:, span] = result.astype(jnp.bfloat16)


def attend_sentence(place, lengths, query, near, far, key_parts, value_pair):
    rows, features = near.shape
    depth, width = key_parts[0].shape
    hold = pl.BlockSpec(memory_space=pltpu.HBM)
    smem = pl.BlockSpec(memory_space=pltpu.SMEM)
    full = pl.BlockSpec(memory_space=pltpu.VMEM)
    return pl.pallas_call(
        attend_kernel,
        out_shape=jax.ShapeDtypeStruct(query.shape, jnp.bfloat16),
        in_specs=[smem, smem, full] + [hold] * 6,
        out_specs=full,
        scratch_shapes=[
            vmem((2 * rows, features), jnp.bfloat16),
            vmem((2, depth, width), jnp.bfloat16),
            vmem((2, depth, width), jnp.bfloat16),
            vmem((2 * rows, width), jnp.bfloat16),
            vmem((2 * rows, width), jnp.bfloat16),
            pltpu.SemaphoreType.DMA((6,)),
        ],
        compiler_params=pltpu.CompilerParams(vmem_limit_bytes=56 * 1024 * 1024),
        cost_estimate=SHORT,
        name="attend_sentence",
    )(place, lengths, query, near, far, *key_parts, *value_pair)


def project_kernel(place_ref, mine_ref, done_ref, own_ref, other_ref, *refs):
    sent_mine, sent_other, kept_mine, kept_other, context = refs
    y, core, x = place_ref[0], place_ref[1], place_ref[2]
    targets = mine_ref.shape[0]
    for part, sentence in ((mine_ref, x), (done_ref, 1 - x)):
        context[pl.ds(pl.multiple_of(sentence * targets, targets), targets), :] = part[...]
    columns = kept_mine.shape[1]
    outs = ((sent_mine, kept_mine), (sent_other, kept_other))

    def write(weight_ref, chosen):
        for side, out_ref in zip((1 - core, core), chosen):
            span = pl.ds(pl.multiple_of(side * columns, columns), columns)
            part = jnp.dot(context[...], weight_ref[:, span], preferred_element_type=jnp.float32)
            out_ref[...] = part.astype(out_ref.dtype)

    @pl.when(x == y)
    def _():
        write(own_ref, outs[0])
        write(other_ref, outs[1])

    @pl.when(x != y)
    def _():
        write(other_ref, outs[0])
        write(own_ref, outs[1])


def project(place, mine, done, out_own, out_other):
    targets, width = 2 * mine.shape[0], mine.shape[1]
    columns = out_own.shape[1] // 2
    full = pl.BlockSpec(memory_space=pltpu.VMEM)
    sent = jax.ShapeDtypeStruct((targets, columns), jnp.bfloat16)
    kept = jax.ShapeDtypeStruct((targets, columns), jnp.float32)
    return pl.pallas_call(
        project_kernel,
        out_shape=(sent, sent, kept, kept),
        in_specs=[pl.BlockSpec(memory_space=pltpu.SMEM)] + [full] * 4,
        out_specs=[full] * 4,
        scratch_shapes=[vmem((targets, width), jnp.bfloat16)],
        compiler_params=pltpu.CompilerParams(vmem_limit_bytes=16 * 1024 * 1024),
        cost_estimate=SHORT,
        name="project",
    )(place, mine, done, out_own, out_other)


def slope_kernel(codes, here_ref, own_ref, core_ref, rise_own, rise_core, out_ref, slope, *refs):
    grads, rise, weight_out, sems = refs
    rows = own_ref.shape[0]
    hidden = weight_out.shape[0]
    chunk = hidden // 4
    moves = []
    block = 2 * rows // len(codes)
    for order, code in enumerate(codes):
        source = here_ref[0] ^ code
        there = pl.ds(pl.multiple_of(source * block, 16), block)
        here = pl.ds(order * block % rows, block)
        own = order * block < rows
        moves.append(((own_ref if own else core_ref).at[here], grads.at[there]))
        moves.append(((rise_own if own else rise_core).at[here], rise.at[there]))
    for part in range(4):
        span = pl.ds(part * chunk, chunk)
        moves.append((out_ref.at[span], weight_out.at[span]))
    copies = [
        pltpu.make_async_copy(here, there, sems.at[i]) for i, (here, there) in enumerate(moves)
    ]
    for copy in copies:
        copy.start()
    for copy in copies[:-4]:
        copy.wait()
    for part in range(4):
        copies[part - 4].wait()
        span = slice(part * chunk, (part + 1) * chunk)
        back = contract_last(grads[...], weight_out[span, :])
        slope[:, span] = (back * rise[:, span]).astype(jnp.bfloat16)


def expert_slope(here, codes, grads_own, grads_core, rise_own, rise_core, weight_out):
    rows = 2 * grads_own.shape[0]
    hidden, features = weight_out.shape
    hold = pl.BlockSpec(memory_space=pltpu.HBM)
    return pl.pallas_call(
        functools.partial(slope_kernel, codes),
        out_shape=jax.ShapeDtypeStruct((rows, hidden), jnp.bfloat16),
        in_specs=[pl.BlockSpec(memory_space=pltpu.SMEM)] + [hold] * 5,
        out_specs=pl.BlockSpec(memory_space=pltpu.VMEM),
        scratch_shapes=[
            vmem((rows, features), jnp.bfloat16),
            vmem((rows, hidden), jnp.float32),
            vmem((hidden, features), jnp.bfloat16),
            pltpu.SemaphoreType.DMA((4 + 2 * len(codes),)),
        ],
        compiler_params=pltpu.CompilerParams(vmem_limit_bytes=56 * 1024 * 1024),
        cost_estimate=SHORT,
        name="expert_slope",
    )(here, grads_own, grads_core, rise_own, rise_core, weight_out)


def backward_kernel(split, section_ref, slope_ref, in_ref, sent_ref, kept_first, kept_second, *refs):
    weight_in, sems = refs
    width = weight_in.shape[0] // split
    outs = (sent_ref.at[0], sent_ref.at[1], kept_first, kept_second)
    spans, copies = [], []
    for i, step in enumerate((1, 3, 0, 2)):
        start = pl.multiple_of((section_ref[0] ^ step) * width, width)
        spans.append(pl.ds(start, width))
        copies.append(
            pltpu.make_async_copy(in_ref.at[spans[i]], weight_in.at[spans[i]], sems.at[i])
        )
    for copy in copies:
        copy.start()
    for copy, span, out_ref in zip(copies, spans, outs):
        copy.wait()
        part = contract_last(slope_ref[...], weight_in[span, :])
        out_ref[...] = part.astype(out_ref.dtype)


def expert_backward(section, slope, weight_in, split):
    rows, hidden = slope.shape
    features = weight_in.shape[0]
    width = features // split
    full = pl.BlockSpec(memory_space=pltpu.VMEM)
    kept = jax.ShapeDtypeStruct((rows, width), jnp.float32)
    return pl.pallas_call(
        functools.partial(backward_kernel, split),
        out_shape=(jax.ShapeDtypeStruct((2, rows, width), jnp.bfloat16), kept, kept),
        in_specs=[pl.BlockSpec(memory_space=pltpu.SMEM), full, pl.BlockSpec(memory_space=pltpu.HBM)],
        out_specs=[full] * 3,
        scratch_shapes=[
            vmem((features, hidden), jnp.bfloat16),
            pltpu.SemaphoreType.DMA((split,)),
        ],
        compiler_params=pltpu.CompilerParams(vmem_limit_bytes=56 * 1024 * 1024),
        cost_estimate=SHORT,
        name="expert_backward",
    )(section, slope, weight_in)


def small_body(
    tokens,
    expert_ids,
    gate_weights,
    out_grad,
    inner_weight,
    outer_weight,
    final_gain,
    dec_states,
    src_lengths,
    tgt_lengths,
    norm_gain,
    query_weight,
    key_weight,
    value_weight,
    out_weight,
):
    token_count, feature_count = tokens.shape
    group_size = lax.axis_size(("expert", "dp"))
    capacity = 3 * token_count // group_size
    here = lax.axis_index(("expert", "dp"))
    y = lax.axis_index("expert")
    d = lax.axis_index("dp")
    section = lax.axis_index("section")
    sections = lax.axis_size("section")
    half = feature_count // 2
    weight_in = inner_weight[0]
    weight_out = outer_weight[0]
    key_own, value_own, out_own = key_weight[0], value_weight[0], out_weight[0]
    query_own = query_weight[0]

    size = group_size
    near_codes = (0, 2, 4, 6)
    core_codes = (1, 3, 5, 7)
    core, x = d % 2, d // 2
    which_section = section.astype(jnp.int32).reshape(1)

    token_y = swap(tokens, "expert", 1)
    token_x = swap(tokens, "dp", 2)
    row = lax.broadcasted_iota(jnp.int32, (token_count, token_count), 0)
    column = lax.broadcasted_iota(jnp.int32, (token_count, token_count), 1)
    named = expert_ids[:, :, None] == jnp.arange(size, dtype=jnp.int32)[None, None, :]
    either = (named[:, 0] | named[:, 1]).astype(jnp.bfloat16)
    earlier = jnp.dot(
        (column < row).astype(jnp.bfloat16), either, preferred_element_type=jnp.float32
    ).astype(jnp.int32)
    rank = jnp.sum(jnp.where(named, earlier[:, None, :], 0), axis=2)
    codes_of = expert_ids ^ here
    position = ((codes_of >> 1) + 4 * (codes_of & 1)) * capacity + rank

    ids_own = expert_ids.T
    ids_x, ids_y = swap(ids_own, "dp", 2), swap(ids_own, "expert", 1)
    ids_far = swap(ids_x, "expert", 1)
    token_far = swap(gate(token_y, ids_x), "dp", 2)

    side = lax.rem(section, 2)
    share = token_count // 2
    grad_half = lax.dynamic_slice_in_dim(out_grad, side * share, share, 0)
    half_y = swap(gate(grad_half, token_y, token_x), "expert", 1)
    states = dec_states[0]
    normed_own, asked = normed_halves(y, states, norm_gain)
    asked_here = swap(gate(asked, half_y), "expert", 1)
    query_there = jnp.dot(asked_here, query_own, preferred_element_type=jnp.float32)
    other_y = swap(half_y, "section", 1)
    half_x = swap(gate(grad_half, token_far), "dp", 2)

    ids = jnp.stack([ids_own, ids_x, ids_y, ids_far])
    named_there = jnp.concatenate([(ids == here).any(axis=1), (ids == (here ^ 1)).any(axis=1)])
    before = jnp.dot(
        named_there.astype(jnp.bfloat16),
        (row < column).astype(jnp.bfloat16),
        preferred_element_type=jnp.float32,
    ).astype(jnp.int32)
    code = jnp.where(named_there, before, -1)

    def forward(rows, *after):
        pre_act = jnp.dot(rows, weight_in, preferred_element_type=jnp.float32)
        hidden = jax.nn.gelu(gate(pre_act, *after)).astype(jnp.bfloat16)
        part = jnp.dot(hidden, weight_out, preferred_element_type=jnp.float32)
        return pre_act, part.astype(jnp.bfloat16)

    def slope_of(pre_act):
        return jax.vjp(jax.nn.gelu, pre_act)[1](jnp.ones_like(pre_act))[0]

    rows_own, rows_sent = dispatch(
        which_section,
        gate(code, asked),
        [tokens, token_x, token_y, token_far],
        tuple(((place, 0, token_count, None),) for place in range(4)),
        capacity,
    )
    rows_core = swap(rows_sent, "dp", 1)
    pre_own, part_own = forward(rows_own, other_y, half_x)
    pre_core, part_core = forward(gate(rows_core, part_own))
    home = send_home(part_own, near_codes, capacity) + send_home(part_core, core_codes, capacity)
    other_x = swap(gate(half_x, home[1], home[2], home[3]), "section", 1)
    grad_y = jnp.concatenate([gate(half_y, home[4]), other_y], axis=0)
    query_back = swap(gate(query_there.astype(jnp.bfloat16), home[5], home[6]), "expert", 1)

    rise_own, rise_core = slope_of(gate(pre_own, home[5])), slope_of(gate(pre_core, home[5]))
    held_gates = gate(gate_weights, rise_own, rise_core, query_there, grad_y, other_x)
    sent_pair, first, second = combine(which_section, position, held_gates, home, sections)
    from_pair = swap(sent_pair, "section", 1)
    grad_far = swap(gate(grad_y, first), "dp", 2)
    to_other = (second + from_pair[1].astype(jnp.float32)).astype(jnp.bfloat16)
    from_other = swap(to_other, "section", 2)
    grads_own, grads_sent = dispatch(
        which_section,
        gate(code, to_other),
        [out_grad, half_x, other_x, grad_y, grad_far],
        (
            ((0, 0, token_count, None),),
            ((1, 0, share, 0), (2, 0, share, 1)),
            ((3, 0, share, 0), (3, share, share, 1)),
            ((4, 0, share, 0), (4, share, share, 1)),
        ),
        capacity,
    )
    grads_core = swap(grads_sent, "dp", 1)
    grads_core = swap(grads_sent, "dp", 1)
    mixed_sum = gate(first, query_back, grads_sent) + from_pair[0].astype(jnp.float32)
    mixed_slice = (mixed_sum + from_other.astype(jnp.float32)).astype(jnp.bfloat16)
    key_other = swap(gate(key_own, first), "expert", 1)
    mixed_near = swap(mixed_slice, "section", 1)
    slope = expert_slope(
        gate(here.astype(jnp.int32).reshape(1), mixed_near),
        near_codes + core_codes,
        grads_own,
        grads_core,
        rise_own,
        rise_core,
        weight_out,
    )
    back_pair, back_first, back_second = expert_backward(
        gate(which_section, key_other), slope, weight_in, sections
    )
    mixed_far = swap(jnp.stack([mixed_slice, mixed_near]), "section", 2)
    slices = [mixed_slice, mixed_near, mixed_far[0], mixed_far[1]]

    value_other = swap(gate(value_own, mixed_near), "expert", 1)

    query_here = jnp.dot(normed_own, query_own, preferred_element_type=jnp.float32)
    query = (query_here + query_back.astype(jnp.float32)).astype(jnp.bfloat16)

    memory = make_memory(which_section, tokens, slices, final_gain)
    out_other = swap(gate(out_own, memory), "expert", 1)
    memory_x = swap(memory, "dp", 2)
    memory_core = swap(memory, "dp", 1)

    def sentence(which, near, far, *after):
        place = gate(jnp.stack([y, core, which]).astype(jnp.int32), *after)
        rows_of = lax.dynamic_slice_in_dim(query, which * TGT_LEN, TGT_LEN, 0)
        parts = (key_own, key_other), (value_own, value_other)
        return attend_sentence(place, src_lengths, rows_of, near, far, *parts)

    back_from_pair = swap(back_pair, "section", 1)
    back_to_other = (back_second + back_from_pair[1].astype(jnp.float32)).astype(jnp.bfloat16)
    back_from_other = swap(back_to_other, "section", 2)
    backward_sum = back_first + back_from_pair[0].astype(jnp.float32)
    backward_sum = backward_sum + back_from_other.astype(jnp.float32)
    context_own = sentence(x, memory, memory_core)
    memory_far = swap(gate(memory_x, context_own), "dp", 1)
    context_other = sentence(1 - x, memory_x, memory_far)
    place = jnp.stack([y, core, x]).astype(jnp.int32)
    sent_mine, sent_other, kept_mine, kept_other = project(
        place, context_own, context_other, out_own, out_other
    )

    core_other = swap(sent_other, "dp", 1)
    core_mine = swap(sent_mine, "dp", 1)
    last = gate(kept_other, back_from_other) + core_other.astype(jnp.float32)
    from_x = swap(last.astype(jnp.bfloat16), "dp", 2)
    attended = kept_mine + core_mine.astype(jnp.float32) + from_x.astype(jnp.float32)
    dec_out = add_residual(attended, states, tgt_lengths)

    grads_home = exchange(gate(backward_sum.astype(jnp.bfloat16), last), group_size, capacity)
    natural = expert_ids * capacity + rank
    (token_grad,) = combine(
        which_section, natural, gate_weights, [grads_home], 1
    )
    return (dec_out[None], token_grad)


def add_residual(attended, states, tgt_lengths):
    my_columns = attended.shape[1]
    residual = lax.dynamic_slice_in_dim(
        states, lax.axis_index("dp") * my_columns, my_columns, 1
    ).astype(jnp.float32)
    row_mask = (jnp.arange(TGT_LEN, dtype=jnp.int32)[None, :] < tgt_lengths[:, None]).reshape(-1, 1)
    return (residual + jnp.where(row_mask, attended, 0.0)).astype(jnp.bfloat16)


def body(
    tokens,
    expert_ids,
    gate_weights,
    out_grad,
    inner_weight,
    outer_weight,
    final_gain,
    dec_states,
    src_lengths,
    tgt_lengths,
    norm_gain,
    query_weight,
    key_weight,
    value_weight,
    out_weight,
):
    token_count, feature_count = tokens.shape
    group_size = lax.axis_size(("expert", "dp"))
    capacity = 3 * token_count // group_size
    slots = group_size * capacity

    named = expert_ids[:, :, None] == jnp.arange(group_size, dtype=jnp.int32)[None, None, :]
    either = (named[:, 0] | named[:, 1]).astype(jnp.bfloat16)
    row = lax.broadcasted_iota(jnp.int32, (token_count, token_count), 0)
    column = lax.broadcasted_iota(jnp.int32, (token_count, token_count), 1)
    earlier = jnp.dot(
        (column < row).astype(jnp.bfloat16), either, preferred_element_type=jnp.float32
    ).astype(jnp.int32)
    rank = jnp.sum(jnp.where(named, earlier[:, None, :], 0), axis=2)
    position = expert_ids * capacity + rank
    pick_first = slot_matrix(position[:, 0], slots)
    pick_second = slot_matrix(position[:, 1], slots)
    fill = (pick_first + pick_second).T

    def place(values):
        return jnp.dot(fill, values, preferred_element_type=jnp.float32).astype(jnp.bfloat16)

    def combine(arrived):
        first = jnp.dot(pick_first, arrived, preferred_element_type=jnp.float32)
        second = jnp.dot(pick_second, arrived, preferred_element_type=jnp.float32)
        return gate_weights[:, :1] * first + gate_weights[:, 1:] * second

    weight_in = inner_weight[0]
    weight_out = outer_weight[0]
    arrived_rows = exchange(place(tokens), group_size, capacity)
    pre_act = jnp.dot(arrived_rows, weight_in, preferred_element_type=jnp.float32)
    hidden = jax.nn.gelu(pre_act).astype(jnp.bfloat16)
    forward_part = jnp.dot(hidden, weight_out, preferred_element_type=jnp.float32)
    arrived_grads = exchange(place(out_grad), group_size, capacity)
    outputs_home = exchange(forward_part.astype(jnp.bfloat16), group_size, capacity)
    mixed_slice = sum_sections(combine(outputs_home)).astype(jnp.bfloat16)
    mixed = gather_sections(mixed_slice).astype(jnp.float32)
    memory = normalize(tokens.astype(jnp.float32) + mixed, final_gain).astype(jnp.bfloat16)

    back = contract_last(arrived_grads, weight_out)
    slope = jax.vjp(jax.nn.gelu, pre_act)[1](back)[0].astype(jnp.bfloat16)
    backward_part = contract_last(slope, weight_in)
    backward_slice = sum_sections(backward_part).astype(jnp.bfloat16)
    grads_home = exchange(backward_slice, group_size, capacity)
    token_grad = combine(grads_home).astype(jnp.bfloat16)

    states = dec_states[0]
    normed = normalize(states.astype(jnp.float32), norm_gain[0]).astype(jnp.bfloat16)
    full_query = gather_weight(query_weight[0], 0)
    full_key = gather_weight(key_weight[0], 0)
    full_value = gather_weight(value_weight[0], 0)
    full_out = gather_weight(out_weight[0], 1)
    query_sum = jnp.dot(normed, full_query, preferred_element_type=jnp.float32)
    source = gather_rows(memory, "dp")
    key_sum = jnp.dot(source, full_key, preferred_element_type=jnp.float32)
    value_sum = jnp.dot(source, full_value, preferred_element_type=jnp.float32)
    key_mask = jnp.arange(SRC_LEN, dtype=jnp.int32)[None, :] < src_lengths[:, None]
    context = attend(
        query_sum.astype(jnp.bfloat16),
        key_sum.astype(jnp.bfloat16),
        value_sum.astype(jnp.bfloat16),
        key_mask,
    )
    attended = sum_heads(jnp.dot(context, full_out, preferred_element_type=jnp.float32))
    dec_out = add_residual(attended, states, tgt_lengths)
    return (dec_out[None], token_grad)


def solution(mesh):
    in_specs = (
        P(("expert", "dp"), None),
        P(("expert", "dp"), None),
        P(("expert", "dp"), None),
        P(("expert", "dp"), None),
        P(("expert", "dp"), None, "section"),
        P(("expert", "dp"), "section", None),
        P(),
        P("section", "expert", None),
        P("expert"),
        P("expert"),
        P("section", None),
        P("section", "expert", "dp"),
        P("section", "expert", "dp"),
        P("section", "expert", "dp"),
        P("section", "dp", "expert"),
    )
    out_specs = (P("section", "expert", "dp"), P(("expert", "dp"), "section"))
    small = (mesh.shape["section"], mesh.shape["expert"], mesh.shape["dp"]) == (4, 2, 4)
    chosen = small_body if small else body
    return jax.shard_map(chosen, mesh=mesh, in_specs=in_specs, out_specs=out_specs, check_vma=False)
```

```python
import functools

import jax
import jax.numpy as jnp
from jax import lax
from jax.experimental import pallas as pl
from jax.experimental.pallas import tpu as pltpu
from jax.sharding import PartitionSpec as P

HEAD_DIM = 128
SRC_LEN = 256
TGT_LEN = 128


EPSILON = 1e-05


def normalize(values, gain):
    centre = jnp.mean(values, axis=-1, keepdims=True)
    centred = values - centre
    spread = jnp.mean(centred * centred, axis=-1, keepdims=True)
    return centred * lax.rsqrt(spread + EPSILON) * gain


def contract_last(left, right):
    return lax.dot_general(
        left, right, (((1,), (1,)), ((), ())), preferred_element_type=jnp.float32
    )


def shift(value, axis, step):
    size = lax.axis_size(axis)
    return lax.ppermute(value, axis, [(i, (i + step) % size) for i in range(size)])


def swap(value, axis, mask):
    size = lax.axis_size(axis)
    return lax.ppermute(value, axis, [(i, i ^ mask) for i in range(size)])


def sum_sections(partial):
    count = lax.axis_size("section")
    me = lax.axis_index("section")
    width = partial.shape[1] // count

    def piece(owner):
        return lax.dynamic_slice_in_dim(partial, owner * width, width, 1)

    total = piece(me).astype(jnp.float32)
    for step in range(1, count):
        sent = piece(lax.rem(me + step, count)).astype(jnp.bfloat16)
        total = total + shift(sent, "section", step).astype(jnp.float32)
    return total


def gather_sections(mine):
    count = lax.axis_size("section")
    me = lax.axis_index("section")
    width = mine.shape[1]
    whole = jnp.zeros((mine.shape[0], width * count), mine.dtype)
    whole = lax.dynamic_update_slice_in_dim(whole, mine, me * width, 1)
    for step in range(1, count):
        owner = lax.rem(me - step + count, count)
        whole = lax.dynamic_update_slice_in_dim(
            whole, shift(mine, "section", step), owner * width, 1
        )
    return whole


def gather_rows(mine, axis):
    held = mine
    me = lax.axis_index(axis)
    mask = lax.axis_size(axis) // 2
    blocks = [mine]
    while mask >= 1:
        blocks = blocks + [swap(block, axis, mask) for block in blocks]
        mask //= 2
    codes = [0]
    mask = lax.axis_size(axis) // 2
    while mask >= 1:
        codes = codes + [code ^ mask for code in codes]
        mask //= 2
    ordered = []
    for place in range(len(blocks)):
        chosen = blocks[0]
        for code, block in zip(codes[1:], blocks[1:]):
            chosen = jnp.where((me ^ code) == place, block, chosen)
        ordered.append(chosen)
    return jnp.concatenate(ordered, axis=0)


def gather_weight(weight, dimension):
    if lax.axis_size("expert") != 2:
        return lax.all_gather(weight, "expert", axis=dimension, tiled=True)
    other = swap(weight, "expert", 1)
    first = lax.axis_index("expert") == 0
    return jnp.concatenate(
        [jnp.where(first, weight, other), jnp.where(first, other, weight)], axis=dimension
    )


def sum_heads(partial):
    me = lax.axis_index("dp")
    count = lax.axis_size("dp")
    rows, columns = partial.shape
    total = partial.reshape(rows, count, columns // count)
    mask = 1
    while mask < count:
        paired = total.reshape(rows, -1, 2, columns // count)
        bit = (me // mask) % 2
        sent = lax.dynamic_index_in_dim(paired, 1 - bit, 2, False).astype(jnp.bfloat16)
        kept = lax.dynamic_index_in_dim(paired, bit, 2, False)
        total = kept + swap(sent, "dp", mask).astype(jnp.float32)
        mask *= 2
    return total.reshape(rows, columns // count)


def slot_matrix(positions, slots):
    places = lax.broadcasted_iota(jnp.int32, (positions.shape[0], slots), 1)
    return (positions[:, None] == places).astype(jnp.bfloat16)


def attend(query, keys, values, key_mask):
    sequences = key_mask.shape[0]
    head_count = query.shape[1] // HEAD_DIM
    query_split = query.reshape(sequences, -1, head_count, HEAD_DIM)
    keys_split = keys.reshape(sequences, -1, head_count, HEAD_DIM)
    values_split = values.reshape(sequences, -1, head_count, HEAD_DIM)
    scores = jnp.einsum(
        "bqhd,bkhd->bhqk", query_split, keys_split, preferred_element_type=jnp.float32
    ) * HEAD_DIM ** (-0.5)
    scores = jnp.where(key_mask[:, None, None, :], scores, -1e30)
    highest = jnp.max(scores, axis=-1, keepdims=True)
    weights = jnp.exp(scores - highest)
    probs = (weights / jnp.sum(weights, axis=-1, keepdims=True)).astype(jnp.bfloat16)
    context = jnp.einsum("bhqk,bkhd->bqhd", probs, values_split, preferred_element_type=jnp.float32)
    return context.astype(jnp.bfloat16).reshape(-1, head_count * HEAD_DIM)


def exchange(values, group_size, capacity):
    sent = values.reshape(group_size, capacity, values.shape[1])
    arrived = lax.all_to_all(sent, ("expert", "dp"), split_axis=0, concat_axis=0, tiled=True)
    return arrived.reshape(values.shape)


SHORT = pl.CostEstimate(flops=1, bytes_accessed=1, transcendentals=0)


def gate(value, *after):
    return lax.optimization_barrier((value,) + after)[0]


def vmem(shape, dtype):
    return pltpu.VMEM(shape, dtype)


def dispatch_kernel(capacity, layout, section_ref, code_ref, *refs):
    blocks = refs[:-4]
    outs, held, sems = refs[-4:-2], refs[-2], refs[-1]
    count, rows = held.shape[0], held.shape[1]
    half = lax.rem(section_ref[0], 2)
    copies = []
    for place, pieces in enumerate(layout):
        group = []
        for i, (which, start, length, side) in enumerate(pieces):
            there = held.at[place]
            if side is not None:
                offset = (half if side == 0 else 1 - half) * length
                there = held.at[place, pl.ds(pl.multiple_of(offset, length), length)]
            here = blocks[which].at[pl.ds(start, length)]
            group.append(pltpu.make_async_copy(here, there, sems.at[place, i]))
        copies.append(group)
    for group in copies:
        for copy in group:
            copy.start()
    for place, group in enumerate(copies):
        picks = []
        for which in range(2):
            line = which * count + place
            code = code_ref[line : line + 1, :]
            slot = lax.broadcasted_iota(jnp.int32, (capacity, code.shape[1]), 0)
            picks.append(jnp.where(slot == code, 1.0, 0.0))
        pick = jnp.concatenate(picks, axis=0).astype(jnp.bfloat16)
        for copy in group:
            copy.wait()
        picked = jnp.dot(pick, held[place], preferred_element_type=jnp.float32)
        picked = picked.astype(jnp.bfloat16)
        for which, out_ref in enumerate(outs):
            out_ref[place * capacity : (place + 1) * capacity, :] = picked[
                which * capacity : (which + 1) * capacity
            ]


def dispatch(section, code, blocks, layout, capacity):
    rows, features = blocks[0].shape
    count = len(layout)
    picked = jax.ShapeDtypeStruct((count * capacity, features), jnp.bfloat16)
    return pl.pallas_call(
        functools.partial(dispatch_kernel, capacity, layout),
        out_shape=(picked, picked),
        in_specs=[
            pl.BlockSpec(memory_space=pltpu.SMEM),
            pl.BlockSpec(memory_space=pltpu.VMEM),
        ]
        + [pl.BlockSpec(memory_space=pltpu.HBM)] * len(blocks),
        out_specs=[pl.BlockSpec(memory_space=pltpu.VMEM)] * 2,
        scratch_shapes=[
            vmem((count, rows, features), jnp.bfloat16),
            pltpu.SemaphoreType.DMA((count, 2)),
        ],
        compiler_params=pltpu.CompilerParams(vmem_limit_bytes=10 * 1024 * 1024),
        cost_estimate=SHORT,
        name="dispatch",
    )(section, code, *blocks)


def send_home(part, codes, capacity):
    size = lax.axis_size(("expert", "dp"))
    arrived = []
    for place, code in enumerate(codes):
        block = part[place * capacity : (place + 1) * capacity]
        if code:
            block = lax.ppermute(block, ("expert", "dp"), [(i, i ^ code) for i in range(size)])
        arrived.append(block)
    return arrived


def combine_kernel(count, split, section_ref, position_ref, gates_ref, *refs):
    blocks = refs[:count]
    outs, (held, total) = refs[count:-2], refs[-2:]
    capacity, features = blocks[0].shape
    position = position_ref[...]
    slot = lax.broadcasted_iota(jnp.int32, (position.shape[0], count * capacity), 1)
    picks = [
        jnp.where(position[:, k : k + 1] == slot, 1.0, 0.0).astype(jnp.bfloat16) for k in range(2)
    ]
    for i, block in enumerate(blocks):
        held[i * capacity : (i + 1) * capacity, :] = block[...]
    pick = jnp.concatenate(picks, axis=0)
    rows = position.shape[0]
    both = jnp.dot(pick, held[...], preferred_element_type=jnp.float32)
    total[...] = gates_ref[:, 0:1] * both[:rows] + gates_ref[:, 1:2] * both[rows:]
    if split == 1:
        outs[0][...] = total[...].astype(outs[0].dtype)
        return
    sent_ref, kept_first, kept_second = outs
    width = features // split
    for step, out_ref in enumerate((kept_first, sent_ref.at[0], kept_second, sent_ref.at[1])):
        start = pl.multiple_of((section_ref[0] ^ step) * width, width)
        out_ref[...] = total[:, pl.ds(start, width)].astype(out_ref.dtype)


def combine(section, position, gates, blocks, split):
    capacity, features = blocks[0].shape
    rows = position.shape[0]
    count = len(blocks)
    width = features // split
    kept = jax.ShapeDtypeStruct((rows, width), jnp.float32)
    if split == 1:
        out_shape = (jax.ShapeDtypeStruct((rows, width), jnp.bfloat16),)
    else:
        out_shape = (jax.ShapeDtypeStruct((2, rows, width), jnp.bfloat16), kept, kept)
    full = pl.BlockSpec(memory_space=pltpu.VMEM)
    return pl.pallas_call(
        functools.partial(combine_kernel, count, split),
        out_shape=out_shape,
        in_specs=[pl.BlockSpec(memory_space=pltpu.SMEM)] + [full] * (2 + count),
        out_specs=[full] * len(out_shape),
        scratch_shapes=[
            vmem((count * capacity, features), jnp.bfloat16),
            vmem((rows, features), jnp.float32),
        ],
        compiler_params=pltpu.CompilerParams(vmem_limit_bytes=14 * 1024 * 1024),
        cost_estimate=SHORT,
        name="combine",
    )(section, position, gates, *blocks)


def memory_kernel(count, section_ref, tokens_ref, gain_ref, *refs):
    slices, out_ref, mixed = refs[:count], refs[count], refs[count + 1]
    me = section_ref[0]
    width = slices[0].shape[1]
    for step, piece in enumerate(slices):
        owner = me ^ step
        mixed[:, pl.ds(pl.multiple_of(owner * width, width), width)] = piece[...].astype(
            jnp.float32
        )
    values = tokens_ref[...].astype(jnp.float32) + mixed[...]
    out_ref[...] = normalize(values, gain_ref[...]).astype(jnp.bfloat16)


def make_memory(me, tokens, slices, gain):
    return pl.pallas_call(
        functools.partial(memory_kernel, len(slices)),
        out_shape=jax.ShapeDtypeStruct(tokens.shape, jnp.bfloat16),
        in_specs=[
            pl.BlockSpec(memory_space=pltpu.SMEM),
        ]
        + [pl.BlockSpec(memory_space=pltpu.VMEM)] * (2 + len(slices)),
        out_specs=pl.BlockSpec(memory_space=pltpu.VMEM),
        scratch_shapes=[vmem(tokens.shape, jnp.float32)],
        compiler_params=pltpu.CompilerParams(vmem_limit_bytes=8 * 1024 * 1024),
        cost_estimate=SHORT,
        name="memory",
    )(me, tokens, gain[None], *slices)


def normed_kernel(y_ref, states_ref, gain_ref, own_ref, other_ref):
    values = normalize(states_ref[...].astype(jnp.float32), gain_ref[...]).astype(jnp.bfloat16)
    width = own_ref.shape[1]
    for out_ref, first in ((own_ref, y_ref[0] == 0), (other_ref, y_ref[0] == 1)):
        out_ref[...] = jnp.where(first, values[:, :width], values[:, width:])


def normed_halves(y, states, gain):
    rows, features = states.shape
    full = pl.BlockSpec(memory_space=pltpu.VMEM)
    return pl.pallas_call(
        normed_kernel,
        out_shape=(jax.ShapeDtypeStruct((rows, features // 2), jnp.bfloat16),) * 2,
        in_specs=[pl.BlockSpec(memory_space=pltpu.SMEM), full, full],
        out_specs=[full] * 2,
        compiler_params=pltpu.CompilerParams(vmem_limit_bytes=12 * 1024 * 1024),
        cost_estimate=SHORT,
        name="normed",
    )(y.astype(jnp.int32).reshape(1), states, gain)


def attend_kernel(place_ref, lengths_ref, query_ref, *refs):
    near_ref, far_ref, key_own, key_other, value_own, value_other, out_ref = refs[:7]
    source, key_weight, value_weight, keys, values, sems = refs[7:]
    y, core, sentence = place_ref[0], place_ref[1], place_ref[2]
    rows = near_ref.shape[0]
    depth = key_own.shape[0]
    moves = [
        (near_ref, source.at[pl.ds(0, rows)]),
        (far_ref, source.at[pl.ds(rows, rows)]),
        (key_own, key_weight.at[y]),
        (key_other, key_weight.at[1 - y]),
        (value_own, value_weight.at[y]),
        (value_other, value_weight.at[1 - y]),
    ]
    copies = [
        pltpu.make_async_copy(here, there, sems.at[i]) for i, (here, there) in enumerate(moves)
    ]
    for copy in copies:
        copy.start()

    def linear(weight, result):
        total = jnp.dot(source[:, :depth], weight[0], preferred_element_type=jnp.float32)
        total += jnp.dot(source[:, depth:], weight[1], preferred_element_type=jnp.float32)
        result[...] = total.astype(jnp.bfloat16)

    for copy in copies[:4]:
        copy.wait()
    linear(key_weight, keys)
    for copy in copies[4:]:
        copy.wait()
    linear(value_weight, values)

    column = lax.broadcasted_iota(jnp.int32, (query_ref.shape[0], 2 * rows), 1)
    position = jnp.where(column < rows, column + core * rows, column - core * rows)
    valid = position < lengths_ref[sentence]
    for head in range(query_ref.shape[1] // HEAD_DIM):
        span = slice(head * HEAD_DIM, (head + 1) * HEAD_DIM)
        scores = contract_last(query_ref[:, span], keys[:, span]) * HEAD_DIM ** (-0.5)
        scores = jnp.where(valid, scores, -1e30)
        weights = jnp.exp(scores - jnp.max(scores, axis=-1, keepdims=True))
        probs = (weights / jnp.sum(weights, axis=-1, keepdims=True)).astype(jnp.bfloat16)
        result = jnp.dot(probs, values[:, span], preferred_element_type=jnp.float32)
        out_ref[:, span] = result.astype(jnp.bfloat16)


def attend_sentence(place, lengths, query, near, far, key_parts, value_pair):
    rows, features = near.shape
    depth, width = key_parts[0].shape
    hold = pl.BlockSpec(memory_space=pltpu.HBM)
    smem = pl.BlockSpec(memory_space=pltpu.SMEM)
    full = pl.BlockSpec(memory_space=pltpu.VMEM)
    return pl.pallas_call(
        attend_kernel,
        out_shape=jax.ShapeDtypeStruct(query.shape, jnp.bfloat16),
        in_specs=[smem, smem, full] + [hold] * 6,
        out_specs=full,
        scratch_shapes=[
            vmem((2 * rows, features), jnp.bfloat16),
            vmem((2, depth, width), jnp.bfloat16),
            vmem((2, depth, width), jnp.bfloat16),
            vmem((2 * rows, width), jnp.bfloat16),
            vmem((2 * rows, width), jnp.bfloat16),
            pltpu.SemaphoreType.DMA((6,)),
        ],
        compiler_params=pltpu.CompilerParams(vmem_limit_bytes=56 * 1024 * 1024),
        cost_estimate=SHORT,
        name="attend_sentence",
    )(place, lengths, query, near, far, *key_parts, *value_pair)


def project_kernel(place_ref, mine_ref, done_ref, own_ref, other_ref, *refs):
    sent_mine, sent_other, kept_mine, kept_other, context = refs
    y, core, x = place_ref[0], place_ref[1], place_ref[2]
    targets = mine_ref.shape[0]
    for part, sentence in ((mine_ref, x), (done_ref, 1 - x)):
        context[pl.ds(pl.multiple_of(sentence * targets, targets), targets), :] = part[...]
    columns = kept_mine.shape[1]
    outs = ((sent_mine, kept_mine), (sent_other, kept_other))

    def write(weight_ref, chosen):
        for side, out_ref in zip((1 - core, core), chosen):
            span = pl.ds(pl.multiple_of(side * columns, columns), columns)
            part = jnp.dot(context[...], weight_ref[:, span], preferred_element_type=jnp.float32)
            out_ref[...] = part.astype(out_ref.dtype)

    @pl.when(x == y)
    def _():
        write(own_ref, outs[0])
        write(other_ref, outs[1])

    @pl.when(x != y)
    def _():
        write(other_ref, outs[0])
        write(own_ref, outs[1])


def project(place, mine, done, out_own, out_other):
    targets, width = 2 * mine.shape[0], mine.shape[1]
    columns = out_own.shape[1] // 2
    full = pl.BlockSpec(memory_space=pltpu.VMEM)
    sent = jax.ShapeDtypeStruct((targets, columns), jnp.bfloat16)
    kept = jax.ShapeDtypeStruct((targets, columns), jnp.float32)
    return pl.pallas_call(
        project_kernel,
        out_shape=(sent, sent, kept, kept),
        in_specs=[pl.BlockSpec(memory_space=pltpu.SMEM)] + [full] * 4,
        out_specs=[full] * 4,
        scratch_shapes=[vmem((targets, width), jnp.bfloat16)],
        compiler_params=pltpu.CompilerParams(vmem_limit_bytes=16 * 1024 * 1024),
        cost_estimate=SHORT,
        name="project",
    )(place, mine, done, out_own, out_other)


def slope_kernel(codes, here_ref, own_ref, core_ref, rise_own, rise_core, out_ref, slope, *refs):
    grads, rise, weight_out, sems = refs
    rows = own_ref.shape[0]
    hidden = weight_out.shape[0]
    chunk = hidden // 4
    moves = []
    block = 2 * rows // len(codes)
    for order, code in enumerate(codes):
        source = here_ref[0] ^ code
        there = pl.ds(pl.multiple_of(source * block, 16), block)
        here = pl.ds(order * block % rows, block)
        own = order * block < rows
        moves.append(((own_ref if own else core_ref).at[here], grads.at[there]))
        moves.append(((rise_own if own else rise_core).at[here], rise.at[there]))
    for part in range(4):
        span = pl.ds(part * chunk, chunk)
        moves.append((out_ref.at[span], weight_out.at[span]))
    copies = [
        pltpu.make_async_copy(here, there, sems.at[i]) for i, (here, there) in enumerate(moves)
    ]
    for copy in copies:
        copy.start()
    for copy in copies[:-4]:
        copy.wait()
    for part in range(4):
        copies[part - 4].wait()
        span = slice(part * chunk, (part + 1) * chunk)
        back = contract_last(grads[...], weight_out[span, :])
        slope[:, span] = (back * rise[:, span]).astype(jnp.bfloat16)


def expert_slope(here, codes, grads_own, grads_core, rise_own, rise_core, weight_out):
    rows = 2 * grads_own.shape[0]
    hidden, features = weight_out.shape
    hold = pl.BlockSpec(memory_space=pltpu.HBM)
    return pl.pallas_call(
        functools.partial(slope_kernel, codes),
        out_shape=jax.ShapeDtypeStruct((rows, hidden), jnp.bfloat16),
        in_specs=[pl.BlockSpec(memory_space=pltpu.SMEM)] + [hold] * 5,
        out_specs=pl.BlockSpec(memory_space=pltpu.VMEM),
        scratch_shapes=[
            vmem((rows, features), jnp.bfloat16),
            vmem((rows, hidden), jnp.float32),
            vmem((hidden, features), jnp.bfloat16),
            pltpu.SemaphoreType.DMA((4 + 2 * len(codes),)),
        ],
        compiler_params=pltpu.CompilerParams(vmem_limit_bytes=56 * 1024 * 1024),
        cost_estimate=SHORT,
        name="expert_slope",
    )(here, grads_own, grads_core, rise_own, rise_core, weight_out)


def backward_kernel(split, section_ref, slope_ref, in_ref, sent_ref, kept_first, kept_second, *refs):
    weight_in, sems = refs
    width = weight_in.shape[0] // split
    outs = (sent_ref.at[0], sent_ref.at[1], kept_first, kept_second)
    spans, copies = [], []
    for i, step in enumerate((1, 3, 0, 2)):
        start = pl.multiple_of((section_ref[0] ^ step) * width, width)
        spans.append(pl.ds(start, width))
        copies.append(
            pltpu.make_async_copy(in_ref.at[spans[i]], weight_in.at[spans[i]], sems.at[i])
        )
    for copy in copies:
        copy.start()
    for copy, span, out_ref in zip(copies, spans, outs):
        copy.wait()
        part = contract_last(slope_ref[...], weight_in[span, :])
        out_ref[...] = part.astype(out_ref.dtype)


def expert_backward(section, slope, weight_in, split):
    rows, hidden = slope.shape
    features = weight_in.shape[0]
    width = features // split
    full = pl.BlockSpec(memory_space=pltpu.VMEM)
    kept = jax.ShapeDtypeStruct((rows, width), jnp.float32)
    return pl.pallas_call(
        functools.partial(backward_kernel, split),
        out_shape=(jax.ShapeDtypeStruct((2, rows, width), jnp.bfloat16), kept, kept),
        in_specs=[pl.BlockSpec(memory_space=pltpu.SMEM), full, pl.BlockSpec(memory_space=pltpu.HBM)],
        out_specs=[full] * 3,
        scratch_shapes=[
            vmem((features, hidden), jnp.bfloat16),
            pltpu.SemaphoreType.DMA((split,)),
        ],
        compiler_params=pltpu.CompilerParams(vmem_limit_bytes=56 * 1024 * 1024),
        cost_estimate=SHORT,
        name="expert_backward",
    )(section, slope, weight_in)


def small_body(
    tokens,
    expert_ids,
    gate_weights,
    out_grad,
    inner_weight,
    outer_weight,
    final_gain,
    dec_states,
    src_lengths,
    tgt_lengths,
    norm_gain,
    query_weight,
    key_weight,
    value_weight,
    out_weight,
):
    token_count, feature_count = tokens.shape
    group_size = lax.axis_size(("expert", "dp"))
    capacity = 3 * token_count // group_size
    here = lax.axis_index(("expert", "dp"))
    y = lax.axis_index("expert")
    d = lax.axis_index("dp")
    section = lax.axis_index("section")
    sections = lax.axis_size("section")
    half = feature_count // 2
    weight_in = inner_weight[0]
    weight_out = outer_weight[0]
    key_own, value_own, out_own = key_weight[0], value_weight[0], out_weight[0]
    query_own = query_weight[0]

    size = group_size
    near_codes = (0, 2, 4, 6)
    core_codes = (1, 3, 5, 7)
    core, x = d % 2, d // 2
    which_section = section.astype(jnp.int32).reshape(1)

    token_y = swap(tokens, "expert", 1)
    token_x = swap(tokens, "dp", 2)
    row = lax.broadcasted_iota(jnp.int32, (token_count, token_count), 0)
    column = lax.broadcasted_iota(jnp.int32, (token_count, token_count), 1)
    named = expert_ids[:, :, None] == jnp.arange(size, dtype=jnp.int32)[None, None, :]
    either = (named[:, 0] | named[:, 1]).astype(jnp.bfloat16)
    earlier = jnp.dot(
        (column < row).astype(jnp.bfloat16), either, preferred_element_type=jnp.float32
    ).astype(jnp.int32)
    rank = jnp.sum(jnp.where(named, earlier[:, None, :], 0), axis=2)
    codes_of = expert_ids ^ here
    position = ((codes_of >> 1) + 4 * (codes_of & 1)) * capacity + rank

    ids_own = expert_ids.T
    ids_x, ids_y = swap(ids_own, "dp", 2), swap(ids_own, "expert", 1)
    ids_far = swap(ids_x, "expert", 1)
    token_far = swap(gate(token_y, ids_x, ids_y), "dp", 2)

    side = lax.rem(section, 2)
    share = token_count // 2
    grad_half = lax.dynamic_slice_in_dim(out_grad, side * share, share, 0)
    half_y = swap(gate(grad_half, token_y), "expert", 1)
    states = dec_states[0]
    normed_own, asked = normed_halves(y, states, norm_gain)
    asked_here = swap(gate(asked, half_y), "expert", 1)
    query_there = jnp.dot(asked_here, query_own, preferred_element_type=jnp.float32)
    other_y = swap(half_y, "section", 1)

    ids = jnp.stack([ids_own, ids_x, ids_y, ids_far])
    named_there = jnp.concatenate([(ids == here).any(axis=1), (ids == (here ^ 1)).any(axis=1)])
    before = jnp.dot(
        named_there.astype(jnp.bfloat16),
        (row < column).astype(jnp.bfloat16),
        preferred_element_type=jnp.float32,
    ).astype(jnp.int32)
    code = jnp.where(named_there, before, -1)

    def forward(rows, *after):
        pre_act = jnp.dot(rows, weight_in, preferred_element_type=jnp.float32)
        hidden = jax.nn.gelu(gate(pre_act, *after)).astype(jnp.bfloat16)
        part = jnp.dot(hidden, weight_out, preferred_element_type=jnp.float32)
        return pre_act, part.astype(jnp.bfloat16)

    def slope_of(pre_act):
        return jax.vjp(jax.nn.gelu, pre_act)[1](jnp.ones_like(pre_act))[0]

    rows_own, rows_sent = dispatch(
        which_section,
        gate(code, asked),
        [tokens, token_x, token_y, token_far],
        tuple(((place, 0, token_count, None),) for place in range(4)),
        capacity,
    )
    rows_core = swap(rows_sent, "dp", 1)
    pre_own, part_own = forward(rows_own, other_y)
    pre_core, part_core = forward(gate(rows_core, part_own))
    home = send_home(part_own, near_codes, capacity) + send_home(part_core, core_codes, capacity)
    grad_y = jnp.concatenate([gate(half_y, home[4]), other_y], axis=0)

    rise_own, rise_core = slope_of(gate(pre_own, home[1])), slope_of(gate(pre_core, home[1]))
    held_gates = gate(gate_weights, rise_own, rise_core, query_there, grad_y)
    sent_pair, first, second = combine(which_section, position, held_gates, home, sections)
    from_pair = swap(sent_pair, "section", 1)
    grad_x = swap(gate(out_grad, home[5]), "dp", 2)
    grad_far = swap(gate(grad_y, first), "dp", 2)
    to_other = (second + from_pair[1].astype(jnp.float32)).astype(jnp.bfloat16)
    from_other = swap(to_other, "section", 2)
    mixed_sum = first + from_pair[0].astype(jnp.float32)
    mixed_slice = (mixed_sum + from_other.astype(jnp.float32)).astype(jnp.bfloat16)
    key_other = swap(gate(key_own, first), "expert", 1)
    query_back = swap(gate(query_there.astype(jnp.bfloat16), key_other), "expert", 1)
    mixed_near = swap(mixed_slice, "section", 1)
    grads_own, grads_sent = dispatch(
        which_section,
        gate(code, mixed_near),
        [out_grad, grad_x, grad_y, grad_far],
        (
            ((0, 0, token_count, None),),
            ((1, 0, token_count, None),),
            ((2, 0, share, 0), (2, share, share, 1)),
            ((3, 0, share, 0), (3, share, share, 1)),
        ),
        capacity,
    )
    grads_core = swap(grads_sent, "dp", 1)
    grads_core = swap(grads_sent, "dp", 1)
    slope = expert_slope(
        here.astype(jnp.int32).reshape(1),
        near_codes + core_codes,
        grads_own,
        grads_core,
        rise_own,
        rise_core,
        weight_out,
    )
    back_pair, back_first, back_second = expert_backward(
        which_section, slope, weight_in, sections
    )
    mixed_far = swap(jnp.stack([mixed_slice, gate(mixed_near, key_other)]), "section", 2)
    slices = [mixed_slice, mixed_near, mixed_far[0], mixed_far[1]]

    value_other = swap(gate(value_own, mixed_near), "expert", 1)

    query_here = jnp.dot(normed_own, query_own, preferred_element_type=jnp.float32)
    query = (query_here + query_back.astype(jnp.float32)).astype(jnp.bfloat16)

    memory = make_memory(which_section, gate(tokens, query_back), slices, final_gain)
    out_other = swap(gate(out_own, memory), "expert", 1)
    memory_x = swap(memory, "dp", 2)
    memory_core = swap(memory, "dp", 1)

    def sentence(which, near, far, *after):
        place = gate(jnp.stack([y, core, which]).astype(jnp.int32), *after)
        rows_of = lax.dynamic_slice_in_dim(query, which * TGT_LEN, TGT_LEN, 0)
        parts = (key_own, key_other), (value_own, value_other)
        return attend_sentence(place, src_lengths, rows_of, near, far, *parts)

    back_from_pair = swap(back_pair, "section", 1)
    back_to_other = (back_second + back_from_pair[1].astype(jnp.float32)).astype(jnp.bfloat16)
    back_from_other = swap(back_to_other, "section", 2)
    backward_sum = back_first + back_from_pair[0].astype(jnp.float32)
    backward_sum = backward_sum + back_from_other.astype(jnp.float32)
    context_own = sentence(x, memory, memory_core)
    memory_far = swap(gate(memory_x, context_own), "dp", 1)
    context_other = sentence(1 - x, memory_x, memory_far)
    place = jnp.stack([y, core, x]).astype(jnp.int32)
    sent_mine, sent_other, kept_mine, kept_other = project(
        place, context_own, context_other, out_own, out_other
    )

    core_other = swap(sent_other, "dp", 1)
    core_mine = swap(sent_mine, "dp", 1)
    last = gate(kept_other, back_from_other) + core_other.astype(jnp.float32)
    from_x = swap(last.astype(jnp.bfloat16), "dp", 2)
    attended = kept_mine + core_mine.astype(jnp.float32) + from_x.astype(jnp.float32)
    dec_out = add_residual(attended, states, tgt_lengths)

    grads_home = exchange(gate(backward_sum.astype(jnp.bfloat16), last), group_size, capacity)
    natural = expert_ids * capacity + rank
    (token_grad,) = combine(
        which_section, natural, gate_weights, [grads_home], 1
    )
    return (dec_out[None], token_grad)


def add_residual(attended, states, tgt_lengths):
    my_columns = attended.shape[1]
    residual = lax.dynamic_slice_in_dim(
        states, lax.axis_index("dp") * my_columns, my_columns, 1
    ).astype(jnp.float32)
    row_mask = (jnp.arange(TGT_LEN, dtype=jnp.int32)[None, :] < tgt_lengths[:, None]).reshape(-1, 1)
    return (residual + jnp.where(row_mask, attended, 0.0)).astype(jnp.bfloat16)


def body(
    tokens,
    expert_ids,
    gate_weights,
    out_grad,
    inner_weight,
    outer_weight,
    final_gain,
    dec_states,
    src_lengths,
    tgt_lengths,
    norm_gain,
    query_weight,
    key_weight,
    value_weight,
    out_weight,
):
    token_count, feature_count = tokens.shape
    group_size = lax.axis_size(("expert", "dp"))
    capacity = 3 * token_count // group_size
    slots = group_size * capacity

    named = expert_ids[:, :, None] == jnp.arange(group_size, dtype=jnp.int32)[None, None, :]
    either = (named[:, 0] | named[:, 1]).astype(jnp.bfloat16)
    row = lax.broadcasted_iota(jnp.int32, (token_count, token_count), 0)
    column = lax.broadcasted_iota(jnp.int32, (token_count, token_count), 1)
    earlier = jnp.dot(
        (column < row).astype(jnp.bfloat16), either, preferred_element_type=jnp.float32
    ).astype(jnp.int32)
    rank = jnp.sum(jnp.where(named, earlier[:, None, :], 0), axis=2)
    position = expert_ids * capacity + rank
    pick_first = slot_matrix(position[:, 0], slots)
    pick_second = slot_matrix(position[:, 1], slots)
    fill = (pick_first + pick_second).T

    def place(values):
        return jnp.dot(fill, values, preferred_element_type=jnp.float32).astype(jnp.bfloat16)

    def combine(arrived):
        first = jnp.dot(pick_first, arrived, preferred_element_type=jnp.float32)
        second = jnp.dot(pick_second, arrived, preferred_element_type=jnp.float32)
        return gate_weights[:, :1] * first + gate_weights[:, 1:] * second

    weight_in = inner_weight[0]
    weight_out = outer_weight[0]
    arrived_rows = exchange(place(tokens), group_size, capacity)
    pre_act = jnp.dot(arrived_rows, weight_in, preferred_element_type=jnp.float32)
    hidden = jax.nn.gelu(pre_act).astype(jnp.bfloat16)
    forward_part = jnp.dot(hidden, weight_out, preferred_element_type=jnp.float32)
    arrived_grads = exchange(place(out_grad), group_size, capacity)
    outputs_home = exchange(forward_part.astype(jnp.bfloat16), group_size, capacity)
    mixed_slice = sum_sections(combine(outputs_home)).astype(jnp.bfloat16)
    mixed = gather_sections(mixed_slice).astype(jnp.float32)
    memory = normalize(tokens.astype(jnp.float32) + mixed, final_gain).astype(jnp.bfloat16)

    back = contract_last(arrived_grads, weight_out)
    slope = jax.vjp(jax.nn.gelu, pre_act)[1](back)[0].astype(jnp.bfloat16)
    backward_part = contract_last(slope, weight_in)
    backward_slice = sum_sections(backward_part).astype(jnp.bfloat16)
    grads_home = exchange(backward_slice, group_size, capacity)
    token_grad = combine(grads_home).astype(jnp.bfloat16)

    states = dec_states[0]
    normed = normalize(states.astype(jnp.float32), norm_gain[0]).astype(jnp.bfloat16)
    full_query = gather_weight(query_weight[0], 0)
    full_key = gather_weight(key_weight[0], 0)
    full_value = gather_weight(value_weight[0], 0)
    full_out = gather_weight(out_weight[0], 1)
    query_sum = jnp.dot(normed, full_query, preferred_element_type=jnp.float32)
    source = gather_rows(memory, "dp")
    key_sum = jnp.dot(source, full_key, preferred_element_type=jnp.float32)
    value_sum = jnp.dot(source, full_value, preferred_element_type=jnp.float32)
    key_mask = jnp.arange(SRC_LEN, dtype=jnp.int32)[None, :] < src_lengths[:, None]
    context = attend(
        query_sum.astype(jnp.bfloat16),
        key_sum.astype(jnp.bfloat16),
        value_sum.astype(jnp.bfloat16),
        key_mask,
    )
    attended = sum_heads(jnp.dot(context, full_out, preferred_element_type=jnp.float32))
    dec_out = add_residual(attended, states, tgt_lengths)
    return (dec_out[None], token_grad)


def solution(mesh):
    in_specs = (
        P(("expert", "dp"), None),
        P(("expert", "dp"), None),
        P(("expert", "dp"), None),
        P(("expert", "dp"), None),
        P(("expert", "dp"), None, "section"),
        P(("expert", "dp"), "section", None),
        P(),
        P("section", "expert", None),
        P("expert"),
        P("expert"),
        P("section", None),
        P("section", "expert", "dp"),
        P("section", "expert", "dp"),
        P("section", "expert", "dp"),
        P("section", "dp", "expert"),
    )
    out_specs = (P("section", "expert", "dp"), P(("expert", "dp"), "section"))
    small = (mesh.shape["section"], mesh.shape["expert"], mesh.shape["dp"]) == (4, 2, 4)
    chosen = small_body if small else body
    return jax.shard_map(chosen, mesh=mesh, in_specs=in_specs, out_specs=out_specs, check_vma=False)
```

```python
import functools

import jax
import jax.numpy as jnp
from jax import lax
from jax.experimental import pallas as pl
from jax.experimental.pallas import tpu as pltpu
from jax.sharding import PartitionSpec as P

HEAD_DIM = 128
SRC_LEN = 256
TGT_LEN = 128


EPSILON = 1e-05


def normalize(values, gain):
    centre = jnp.mean(values, axis=-1, keepdims=True)
    centred = values - centre
    spread = jnp.mean(centred * centred, axis=-1, keepdims=True)
    return centred * lax.rsqrt(spread + EPSILON) * gain


def contract_last(left, right):
    return lax.dot_general(
        left, right, (((1,), (1,)), ((), ())), preferred_element_type=jnp.float32
    )


def shift(value, axis, step):
    size = lax.axis_size(axis)
    return lax.ppermute(value, axis, [(i, (i + step) % size) for i in range(size)])


def swap(value, axis, mask):
    size = lax.axis_size(axis)
    return lax.ppermute(value, axis, [(i, i ^ mask) for i in range(size)])


def sum_sections(partial):
    count = lax.axis_size("section")
    me = lax.axis_index("section")
    width = partial.shape[1] // count

    def piece(owner):
        return lax.dynamic_slice_in_dim(partial, owner * width, width, 1)

    total = piece(me).astype(jnp.float32)
    for step in range(1, count):
        sent = piece(lax.rem(me + step, count)).astype(jnp.bfloat16)
        total = total + shift(sent, "section", step).astype(jnp.float32)
    return total


def gather_sections(mine):
    count = lax.axis_size("section")
    me = lax.axis_index("section")
    width = mine.shape[1]
    whole = jnp.zeros((mine.shape[0], width * count), mine.dtype)
    whole = lax.dynamic_update_slice_in_dim(whole, mine, me * width, 1)
    for step in range(1, count):
        owner = lax.rem(me - step + count, count)
        whole = lax.dynamic_update_slice_in_dim(
            whole, shift(mine, "section", step), owner * width, 1
        )
    return whole


def gather_rows(mine, axis):
    held = mine
    me = lax.axis_index(axis)
    mask = lax.axis_size(axis) // 2
    blocks = [mine]
    while mask >= 1:
        blocks = blocks + [swap(block, axis, mask) for block in blocks]
        mask //= 2
    codes = [0]
    mask = lax.axis_size(axis) // 2
    while mask >= 1:
        codes = codes + [code ^ mask for code in codes]
        mask //= 2
    ordered = []
    for place in range(len(blocks)):
        chosen = blocks[0]
        for code, block in zip(codes[1:], blocks[1:]):
            chosen = jnp.where((me ^ code) == place, block, chosen)
        ordered.append(chosen)
    return jnp.concatenate(ordered, axis=0)


def gather_weight(weight, dimension):
    if lax.axis_size("expert") != 2:
        return lax.all_gather(weight, "expert", axis=dimension, tiled=True)
    other = swap(weight, "expert", 1)
    first = lax.axis_index("expert") == 0
    return jnp.concatenate(
        [jnp.where(first, weight, other), jnp.where(first, other, weight)], axis=dimension
    )


def sum_heads(partial):
    me = lax.axis_index("dp")
    count = lax.axis_size("dp")
    rows, columns = partial.shape
    total = partial.reshape(rows, count, columns // count)
    mask = 1
    while mask < count:
        paired = total.reshape(rows, -1, 2, columns // count)
        bit = (me // mask) % 2
        sent = lax.dynamic_index_in_dim(paired, 1 - bit, 2, False).astype(jnp.bfloat16)
        kept = lax.dynamic_index_in_dim(paired, bit, 2, False)
        total = kept + swap(sent, "dp", mask).astype(jnp.float32)
        mask *= 2
    return total.reshape(rows, columns // count)


def slot_matrix(positions, slots):
    places = lax.broadcasted_iota(jnp.int32, (positions.shape[0], slots), 1)
    return (positions[:, None] == places).astype(jnp.bfloat16)


def attend(query, keys, values, key_mask):
    sequences = key_mask.shape[0]
    head_count = query.shape[1] // HEAD_DIM
    query_split = query.reshape(sequences, -1, head_count, HEAD_DIM)
    keys_split = keys.reshape(sequences, -1, head_count, HEAD_DIM)
    values_split = values.reshape(sequences, -1, head_count, HEAD_DIM)
    scores = jnp.einsum(
        "bqhd,bkhd->bhqk", query_split, keys_split, preferred_element_type=jnp.float32
    ) * HEAD_DIM ** (-0.5)
    scores = jnp.where(key_mask[:, None, None, :], scores, -1e30)
    highest = jnp.max(scores, axis=-1, keepdims=True)
    weights = jnp.exp(scores - highest)
    probs = (weights / jnp.sum(weights, axis=-1, keepdims=True)).astype(jnp.bfloat16)
    context = jnp.einsum("bhqk,bkhd->bqhd", probs, values_split, preferred_element_type=jnp.float32)
    return context.astype(jnp.bfloat16).reshape(-1, head_count * HEAD_DIM)


def exchange(values, group_size, capacity):
    sent = values.reshape(group_size, capacity, values.shape[1])
    arrived = lax.all_to_all(sent, ("expert", "dp"), split_axis=0, concat_axis=0, tiled=True)
    return arrived.reshape(values.shape)


SHORT = pl.CostEstimate(flops=1, bytes_accessed=1, transcendentals=0)


def gate(value, *after):
    return lax.optimization_barrier((value,) + after)[0]


def vmem(shape, dtype):
    return pltpu.VMEM(shape, dtype)


def dispatch_kernel(capacity, layout, section_ref, code_ref, *refs):
    blocks = refs[:-4]
    outs, held, sems = refs[-4:-2], refs[-2], refs[-1]
    count, rows = held.shape[0], held.shape[1]
    half = lax.rem(section_ref[0], 2)
    copies = []
    for place, pieces in enumerate(layout):
        group = []
        for i, (which, start, length, side) in enumerate(pieces):
            there = held.at[place]
            if side is not None:
                offset = (half if side == 0 else 1 - half) * length
                there = held.at[place, pl.ds(pl.multiple_of(offset, length), length)]
            here = blocks[which].at[pl.ds(start, length)]
            group.append(pltpu.make_async_copy(here, there, sems.at[place, i]))
        copies.append(group)
    for group in copies:
        for copy in group:
            copy.start()
    for place, group in enumerate(copies):
        picks = []
        for which in range(2):
            line = which * count + place
            code = code_ref[line : line + 1, :]
            slot = lax.broadcasted_iota(jnp.int32, (capacity, code.shape[1]), 0)
            picks.append(jnp.where(slot == code, 1.0, 0.0))
        pick = jnp.concatenate(picks, axis=0).astype(jnp.bfloat16)
        for copy in group:
            copy.wait()
        picked = jnp.dot(pick, held[place], preferred_element_type=jnp.float32)
        picked = picked.astype(jnp.bfloat16)
        for which, out_ref in enumerate(outs):
            out_ref[place * capacity : (place + 1) * capacity, :] = picked[
                which * capacity : (which + 1) * capacity
            ]


def dispatch(section, code, blocks, layout, capacity):
    rows, features = blocks[0].shape
    count = len(layout)
    picked = jax.ShapeDtypeStruct((count * capacity, features), jnp.bfloat16)
    return pl.pallas_call(
        functools.partial(dispatch_kernel, capacity, layout),
        out_shape=(picked, picked),
        in_specs=[
            pl.BlockSpec(memory_space=pltpu.SMEM),
            pl.BlockSpec(memory_space=pltpu.VMEM),
        ]
        + [pl.BlockSpec(memory_space=pltpu.HBM)] * len(blocks),
        out_specs=[pl.BlockSpec(memory_space=pltpu.VMEM)] * 2,
        scratch_shapes=[
            vmem((count, rows, features), jnp.bfloat16),
            pltpu.SemaphoreType.DMA((count, 2)),
        ],
        compiler_params=pltpu.CompilerParams(vmem_limit_bytes=10 * 1024 * 1024),
        cost_estimate=SHORT,
        name="dispatch",
    )(section, code, *blocks)


def send_home(part, codes, capacity):
    size = lax.axis_size(("expert", "dp"))
    arrived = []
    for place, code in enumerate(codes):
        block = part[place * capacity : (place + 1) * capacity]
        if code:
            block = lax.ppermute(block, ("expert", "dp"), [(i, i ^ code) for i in range(size)])
        arrived.append(block)
    return arrived


def combine_kernel(count, split, section_ref, position_ref, gates_ref, *refs):
    blocks = refs[:count]
    outs, (held, total) = refs[count:-2], refs[-2:]
    capacity, features = blocks[0].shape
    position = position_ref[...]
    slot = lax.broadcasted_iota(jnp.int32, (position.shape[0], count * capacity), 1)
    picks = [
        jnp.where(position[:, k : k + 1] == slot, 1.0, 0.0).astype(jnp.bfloat16) for k in range(2)
    ]
    for i, block in enumerate(blocks):
        held[i * capacity : (i + 1) * capacity, :] = block[...]
    pick = jnp.concatenate(picks, axis=0)
    rows = position.shape[0]
    both = jnp.dot(pick, held[...], preferred_element_type=jnp.float32)
    total[...] = gates_ref[:, 0:1] * both[:rows] + gates_ref[:, 1:2] * both[rows:]
    if split == 1:
        outs[0][...] = total[...].astype(outs[0].dtype)
        return
    sent_ref, kept_first, kept_second = outs
    width = features // split
    for step, out_ref in enumerate((kept_first, sent_ref.at[0], kept_second, sent_ref.at[1])):
        start = pl.multiple_of((section_ref[0] ^ step) * width, width)
        out_ref[...] = total[:, pl.ds(start, width)].astype(out_ref.dtype)


def combine(section, position, gates, blocks, split):
    capacity, features = blocks[0].shape
    rows = position.shape[0]
    count = len(blocks)
    width = features // split
    kept = jax.ShapeDtypeStruct((rows, width), jnp.float32)
    if split == 1:
        out_shape = (jax.ShapeDtypeStruct((rows, width), jnp.bfloat16),)
    else:
        out_shape = (jax.ShapeDtypeStruct((2, rows, width), jnp.bfloat16), kept, kept)
    full = pl.BlockSpec(memory_space=pltpu.VMEM)
    return pl.pallas_call(
        functools.partial(combine_kernel, count, split),
        out_shape=out_shape,
        in_specs=[pl.BlockSpec(memory_space=pltpu.SMEM)] + [full] * (2 + count),
        out_specs=[full] * len(out_shape),
        scratch_shapes=[
            vmem((count * capacity, features), jnp.bfloat16),
            vmem((rows, features), jnp.float32),
        ],
        compiler_params=pltpu.CompilerParams(vmem_limit_bytes=14 * 1024 * 1024),
        cost_estimate=SHORT,
        name="combine",
    )(section, position, gates, *blocks)


def memory_kernel(count, section_ref, tokens_ref, gain_ref, *refs):
    slices, out_ref, mixed = refs[:count], refs[count], refs[count + 1]
    me = section_ref[0]
    width = slices[0].shape[1]
    for step, piece in enumerate(slices):
        owner = me ^ step
        mixed[:, pl.ds(pl.multiple_of(owner * width, width), width)] = piece[...].astype(
            jnp.float32
        )
    values = tokens_ref[...].astype(jnp.float32) + mixed[...]
    out_ref[...] = normalize(values, gain_ref[...]).astype(jnp.bfloat16)


def make_memory(me, tokens, slices, gain):
    return pl.pallas_call(
        functools.partial(memory_kernel, len(slices)),
        out_shape=jax.ShapeDtypeStruct(tokens.shape, jnp.bfloat16),
        in_specs=[
            pl.BlockSpec(memory_space=pltpu.SMEM),
        ]
        + [pl.BlockSpec(memory_space=pltpu.VMEM)] * (2 + len(slices)),
        out_specs=pl.BlockSpec(memory_space=pltpu.VMEM),
        scratch_shapes=[vmem(tokens.shape, jnp.float32)],
        compiler_params=pltpu.CompilerParams(vmem_limit_bytes=8 * 1024 * 1024),
        cost_estimate=SHORT,
        name="memory",
    )(me, tokens, gain[None], *slices)


def normed_kernel(y_ref, states_ref, gain_ref, own_ref, other_ref):
    values = normalize(states_ref[...].astype(jnp.float32), gain_ref[...]).astype(jnp.bfloat16)
    width = own_ref.shape[1]
    for out_ref, first in ((own_ref, y_ref[0] == 0), (other_ref, y_ref[0] == 1)):
        out_ref[...] = jnp.where(first, values[:, :width], values[:, width:])


def normed_halves(y, states, gain):
    rows, features = states.shape
    full = pl.BlockSpec(memory_space=pltpu.VMEM)
    return pl.pallas_call(
        normed_kernel,
        out_shape=(jax.ShapeDtypeStruct((rows, features // 2), jnp.bfloat16),) * 2,
        in_specs=[pl.BlockSpec(memory_space=pltpu.SMEM), full, full],
        out_specs=[full] * 2,
        compiler_params=pltpu.CompilerParams(vmem_limit_bytes=12 * 1024 * 1024),
        cost_estimate=SHORT,
        name="normed",
    )(y.astype(jnp.int32).reshape(1), states, gain)


def attend_kernel(place_ref, lengths_ref, query_ref, *refs):
    near_ref, far_ref, key_own, key_other, value_own, value_other, out_ref = refs[:7]
    source, key_weight, value_weight, keys, values, sems = refs[7:]
    y, core, sentence = place_ref[0], place_ref[1], place_ref[2]
    rows = near_ref.shape[0]
    depth = key_own.shape[0]
    moves = [
        (near_ref, source.at[pl.ds(0, rows)]),
        (far_ref, source.at[pl.ds(rows, rows)]),
        (key_own, key_weight.at[y]),
        (key_other, key_weight.at[1 - y]),
        (value_own, value_weight.at[y]),
        (value_other, value_weight.at[1 - y]),
    ]
    copies = [
        pltpu.make_async_copy(here, there, sems.at[i]) for i, (here, there) in enumerate(moves)
    ]
    for copy in copies:
        copy.start()

    def linear(weight, result):
        total = jnp.dot(source[:, :depth], weight[0], preferred_element_type=jnp.float32)
        total += jnp.dot(source[:, depth:], weight[1], preferred_element_type=jnp.float32)
        result[...] = total.astype(jnp.bfloat16)

    for copy in copies[:4]:
        copy.wait()
    linear(key_weight, keys)
    for copy in copies[4:]:
        copy.wait()
    linear(value_weight, values)

    column = lax.broadcasted_iota(jnp.int32, (query_ref.shape[0], 2 * rows), 1)
    position = jnp.where(column < rows, column + core * rows, column - core * rows)
    valid = position < lengths_ref[sentence]
    for head in range(query_ref.shape[1] // HEAD_DIM):
        span = slice(head * HEAD_DIM, (head + 1) * HEAD_DIM)
        scores = contract_last(query_ref[:, span], keys[:, span]) * HEAD_DIM ** (-0.5)
        scores = jnp.where(valid, scores, -1e30)
        weights = jnp.exp(scores - jnp.max(scores, axis=-1, keepdims=True))
        probs = (weights / jnp.sum(weights, axis=-1, keepdims=True)).astype(jnp.bfloat16)
        result = jnp.dot(probs, values[:, span], preferred_element_type=jnp.float32)
        out_ref[:, span] = result.astype(jnp.bfloat16)


def attend_sentence(place, lengths, query, near, far, key_parts, value_pair):
    rows, features = near.shape
    depth, width = key_parts[0].shape
    hold = pl.BlockSpec(memory_space=pltpu.HBM)
    smem = pl.BlockSpec(memory_space=pltpu.SMEM)
    full = pl.BlockSpec(memory_space=pltpu.VMEM)
    return pl.pallas_call(
        attend_kernel,
        out_shape=jax.ShapeDtypeStruct(query.shape, jnp.bfloat16),
        in_specs=[smem, smem, full] + [hold] * 6,
        out_specs=full,
        scratch_shapes=[
            vmem((2 * rows, features), jnp.bfloat16),
            vmem((2, depth, width), jnp.bfloat16),
            vmem((2, depth, width), jnp.bfloat16),
            vmem((2 * rows, width), jnp.bfloat16),
            vmem((2 * rows, width), jnp.bfloat16),
            pltpu.SemaphoreType.DMA((6,)),
        ],
        compiler_params=pltpu.CompilerParams(vmem_limit_bytes=56 * 1024 * 1024),
        cost_estimate=SHORT,
        name="attend_sentence",
    )(place, lengths, query, near, far, *key_parts, *value_pair)


def project_kernel(place_ref, mine_ref, done_ref, own_ref, other_ref, *refs):
    sent_mine, sent_other, kept_mine, kept_other, context = refs
    y, core, x = place_ref[0], place_ref[1], place_ref[2]
    targets = mine_ref.shape[0]
    for part, sentence in ((mine_ref, x), (done_ref, 1 - x)):
        context[pl.ds(pl.multiple_of(sentence * targets, targets), targets), :] = part[...]
    columns = kept_mine.shape[1]
    outs = ((sent_mine, kept_mine), (sent_other, kept_other))

    def write(weight_ref, chosen):
        for side, out_ref in zip((1 - core, core), chosen):
            span = pl.ds(pl.multiple_of(side * columns, columns), columns)
            part = jnp.dot(context[...], weight_ref[:, span], preferred_element_type=jnp.float32)
            out_ref[...] = part.astype(out_ref.dtype)

    @pl.when(x == y)
    def _():
        write(own_ref, outs[0])
        write(other_ref, outs[1])

    @pl.when(x != y)
    def _():
        write(other_ref, outs[0])
        write(own_ref, outs[1])


def project(place, mine, done, out_own, out_other):
    targets, width = 2 * mine.shape[0], mine.shape[1]
    columns = out_own.shape[1] // 2
    full = pl.BlockSpec(memory_space=pltpu.VMEM)
    sent = jax.ShapeDtypeStruct((targets, columns), jnp.bfloat16)
    kept = jax.ShapeDtypeStruct((targets, columns), jnp.float32)
    return pl.pallas_call(
        project_kernel,
        out_shape=(sent, sent, kept, kept),
        in_specs=[pl.BlockSpec(memory_space=pltpu.SMEM)] + [full] * 4,
        out_specs=[full] * 4,
        scratch_shapes=[vmem((targets, width), jnp.bfloat16)],
        compiler_params=pltpu.CompilerParams(vmem_limit_bytes=16 * 1024 * 1024),
        cost_estimate=SHORT,
        name="project",
    )(place, mine, done, out_own, out_other)


def slope_kernel(codes, here_ref, own_ref, core_ref, rise_own, rise_core, out_ref, slope, *refs):
    grads, rise, weight_out, sems = refs
    rows = own_ref.shape[0]
    hidden = weight_out.shape[0]
    chunk = hidden // 4
    moves = []
    block = 2 * rows // len(codes)
    for order, code in enumerate(codes):
        source = here_ref[0] ^ code
        there = pl.ds(pl.multiple_of(source * block, 16), block)
        here = pl.ds(order * block % rows, block)
        own = order * block < rows
        moves.append(((own_ref if own else core_ref).at[here], grads.at[there]))
        moves.append(((rise_own if own else rise_core).at[here], rise.at[there]))
    for part in range(4):
        span = pl.ds(part * chunk, chunk)
        moves.append((out_ref.at[span], weight_out.at[span]))
    copies = [
        pltpu.make_async_copy(here, there, sems.at[i]) for i, (here, there) in enumerate(moves)
    ]
    for copy in copies:
        copy.start()
    for copy in copies[:-4]:
        copy.wait()
    for part in range(4):
        copies[part - 4].wait()
        span = slice(part * chunk, (part + 1) * chunk)
        back = contract_last(grads[...], weight_out[span, :])
        slope[:, span] = (back * rise[:, span]).astype(jnp.bfloat16)


def expert_slope(here, codes, grads_own, grads_core, rise_own, rise_core, weight_out):
    rows = 2 * grads_own.shape[0]
    hidden, features = weight_out.shape
    hold = pl.BlockSpec(memory_space=pltpu.HBM)
    return pl.pallas_call(
        functools.partial(slope_kernel, codes),
        out_shape=jax.ShapeDtypeStruct((rows, hidden), jnp.bfloat16),
        in_specs=[pl.BlockSpec(memory_space=pltpu.SMEM)] + [hold] * 5,
        out_specs=pl.BlockSpec(memory_space=pltpu.VMEM),
        scratch_shapes=[
            vmem((rows, features), jnp.bfloat16),
            vmem((rows, hidden), jnp.float32),
            vmem((hidden, features), jnp.bfloat16),
            pltpu.SemaphoreType.DMA((4 + 2 * len(codes),)),
        ],
        compiler_params=pltpu.CompilerParams(vmem_limit_bytes=56 * 1024 * 1024),
        cost_estimate=SHORT,
        name="expert_slope",
    )(here, grads_own, grads_core, rise_own, rise_core, weight_out)


def backward_kernel(split, section_ref, slope_ref, in_ref, sent_ref, kept_first, kept_second, *refs):
    weight_in, sems = refs
    width = weight_in.shape[0] // split
    outs = (sent_ref.at[0], sent_ref.at[1], kept_first, kept_second)
    spans, copies = [], []
    for i, step in enumerate((1, 3, 0, 2)):
        start = pl.multiple_of((section_ref[0] ^ step) * width, width)
        spans.append(pl.ds(start, width))
        copies.append(
            pltpu.make_async_copy(in_ref.at[spans[i]], weight_in.at[spans[i]], sems.at[i])
        )
    for copy in copies:
        copy.start()
    for copy, span, out_ref in zip(copies, spans, outs):
        copy.wait()
        part = contract_last(slope_ref[...], weight_in[span, :])
        out_ref[...] = part.astype(out_ref.dtype)


def expert_backward(section, slope, weight_in, split):
    rows, hidden = slope.shape
    features = weight_in.shape[0]
    width = features // split
    full = pl.BlockSpec(memory_space=pltpu.VMEM)
    kept = jax.ShapeDtypeStruct((rows, width), jnp.float32)
    return pl.pallas_call(
        functools.partial(backward_kernel, split),
        out_shape=(jax.ShapeDtypeStruct((2, rows, width), jnp.bfloat16), kept, kept),
        in_specs=[pl.BlockSpec(memory_space=pltpu.SMEM), full, pl.BlockSpec(memory_space=pltpu.HBM)],
        out_specs=[full] * 3,
        scratch_shapes=[
            vmem((features, hidden), jnp.bfloat16),
            pltpu.SemaphoreType.DMA((split,)),
        ],
        compiler_params=pltpu.CompilerParams(vmem_limit_bytes=56 * 1024 * 1024),
        cost_estimate=SHORT,
        name="expert_backward",
    )(section, slope, weight_in)


def small_body(
    tokens,
    expert_ids,
    gate_weights,
    out_grad,
    inner_weight,
    outer_weight,
    final_gain,
    dec_states,
    src_lengths,
    tgt_lengths,
    norm_gain,
    query_weight,
    key_weight,
    value_weight,
    out_weight,
):
    token_count, feature_count = tokens.shape
    group_size = lax.axis_size(("expert", "dp"))
    capacity = 3 * token_count // group_size
    here = lax.axis_index(("expert", "dp"))
    y = lax.axis_index("expert")
    d = lax.axis_index("dp")
    section = lax.axis_index("section")
    sections = lax.axis_size("section")
    half = feature_count // 2
    weight_in = inner_weight[0]
    weight_out = outer_weight[0]
    key_own, value_own, out_own = key_weight[0], value_weight[0], out_weight[0]
    query_own = query_weight[0]

    size = group_size
    near_codes = (0, 2, 4, 6)
    core_codes = (1, 3, 5, 7)
    core, x = d % 2, d // 2
    which_section = section.astype(jnp.int32).reshape(1)

    token_y = swap(tokens, "expert", 1)
    token_x = swap(tokens, "dp", 2)
    row = lax.broadcasted_iota(jnp.int32, (token_count, token_count), 0)
    column = lax.broadcasted_iota(jnp.int32, (token_count, token_count), 1)
    named = expert_ids[:, :, None] == jnp.arange(size, dtype=jnp.int32)[None, None, :]
    either = (named[:, 0] | named[:, 1]).astype(jnp.bfloat16)
    earlier = jnp.dot(
        (column < row).astype(jnp.bfloat16), either, preferred_element_type=jnp.float32
    ).astype(jnp.int32)
    rank = jnp.sum(jnp.where(named, earlier[:, None, :], 0), axis=2)
    codes_of = expert_ids ^ here
    position = ((codes_of >> 1) + 4 * (codes_of & 1)) * capacity + rank

    ids_own = expert_ids.T
    ids_x, ids_y = swap(ids_own, "dp", 2), swap(ids_own, "expert", 1)
    ids_far = swap(ids_x, "expert", 1)
    token_far = swap(gate(token_y, ids_x, ids_y), "dp", 2)

    side = lax.rem(section, 2)
    share = token_count // 2
    grad_half = lax.dynamic_slice_in_dim(out_grad, side * share, share, 0)
    half_y = swap(gate(grad_half, token_y), "expert", 1)
    states = dec_states[0]
    normed_own, asked = normed_halves(y, states, norm_gain)
    asked_here = swap(gate(asked, half_y), "expert", 1)
    query_there = jnp.dot(asked_here, query_own, preferred_element_type=jnp.float32)
    other_y = swap(half_y, "section", 1)

    ids = jnp.stack([ids_own, ids_x, ids_y, ids_far])
    named_there = jnp.concatenate([(ids == here).any(axis=1), (ids == (here ^ 1)).any(axis=1)])
    before = jnp.dot(
        named_there.astype(jnp.bfloat16),
        (row < column).astype(jnp.bfloat16),
        preferred_element_type=jnp.float32,
    ).astype(jnp.int32)
    code = jnp.where(named_there, before, -1)

    def forward(rows, *after):
        pre_act = jnp.dot(rows, weight_in, preferred_element_type=jnp.float32)
        hidden = jax.nn.gelu(gate(pre_act, *after)).astype(jnp.bfloat16)
        part = jnp.dot(hidden, weight_out, preferred_element_type=jnp.float32)
        return pre_act, part.astype(jnp.bfloat16)

    def slope_of(pre_act):
        return jax.vjp(jax.nn.gelu, pre_act)[1](jnp.ones_like(pre_act))[0]

    rows_own, rows_sent = dispatch(
        which_section,
        gate(code, asked),
        [tokens, token_x, token_y, token_far],
        tuple(((place, 0, token_count, None),) for place in range(4)),
        capacity,
    )
    rows_core = swap(rows_sent, "dp", 1)
    pre_own, part_own = forward(rows_own, other_y)
    pre_core, part_core = forward(gate(rows_core, part_own))
    home = send_home(part_own, near_codes, capacity) + send_home(part_core, core_codes, capacity)
    grad_y = jnp.concatenate([gate(half_y, home[4]), other_y], axis=0)

    rise_own, rise_core = slope_of(gate(pre_own, home[1])), slope_of(gate(pre_core, home[1]))
    held_gates = gate(gate_weights, rise_own, rise_core, query_there, grad_y)
    sent_pair, first, second = combine(which_section, position, held_gates, home, sections)
    from_pair = swap(sent_pair, "section", 1)
    grad_x = swap(gate(out_grad, home[5]), "dp", 2)
    grad_far = swap(gate(grad_y, first), "dp", 2)
    to_other = (second + from_pair[1].astype(jnp.float32)).astype(jnp.bfloat16)
    from_other = swap(to_other, "section", 2)
    mixed_sum = first + from_pair[0].astype(jnp.float32)
    mixed_slice = (mixed_sum + from_other.astype(jnp.float32)).astype(jnp.bfloat16)
    key_other = swap(gate(key_own, first), "expert", 1)
    query_back = swap(gate(query_there.astype(jnp.bfloat16), key_other), "expert", 1)
    mixed_near = swap(mixed_slice, "section", 1)
    grads_own, grads_sent = dispatch(
        which_section,
        gate(code, mixed_near),
        [out_grad, grad_x, grad_y, grad_far],
        (
            ((0, 0, token_count, None),),
            ((1, 0, token_count, None),),
            ((2, 0, share, 0), (2, share, share, 1)),
            ((3, 0, share, 0), (3, share, share, 1)),
        ),
        capacity,
    )
    grads_core = swap(grads_sent, "dp", 1)
    slope = expert_slope(
        here.astype(jnp.int32).reshape(1),
        near_codes + core_codes,
        grads_own,
        grads_core,
        rise_own,
        rise_core,
        weight_out,
    )
    back_pair, back_first, back_second = expert_backward(
        which_section, slope, weight_in, sections
    )
    mixed_far = swap(jnp.stack([mixed_slice, gate(mixed_near, key_other)]), "section", 2)
    slices = [mixed_slice, mixed_near, mixed_far[0], mixed_far[1]]

    value_other = swap(gate(value_own, mixed_near), "expert", 1)

    query_here = jnp.dot(normed_own, query_own, preferred_element_type=jnp.float32)
    query = (query_here + query_back.astype(jnp.float32)).astype(jnp.bfloat16)

    memory = make_memory(which_section, tokens, slices, final_gain)
    out_other = swap(gate(out_own, memory), "expert", 1)
    memory_x = swap(memory, "dp", 2)
    memory_core = swap(memory, "dp", 1)

    def sentence(which, near, far, *after):
        place = gate(jnp.stack([y, core, which]).astype(jnp.int32), *after)
        rows_of = lax.dynamic_slice_in_dim(query, which * TGT_LEN, TGT_LEN, 0)
        parts = (key_own, key_other), (value_own, value_other)
        return attend_sentence(place, src_lengths, rows_of, near, far, *parts)

    back_from_pair = swap(back_pair, "section", 1)
    back_to_other = (back_second + back_from_pair[1].astype(jnp.float32)).astype(jnp.bfloat16)
    back_from_other = swap(back_to_other, "section", 2)
    backward_sum = back_first + back_from_pair[0].astype(jnp.float32)
    backward_sum = backward_sum + back_from_other.astype(jnp.float32)
    context_own = sentence(x, memory, memory_core)
    memory_far = swap(gate(memory_x, context_own), "dp", 1)
    context_other = sentence(1 - x, memory_x, memory_far)
    place = jnp.stack([y, core, x]).astype(jnp.int32)
    sent_mine, sent_other, kept_mine, kept_other = project(
        place, context_own, context_other, out_own, out_other
    )

    core_other = swap(sent_other, "dp", 1)
    core_mine = swap(sent_mine, "dp", 1)
    last = gate(kept_other, back_from_other) + core_other.astype(jnp.float32)
    from_x = swap(last.astype(jnp.bfloat16), "dp", 2)
    attended = kept_mine + core_mine.astype(jnp.float32) + from_x.astype(jnp.float32)
    dec_out = add_residual(attended, states, tgt_lengths)

    grads_home = exchange(gate(backward_sum.astype(jnp.bfloat16), last), group_size, capacity)
    natural = expert_ids * capacity + rank
    (token_grad,) = combine(
        which_section, natural, gate_weights, [grads_home], 1
    )
    return (dec_out[None], token_grad)


def add_residual(attended, states, tgt_lengths):
    my_columns = attended.shape[1]
    residual = lax.dynamic_slice_in_dim(
        states, lax.axis_index("dp") * my_columns, my_columns, 1
    ).astype(jnp.float32)
    row_mask = (jnp.arange(TGT_LEN, dtype=jnp.int32)[None, :] < tgt_lengths[:, None]).reshape(-1, 1)
    return (residual + jnp.where(row_mask, attended, 0.0)).astype(jnp.bfloat16)


def body(
    tokens,
    expert_ids,
    gate_weights,
    out_grad,
    inner_weight,
    outer_weight,
    final_gain,
    dec_states,
    src_lengths,
    tgt_lengths,
    norm_gain,
    query_weight,
    key_weight,
    value_weight,
    out_weight,
):
    token_count, feature_count = tokens.shape
    group_size = lax.axis_size(("expert", "dp"))
    capacity = 3 * token_count // group_size
    slots = group_size * capacity

    named = expert_ids[:, :, None] == jnp.arange(group_size, dtype=jnp.int32)[None, None, :]
    either = (named[:, 0] | named[:, 1]).astype(jnp.bfloat16)
    row = lax.broadcasted_iota(jnp.int32, (token_count, token_count), 0)
    column = lax.broadcasted_iota(jnp.int32, (token_count, token_count), 1)
    earlier = jnp.dot(
        (column < row).astype(jnp.bfloat16), either, preferred_element_type=jnp.float32
    ).astype(jnp.int32)
    rank = jnp.sum(jnp.where(named, earlier[:, None, :], 0), axis=2)
    position = expert_ids * capacity + rank
    pick_first = slot_matrix(position[:, 0], slots)
    pick_second = slot_matrix(position[:, 1], slots)
    fill = (pick_first + pick_second).T

    def place(values):
        return jnp.dot(fill, values, preferred_element_type=jnp.float32).astype(jnp.bfloat16)

    def combine(arrived):
        first = jnp.dot(pick_first, arrived, preferred_element_type=jnp.float32)
        second = jnp.dot(pick_second, arrived, preferred_element_type=jnp.float32)
        return gate_weights[:, :1] * first + gate_weights[:, 1:] * second

    weight_in = inner_weight[0]
    weight_out = outer_weight[0]
    arrived_rows = exchange(place(tokens), group_size, capacity)
    pre_act = jnp.dot(arrived_rows, weight_in, preferred_element_type=jnp.float32)
    hidden = jax.nn.gelu(pre_act).astype(jnp.bfloat16)
    forward_part = jnp.dot(hidden, weight_out, preferred_element_type=jnp.float32)
    arrived_grads = exchange(place(out_grad), group_size, capacity)
    outputs_home = exchange(forward_part.astype(jnp.bfloat16), group_size, capacity)
    mixed_slice = sum_sections(combine(outputs_home)).astype(jnp.bfloat16)
    mixed = gather_sections(mixed_slice).astype(jnp.float32)
    memory = normalize(tokens.astype(jnp.float32) + mixed, final_gain).astype(jnp.bfloat16)

    back = contract_last(arrived_grads, weight_out)
    slope = jax.vjp(jax.nn.gelu, pre_act)[1](back)[0].astype(jnp.bfloat16)
    backward_part = contract_last(slope, weight_in)
    backward_slice = sum_sections(backward_part).astype(jnp.bfloat16)
    grads_home = exchange(backward_slice, group_size, capacity)
    token_grad = combine(grads_home).astype(jnp.bfloat16)

    states = dec_states[0]
    normed = normalize(states.astype(jnp.float32), norm_gain[0]).astype(jnp.bfloat16)
    full_query = gather_weight(query_weight[0], 0)
    full_key = gather_weight(key_weight[0], 0)
    full_value = gather_weight(value_weight[0], 0)
    full_out = gather_weight(out_weight[0], 1)
    query_sum = jnp.dot(normed, full_query, preferred_element_type=jnp.float32)
    source = gather_rows(memory, "dp")
    key_sum = jnp.dot(source, full_key, preferred_element_type=jnp.float32)
    value_sum = jnp.dot(source, full_value, preferred_element_type=jnp.float32)
    key_mask = jnp.arange(SRC_LEN, dtype=jnp.int32)[None, :] < src_lengths[:, None]
    context = attend(
        query_sum.astype(jnp.bfloat16),
        key_sum.astype(jnp.bfloat16),
        value_sum.astype(jnp.bfloat16),
        key_mask,
    )
    attended = sum_heads(jnp.dot(context, full_out, preferred_element_type=jnp.float32))
    dec_out = add_residual(attended, states, tgt_lengths)
    return (dec_out[None], token_grad)


def solution(mesh):
    in_specs = (
        P(("expert", "dp"), None),
        P(("expert", "dp"), None),
        P(("expert", "dp"), None),
        P(("expert", "dp"), None),
        P(("expert", "dp"), None, "section"),
        P(("expert", "dp"), "section", None),
        P(),
        P("section", "expert", None),
        P("expert"),
        P("expert"),
        P("section", None),
        P("section", "expert", "dp"),
        P("section", "expert", "dp"),
        P("section", "expert", "dp"),
        P("section", "dp", "expert"),
    )
    out_specs = (P("section", "expert", "dp"), P(("expert", "dp"), "section"))
    small = (mesh.shape["section"], mesh.shape["expert"], mesh.shape["dp"]) == (4, 2, 4)
    chosen = small_body if small else body
    return jax.shard_map(chosen, mesh=mesh, in_specs=in_specs, out_specs=out_specs, check_vma=False)
```

```python
import functools

import jax
import jax.numpy as jnp
from jax import lax
from jax.experimental import pallas as pl
from jax.experimental.pallas import tpu as pltpu
from jax.sharding import PartitionSpec as P

HEAD_DIM = 128
SRC_LEN = 256
TGT_LEN = 128


EPSILON = 1e-05


def normalize(values, gain):
    centre = jnp.mean(values, axis=-1, keepdims=True)
    centred = values - centre
    spread = jnp.mean(centred * centred, axis=-1, keepdims=True)
    return centred * lax.rsqrt(spread + EPSILON) * gain


def contract_last(left, right):
    return lax.dot_general(
        left, right, (((1,), (1,)), ((), ())), preferred_element_type=jnp.float32
    )


def shift(value, axis, step):
    size = lax.axis_size(axis)
    return lax.ppermute(value, axis, [(i, (i + step) % size) for i in range(size)])


def swap(value, axis, mask):
    size = lax.axis_size(axis)
    return lax.ppermute(value, axis, [(i, i ^ mask) for i in range(size)])


def sum_sections(partial):
    count = lax.axis_size("section")
    me = lax.axis_index("section")
    width = partial.shape[1] // count

    def piece(owner):
        return lax.dynamic_slice_in_dim(partial, owner * width, width, 1)

    total = piece(me).astype(jnp.float32)
    for step in range(1, count):
        sent = piece(lax.rem(me + step, count)).astype(jnp.bfloat16)
        total = total + shift(sent, "section", step).astype(jnp.float32)
    return total


def gather_sections(mine):
    count = lax.axis_size("section")
    me = lax.axis_index("section")
    width = mine.shape[1]
    whole = jnp.zeros((mine.shape[0], width * count), mine.dtype)
    whole = lax.dynamic_update_slice_in_dim(whole, mine, me * width, 1)
    for step in range(1, count):
        owner = lax.rem(me - step + count, count)
        whole = lax.dynamic_update_slice_in_dim(
            whole, shift(mine, "section", step), owner * width, 1
        )
    return whole


def gather_rows(mine, axis):
    held = mine
    me = lax.axis_index(axis)
    mask = lax.axis_size(axis) // 2
    blocks = [mine]
    while mask >= 1:
        blocks = blocks + [swap(block, axis, mask) for block in blocks]
        mask //= 2
    codes = [0]
    mask = lax.axis_size(axis) // 2
    while mask >= 1:
        codes = codes + [code ^ mask for code in codes]
        mask //= 2
    ordered = []
    for place in range(len(blocks)):
        chosen = blocks[0]
        for code, block in zip(codes[1:], blocks[1:]):
            chosen = jnp.where((me ^ code) == place, block, chosen)
        ordered.append(chosen)
    return jnp.concatenate(ordered, axis=0)


def gather_weight(weight, dimension):
    if lax.axis_size("expert") != 2:
        return lax.all_gather(weight, "expert", axis=dimension, tiled=True)
    other = swap(weight, "expert", 1)
    first = lax.axis_index("expert") == 0
    return jnp.concatenate(
        [jnp.where(first, weight, other), jnp.where(first, other, weight)], axis=dimension
    )


def sum_heads(partial):
    me = lax.axis_index("dp")
    count = lax.axis_size("dp")
    rows, columns = partial.shape
    total = partial.reshape(rows, count, columns // count)
    mask = 1
    while mask < count:
        paired = total.reshape(rows, -1, 2, columns // count)
        bit = (me // mask) % 2
        sent = lax.dynamic_index_in_dim(paired, 1 - bit, 2, False).astype(jnp.bfloat16)
        kept = lax.dynamic_index_in_dim(paired, bit, 2, False)
        total = kept + swap(sent, "dp", mask).astype(jnp.float32)
        mask *= 2
    return total.reshape(rows, columns // count)


def slot_matrix(positions, slots):
    places = lax.broadcasted_iota(jnp.int32, (positions.shape[0], slots), 1)
    return (positions[:, None] == places).astype(jnp.bfloat16)


def attend(query, keys, values, key_mask):
    sequences = key_mask.shape[0]
    head_count = query.shape[1] // HEAD_DIM
    query_split = query.reshape(sequences, -1, head_count, HEAD_DIM)
    keys_split = keys.reshape(sequences, -1, head_count, HEAD_DIM)
    values_split = values.reshape(sequences, -1, head_count, HEAD_DIM)
    scores = jnp.einsum(
        "bqhd,bkhd->bhqk", query_split, keys_split, preferred_element_type=jnp.float32
    ) * HEAD_DIM ** (-0.5)
    scores = jnp.where(key_mask[:, None, None, :], scores, -1e30)
    highest = jnp.max(scores, axis=-1, keepdims=True)
    weights = jnp.exp(scores - highest)
    probs = (weights / jnp.sum(weights, axis=-1, keepdims=True)).astype(jnp.bfloat16)
    context = jnp.einsum("bhqk,bkhd->bqhd", probs, values_split, preferred_element_type=jnp.float32)
    return context.astype(jnp.bfloat16).reshape(-1, head_count * HEAD_DIM)


def exchange(values, group_size, capacity):
    sent = values.reshape(group_size, capacity, values.shape[1])
    arrived = lax.all_to_all(sent, ("expert", "dp"), split_axis=0, concat_axis=0, tiled=True)
    return arrived.reshape(values.shape)


SHORT = pl.CostEstimate(flops=1, bytes_accessed=1, transcendentals=0)


def gate(value, *after):
    return lax.optimization_barrier((value,) + after)[0]


def vmem(shape, dtype):
    return pltpu.VMEM(shape, dtype)


def dispatch_kernel(capacity, layout, section_ref, code_ref, *refs):
    blocks = refs[:-4]
    outs, held, sems = refs[-4:-2], refs[-2], refs[-1]
    count, rows = held.shape[0], held.shape[1]
    half = lax.rem(section_ref[0], 2)
    copies = []
    for place, pieces in enumerate(layout):
        group = []
        for i, (which, start, length, side) in enumerate(pieces):
            there = held.at[place]
            if side is not None:
                offset = (half if side == 0 else 1 - half) * length
                there = held.at[place, pl.ds(pl.multiple_of(offset, length), length)]
            here = blocks[which].at[pl.ds(start, length)]
            group.append(pltpu.make_async_copy(here, there, sems.at[place, i]))
        copies.append(group)
    for group in copies:
        for copy in group:
            copy.start()
    for place, group in enumerate(copies):
        picks = []
        for which in range(2):
            line = which * count + place
            code = code_ref[line : line + 1, :]
            slot = lax.broadcasted_iota(jnp.int32, (capacity, code.shape[1]), 0)
            picks.append(jnp.where(slot == code, 1.0, 0.0))
        pick = jnp.concatenate(picks, axis=0).astype(jnp.bfloat16)
        for copy in group:
            copy.wait()
        picked = jnp.dot(pick, held[place], preferred_element_type=jnp.float32)
        picked = picked.astype(jnp.bfloat16)
        for which, out_ref in enumerate(outs):
            out_ref[place * capacity : (place + 1) * capacity, :] = picked[
                which * capacity : (which + 1) * capacity
            ]


def dispatch(section, code, blocks, layout, capacity):
    rows, features = blocks[0].shape
    count = len(layout)
    picked = jax.ShapeDtypeStruct((count * capacity, features), jnp.bfloat16)
    return pl.pallas_call(
        functools.partial(dispatch_kernel, capacity, layout),
        out_shape=(picked, picked),
        in_specs=[
            pl.BlockSpec(memory_space=pltpu.SMEM),
            pl.BlockSpec(memory_space=pltpu.VMEM),
        ]
        + [pl.BlockSpec(memory_space=pltpu.HBM)] * len(blocks),
        out_specs=[pl.BlockSpec(memory_space=pltpu.VMEM)] * 2,
        scratch_shapes=[
            vmem((count, rows, features), jnp.bfloat16),
            pltpu.SemaphoreType.DMA((count, 2)),
        ],
        compiler_params=pltpu.CompilerParams(vmem_limit_bytes=10 * 1024 * 1024),
        cost_estimate=SHORT,
        name="dispatch",
    )(section, code, *blocks)


def send_home(part, codes, capacity):
    size = lax.axis_size(("expert", "dp"))
    arrived = []
    for place, code in enumerate(codes):
        block = part[place * capacity : (place + 1) * capacity]
        if code:
            block = lax.ppermute(block, ("expert", "dp"), [(i, i ^ code) for i in range(size)])
        arrived.append(block)
    return arrived


def combine_kernel(count, split, section_ref, position_ref, gates_ref, *refs):
    blocks = refs[:count]
    outs, (held, total) = refs[count:-2], refs[-2:]
    capacity, features = blocks[0].shape
    position = position_ref[...]
    slot = lax.broadcasted_iota(jnp.int32, (position.shape[0], count * capacity), 1)
    picks = [
        jnp.where(position[:, k : k + 1] == slot, 1.0, 0.0).astype(jnp.bfloat16) for k in range(2)
    ]
    for i, block in enumerate(blocks):
        held[i * capacity : (i + 1) * capacity, :] = block[...]
    pick = jnp.concatenate(picks, axis=0)
    rows = position.shape[0]
    both = jnp.dot(pick, held[...], preferred_element_type=jnp.float32)
    total[...] = gates_ref[:, 0:1] * both[:rows] + gates_ref[:, 1:2] * both[rows:]
    if split == 1:
        outs[0][...] = total[...].astype(outs[0].dtype)
        return
    sent_ref, kept_first, kept_second = outs
    width = features // split
    for step, out_ref in enumerate((kept_first, sent_ref.at[0], kept_second, sent_ref.at[1])):
        start = pl.multiple_of((section_ref[0] ^ step) * width, width)
        out_ref[...] = total[:, pl.ds(start, width)].astype(out_ref.dtype)


def combine(section, position, gates, blocks, split):
    capacity, features = blocks[0].shape
    rows = position.shape[0]
    count = len(blocks)
    width = features // split
    kept = jax.ShapeDtypeStruct((rows, width), jnp.float32)
    if split == 1:
        out_shape = (jax.ShapeDtypeStruct((rows, width), jnp.bfloat16),)
    else:
        out_shape = (jax.ShapeDtypeStruct((2, rows, width), jnp.bfloat16), kept, kept)
    full = pl.BlockSpec(memory_space=pltpu.VMEM)
    return pl.pallas_call(
        functools.partial(combine_kernel, count, split),
        out_shape=out_shape,
        in_specs=[pl.BlockSpec(memory_space=pltpu.SMEM)] + [full] * (2 + count),
        out_specs=[full] * len(out_shape),
        scratch_shapes=[
            vmem((count * capacity, features), jnp.bfloat16),
            vmem((rows, features), jnp.float32),
        ],
        compiler_params=pltpu.CompilerParams(vmem_limit_bytes=14 * 1024 * 1024),
        cost_estimate=SHORT,
        name="combine",
    )(section, position, gates, *blocks)


def memory_kernel(count, section_ref, tokens_ref, gain_ref, *refs):
    slices, out_ref, mixed = refs[:count], refs[count], refs[count + 1]
    me = section_ref[0]
    width = slices[0].shape[1]
    for step, piece in enumerate(slices):
        owner = me ^ step
        mixed[:, pl.ds(pl.multiple_of(owner * width, width), width)] = piece[...].astype(
            jnp.float32
        )
    values = tokens_ref[...].astype(jnp.float32) + mixed[...]
    out_ref[...] = normalize(values, gain_ref[...]).astype(jnp.bfloat16)


def make_memory(me, tokens, slices, gain):
    return pl.pallas_call(
        functools.partial(memory_kernel, len(slices)),
        out_shape=jax.ShapeDtypeStruct(tokens.shape, jnp.bfloat16),
        in_specs=[
            pl.BlockSpec(memory_space=pltpu.SMEM),
        ]
        + [pl.BlockSpec(memory_space=pltpu.VMEM)] * (2 + len(slices)),
        out_specs=pl.BlockSpec(memory_space=pltpu.VMEM),
        scratch_shapes=[vmem(tokens.shape, jnp.float32)],
        compiler_params=pltpu.CompilerParams(vmem_limit_bytes=8 * 1024 * 1024),
        cost_estimate=SHORT,
        name="memory",
    )(me, tokens, gain[None], *slices)


def normed_kernel(y_ref, states_ref, gain_ref, own_ref, other_ref):
    values = normalize(states_ref[...].astype(jnp.float32), gain_ref[...]).astype(jnp.bfloat16)
    width = own_ref.shape[1]
    for out_ref, first in ((own_ref, y_ref[0] == 0), (other_ref, y_ref[0] == 1)):
        out_ref[...] = jnp.where(first, values[:, :width], values[:, width:])


def normed_halves(y, states, gain):
    rows, features = states.shape
    full = pl.BlockSpec(memory_space=pltpu.VMEM)
    return pl.pallas_call(
        normed_kernel,
        out_shape=(jax.ShapeDtypeStruct((rows, features // 2), jnp.bfloat16),) * 2,
        in_specs=[pl.BlockSpec(memory_space=pltpu.SMEM), full, full],
        out_specs=[full] * 2,
        compiler_params=pltpu.CompilerParams(vmem_limit_bytes=12 * 1024 * 1024),
        cost_estimate=SHORT,
        name="normed",
    )(y.astype(jnp.int32).reshape(1), states, gain)


def attend_kernel(place_ref, lengths_ref, query_ref, *refs):
    near_ref, far_ref, key_own, key_other, value_own, value_other, out_ref = refs[:7]
    source, key_weight, value_weight, keys, values, sems = refs[7:]
    y, core, sentence = place_ref[0], place_ref[1], place_ref[2]
    rows = near_ref.shape[0]
    depth = key_own.shape[0]
    moves = [
        (near_ref, source.at[pl.ds(0, rows)]),
        (far_ref, source.at[pl.ds(rows, rows)]),
        (key_own, key_weight.at[y]),
        (key_other, key_weight.at[1 - y]),
        (value_own, value_weight.at[y]),
        (value_other, value_weight.at[1 - y]),
    ]
    copies = [
        pltpu.make_async_copy(here, there, sems.at[i]) for i, (here, there) in enumerate(moves)
    ]
    for copy in copies:
        copy.start()

    def linear(weight, result):
        total = jnp.dot(source[:, :depth], weight[0], preferred_element_type=jnp.float32)
        total += jnp.dot(source[:, depth:], weight[1], preferred_element_type=jnp.float32)
        result[...] = total.astype(jnp.bfloat16)

    for copy in copies[:4]:
        copy.wait()
    linear(key_weight, keys)
    for copy in copies[4:]:
        copy.wait()
    linear(value_weight, values)

    column = lax.broadcasted_iota(jnp.int32, (query_ref.shape[0], 2 * rows), 1)
    position = jnp.where(column < rows, column + core * rows, column - core * rows)
    valid = position < lengths_ref[sentence]
    for head in range(query_ref.shape[1] // HEAD_DIM):
        span = slice(head * HEAD_DIM, (head + 1) * HEAD_DIM)
        scores = contract_last(query_ref[:, span], keys[:, span]) * HEAD_DIM ** (-0.5)
        scores = jnp.where(valid, scores, -1e30)
        weights = jnp.exp(scores - jnp.max(scores, axis=-1, keepdims=True))
        probs = (weights / jnp.sum(weights, axis=-1, keepdims=True)).astype(jnp.bfloat16)
        result = jnp.dot(probs, values[:, span], preferred_element_type=jnp.float32)
        out_ref[:, span] = result.astype(jnp.bfloat16)


def attend_sentence(place, lengths, query, near, far, key_parts, value_pair):
    rows, features = near.shape
    depth, width = key_parts[0].shape
    hold = pl.BlockSpec(memory_space=pltpu.HBM)
    smem = pl.BlockSpec(memory_space=pltpu.SMEM)
    full = pl.BlockSpec(memory_space=pltpu.VMEM)
    return pl.pallas_call(
        attend_kernel,
        out_shape=jax.ShapeDtypeStruct(query.shape, jnp.bfloat16),
        in_specs=[smem, smem, full] + [hold] * 6,
        out_specs=full,
        scratch_shapes=[
            vmem((2 * rows, features), jnp.bfloat16),
            vmem((2, depth, width), jnp.bfloat16),
            vmem((2, depth, width), jnp.bfloat16),
            vmem((2 * rows, width), jnp.bfloat16),
            vmem((2 * rows, width), jnp.bfloat16),
            pltpu.SemaphoreType.DMA((6,)),
        ],
        compiler_params=pltpu.CompilerParams(vmem_limit_bytes=56 * 1024 * 1024),
        cost_estimate=SHORT,
        name="attend_sentence",
    )(place, lengths, query, near, far, *key_parts, *value_pair)


def project_kernel(place_ref, mine_ref, done_ref, own_ref, other_ref, *refs):
    sent_mine, sent_other, kept_mine, kept_other, context = refs
    y, core, x = place_ref[0], place_ref[1], place_ref[2]
    targets = mine_ref.shape[0]
    for part, sentence in ((mine_ref, x), (done_ref, 1 - x)):
        context[pl.ds(pl.multiple_of(sentence * targets, targets), targets), :] = part[...]
    columns = kept_mine.shape[1]
    outs = ((sent_mine, kept_mine), (sent_other, kept_other))

    def write(weight_ref, chosen):
        for side, out_ref in zip((1 - core, core), chosen):
            span = pl.ds(pl.multiple_of(side * columns, columns), columns)
            part = jnp.dot(context[...], weight_ref[:, span], preferred_element_type=jnp.float32)
            out_ref[...] = part.astype(out_ref.dtype)

    @pl.when(x == y)
    def _():
        write(own_ref, outs[0])
        write(other_ref, outs[1])

    @pl.when(x != y)
    def _():
        write(other_ref, outs[0])
        write(own_ref, outs[1])


def project(place, mine, done, out_own, out_other):
    targets, width = 2 * mine.shape[0], mine.shape[1]
    columns = out_own.shape[1] // 2
    full = pl.BlockSpec(memory_space=pltpu.VMEM)
    sent = jax.ShapeDtypeStruct((targets, columns), jnp.bfloat16)
    kept = jax.ShapeDtypeStruct((targets, columns), jnp.float32)
    return pl.pallas_call(
        project_kernel,
        out_shape=(sent, sent, kept, kept),
        in_specs=[pl.BlockSpec(memory_space=pltpu.SMEM)] + [full] * 4,
        out_specs=[full] * 4,
        scratch_shapes=[vmem((targets, width), jnp.bfloat16)],
        compiler_params=pltpu.CompilerParams(vmem_limit_bytes=16 * 1024 * 1024),
        cost_estimate=SHORT,
        name="project",
    )(place, mine, done, out_own, out_other)


def slope_kernel(codes, here_ref, own_ref, core_ref, rise_own, rise_core, out_ref, slope, *refs):
    grads, rise, weight_out, sems = refs
    rows = own_ref.shape[0]
    hidden = weight_out.shape[0]
    chunk = hidden // 4
    moves = []
    block = 2 * rows // len(codes)
    for order, code in enumerate(codes):
        source = here_ref[0] ^ code
        there = pl.ds(pl.multiple_of(source * block, 16), block)
        here = pl.ds(order * block % rows, block)
        own = order * block < rows
        moves.append(((own_ref if own else core_ref).at[here], grads.at[there]))
        moves.append(((rise_own if own else rise_core).at[here], rise.at[there]))
    for part in range(4):
        span = pl.ds(part * chunk, chunk)
        moves.append((out_ref.at[span], weight_out.at[span]))
    copies = [
        pltpu.make_async_copy(here, there, sems.at[i]) for i, (here, there) in enumerate(moves)
    ]
    for copy in copies:
        copy.start()
    for copy in copies[:-4]:
        copy.wait()
    for part in range(4):
        copies[part - 4].wait()
        span = slice(part * chunk, (part + 1) * chunk)
        back = contract_last(grads[...], weight_out[span, :])
        slope[:, span] = (back * rise[:, span]).astype(jnp.bfloat16)


def expert_slope(here, codes, grads_own, grads_core, rise_own, rise_core, weight_out):
    rows = 2 * grads_own.shape[0]
    hidden, features = weight_out.shape
    hold = pl.BlockSpec(memory_space=pltpu.HBM)
    return pl.pallas_call(
        functools.partial(slope_kernel, codes),
        out_shape=jax.ShapeDtypeStruct((rows, hidden), jnp.bfloat16),
        in_specs=[pl.BlockSpec(memory_space=pltpu.SMEM)] + [hold] * 5,
        out_specs=pl.BlockSpec(memory_space=pltpu.VMEM),
        scratch_shapes=[
            vmem((rows, features), jnp.bfloat16),
            vmem((rows, hidden), jnp.float32),
            vmem((hidden, features), jnp.bfloat16),
            pltpu.SemaphoreType.DMA((4 + 2 * len(codes),)),
        ],
        compiler_params=pltpu.CompilerParams(vmem_limit_bytes=56 * 1024 * 1024),
        cost_estimate=SHORT,
        name="expert_slope",
    )(here, grads_own, grads_core, rise_own, rise_core, weight_out)


def backward_kernel(split, section_ref, slope_ref, in_ref, sent_ref, kept_first, kept_second, *refs):
    weight_in, sems = refs
    width = weight_in.shape[0] // split
    outs = (sent_ref.at[0], sent_ref.at[1], kept_first, kept_second)
    spans, copies = [], []
    for i, step in enumerate((1, 3, 0, 2)):
        start = pl.multiple_of((section_ref[0] ^ step) * width, width)
        spans.append(pl.ds(start, width))
        copies.append(
            pltpu.make_async_copy(in_ref.at[spans[i]], weight_in.at[spans[i]], sems.at[i])
        )
    for copy in copies:
        copy.start()
    for copy, span, out_ref in zip(copies, spans, outs):
        copy.wait()
        part = contract_last(slope_ref[...], weight_in[span, :])
        out_ref[...] = part.astype(out_ref.dtype)


def expert_backward(section, slope, weight_in, split):
    rows, hidden = slope.shape
    features = weight_in.shape[0]
    width = features // split
    full = pl.BlockSpec(memory_space=pltpu.VMEM)
    kept = jax.ShapeDtypeStruct((rows, width), jnp.float32)
    return pl.pallas_call(
        functools.partial(backward_kernel, split),
        out_shape=(jax.ShapeDtypeStruct((2, rows, width), jnp.bfloat16), kept, kept),
        in_specs=[pl.BlockSpec(memory_space=pltpu.SMEM), full, pl.BlockSpec(memory_space=pltpu.HBM)],
        out_specs=[full] * 3,
        scratch_shapes=[
            vmem((features, hidden), jnp.bfloat16),
            pltpu.SemaphoreType.DMA((split,)),
        ],
        compiler_params=pltpu.CompilerParams(vmem_limit_bytes=56 * 1024 * 1024),
        cost_estimate=SHORT,
        name="expert_backward",
    )(section, slope, weight_in)


def small_body(
    tokens,
    expert_ids,
    gate_weights,
    out_grad,
    inner_weight,
    outer_weight,
    final_gain,
    dec_states,
    src_lengths,
    tgt_lengths,
    norm_gain,
    query_weight,
    key_weight,
    value_weight,
    out_weight,
):
    token_count, feature_count = tokens.shape
    group_size = lax.axis_size(("expert", "dp"))
    capacity = 3 * token_count // group_size
    here = lax.axis_index(("expert", "dp"))
    y = lax.axis_index("expert")
    d = lax.axis_index("dp")
    section = lax.axis_index("section")
    sections = lax.axis_size("section")
    half = feature_count // 2
    weight_in = inner_weight[0]
    weight_out = outer_weight[0]
    key_own, value_own, out_own = key_weight[0], value_weight[0], out_weight[0]
    query_own = query_weight[0]

    size = group_size
    near_codes = (0, 2, 4, 6)
    core_codes = (1, 3, 5, 7)
    core, x = d % 2, d // 2
    which_section = section.astype(jnp.int32).reshape(1)

    token_y = swap(tokens, "expert", 1)
    token_x = swap(tokens, "dp", 2)
    row = lax.broadcasted_iota(jnp.int32, (token_count, token_count), 0)
    column = lax.broadcasted_iota(jnp.int32, (token_count, token_count), 1)
    named = expert_ids[:, :, None] == jnp.arange(size, dtype=jnp.int32)[None, None, :]
    either = (named[:, 0] | named[:, 1]).astype(jnp.bfloat16)
    earlier = jnp.dot(
        (column < row).astype(jnp.bfloat16), either, preferred_element_type=jnp.float32
    ).astype(jnp.int32)
    rank = jnp.sum(jnp.where(named, earlier[:, None, :], 0), axis=2)
    codes_of = expert_ids ^ here
    position = ((codes_of >> 1) + 4 * (codes_of & 1)) * capacity + rank

    ids_own = expert_ids.T
    ids_x, ids_y = swap(ids_own, "dp", 2), swap(ids_own, "expert", 1)
    ids_far = swap(ids_x, "expert", 1)
    token_far = swap(gate(token_y, ids_x, ids_y), "dp", 2)

    side = lax.rem(section, 2)
    share = token_count // 2
    grad_half = lax.dynamic_slice_in_dim(out_grad, side * share, share, 0)
    half_y = swap(gate(grad_half, token_y), "expert", 1)
    states = dec_states[0]
    normed_own, asked = normed_halves(y, states, norm_gain)
    asked_here = swap(gate(asked, half_y), "expert", 1)
    query_there = jnp.dot(asked_here, query_own, preferred_element_type=jnp.float32)
    other_y = swap(half_y, "section", 1)

    ids = jnp.stack([ids_own, ids_x, ids_y, ids_far])
    named_there = jnp.concatenate([(ids == here).any(axis=1), (ids == (here ^ 1)).any(axis=1)])
    before = jnp.dot(
        named_there.astype(jnp.bfloat16),
        (row < column).astype(jnp.bfloat16),
        preferred_element_type=jnp.float32,
    ).astype(jnp.int32)
    code = jnp.where(named_there, before, -1)

    def forward(rows, *after):
        pre_act = jnp.dot(rows, weight_in, preferred_element_type=jnp.float32)
        hidden = jax.nn.gelu(gate(pre_act, *after)).astype(jnp.bfloat16)
        part = jnp.dot(hidden, weight_out, preferred_element_type=jnp.float32)
        return pre_act, part.astype(jnp.bfloat16)

    def slope_of(pre_act):
        return jax.vjp(jax.nn.gelu, pre_act)[1](jnp.ones_like(pre_act))[0]

    rows_own, rows_sent = dispatch(
        which_section,
        gate(code, asked),
        [tokens, token_x, token_y, token_far],
        tuple(((place, 0, token_count, None),) for place in range(4)),
        capacity,
    )
    rows_core = swap(rows_sent, "dp", 1)
    pre_own, part_own = forward(rows_own, other_y)
    pre_core, part_core = forward(gate(rows_core, part_own))
    home = send_home(part_own, near_codes, capacity) + send_home(part_core, core_codes, capacity)
    grad_y = jnp.concatenate([gate(half_y, home[4]), other_y], axis=0)

    rise_own, rise_core = slope_of(gate(pre_own, home[1])), slope_of(gate(pre_core, home[1]))
    held_gates = gate(gate_weights, rise_own, rise_core, query_there, grad_y)
    sent_pair, first, second = combine(which_section, position, held_gates, home, sections)
    from_pair = swap(sent_pair, "section", 1)
    query_back = swap(gate(query_there.astype(jnp.bfloat16), home[5], home[6]), "expert", 1)
    grad_x = swap(gate(out_grad, home[5]), "dp", 2)
    grad_far = swap(gate(grad_y, first), "dp", 2)
    to_other = (second + from_pair[1].astype(jnp.float32)).astype(jnp.bfloat16)
    from_other = swap(to_other, "section", 2)
    mixed_sum = gate(first, query_back) + from_pair[0].astype(jnp.float32)
    mixed_slice = (mixed_sum + from_other.astype(jnp.float32)).astype(jnp.bfloat16)
    key_other = swap(gate(key_own, first), "expert", 1)
    mixed_near = swap(mixed_slice, "section", 1)
    grads_own, grads_sent = dispatch(
        which_section,
        gate(code, mixed_near),
        [out_grad, grad_x, grad_y, grad_far],
        (
            ((0, 0, token_count, None),),
            ((1, 0, token_count, None),),
            ((2, 0, share, 0), (2, share, share, 1)),
            ((3, 0, share, 0), (3, share, share, 1)),
        ),
        capacity,
    )
    grads_core = swap(grads_sent, "dp", 1)
    slope = expert_slope(
        here.astype(jnp.int32).reshape(1),
        near_codes + core_codes,
        grads_own,
        grads_core,
        rise_own,
        rise_core,
        weight_out,
    )
    back_pair, back_first, back_second = expert_backward(
        which_section, slope, weight_in, sections
    )
    mixed_far = swap(jnp.stack([mixed_slice, gate(mixed_near, key_other)]), "section", 2)
    slices = [mixed_slice, mixed_near, mixed_far[0], mixed_far[1]]

    value_other = swap(gate(value_own, mixed_near), "expert", 1)

    query_here = jnp.dot(normed_own, query_own, preferred_element_type=jnp.float32)
    query = (query_here + query_back.astype(jnp.float32)).astype(jnp.bfloat16)

    memory = make_memory(which_section, tokens, slices, final_gain)
    out_other = swap(gate(out_own, memory), "expert", 1)
    memory_x = swap(memory, "dp", 2)
    memory_core = swap(memory, "dp", 1)

    def sentence(which, near, far, *after):
        place = gate(jnp.stack([y, core, which]).astype(jnp.int32), *after)
        rows_of = lax.dynamic_slice_in_dim(query, which * TGT_LEN, TGT_LEN, 0)
        parts = (key_own, key_other), (value_own, value_other)
        return attend_sentence(place, src_lengths, rows_of, near, far, *parts)

    back_from_pair = swap(back_pair, "section", 1)
    back_to_other = (back_second + back_from_pair[1].astype(jnp.float32)).astype(jnp.bfloat16)
    back_from_other = swap(back_to_other, "section", 2)
    backward_sum = back_first + back_from_pair[0].astype(jnp.float32)
    backward_sum = backward_sum + back_from_other.astype(jnp.float32)
    context_own = sentence(x, memory, memory_core)
    memory_far = swap(gate(memory_x, context_own), "dp", 1)
    context_other = sentence(1 - x, memory_x, memory_far)
    place = jnp.stack([y, core, x]).astype(jnp.int32)
    sent_mine, sent_other, kept_mine, kept_other = project(
        place, context_own, context_other, out_own, out_other
    )

    core_other = swap(sent_other, "dp", 1)
    core_mine = swap(sent_mine, "dp", 1)
    last = gate(kept_other, back_from_other) + core_other.astype(jnp.float32)
    from_x = swap(last.astype(jnp.bfloat16), "dp", 2)
    attended = kept_mine + core_mine.astype(jnp.float32) + from_x.astype(jnp.float32)
    dec_out = add_residual(attended, states, tgt_lengths)

    grads_home = exchange(gate(backward_sum.astype(jnp.bfloat16), last), group_size, capacity)
    natural = expert_ids * capacity + rank
    (token_grad,) = combine(
        which_section, natural, gate_weights, [grads_home], 1
    )
    return (dec_out[None], token_grad)


def add_residual(attended, states, tgt_lengths):
    my_columns = attended.shape[1]
    residual = lax.dynamic_slice_in_dim(
        states, lax.axis_index("dp") * my_columns, my_columns, 1
    ).astype(jnp.float32)
    row_mask = (jnp.arange(TGT_LEN, dtype=jnp.int32)[None, :] < tgt_lengths[:, None]).reshape(-1, 1)
    return (residual + jnp.where(row_mask, attended, 0.0)).astype(jnp.bfloat16)


def body(
    tokens,
    expert_ids,
    gate_weights,
    out_grad,
    inner_weight,
    outer_weight,
    final_gain,
    dec_states,
    src_lengths,
    tgt_lengths,
    norm_gain,
    query_weight,
    key_weight,
    value_weight,
    out_weight,
):
    token_count, feature_count = tokens.shape
    group_size = lax.axis_size(("expert", "dp"))
    capacity = 3 * token_count // group_size
    slots = group_size * capacity

    named = expert_ids[:, :, None] == jnp.arange(group_size, dtype=jnp.int32)[None, None, :]
    either = (named[:, 0] | named[:, 1]).astype(jnp.bfloat16)
    row = lax.broadcasted_iota(jnp.int32, (token_count, token_count), 0)
    column = lax.broadcasted_iota(jnp.int32, (token_count, token_count), 1)
    earlier = jnp.dot(
        (column < row).astype(jnp.bfloat16), either, preferred_element_type=jnp.float32
    ).astype(jnp.int32)
    rank = jnp.sum(jnp.where(named, earlier[:, None, :], 0), axis=2)
    position = expert_ids * capacity + rank
    pick_first = slot_matrix(position[:, 0], slots)
    pick_second = slot_matrix(position[:, 1], slots)
    fill = (pick_first + pick_second).T

    def place(values):
        return jnp.dot(fill, values, preferred_element_type=jnp.float32).astype(jnp.bfloat16)

    def combine(arrived):
        first = jnp.dot(pick_first, arrived, preferred_element_type=jnp.float32)
        second = jnp.dot(pick_second, arrived, preferred_element_type=jnp.float32)
        return gate_weights[:, :1] * first + gate_weights[:, 1:] * second

    weight_in = inner_weight[0]
    weight_out = outer_weight[0]
    arrived_rows = exchange(place(tokens), group_size, capacity)
    pre_act = jnp.dot(arrived_rows, weight_in, preferred_element_type=jnp.float32)
    hidden = jax.nn.gelu(pre_act).astype(jnp.bfloat16)
    forward_part = jnp.dot(hidden, weight_out, preferred_element_type=jnp.float32)
    arrived_grads = exchange(place(out_grad), group_size, capacity)
    outputs_home = exchange(forward_part.astype(jnp.bfloat16), group_size, capacity)
    mixed_slice = sum_sections(combine(outputs_home)).astype(jnp.bfloat16)
    mixed = gather_sections(mixed_slice).astype(jnp.float32)
    memory = normalize(tokens.astype(jnp.float32) + mixed, final_gain).astype(jnp.bfloat16)

    back = contract_last(arrived_grads, weight_out)
    slope = jax.vjp(jax.nn.gelu, pre_act)[1](back)[0].astype(jnp.bfloat16)
    backward_part = contract_last(slope, weight_in)
    backward_slice = sum_sections(backward_part).astype(jnp.bfloat16)
    grads_home = exchange(backward_slice, group_size, capacity)
    token_grad = combine(grads_home).astype(jnp.bfloat16)

    states = dec_states[0]
    normed = normalize(states.astype(jnp.float32), norm_gain[0]).astype(jnp.bfloat16)
    full_query = gather_weight(query_weight[0], 0)
    full_key = gather_weight(key_weight[0], 0)
    full_value = gather_weight(value_weight[0], 0)
    full_out = gather_weight(out_weight[0], 1)
    query_sum = jnp.dot(normed, full_query, preferred_element_type=jnp.float32)
    source = gather_rows(memory, "dp")
    key_sum = jnp.dot(source, full_key, preferred_element_type=jnp.float32)
    value_sum = jnp.dot(source, full_value, preferred_element_type=jnp.float32)
    key_mask = jnp.arange(SRC_LEN, dtype=jnp.int32)[None, :] < src_lengths[:, None]
    context = attend(
        query_sum.astype(jnp.bfloat16),
        key_sum.astype(jnp.bfloat16),
        value_sum.astype(jnp.bfloat16),
        key_mask,
    )
    attended = sum_heads(jnp.dot(context, full_out, preferred_element_type=jnp.float32))
    dec_out = add_residual(attended, states, tgt_lengths)
    return (dec_out[None], token_grad)


def solution(mesh):
    in_specs = (
        P(("expert", "dp"), None),
        P(("expert", "dp"), None),
        P(("expert", "dp"), None),
        P(("expert", "dp"), None),
        P(("expert", "dp"), None, "section"),
        P(("expert", "dp"), "section", None),
        P(),
        P("section", "expert", None),
        P("expert"),
        P("expert"),
        P("section", None),
        P("section", "expert", "dp"),
        P("section", "expert", "dp"),
        P("section", "expert", "dp"),
        P("section", "dp", "expert"),
    )
    out_specs = (P("section", "expert", "dp"), P(("expert", "dp"), "section"))
    small = (mesh.shape["section"], mesh.shape["expert"], mesh.shape["dp"]) == (4, 2, 4)
    chosen = small_body if small else body
    return jax.shard_map(chosen, mesh=mesh, in_specs=in_specs, out_specs=out_specs, check_vma=False)
```

```python
import functools

import jax
import jax.numpy as jnp
from jax import lax
from jax.experimental import pallas as pl
from jax.experimental.pallas import tpu as pltpu
from jax.sharding import PartitionSpec as P

HEAD_DIM = 128
SRC_LEN = 256
TGT_LEN = 128


EPSILON = 1e-05


def normalize(values, gain):
    centre = jnp.mean(values, axis=-1, keepdims=True)
    centred = values - centre
    spread = jnp.mean(centred * centred, axis=-1, keepdims=True)
    return centred * lax.rsqrt(spread + EPSILON) * gain


def contract_last(left, right):
    return lax.dot_general(
        left, right, (((1,), (1,)), ((), ())), preferred_element_type=jnp.float32
    )


def shift(value, axis, step):
    size = lax.axis_size(axis)
    return lax.ppermute(value, axis, [(i, (i + step) % size) for i in range(size)])


def swap(value, axis, mask):
    size = lax.axis_size(axis)
    return lax.ppermute(value, axis, [(i, i ^ mask) for i in range(size)])


def sum_sections(partial):
    count = lax.axis_size("section")
    me = lax.axis_index("section")
    width = partial.shape[1] // count

    def piece(owner):
        return lax.dynamic_slice_in_dim(partial, owner * width, width, 1)

    total = piece(me).astype(jnp.float32)
    for step in range(1, count):
        sent = piece(lax.rem(me + step, count)).astype(jnp.bfloat16)
        total = total + shift(sent, "section", step).astype(jnp.float32)
    return total


def gather_sections(mine):
    count = lax.axis_size("section")
    me = lax.axis_index("section")
    width = mine.shape[1]
    whole = jnp.zeros((mine.shape[0], width * count), mine.dtype)
    whole = lax.dynamic_update_slice_in_dim(whole, mine, me * width, 1)
    for step in range(1, count):
        owner = lax.rem(me - step + count, count)
        whole = lax.dynamic_update_slice_in_dim(
            whole, shift(mine, "section", step), owner * width, 1
        )
    return whole


def gather_rows(mine, axis):
    held = mine
    me = lax.axis_index(axis)
    mask = lax.axis_size(axis) // 2
    blocks = [mine]
    while mask >= 1:
        blocks = blocks + [swap(block, axis, mask) for block in blocks]
        mask //= 2
    codes = [0]
    mask = lax.axis_size(axis) // 2
    while mask >= 1:
        codes = codes + [code ^ mask for code in codes]
        mask //= 2
    ordered = []
    for place in range(len(blocks)):
        chosen = blocks[0]
        for code, block in zip(codes[1:], blocks[1:]):
            chosen = jnp.where((me ^ code) == place, block, chosen)
        ordered.append(chosen)
    return jnp.concatenate(ordered, axis=0)


def gather_weight(weight, dimension):
    if lax.axis_size("expert") != 2:
        return lax.all_gather(weight, "expert", axis=dimension, tiled=True)
    other = swap(weight, "expert", 1)
    first = lax.axis_index("expert") == 0
    return jnp.concatenate(
        [jnp.where(first, weight, other), jnp.where(first, other, weight)], axis=dimension
    )


def sum_heads(partial):
    me = lax.axis_index("dp")
    count = lax.axis_size("dp")
    rows, columns = partial.shape
    total = partial.reshape(rows, count, columns // count)
    mask = 1
    while mask < count:
        paired = total.reshape(rows, -1, 2, columns // count)
        bit = (me // mask) % 2
        sent = lax.dynamic_index_in_dim(paired, 1 - bit, 2, False).astype(jnp.bfloat16)
        kept = lax.dynamic_index_in_dim(paired, bit, 2, False)
        total = kept + swap(sent, "dp", mask).astype(jnp.float32)
        mask *= 2
    return total.reshape(rows, columns // count)


def slot_matrix(positions, slots):
    places = lax.broadcasted_iota(jnp.int32, (positions.shape[0], slots), 1)
    return (positions[:, None] == places).astype(jnp.bfloat16)


def attend(query, keys, values, key_mask):
    sequences = key_mask.shape[0]
    head_count = query.shape[1] // HEAD_DIM
    query_split = query.reshape(sequences, -1, head_count, HEAD_DIM)
    keys_split = keys.reshape(sequences, -1, head_count, HEAD_DIM)
    values_split = values.reshape(sequences, -1, head_count, HEAD_DIM)
    scores = jnp.einsum(
        "bqhd,bkhd->bhqk", query_split, keys_split, preferred_element_type=jnp.float32
    ) * HEAD_DIM ** (-0.5)
    scores = jnp.where(key_mask[:, None, None, :], scores, -1e30)
    highest = jnp.max(scores, axis=-1, keepdims=True)
    weights = jnp.exp(scores - highest)
    probs = (weights / jnp.sum(weights, axis=-1, keepdims=True)).astype(jnp.bfloat16)
    context = jnp.einsum("bhqk,bkhd->bqhd", probs, values_split, preferred_element_type=jnp.float32)
    return context.astype(jnp.bfloat16).reshape(-1, head_count * HEAD_DIM)


def exchange(values, group_size, capacity):
    sent = values.reshape(group_size, capacity, values.shape[1])
    arrived = lax.all_to_all(sent, ("expert", "dp"), split_axis=0, concat_axis=0, tiled=True)
    return arrived.reshape(values.shape)


SHORT = pl.CostEstimate(flops=1, bytes_accessed=1, transcendentals=0)


def gate(value, *after):
    return lax.optimization_barrier((value,) + after)[0]


def vmem(shape, dtype):
    return pltpu.VMEM(shape, dtype)


def dispatch_kernel(capacity, layout, section_ref, code_ref, *refs):
    blocks = refs[:-4]
    outs, held, sems = refs[-4:-2], refs[-2], refs[-1]
    count, rows = held.shape[0], held.shape[1]
    half = lax.rem(section_ref[0], 2)
    copies = []
    for place, pieces in enumerate(layout):
        group = []
        for i, (which, start, length, side) in enumerate(pieces):
            there = held.at[place]
            if side is not None:
                offset = (half if side == 0 else 1 - half) * length
                there = held.at[place, pl.ds(pl.multiple_of(offset, length), length)]
            here = blocks[which].at[pl.ds(start, length)]
            group.append(pltpu.make_async_copy(here, there, sems.at[place, i]))
        copies.append(group)
    for group in copies:
        for copy in group:
            copy.start()
    for place, group in enumerate(copies):
        picks = []
        for which in range(2):
            line = which * count + place
            code = code_ref[line : line + 1, :]
            slot = lax.broadcasted_iota(jnp.int32, (capacity, code.shape[1]), 0)
            picks.append(jnp.where(slot == code, 1.0, 0.0))
        pick = jnp.concatenate(picks, axis=0).astype(jnp.bfloat16)
        for copy in group:
            copy.wait()
        picked = jnp.dot(pick, held[place], preferred_element_type=jnp.float32)
        picked = picked.astype(jnp.bfloat16)
        for which, out_ref in enumerate(outs):
            out_ref[place * capacity : (place + 1) * capacity, :] = picked[
                which * capacity : (which + 1) * capacity
            ]


def dispatch(section, code, blocks, layout, capacity):
    rows, features = blocks[0].shape
    count = len(layout)
    picked = jax.ShapeDtypeStruct((count * capacity, features), jnp.bfloat16)
    return pl.pallas_call(
        functools.partial(dispatch_kernel, capacity, layout),
        out_shape=(picked, picked),
        in_specs=[
            pl.BlockSpec(memory_space=pltpu.SMEM),
            pl.BlockSpec(memory_space=pltpu.VMEM),
        ]
        + [pl.BlockSpec(memory_space=pltpu.HBM)] * len(blocks),
        out_specs=[pl.BlockSpec(memory_space=pltpu.VMEM)] * 2,
        scratch_shapes=[
            vmem((count, rows, features), jnp.bfloat16),
            pltpu.SemaphoreType.DMA((count, 2)),
        ],
        compiler_params=pltpu.CompilerParams(vmem_limit_bytes=10 * 1024 * 1024),
        cost_estimate=SHORT,
        name="dispatch",
    )(section, code, *blocks)


def send_home(part, codes, capacity):
    size = lax.axis_size(("expert", "dp"))
    arrived = []
    for place, code in enumerate(codes):
        block = part[place * capacity : (place + 1) * capacity]
        if code:
            block = lax.ppermute(block, ("expert", "dp"), [(i, i ^ code) for i in range(size)])
        arrived.append(block)
    return arrived


def combine_kernel(count, split, section_ref, position_ref, gates_ref, *refs):
    blocks = refs[:count]
    outs, (held, total) = refs[count:-2], refs[-2:]
    capacity, features = blocks[0].shape
    position = position_ref[...]
    slot = lax.broadcasted_iota(jnp.int32, (position.shape[0], count * capacity), 1)
    picks = [
        jnp.where(position[:, k : k + 1] == slot, 1.0, 0.0).astype(jnp.bfloat16) for k in range(2)
    ]
    for i, block in enumerate(blocks):
        held[i * capacity : (i + 1) * capacity, :] = block[...]
    pick = jnp.concatenate(picks, axis=0)
    rows = position.shape[0]
    both = jnp.dot(pick, held[...], preferred_element_type=jnp.float32)
    total[...] = gates_ref[:, 0:1] * both[:rows] + gates_ref[:, 1:2] * both[rows:]
    if split == 1:
        outs[0][...] = total[...].astype(outs[0].dtype)
        return
    sent_ref, kept_first, kept_second = outs
    width = features // split
    for step, out_ref in enumerate((kept_first, sent_ref.at[0], kept_second, sent_ref.at[1])):
        start = pl.multiple_of((section_ref[0] ^ step) * width, width)
        out_ref[...] = total[:, pl.ds(start, width)].astype(out_ref.dtype)


def combine(section, position, gates, blocks, split):
    capacity, features = blocks[0].shape
    rows = position.shape[0]
    count = len(blocks)
    width = features // split
    kept = jax.ShapeDtypeStruct((rows, width), jnp.float32)
    if split == 1:
        out_shape = (jax.ShapeDtypeStruct((rows, width), jnp.bfloat16),)
    else:
        out_shape = (jax.ShapeDtypeStruct((2, rows, width), jnp.bfloat16), kept, kept)
    full = pl.BlockSpec(memory_space=pltpu.VMEM)
    return pl.pallas_call(
        functools.partial(combine_kernel, count, split),
        out_shape=out_shape,
        in_specs=[pl.BlockSpec(memory_space=pltpu.SMEM)] + [full] * (2 + count),
        out_specs=[full] * len(out_shape),
        scratch_shapes=[
            vmem((count * capacity, features), jnp.bfloat16),
            vmem((rows, features), jnp.float32),
        ],
        compiler_params=pltpu.CompilerParams(vmem_limit_bytes=14 * 1024 * 1024),
        cost_estimate=SHORT,
        name="combine",
    )(section, position, gates, *blocks)


def memory_kernel(count, section_ref, tokens_ref, gain_ref, *refs):
    slices, out_ref, mixed = refs[:count], refs[count], refs[count + 1]
    me = section_ref[0]
    width = slices[0].shape[1]
    for step, piece in enumerate(slices):
        owner = me ^ step
        mixed[:, pl.ds(pl.multiple_of(owner * width, width), width)] = piece[...].astype(
            jnp.float32
        )
    values = tokens_ref[...].astype(jnp.float32) + mixed[...]
    out_ref[...] = normalize(values, gain_ref[...]).astype(jnp.bfloat16)


def make_memory(me, tokens, slices, gain):
    return pl.pallas_call(
        functools.partial(memory_kernel, len(slices)),
        out_shape=jax.ShapeDtypeStruct(tokens.shape, jnp.bfloat16),
        in_specs=[
            pl.BlockSpec(memory_space=pltpu.SMEM),
        ]
        + [pl.BlockSpec(memory_space=pltpu.VMEM)] * (2 + len(slices)),
        out_specs=pl.BlockSpec(memory_space=pltpu.VMEM),
        scratch_shapes=[vmem(tokens.shape, jnp.float32)],
        compiler_params=pltpu.CompilerParams(vmem_limit_bytes=8 * 1024 * 1024),
        cost_estimate=SHORT,
        name="memory",
    )(me, tokens, gain[None], *slices)


def normed_kernel(y_ref, states_ref, gain_ref, own_ref, other_ref):
    values = normalize(states_ref[...].astype(jnp.float32), gain_ref[...]).astype(jnp.bfloat16)
    width = own_ref.shape[1]
    for out_ref, first in ((own_ref, y_ref[0] == 0), (other_ref, y_ref[0] == 1)):
        out_ref[...] = jnp.where(first, values[:, :width], values[:, width:])


def normed_halves(y, states, gain):
    rows, features = states.shape
    full = pl.BlockSpec(memory_space=pltpu.VMEM)
    return pl.pallas_call(
        normed_kernel,
        out_shape=(jax.ShapeDtypeStruct((rows, features // 2), jnp.bfloat16),) * 2,
        in_specs=[pl.BlockSpec(memory_space=pltpu.SMEM), full, full],
        out_specs=[full] * 2,
        compiler_params=pltpu.CompilerParams(vmem_limit_bytes=12 * 1024 * 1024),
        cost_estimate=SHORT,
        name="normed",
    )(y.astype(jnp.int32).reshape(1), states, gain)


def attend_kernel(place_ref, lengths_ref, query_ref, *refs):
    near_ref, far_ref, key_own, key_other, value_own, value_other, out_ref = refs[:7]
    source, key_weight, value_weight, keys, values, sems = refs[7:]
    y, core, sentence = place_ref[0], place_ref[1], place_ref[2]
    rows = near_ref.shape[0]
    depth = key_own.shape[0]
    moves = [
        (near_ref, source.at[pl.ds(0, rows)]),
        (far_ref, source.at[pl.ds(rows, rows)]),
        (key_own, key_weight.at[y]),
        (key_other, key_weight.at[1 - y]),
        (value_own, value_weight.at[y]),
        (value_other, value_weight.at[1 - y]),
    ]
    copies = [
        pltpu.make_async_copy(here, there, sems.at[i]) for i, (here, there) in enumerate(moves)
    ]
    for copy in copies:
        copy.start()

    def linear(weight, result):
        total = jnp.dot(source[:, :depth], weight[0], preferred_element_type=jnp.float32)
        total += jnp.dot(source[:, depth:], weight[1], preferred_element_type=jnp.float32)
        result[...] = total.astype(jnp.bfloat16)

    for copy in copies[:4]:
        copy.wait()
    linear(key_weight, keys)
    for copy in copies[4:]:
        copy.wait()
    linear(value_weight, values)

    column = lax.broadcasted_iota(jnp.int32, (query_ref.shape[0], 2 * rows), 1)
    position = jnp.where(column < rows, column + core * rows, column - core * rows)
    valid = position < lengths_ref[sentence]
    for head in range(query_ref.shape[1] // HEAD_DIM):
        span = slice(head * HEAD_DIM, (head + 1) * HEAD_DIM)
        scores = contract_last(query_ref[:, span], keys[:, span]) * HEAD_DIM ** (-0.5)
        scores = jnp.where(valid, scores, -1e30)
        weights = jnp.exp(scores - jnp.max(scores, axis=-1, keepdims=True))
        probs = (weights / jnp.sum(weights, axis=-1, keepdims=True)).astype(jnp.bfloat16)
        result = jnp.dot(probs, values[:, span], preferred_element_type=jnp.float32)
        out_ref[:, span] = result.astype(jnp.bfloat16)


def attend_sentence(place, lengths, query, near, far, key_parts, value_pair):
    rows, features = near.shape
    depth, width = key_parts[0].shape
    hold = pl.BlockSpec(memory_space=pltpu.HBM)
    smem = pl.BlockSpec(memory_space=pltpu.SMEM)
    full = pl.BlockSpec(memory_space=pltpu.VMEM)
    return pl.pallas_call(
        attend_kernel,
        out_shape=jax.ShapeDtypeStruct(query.shape, jnp.bfloat16),
        in_specs=[smem, smem, full] + [hold] * 6,
        out_specs=full,
        scratch_shapes=[
            vmem((2 * rows, features), jnp.bfloat16),
            vmem((2, depth, width), jnp.bfloat16),
            vmem((2, depth, width), jnp.bfloat16),
            vmem((2 * rows, width), jnp.bfloat16),
            vmem((2 * rows, width), jnp.bfloat16),
            pltpu.SemaphoreType.DMA((6,)),
        ],
        compiler_params=pltpu.CompilerParams(vmem_limit_bytes=56 * 1024 * 1024),
        cost_estimate=SHORT,
        name="attend_sentence",
    )(place, lengths, query, near, far, *key_parts, *value_pair)


def project_kernel(place_ref, mine_ref, done_ref, own_ref, other_ref, *refs):
    sent_mine, sent_other, kept_mine, kept_other, context = refs
    y, core, x = place_ref[0], place_ref[1], place_ref[2]
    targets = mine_ref.shape[0]
    for part, sentence in ((mine_ref, x), (done_ref, 1 - x)):
        context[pl.ds(pl.multiple_of(sentence * targets, targets), targets), :] = part[...]
    columns = kept_mine.shape[1]
    outs = ((sent_mine, kept_mine), (sent_other, kept_other))

    def write(weight_ref, chosen):
        for side, out_ref in zip((1 - core, core), chosen):
            span = pl.ds(pl.multiple_of(side * columns, columns), columns)
            part = jnp.dot(context[...], weight_ref[:, span], preferred_element_type=jnp.float32)
            out_ref[...] = part.astype(out_ref.dtype)

    @pl.when(x == y)
    def _():
        write(own_ref, outs[0])
        write(other_ref, outs[1])

    @pl.when(x != y)
    def _():
        write(other_ref, outs[0])
        write(own_ref, outs[1])


def project(place, mine, done, out_own, out_other):
    targets, width = 2 * mine.shape[0], mine.shape[1]
    columns = out_own.shape[1] // 2
    full = pl.BlockSpec(memory_space=pltpu.VMEM)
    sent = jax.ShapeDtypeStruct((targets, columns), jnp.bfloat16)
    kept = jax.ShapeDtypeStruct((targets, columns), jnp.float32)
    return pl.pallas_call(
        project_kernel,
        out_shape=(sent, sent, kept, kept),
        in_specs=[pl.BlockSpec(memory_space=pltpu.SMEM)] + [full] * 4,
        out_specs=[full] * 4,
        scratch_shapes=[vmem((targets, width), jnp.bfloat16)],
        compiler_params=pltpu.CompilerParams(vmem_limit_bytes=16 * 1024 * 1024),
        cost_estimate=SHORT,
        name="project",
    )(place, mine, done, out_own, out_other)


def slope_kernel(codes, here_ref, own_ref, core_ref, rise_own, rise_core, out_ref, slope, *refs):
    grads, rise, weight_out, sems = refs
    rows = own_ref.shape[0]
    hidden = weight_out.shape[0]
    chunk = hidden // 4
    moves = []
    block = 2 * rows // len(codes)
    for order, code in enumerate(codes):
        source = here_ref[0] ^ code
        there = pl.ds(pl.multiple_of(source * block, 16), block)
        here = pl.ds(order * block % rows, block)
        own = order * block < rows
        moves.append(((own_ref if own else core_ref).at[here], grads.at[there]))
        moves.append(((rise_own if own else rise_core).at[here], rise.at[there]))
    for part in range(4):
        span = pl.ds(part * chunk, chunk)
        moves.append((out_ref.at[span], weight_out.at[span]))
    copies = [
        pltpu.make_async_copy(here, there, sems.at[i]) for i, (here, there) in enumerate(moves)
    ]
    for copy in copies:
        copy.start()
    for copy in copies[:-4]:
        copy.wait()
    for part in range(4):
        copies[part - 4].wait()
        span = slice(part * chunk, (part + 1) * chunk)
        back = contract_last(grads[...], weight_out[span, :])
        slope[:, span] = (back * rise[:, span]).astype(jnp.bfloat16)


def expert_slope(here, codes, grads_own, grads_core, rise_own, rise_core, weight_out):
    rows = 2 * grads_own.shape[0]
    hidden, features = weight_out.shape
    hold = pl.BlockSpec(memory_space=pltpu.HBM)
    return pl.pallas_call(
        functools.partial(slope_kernel, codes),
        out_shape=jax.ShapeDtypeStruct((rows, hidden), jnp.bfloat16),
        in_specs=[pl.BlockSpec(memory_space=pltpu.SMEM)] + [hold] * 5,
        out_specs=pl.BlockSpec(memory_space=pltpu.VMEM),
        scratch_shapes=[
            vmem((rows, features), jnp.bfloat16),
            vmem((rows, hidden), jnp.float32),
            vmem((hidden, features), jnp.bfloat16),
            pltpu.SemaphoreType.DMA((4 + 2 * len(codes),)),
        ],
        compiler_params=pltpu.CompilerParams(vmem_limit_bytes=56 * 1024 * 1024),
        cost_estimate=SHORT,
        name="expert_slope",
    )(here, grads_own, grads_core, rise_own, rise_core, weight_out)


def backward_kernel(split, section_ref, slope_ref, in_ref, sent_ref, kept_first, kept_second, *refs):
    weight_in, sems = refs
    width = weight_in.shape[0] // split
    outs = (sent_ref.at[0], sent_ref.at[1], kept_first, kept_second)
    spans, copies = [], []
    for i, step in enumerate((1, 3, 0, 2)):
        start = pl.multiple_of((section_ref[0] ^ step) * width, width)
        spans.append(pl.ds(start, width))
        copies.append(
            pltpu.make_async_copy(in_ref.at[spans[i]], weight_in.at[spans[i]], sems.at[i])
        )
    for copy in copies:
        copy.start()
    for copy, span, out_ref in zip(copies, spans, outs):
        copy.wait()
        part = contract_last(slope_ref[...], weight_in[span, :])
        out_ref[...] = part.astype(out_ref.dtype)


def expert_backward(section, slope, weight_in, split):
    rows, hidden = slope.shape
    features = weight_in.shape[0]
    width = features // split
    full = pl.BlockSpec(memory_space=pltpu.VMEM)
    kept = jax.ShapeDtypeStruct((rows, width), jnp.float32)
    return pl.pallas_call(
        functools.partial(backward_kernel, split),
        out_shape=(jax.ShapeDtypeStruct((2, rows, width), jnp.bfloat16), kept, kept),
        in_specs=[pl.BlockSpec(memory_space=pltpu.SMEM), full, pl.BlockSpec(memory_space=pltpu.HBM)],
        out_specs=[full] * 3,
        scratch_shapes=[
            vmem((features, hidden), jnp.bfloat16),
            pltpu.SemaphoreType.DMA((split,)),
        ],
        compiler_params=pltpu.CompilerParams(vmem_limit_bytes=56 * 1024 * 1024),
        cost_estimate=SHORT,
        name="expert_backward",
    )(section, slope, weight_in)


def small_body(
    tokens,
    expert_ids,
    gate_weights,
    out_grad,
    inner_weight,
    outer_weight,
    final_gain,
    dec_states,
    src_lengths,
    tgt_lengths,
    norm_gain,
    query_weight,
    key_weight,
    value_weight,
    out_weight,
):
    token_count, feature_count = tokens.shape
    group_size = lax.axis_size(("expert", "dp"))
    capacity = 3 * token_count // group_size
    here = lax.axis_index(("expert", "dp"))
    y = lax.axis_index("expert")
    d = lax.axis_index("dp")
    section = lax.axis_index("section")
    sections = lax.axis_size("section")
    half = feature_count // 2
    weight_in = inner_weight[0]
    weight_out = outer_weight[0]
    key_own, value_own, out_own = key_weight[0], value_weight[0], out_weight[0]
    query_own = query_weight[0]

    size = group_size
    near_codes = (0, 2, 4, 6)
    core_codes = (1, 3, 5, 7)
    core, x = d % 2, d // 2
    which_section = section.astype(jnp.int32).reshape(1)

    token_y = swap(tokens, "expert", 1)
    token_x = swap(tokens, "dp", 2)
    row = lax.broadcasted_iota(jnp.int32, (token_count, token_count), 0)
    column = lax.broadcasted_iota(jnp.int32, (token_count, token_count), 1)
    named = expert_ids[:, :, None] == jnp.arange(size, dtype=jnp.int32)[None, None, :]
    either = (named[:, 0] | named[:, 1]).astype(jnp.bfloat16)
    earlier = jnp.dot(
        (column < row).astype(jnp.bfloat16), either, preferred_element_type=jnp.float32
    ).astype(jnp.int32)
    rank = jnp.sum(jnp.where(named, earlier[:, None, :], 0), axis=2)
    codes_of = expert_ids ^ here
    position = ((codes_of >> 1) + 4 * (codes_of & 1)) * capacity + rank

    ids_own = expert_ids.T
    ids_x, ids_y = swap(ids_own, "dp", 2), swap(ids_own, "expert", 1)
    ids_far = swap(ids_x, "expert", 1)
    token_far = swap(gate(token_y, ids_x, ids_y), "dp", 2)

    side = lax.rem(section, 2)
    share = token_count // 2
    grad_half = lax.dynamic_slice_in_dim(out_grad, side * share, share, 0)
    half_y = swap(gate(grad_half, token_y), "expert", 1)
    states = dec_states[0]
    normed_own, asked = normed_halves(y, states, norm_gain)
    asked_here = swap(gate(asked, half_y), "expert", 1)
    query_there = jnp.dot(asked_here, query_own, preferred_element_type=jnp.float32)
    other_y = swap(half_y, "section", 1)

    ids = jnp.stack([ids_own, ids_x, ids_y, ids_far])
    named_there = jnp.concatenate([(ids == here).any(axis=1), (ids == (here ^ 1)).any(axis=1)])
    before = jnp.dot(
        named_there.astype(jnp.bfloat16),
        (row < column).astype(jnp.bfloat16),
        preferred_element_type=jnp.float32,
    ).astype(jnp.int32)
    code = jnp.where(named_there, before, -1)

    def forward(rows, *after):
        pre_act = jnp.dot(rows, weight_in, preferred_element_type=jnp.float32)
        hidden = jax.nn.gelu(gate(pre_act, *after)).astype(jnp.bfloat16)
        part = jnp.dot(hidden, weight_out, preferred_element_type=jnp.float32)
        return pre_act, part.astype(jnp.bfloat16)

    def slope_of(pre_act):
        return jax.vjp(jax.nn.gelu, pre_act)[1](jnp.ones_like(pre_act))[0]

    rows_own, rows_sent = dispatch(
        which_section,
        gate(code, asked),
        [tokens, token_x, token_y, token_far],
        tuple(((place, 0, token_count, None),) for place in range(4)),
        capacity,
    )
    rows_core = swap(rows_sent, "dp", 1)
    pre_own, part_own = forward(rows_own, other_y)
    pre_core, part_core = forward(gate(rows_core, part_own))
    home = send_home(part_own, near_codes, capacity) + send_home(part_core, core_codes, capacity)
    grad_y = jnp.concatenate([gate(half_y, home[4]), other_y], axis=0)

    rise_own, rise_core = slope_of(gate(pre_own, home[1])), slope_of(gate(pre_core, home[1]))
    held_gates = gate(gate_weights, rise_own, rise_core, query_there, grad_y)
    sent_pair, first, second = combine(which_section, position, held_gates, home, sections)
    from_pair = swap(sent_pair, "section", 1)
    query_back = swap(gate(query_there.astype(jnp.bfloat16), home[5], home[6]), "expert", 1)
    grad_x = swap(gate(out_grad, home[5]), "dp", 2)
    grad_far = swap(gate(grad_y, first), "dp", 2)
    to_other = (second + from_pair[1].astype(jnp.float32)).astype(jnp.bfloat16)
    from_other = swap(to_other, "section", 2)
    mixed_sum = gate(first, query_back) + from_pair[0].astype(jnp.float32)
    mixed_slice = (mixed_sum + from_other.astype(jnp.float32)).astype(jnp.bfloat16)
    key_other = swap(gate(key_own, first), "expert", 1)
    mixed_near = swap(mixed_slice, "section", 1)
    grads_own, grads_sent = dispatch(
        which_section,
        gate(code, mixed_near),
        [out_grad, grad_x, grad_y, grad_far],
        (
            ((0, 0, token_count, None),),
            ((1, 0, token_count, None),),
            ((2, 0, share, 0), (2, share, share, 1)),
            ((3, 0, share, 0), (3, share, share, 1)),
        ),
        capacity,
    )
    grads_core = swap(grads_sent, "dp", 1)
    slope = expert_slope(
        here.astype(jnp.int32).reshape(1),
        near_codes + core_codes,
        grads_own,
        grads_core,
        rise_own,
        rise_core,
        weight_out,
    )
    back_pair, back_first, back_second = expert_backward(
        which_section, slope, weight_in, sections
    )
    mixed_far = swap(jnp.stack([mixed_slice, gate(mixed_near, key_other)]), "section", 2)
    slices = [mixed_slice, mixed_near, mixed_far[0], mixed_far[1]]

    value_other = swap(gate(value_own, mixed_near, key_other), "expert", 1)

    query_here = jnp.dot(normed_own, query_own, preferred_element_type=jnp.float32)
    query = (query_here + query_back.astype(jnp.float32)).astype(jnp.bfloat16)

    memory = make_memory(which_section, tokens, slices, final_gain)
    out_other = swap(gate(out_own, memory), "expert", 1)
    memory_x = swap(memory, "dp", 2)
    memory_core = swap(memory, "dp", 1)

    def sentence(which, near, far, *after):
        place = gate(jnp.stack([y, core, which]).astype(jnp.int32), *after)
        rows_of = lax.dynamic_slice_in_dim(query, which * TGT_LEN, TGT_LEN, 0)
        parts = (key_own, key_other), (value_own, value_other)
        return attend_sentence(place, src_lengths, rows_of, near, far, *parts)

    back_from_pair = swap(back_pair, "section", 1)
    back_to_other = (back_second + back_from_pair[1].astype(jnp.float32)).astype(jnp.bfloat16)
    back_from_other = swap(back_to_other, "section", 2)
    backward_sum = back_first + back_from_pair[0].astype(jnp.float32)
    backward_sum = backward_sum + back_from_other.astype(jnp.float32)
    context_own = sentence(x, memory, memory_core)
    memory_far = swap(gate(memory_x, context_own), "dp", 1)
    context_other = sentence(1 - x, memory_x, memory_far)
    place = jnp.stack([y, core, x]).astype(jnp.int32)
    sent_mine, sent_other, kept_mine, kept_other = project(
        place, context_own, context_other, out_own, out_other
    )

    core_other = swap(sent_other, "dp", 1)
    core_mine = swap(sent_mine, "dp", 1)
    last = gate(kept_other, back_from_other) + core_other.astype(jnp.float32)
    from_x = swap(last.astype(jnp.bfloat16), "dp", 2)
    attended = kept_mine + core_mine.astype(jnp.float32) + from_x.astype(jnp.float32)
    dec_out = add_residual(attended, states, tgt_lengths)

    grads_home = exchange(gate(backward_sum.astype(jnp.bfloat16), last), group_size, capacity)
    natural = expert_ids * capacity + rank
    (token_grad,) = combine(
        which_section, natural, gate_weights, [grads_home], 1
    )
    return (dec_out[None], token_grad)


def add_residual(attended, states, tgt_lengths):
    my_columns = attended.shape[1]
    residual = lax.dynamic_slice_in_dim(
        states, lax.axis_index("dp") * my_columns, my_columns, 1
    ).astype(jnp.float32)
    row_mask = (jnp.arange(TGT_LEN, dtype=jnp.int32)[None, :] < tgt_lengths[:, None]).reshape(-1, 1)
    return (residual + jnp.where(row_mask, attended, 0.0)).astype(jnp.bfloat16)


def body(
    tokens,
    expert_ids,
    gate_weights,
    out_grad,
    inner_weight,
    outer_weight,
    final_gain,
    dec_states,
    src_lengths,
    tgt_lengths,
    norm_gain,
    query_weight,
    key_weight,
    value_weight,
    out_weight,
):
    token_count, feature_count = tokens.shape
    group_size = lax.axis_size(("expert", "dp"))
    capacity = 3 * token_count // group_size
    slots = group_size * capacity

    named = expert_ids[:, :, None] == jnp.arange(group_size, dtype=jnp.int32)[None, None, :]
    either = (named[:, 0] | named[:, 1]).astype(jnp.bfloat16)
    row = lax.broadcasted_iota(jnp.int32, (token_count, token_count), 0)
    column = lax.broadcasted_iota(jnp.int32, (token_count, token_count), 1)
    earlier = jnp.dot(
        (column < row).astype(jnp.bfloat16), either, preferred_element_type=jnp.float32
    ).astype(jnp.int32)
    rank = jnp.sum(jnp.where(named, earlier[:, None, :], 0), axis=2)
    position = expert_ids * capacity + rank
    pick_first = slot_matrix(position[:, 0], slots)
    pick_second = slot_matrix(position[:, 1], slots)
    fill = (pick_first + pick_second).T

    def place(values):
        return jnp.dot(fill, values, preferred_element_type=jnp.float32).astype(jnp.bfloat16)

    def combine(arrived):
        first = jnp.dot(pick_first, arrived, preferred_element_type=jnp.float32)
        second = jnp.dot(pick_second, arrived, preferred_element_type=jnp.float32)
        return gate_weights[:, :1] * first + gate_weights[:, 1:] * second

    weight_in = inner_weight[0]
    weight_out = outer_weight[0]
    arrived_rows = exchange(place(tokens), group_size, capacity)
    pre_act = jnp.dot(arrived_rows, weight_in, preferred_element_type=jnp.float32)
    hidden = jax.nn.gelu(pre_act).astype(jnp.bfloat16)
    forward_part = jnp.dot(hidden, weight_out, preferred_element_type=jnp.float32)
    arrived_grads = exchange(place(out_grad), group_size, capacity)
    outputs_home = exchange(forward_part.astype(jnp.bfloat16), group_size, capacity)
    mixed_slice = sum_sections(combine(outputs_home)).astype(jnp.bfloat16)
    mixed = gather_sections(mixed_slice).astype(jnp.float32)
    memory = normalize(tokens.astype(jnp.float32) + mixed, final_gain).astype(jnp.bfloat16)

    back = contract_last(arrived_grads, weight_out)
    slope = jax.vjp(jax.nn.gelu, pre_act)[1](back)[0].astype(jnp.bfloat16)
    backward_part = contract_last(slope, weight_in)
    backward_slice = sum_sections(backward_part).astype(jnp.bfloat16)
    grads_home = exchange(backward_slice, group_size, capacity)
    token_grad = combine(grads_home).astype(jnp.bfloat16)

    states = dec_states[0]
    normed = normalize(states.astype(jnp.float32), norm_gain[0]).astype(jnp.bfloat16)
    full_query = gather_weight(query_weight[0], 0)
    full_key = gather_weight(key_weight[0], 0)
    full_value = gather_weight(value_weight[0], 0)
    full_out = gather_weight(out_weight[0], 1)
    query_sum = jnp.dot(normed, full_query, preferred_element_type=jnp.float32)
    source = gather_rows(memory, "dp")
    key_sum = jnp.dot(source, full_key, preferred_element_type=jnp.float32)
    value_sum = jnp.dot(source, full_value, preferred_element_type=jnp.float32)
    key_mask = jnp.arange(SRC_LEN, dtype=jnp.int32)[None, :] < src_lengths[:, None]
    context = attend(
        query_sum.astype(jnp.bfloat16),
        key_sum.astype(jnp.bfloat16),
        value_sum.astype(jnp.bfloat16),
        key_mask,
    )
    attended = sum_heads(jnp.dot(context, full_out, preferred_element_type=jnp.float32))
    dec_out = add_residual(attended, states, tgt_lengths)
    return (dec_out[None], token_grad)


def solution(mesh):
    in_specs = (
        P(("expert", "dp"), None),
        P(("expert", "dp"), None),
        P(("expert", "dp"), None),
        P(("expert", "dp"), None),
        P(("expert", "dp"), None, "section"),
        P(("expert", "dp"), "section", None),
        P(),
        P("section", "expert", None),
        P("expert"),
        P("expert"),
        P("section", None),
        P("section", "expert", "dp"),
        P("section", "expert", "dp"),
        P("section", "expert", "dp"),
        P("section", "dp", "expert"),
    )
    out_specs = (P("section", "expert", "dp"), P(("expert", "dp"), "section"))
    small = (mesh.shape["section"], mesh.shape["expert"], mesh.shape["dp"]) == (4, 2, 4)
    chosen = small_body if small else body
    return jax.shard_map(chosen, mesh=mesh, in_specs=in_specs, out_specs=out_specs, check_vma=False)
```
